32 devices in a mesh: section: 2 (over core), seq: 4 (over y, x), fsdp: 4 (over z).
Axes of the slice: x: 2, y: 2, z: 4, core: 2. Of those that a mesh axis runs over, the one named last changes fastest.
Arguments:
- inputs: bfloat16 [2, 1024, 1024], P(None, ('seq', 'fsdp')), may hold values from -6 to 6
- cotangent: bfloat16 [2, 1024, 1024], P(None, ('seq', 'fsdp')), may hold values from -6 to 6
- segment_ids: int32 [2, 1024], replicated, may hold values from 0 to 22, as said below
- ln1_gain: bfloat16 [2, 1024], P('section', 'fsdp'), may hold values from 0.5 to 1.5
- ln1_bias: bfloat16 [2, 1024], P('section', 'fsdp'), may hold values from -1 to 1
- w_qkv: bfloat16 [2, 1024, 3072], P('section', 'fsdp'), may hold values from -0.25 to 0.25
- b_query: bfloat16 [2, 1024], P('section', 'fsdp'), may hold values from -1.5 to 1.5
- b_value: bfloat16 [2, 1024], P('section', 'fsdp'), may hold values from -1.5 to 1.5
- w_out: bfloat16 [2, 1024, 1024], P('section', 'fsdp'), may hold values from -0.75 to 0.75
- b_out: bfloat16 [2, 1024], P('section', 'fsdp'), may hold values from -1.5 to 1.5
- ln2_gain: bfloat16 [2, 1024], P('section', 'fsdp'), may hold values from 0.5 to 1.5
- ln2_bias: bfloat16 [2, 1024], P('section', 'fsdp'), may hold values from -1 to 1
- w_fc: bfloat16 [2, 1024, 4096], P('section', 'fsdp'), may hold values from -0.1875 to 0.1875
- b_fc: bfloat16 [2, 4096], P('section', 'fsdp'), may hold values from -1.5 to 1.5
- w_proj: bfloat16 [2, 4096, 1024], P('section', 'fsdp'), may hold values from -0.125 to 0.125
- b_proj: bfloat16 [2, 1024], P('section', 'fsdp'), may hold values from -1.5 to 1.5
Outputs:
- relay_ends: float32 [2, 2, 1024, 1024], P('section', None, ('seq', 'fsdp'))
- grad_ln1_gain: float32 [2, 1024], P('section', ('seq', 'fsdp'))
- grad_ln1_bias: float32 [2, 1024], P('section', ('seq', 'fsdp'))
- grad_w_qkv: float32 [2, 1024, 3072], P('section', ('seq', 'fsdp'))
- grad_b_query: float32 [2, 1024], P('section', ('seq', 'fsdp'))
- grad_b_value: float32 [2, 1024], P('section', ('seq', 'fsdp'))
- grad_w_out: float32 [2, 1024, 1024], P('section', ('seq', 'fsdp'))
- grad_b_out: float32 [2, 1024], P('section', ('seq', 'fsdp'))
- grad_ln2_gain: float32 [2, 1024], P('section', ('seq', 'fsdp'))
- grad_ln2_bias: float32 [2, 1024], P('section', ('seq', 'fsdp'))
- grad_w_fc: float32 [2, 1024, 4096], P('section', ('seq', 'fsdp'))
- grad_b_fc: float32 [2, 4096], P('section', ('seq', 'fsdp'))
- grad_w_proj: float32 [2, 4096, 1024], P('section', ('seq', 'fsdp'))
- grad_b_proj: float32 [2, 1024], P('section', ('seq', 'fsdp'))
The draws below stay inside these ranges and needn't reach their ends.
Inputs may be any that keep to these rules, and one draw needn't show every extreme that they name: `segment_ids`: each row numbers its documents in order of position, the first 22 and each next one less; every document has 51 to 512 tokens and in every row the first or the second has exactly 512; the tokens after the row's last whole document are padding, numbered 0.
All inputs are finite; a program needn't handle non-finite values.
Results may differ from the reference program's by a relative error of at most 0.024.
Values may be sent and summed in bfloat16 or wider, within the bound.
No kernel may reach another device: no remote copies, remote signals or barrier semaphores. Data moves between devices by JAX's collectives and lax.ppermute only.
A program may use at most 192 MiB of HBM per device.

```python
import jax
import jax.numpy as jnp
from jax import lax

D = 1024
H = 16
DH = 64
FF = 4096
MB = 2
SEQ_LEN = 1024
DOC_MOST = 512
DOC_LEAST = 51


def draw_segment_ids(key, part):
    key = jax.random.fold_in(key, 17)
    count = SEQ_LEN // DOC_LEAST + 2

    def one_row(row_key):
        length_key, pick_key = jax.random.split(row_key)
        lengths = jax.random.randint(length_key, (count,), DOC_LEAST, DOC_MOST + 1, dtype=jnp.int32)
        chosen = jax.random.randint(pick_key, (), 0, 2, dtype=jnp.int32)
        lengths = jnp.where(jnp.arange(count, dtype=jnp.int32) == chosen, DOC_MOST, lengths)
        bounds = jnp.cumsum(lengths).astype(jnp.int32)
        places = jnp.arange(SEQ_LEN, dtype=jnp.int32)
        number = jnp.sum((bounds[None, :] <= places[:, None]).astype(jnp.int32), axis=1)
        closing = jnp.take(bounds, jnp.minimum(number, count - 1))
        return jnp.where((closing <= SEQ_LEN) & (number < count), count - number, 0).astype(jnp.int32)
    return jax.vmap(one_row)(jax.random.split(key, MB))


def with_spikes(result, own_key, source, target, parts, factor):
    def block_of(axis_at):
        return (jnp.arange(result.shape[axis_at]) // (result.shape[axis_at] // parts)).reshape((-1,) + (1,) * (result.ndim - 1 - axis_at))

    near = jax.random.permutation(own_key, parts)[block_of(target)]
    other_side = (block_of(target) + parts // 2) % parts
    return jnp.where((block_of(source) == near) | (block_of(source) == other_side), factor * result, result)


def block_levels(rng, shape, shards, low, largest):
    gain = 1.0
    for dim, shards_of in shards:
        steps = jax.random.uniform(jax.random.fold_in(jax.random.fold_in(rng, 6), dim), (shards_of,), jnp.float32, low / len(shards), largest / len(shards))
        gain = gain * jnp.repeat(jnp.exp(steps), shape[dim] // shards_of).reshape((-1,) + (1,) * (len(shape) - 1 - dim))
    return gain


def noise(own_key, dims, deviation, bound, shards=(), held_as=jnp.bfloat16):
    result = deviation * jax.random.normal(own_key, dims, jnp.float32)
    if shards:
        result = result * block_levels(own_key, dims, shards, -0.22, 0.18)
    return jnp.clip(result, -bound, bound).astype(held_as)


def noise_with(rng, extent, scale, reach, cuts, heavy, kind=jnp.bfloat16):
    array = scale * jax.random.normal(rng, extent, jnp.float32)
    if cuts:
        array = array * block_levels(rng, extent, cuts, -0.22, 0.18)
    return jnp.clip(with_spikes(array, jax.random.fold_in(rng, 3), *heavy), -reach, reach).astype(kind)


def setup_inputs(seed: int = 0) -> dict:
    splits = jax.random.split(jax.random.key(seed), 17)
    inputs = noise(splits[0], (MB, SEQ_LEN, D), 1.0, 6.0, ((1, 16),))
    cotangent = noise_with(splits[1], (MB, SEQ_LEN, D), 1.0, 6.0, ((1, 16),), (1, 2, 16, 2.0))
    segment_ids = draw_segment_ids(jax.random.fold_in(splits[16], 71), 0)
    ln1_gain = jnp.clip(1.0 + 0.1 * jax.random.normal(splits[3], (2, D), jnp.float32), 0.5, 1.5).astype(jnp.bfloat16)
    ln1_bias = noise(splits[4], (2, D), 0.2, 1.0, ((0, 2), (1, 4)))
    w_qkv = noise(splits[5], (2, D, 3 * D), (D // 2) ** -0.5, 0.25, ((0, 2), (1, 4)))
    b_query = noise(splits[6], (2, D), 0.3, 1.5, ((0, 2), (1, 4)))
    b_value = noise(splits[7], (2, D), 0.3, 1.5, ((0, 2), (1, 4)))
    w_out = noise(splits[8], (2, D, D), (D // 16) ** -0.5, 0.75, ((0, 2), (1, 4)))
    b_out = noise(splits[9], (2, D), 0.3, 1.5, ((0, 2), (1, 4)))
    ln2_gain = jnp.clip(1.0 + 0.1 * jax.random.normal(splits[10], (2, D), jnp.float32), 0.5, 1.5).astype(jnp.bfloat16)
    ln2_bias = noise(splits[11], (2, D), 0.2, 1.0, ((0, 2), (1, 4)))
    w_fc = noise(splits[12], (2, D, FF), D ** -0.5, 0.1875, ((0, 2), (1, 4)))
    b_fc = noise(splits[13], (2, FF), 0.3, 1.5, ((0, 2), (1, 4)))
    w_proj = noise(splits[14], (2, FF, D), (FF // 2) ** -0.5, 0.125, ((0, 2), (1, 4)))
    b_proj = noise(splits[15], (2, D), 0.3, 1.5, ((0, 2), (1, 4)))
    return {"inputs": inputs, "cotangent": cotangent, "segment_ids": segment_ids, "ln1_gain": ln1_gain, "ln1_bias": ln1_bias, "w_qkv": w_qkv, "b_query": b_query, "b_value": b_value, "w_out": w_out, "b_out": b_out, "ln2_gain": ln2_gain, "ln2_bias": ln2_bias, "w_fc": w_fc, "b_fc": b_fc, "w_proj": w_proj, "b_proj": b_proj}


@jax.custom_vjp
def low(v):
    return lax.optimization_barrier(v.astype(jnp.bfloat16)).astype(jnp.float32)

@jax.custom_vjp
def low_back(v):
    return v

def low_keep(v):
    return (low(v), None)

def low_pass(kept, grad):
    return (grad,)

def back_keep(v):
    return (v, None)

def back_low(kept, grad):
    return (low(grad),)
low.defvjp(low_keep, low_pass)
low_back.defvjp(back_keep, back_low)
EPSILON = 1e-05
NEGATIVE = -1e+30

def matmul_high(left, right):
    return jnp.dot(left, right, precision=lax.Precision.HIGHEST)

def layer_norm(values, gain_vec, bias_vec):
    average = lax.optimization_barrier(jnp.mean(values, axis=-1, keepdims=True))
    centred = values - average
    variance = lax.optimization_barrier(jnp.mean(centred * centred, axis=-1, keepdims=True))
    return centred * lax.rsqrt(variance + EPSILON) * gain_vec + bias_vec

def document_mask(seg_row):
    places = jnp.arange(seg_row.shape[0], dtype=jnp.int32)
    same_doc = (seg_row[:, None] == seg_row[None, :]) & (seg_row[:, None] > 0)
    itself = places[:, None] == places[None, :]
    return (places[None, :] <= places[:, None]) & (same_doc | itself)

def heads_of(matrix):
    return matrix.reshape(SEQ_LEN, H, DH).transpose(1, 0, 2)

def section_layer(weight_set, section_index, hidden, allowed):
    gain_one, bias_one, w_mixed, bias_query, bias_value, w_output, bias_output, gain_two, bias_two, w_hidden, bias_hidden, w_back, bias_back = [weight_arr[section_index] for weight_arr in weight_set]
    normed = low(layer_norm(hidden, gain_one, bias_one))
    mixed_proj = matmul_high(normed, w_mixed)
    queries = low_back(low(mixed_proj[:, :D] + bias_query))
    key_cols = low_back(low(mixed_proj[:, D:2 * D]))
    value_cols = low_back(low(mixed_proj[:, 2 * D:] + bias_value))
    score_scale = DH ** (-0.5)

    def one_head(operands):
        query_h, key_h, value_h = operands
        scores = low_back(matmul_high(query_h, key_h.T)) * score_scale
        scores = jnp.where(allowed, scores, NEGATIVE)
        log_total = jax.nn.logsumexp(scores, axis=-1, keepdims=True)
        attn_probs = jnp.exp(scores - log_total)
        return matmul_high(low(attn_probs), value_h)
    head_out = lax.map(jax.checkpoint(one_head), (heads_of(queries), heads_of(key_cols), heads_of(value_cols)))
    attended = low_back(low(head_out.transpose(1, 0, 2).reshape(SEQ_LEN, D)))
    residual = hidden + low_back(matmul_high(attended, w_output) + bias_output)
    normed_two = low(layer_norm(residual, gain_two, bias_two))
    pre_act = low_back(matmul_high(normed_two, w_hidden) + bias_hidden)
    activated = low(jax.nn.gelu(pre_act, approximate=True))
    return residual + low_back(matmul_high(activated, w_back) + bias_back)

def reference(inputs, cotangent, segment_ids, ln1_gain, ln1_bias, w_qkv, b_query, b_value, w_out, b_out, ln2_gain, ln2_bias, w_fc, b_fc, w_proj, b_proj):
    weight_set = tuple((weight_arr.astype(jnp.float32) for weight_arr in (ln1_gain, ln1_bias, w_qkv, b_query, b_value, w_out, b_out, ln2_gain, ln2_bias, w_fc, b_fc, w_proj, b_proj)))
    doc_masks = [document_mask(segment_ids[batch_index]) for batch_index in range(MB)]

    def forward(weights_now, first_in):
        outputs = []
        for batch_index in range(MB):
            middle = low_back(low(section_layer(weights_now, 0, first_in[batch_index], doc_masks[batch_index])))
            outputs.append(section_layer(weights_now, 1, middle, doc_masks[batch_index]))
        return jnp.stack(outputs)
    section_tops, pullback = jax.vjp(forward, weight_set, inputs.astype(jnp.float32))
    weight_grads, input_grads = pullback(cotangent.astype(jnp.float32))
    relay_ends = jnp.stack([input_grads, section_tops])
    grad_gain_one, grad_bias_one, grad_mixed, grad_query, grad_value, grad_output, grad_out_bias, grad_gain_two, grad_bias_two, grad_hidden, grad_hidden_bias, grad_back, grad_back_bias = weight_grads
    return (relay_ends, grad_gain_one, grad_bias_one, grad_mixed, grad_query, grad_value, grad_output, grad_out_bias, grad_gain_two, grad_bias_two, grad_hidden, grad_hidden_bias, grad_back, grad_back_bias)
```

```python
import math

import jax
import jax.numpy as jnp
from jax import lax
from jax.experimental import pallas as pl
from jax.experimental.pallas import tpu as pltpu
from jax.sharding import PartitionSpec as P

DH = 64


EPSILON = 1e-05
NEGATIVE = -1e30


def shifted(block, axis, distance):
    devices = range(lax.axis_size(axis))
    route = [(i - distance, i) for i in devices if i - distance in devices]
    return lax.ppermute(block, axis, route)


def layer_norm(values, gain_vec, bias_vec):
    average = jnp.mean(values, axis=-1, keepdims=True)
    centred = values - average
    variance = jnp.mean(centred * centred, axis=-1, keepdims=True)
    return centred * lax.rsqrt(variance + EPSILON) * gain_vec + bias_vec


def gelu_tanh(values):
    return jax.nn.gelu(values, approximate=True)


def mask_rows(seg_row, fsdp_index, n_seq, n_fsdp, tok_rows):
    places = jnp.arange(seg_row.shape[0], dtype=jnp.int32)
    seg_grid = seg_row.reshape(n_seq, n_fsdp, tok_rows)
    place_grid = places.reshape(n_seq, n_fsdp, tok_rows)
    query_ids = lax.dynamic_index_in_dim(seg_grid, fsdp_index, 1, keepdims=False).reshape(-1)
    query_places = lax.dynamic_index_in_dim(place_grid, fsdp_index, 1, keepdims=False).reshape(-1)
    key_ids = jnp.transpose(seg_grid, (1, 0, 2)).reshape(-1)
    key_places = jnp.transpose(place_grid, (1, 0, 2)).reshape(-1)
    same_doc = (query_ids[:, None] == key_ids[None, :]) & (query_ids[:, None] > 0)
    itself = query_places[:, None] == key_places[None, :]
    return (key_places[None, :] <= query_places[:, None]) & (same_doc | itself)


def split_heads(matrix):
    return matrix.reshape(matrix.shape[0], matrix.shape[1] // DH, DH)


def block_rows(matrix, block_len):
    return matrix.reshape((matrix.shape[0] // block_len, block_len) + matrix.shape[1:])


def masked_scores(queries, key_rows, allowed):
    raw_scores = jnp.einsum(
        "qhd,khd->hqk",
        split_heads(queries),
        split_heads(key_rows),
        preferred_element_type=jnp.float32,
    )
    return jnp.where(allowed[None], raw_scores * DH ** (-0.5), NEGATIVE)


def body(
    inputs,
    cotangent,
    segment_ids,
    ln1_gain,
    ln1_bias,
    w_qkv,
    b_query,
    b_value,
    w_out,
    b_out,
    ln2_gain,
    ln2_bias,
    w_fc,
    b_fc,
    w_proj,
    b_proj,
):
    n_seq = lax.axis_size("seq")
    n_fsdp = lax.axis_size("fsdp")
    section_index = lax.axis_index("section")
    fsdp_index = lax.axis_index("fsdp")
    last_section = section_index == 1
    micro, tok_rows, width = inputs.shape
    score_scale = DH ** (-0.5)
    query_count = tok_rows * n_seq
    block_len = math.gcd(query_count, 512)

    def fetch_params():
        return (
            lax.all_gather(ln1_gain[0], "fsdp", axis=0, tiled=True),
            lax.all_gather(ln1_bias[0], "fsdp", axis=0, tiled=True),
            lax.all_gather(w_qkv[0], "fsdp", axis=0, tiled=True),
            lax.all_gather(b_query[0], "fsdp", axis=0, tiled=True),
            lax.all_gather(b_value[0], "fsdp", axis=0, tiled=True),
            lax.all_gather(w_out[0], "fsdp", axis=0, tiled=True),
            lax.all_gather(b_out[0], "fsdp", axis=0, tiled=True),
            lax.all_gather(ln2_gain[0], "fsdp", axis=0, tiled=True),
            lax.all_gather(ln2_bias[0], "fsdp", axis=0, tiled=True),
            lax.all_gather(w_fc[0], "fsdp", axis=0, tiled=True),
            lax.all_gather(b_fc[0], "fsdp", axis=0, tiled=True),
            lax.all_gather(w_proj[0], "fsdp", axis=0, tiled=True),
            lax.all_gather(b_proj[0], "fsdp", axis=0, tiled=True),
        )

    received = jnp.zeros((tok_rows, width), jnp.bfloat16)
    kept_ticks = []
    layer_outs = []
    for tick_index in range(micro + 1):
        params = fetch_params()
        batch_index = jnp.clip(tick_index - section_index, 0, micro - 1)
        seg_row = lax.dynamic_index_in_dim(segment_ids, batch_index, 0, keepdims=False)
        allowed = mask_rows(seg_row, fsdp_index, n_seq, n_fsdp, tok_rows)
        if tick_index < micro:
            first_in = inputs[tick_index].astype(jnp.float32)
        else:
            first_in = jnp.zeros((tok_rows, width), jnp.float32)
        layer_in = jnp.where(last_section, received.astype(jnp.float32), first_in)
        (
            forward_gain_one,
            forward_bias_one,
            forward_w_mixed,
            forward_bias_query,
            forward_bias_value,
            forward_w_output,
            forward_bias_output,
            forward_gain_two,
            forward_bias_two,
            forward_w_hidden,
            forward_bias_hidden,
            forward_w_back,
            forward_bias_back,
        ) = params
        forward_normed = layer_norm(
            layer_in, forward_gain_one.astype(jnp.float32), forward_bias_one.astype(jnp.float32)
        ).astype(jnp.bfloat16)
        mixed_proj = jnp.dot(forward_normed, forward_w_mixed, preferred_element_type=jnp.float32)
        bias_row = jnp.concatenate(
            [forward_bias_query, jnp.zeros_like(forward_bias_query), forward_bias_value]
        ).astype(jnp.float32)
        mixed_tok = (mixed_proj + bias_row).astype(jnp.bfloat16).reshape(tok_rows, 3, width)
        head_rows = lax.all_to_all(mixed_tok, "seq", split_axis=2, concat_axis=0, tiled=True)
        forward_queries = head_rows[:, 0]
        forward_key_rows = lax.all_gather(head_rows[:, 1], "fsdp", axis=0, tiled=True)
        forward_value_rows = lax.all_gather(head_rows[:, 2], "fsdp", axis=0, tiled=True)

        def attend_block(operands):
            query_block, allowed_block = operands
            scores = masked_scores(query_block, forward_key_rows, allowed_block)
            row_top = jnp.max(scores, axis=-1, keepdims=True)
            log_block = row_top + jnp.log(
                jnp.sum(jnp.exp(scores - row_top), axis=-1, keepdims=True)
            )
            attn_weights = jnp.exp(scores - log_block).astype(jnp.bfloat16)
            head_block = jnp.einsum(
                "hqk,khd->qhd",
                attn_weights,
                split_heads(forward_value_rows),
                preferred_element_type=jnp.float32,
            )
            return (head_block.reshape(query_block.shape).astype(jnp.bfloat16), log_block)

        head_blocks, forward_log_total = lax.map(
            attend_block, (block_rows(forward_queries, block_len), block_rows(allowed, block_len))
        )
        head_out = head_blocks.reshape(forward_queries.shape)
        forward_attended = lax.all_to_all(head_out, "seq", split_axis=0, concat_axis=1, tiled=True)
        forward_residual = (
            layer_in
            + jnp.dot(forward_attended, forward_w_output, preferred_element_type=jnp.float32)
            + forward_bias_output.astype(jnp.float32)
        )
        forward_normed_two = layer_norm(
            forward_residual,
            forward_gain_two.astype(jnp.float32),
            forward_bias_two.astype(jnp.float32),
        ).astype(jnp.bfloat16)
        forward_pre_act = jnp.dot(
            forward_normed_two, forward_w_hidden, preferred_element_type=jnp.float32
        ) + forward_bias_hidden.astype(jnp.float32)
        forward_activated = gelu_tanh(forward_pre_act).astype(jnp.bfloat16)
        layer_out = (
            forward_residual
            + jnp.dot(forward_activated, forward_w_back, preferred_element_type=jnp.float32)
            + forward_bias_back.astype(jnp.float32)
        )
        forward_kept = (
            layer_in,
            forward_normed,
            forward_queries,
            forward_key_rows,
            forward_value_rows,
            forward_log_total,
            allowed,
            forward_attended,
            forward_residual,
            forward_normed_two,
            forward_pre_act,
            forward_activated,
        )
        layer_out, kept = (layer_out, forward_kept)
        kept_ticks.append(kept)
        layer_outs.append(layer_out)
        if tick_index < micro:
            received = shifted(layer_out.astype(jnp.bfloat16), "section", 1)
    sent_back = jnp.zeros((tok_rows, width), jnp.bfloat16)
    input_grads = []
    totals = None
    for tick_index in range(micro + 1):
        params = fetch_params()
        later = kept_ticks[min(tick_index + 1, micro)]
        earlier = kept_ticks[max(tick_index - 1, 0)]
        kept = jax.tree.map(
            lambda upper, lower: jnp.where(last_section, upper, lower), later, earlier
        )
        if tick_index < micro:
            top_grad = cotangent[tick_index].astype(jnp.float32)
        else:
            top_grad = jnp.zeros((tok_rows, width), jnp.float32)
        grad_out = jnp.where(last_section, top_grad, sent_back.astype(jnp.float32))
        (
            gain_one,
            bias_one,
            w_mixed,
            bias_query,
            bias_value,
            w_output,
            bias_output,
            gain_two,
            bias_two,
            w_hidden,
            bias_hidden,
            w_back,
            bias_back,
        ) = params
        (
            backward_layer_in,
            normed,
            queries,
            key_rows,
            value_rows,
            log_total,
            backward_allowed,
            attended,
            residual,
            normed_two,
            pre_act,
            activated,
        ) = kept
        grad_back = grad_out.astype(jnp.bfloat16)
        d_w_back = jnp.einsum("cf,cd->fd", activated, grad_back, preferred_element_type=jnp.float32)
        d_bias_back = jnp.sum(grad_back.astype(jnp.float32), axis=0)
        d_activated = jnp.einsum("cd,fd->cf", grad_back, w_back, preferred_element_type=jnp.float32)
        gelu_pull = jax.vjp(gelu_tanh, pre_act)[1]
        d_pre = gelu_pull(d_activated)[0].astype(jnp.bfloat16)
        d_w_hidden = jnp.einsum("cm,cf->mf", normed_two, d_pre, preferred_element_type=jnp.float32)
        d_bias_hidden = jnp.sum(d_pre.astype(jnp.float32), axis=0)
        d_normed_two = jnp.einsum("cf,mf->cm", d_pre, w_hidden, preferred_element_type=jnp.float32)
        norm_pull_two = jax.vjp(
            layer_norm, residual, gain_two.astype(jnp.float32), bias_two.astype(jnp.float32)
        )[1]
        d_resid_part, d_gain_two, d_bias_two = norm_pull_two(d_normed_two)
        d_residual = grad_out + d_resid_part
        grad_attn = d_residual.astype(jnp.bfloat16)
        d_w_output = jnp.einsum(
            "cm,cd->md", attended, grad_attn, preferred_element_type=jnp.float32
        )
        d_bias_output = jnp.sum(grad_attn.astype(jnp.float32), axis=0)
        d_attended = jnp.einsum(
            "cd,md->cm", grad_attn, w_output, preferred_element_type=jnp.float32
        ).astype(jnp.bfloat16)
        d_head = lax.all_to_all(d_attended, "seq", split_axis=1, concat_axis=0, tiled=True)

        def grad_block(carry, operands):
            key_acc, value_acc = carry
            query_block, head_grad_block, allowed_block, log_block = operands
            scores = masked_scores(query_block, key_rows, allowed_block)
            attn_probs = jnp.exp(scores - log_block)
            d_weights = jnp.einsum(
                "qhd,khd->hqk",
                split_heads(head_grad_block),
                split_heads(value_rows),
                preferred_element_type=jnp.float32,
            )
            row_dot = jnp.sum(attn_probs * d_weights, axis=-1, keepdims=True)
            d_scores = (attn_probs * (d_weights - row_dot) * score_scale).astype(jnp.bfloat16)
            d_query_block = (
                jnp.einsum(
                    "hqk,khd->qhd",
                    d_scores,
                    split_heads(key_rows),
                    preferred_element_type=jnp.float32,
                )
                .reshape(query_block.shape)
                .astype(jnp.bfloat16)
            )
            key_acc = key_acc + jnp.einsum(
                "hqk,qhd->khd",
                d_scores,
                split_heads(query_block),
                preferred_element_type=jnp.float32,
            ).reshape(key_rows.shape)
            value_acc = value_acc + jnp.einsum(
                "hqk,qhd->khd",
                attn_probs.astype(jnp.bfloat16),
                split_heads(head_grad_block),
                preferred_element_type=jnp.float32,
            ).reshape(value_rows.shape)
            return ((key_acc, value_acc), d_query_block)

        empty_terms = (
            jnp.zeros(key_rows.shape, jnp.float32),
            jnp.zeros(value_rows.shape, jnp.float32),
        )
        (key_term, value_term), query_blocks = lax.scan(
            grad_block,
            empty_terms,
            (
                block_rows(queries, block_len),
                block_rows(d_head, block_len),
                block_rows(backward_allowed, block_len),
                log_total,
            ),
        )
        d_query = query_blocks.reshape(queries.shape)
        d_key = lax.psum_scatter(key_term, "fsdp", scatter_dimension=0, tiled=True)
        d_value = lax.psum_scatter(value_term, "fsdp", scatter_dimension=0, tiled=True)
        d_heads = jnp.stack(
            [d_query, d_key.astype(jnp.bfloat16), d_value.astype(jnp.bfloat16)], axis=1
        )
        d_mixed = lax.all_to_all(d_heads, "seq", split_axis=0, concat_axis=2, tiled=True)
        d_flat = d_mixed.reshape(tok_rows, 3 * width)
        d_w_mixed = jnp.einsum("cm,cn->mn", normed, d_flat, preferred_element_type=jnp.float32)
        d_bias_query = jnp.sum(d_mixed[:, 0].astype(jnp.float32), axis=0)
        d_bias_value = jnp.sum(d_mixed[:, 2].astype(jnp.float32), axis=0)
        d_normed = jnp.einsum("cn,mn->cm", d_flat, w_mixed, preferred_element_type=jnp.float32)
        norm_pull_one = jax.vjp(
            layer_norm,
            backward_layer_in,
            gain_one.astype(jnp.float32),
            bias_one.astype(jnp.float32),
        )[1]
        d_in_part, d_gain_one, d_bias_one = norm_pull_one(d_normed)
        d_in = d_residual + d_in_part
        d_in, local_grads = (
            d_in,
            (
                d_gain_one,
                d_bias_one,
                d_w_mixed,
                d_bias_query,
                d_bias_value,
                d_w_output,
                d_bias_output,
                d_gain_two,
                d_bias_two,
                d_w_hidden,
                d_bias_hidden,
                d_w_back,
                d_bias_back,
            ),
        )
        input_grads.append(d_in)
        shared = (
            lax.psum_scatter(local_grads[0], ("seq", "fsdp"), scatter_dimension=0, tiled=True),
            lax.psum_scatter(local_grads[1], ("seq", "fsdp"), scatter_dimension=0, tiled=True),
            lax.psum_scatter(local_grads[2], ("seq", "fsdp"), scatter_dimension=0, tiled=True),
            lax.psum_scatter(local_grads[3], ("seq", "fsdp"), scatter_dimension=0, tiled=True),
            lax.psum_scatter(local_grads[4], ("seq", "fsdp"), scatter_dimension=0, tiled=True),
            lax.psum_scatter(local_grads[5], ("seq", "fsdp"), scatter_dimension=0, tiled=True),
            lax.psum_scatter(local_grads[6], ("seq", "fsdp"), scatter_dimension=0, tiled=True),
            lax.psum_scatter(local_grads[7], ("seq", "fsdp"), scatter_dimension=0, tiled=True),
            lax.psum_scatter(local_grads[8], ("seq", "fsdp"), scatter_dimension=0, tiled=True),
            lax.psum_scatter(local_grads[9], ("seq", "fsdp"), scatter_dimension=0, tiled=True),
            lax.psum_scatter(local_grads[10], ("seq", "fsdp"), scatter_dimension=0, tiled=True),
            lax.psum_scatter(local_grads[11], ("seq", "fsdp"), scatter_dimension=0, tiled=True),
            lax.psum_scatter(local_grads[12], ("seq", "fsdp"), scatter_dimension=0, tiled=True),
        )
        totals = shared if totals is None else jax.tree.map(jnp.add, totals, shared)
        if tick_index < micro:
            sent_back = shifted(d_in.astype(jnp.bfloat16), "section", -1)
    section_tops = jnp.stack(layer_outs[1:])
    bottom_grads = jnp.stack(input_grads[1:])
    relay_ends = jnp.where(last_section, section_tops, bottom_grads)[None]
    return (relay_ends,) + tuple((grad_part[None] for grad_part in totals))


BF = jnp.bfloat16
F32 = jnp.float32
GROUP = 4
KERNEL_VMEM = 56 * 1024 * 1024


def nt(left, right):
    return lax.dot_general(left, right, (((1,), (1,)), ((), ())), preferred_element_type=F32)


def tn(left, right):
    return lax.dot_general(left, right, (((0,), (0,)), ((), ())), preferred_element_type=F32)


def nn(left, right):
    return jnp.dot(left, right, preferred_element_type=F32)


def spot(start, size):
    return pl.ds(pl.multiple_of(start, size), size)


def call(kernel, name, ids, args, outs, scratch=(), anywhere=(), cost=None):
    where = [pl.ANY if i in anywhere else pltpu.VMEM for i in range(len(args))]
    flops, nbytes = cost or (0, 0)
    nbytes = nbytes or sum(a.size * a.dtype.itemsize for a in args)
    return pl.pallas_call(
        kernel,
        name=name,
        out_shape=[jax.ShapeDtypeStruct(shape, dtype) for shape, dtype in outs],
        in_specs=[pl.BlockSpec(memory_space=pltpu.SMEM)]
        + [pl.BlockSpec(memory_space=space) for space in where],
        out_specs=[pl.BlockSpec(memory_space=pltpu.VMEM)] * len(outs),
        scratch_shapes=list(scratch),
        compiler_params=pltpu.CompilerParams(vmem_limit_bytes=KERNEL_VMEM),
        cost_estimate=pl.CostEstimate(flops=flops, bytes_accessed=nbytes, transcendentals=0),
    )(ids, *args)


def trade(blocks, axis):
    got = [blocks[0]]
    for d in range(1, GROUP):
        got.append(lax.ppermute(blocks[d], axis, [(i, i ^ d) for i in range(GROUP)]))
    return got


def gather(block, axis):
    return trade([block] * GROUP, axis)


def swap(block):
    return lax.ppermute(block, "section", [(0, 1), (1, 0)])


def normed_rows(values, gain_vec, bias_vec):
    average = jnp.mean(values, axis=-1, keepdims=True)
    centred = values - average
    variance = jnp.mean(centred * centred, axis=-1, keepdims=True)
    return centred * lax.rsqrt(variance + EPSILON) * gain_vec + bias_vec


def norm_pull(values, gain_vec, grad):
    average = jnp.mean(values, axis=-1, keepdims=True)
    centred = values - average
    variance = jnp.mean(centred * centred, axis=-1, keepdims=True)
    inverse = lax.rsqrt(variance + EPSILON)
    unit = centred * inverse
    scaled = grad * gain_vec
    first = jnp.mean(scaled, axis=-1, keepdims=True)
    second = jnp.mean(scaled * unit, axis=-1, keepdims=True)
    pulled = inverse * (scaled - first - unit * second)
    return (
        pulled,
        jnp.sum(grad * unit, axis=0, keepdims=True),
        jnp.sum(grad, axis=0, keepdims=True),
    )


def pick_mixed_kernel(ids, w_ref, mine_ref, send_ref, tiles, sem):
    s, c = ids[0], ids[2]
    width = w_ref.shape[2] // 3
    odd = (s & 1) == 1
    copies = []
    for t in range(3):
        for j in range(GROUP):
            start = t * width + j * 256 + (s >> 1) * 128
            copy = pltpu.make_async_copy(
                w_ref.at[0, :, spot(start, 128)], tiles.at[t, j], sem.at[t * GROUP + j]
            )
            copy.start()
            copies.append(copy)
    for copy in copies:
        copy.wait()

    def head(t, j):
        tile = tiles[t, j].astype(F32)
        return jnp.where(odd, tile[:, DH:], tile[:, :DH])

    def fill(ref, half):
        for i in range(2):
            j = 2 * half + i
            ref[:, i * 128 : i * 128 + 128] = jnp.concatenate(
                [head(0, j), head(1, j)], axis=1
            ).astype(BF)
        ref[:, 256:384] = jnp.concatenate(
            [head(2, 2 * half), head(2, 2 * half + 1)], axis=1
        ).astype(BF)

    fill(mine_ref, c)
    fill(send_ref, 1 - c)


def pick_rest_kernel(ids, fc_ref, proj_ref, out_ref, a_mine, a_send, p_mine, p_send, sem):
    s, c = ids[0], ids[2]
    copies = []

    def begin(source, target):
        copy = pltpu.make_async_copy(source, target, sem.at[len(copies)])
        copy.start()
        copies.append(copy)

    for a_ref, p_ref, half in ((a_mine, p_mine, c), (a_send, p_send, 1 - c)):
        begin(out_ref.at[0, spot(s * 64, 64), spot(half * 512, 512)], a_ref.at[0:64, :])
        for j in range(GROUP):
            start = j * 1024 + s * 256 + half * 128
            begin(
                fc_ref.at[0, :, spot(start, 128)],
                a_ref.at[64:320, j * 128 : (j + 1) * 128],
            )
        begin(proj_ref.at[0, spot(s * 256 + half * 128, 128), :], p_ref)
    for copy in copies:
        copy.wait()


def mixed_kernel(ids, *refs):
    x_refs, own_refs, oth_refs = refs[:4], refs[4:8], refs[8:12]
    vec = refs[12]
    out_refs, nf_ref = refs[13:17], refs[17]
    packed = refs[18]
    s, z, c = ids[0], ids[1], ids[2]
    gain_vec, bias_vec = vec[0:1, :], vec[1:2, :]
    for d in range(GROUP):
        nf_ref[d * 64 : (d + 1) * 64, :] = normed_rows(
            x_refs[d][...].astype(F32), gain_vec, bias_vec
        ).astype(BF)

    def bias_of(row, j):
        tile = vec[row : row + 1, spot(j * 256 + (s >> 1) * 128, 128)]
        return jnp.where((s & 1) == 1, tile[:, DH:], tile[:, :DH])

    empty = jnp.zeros((1, DH), F32)
    for w_refs, half in ((own_refs, c), (oth_refs, 1 - c)):
        total = jnp.zeros((GROUP * 64, 384), F32)
        for d in range(GROUP):
            total = total + nn(nf_ref[:, spot((z ^ d) * 256, 256)], w_refs[d][...])
        j = 2 * half
        row = jnp.concatenate(
            [
                bias_of(2, j),
                empty,
                bias_of(2, j + 1),
                empty,
                bias_of(3, j),
                bias_of(3, j + 1),
            ],
            axis=1,
        )
        total = total + row
        for i in range(2):
            packed[j + i, 0:256, :] = total[:, i * 128 : (i + 1) * 128].astype(BF)
            values = total[:, 256 + i * DH : 256 + (i + 1) * DH]
            packed[j + i, 256:384, :] = jnp.concatenate(
                [values[:128], values[128:]], axis=1
            ).astype(BF)
    for d in range(GROUP):
        out_refs[d][...] = packed[z ^ d]


def spread(ids, pieces, qk_ref, v_ref):
    s, z = ids[0], ids[1]
    for d in range(GROUP):
        for e in range(GROUP):
            rows = spot(((s ^ e) * GROUP + (z ^ d)) * 64, 64)
            qk_ref[rows, :] = pieces[d][e * 64 : (e + 1) * 64, :]
            lanes = slice(0, DH) if e < 2 else slice(DH, 128)
            start = 256 + (e & 1) * 64
            v_ref[rows, :] = pieces[d][start : start + 64, lanes]


def block_scores(qk_ref, seg_col, seg_row, start, size):
    stop = start + size
    queries = qk_ref[start:stop, 0:DH] * jnp.asarray(DH ** (-0.5), BF)
    scores = nt(queries, qk_ref[0:stop, DH:128])
    q_place = lax.broadcasted_iota(jnp.int32, (size, stop), 0) + start
    k_place = lax.broadcasted_iota(jnp.int32, (size, stop), 1)
    q_doc, k_doc = seg_col[start:stop, :], seg_row[:, 0:stop]
    same = (q_doc == k_doc) & (q_doc > 0)
    allowed = ((k_place <= q_place) & same) | (k_place == q_place)
    return jnp.where(allowed, scores, NEGATIVE)


def attend_kernel(ids, *refs):
    pieces, seg_col, seg_row = refs[:4], refs[4], refs[5]
    out_refs = refs[6:10]
    qk_ref, v_ref, o_ref = refs[10:13]
    s, z = ids[0], ids[1]
    spread(ids, pieces, qk_ref, v_ref)
    count = qk_ref.shape[0]
    size = 256
    for start in range(0, count, size):
        scores = block_scores(qk_ref, seg_col, seg_row, start, size)
        top = jnp.max(scores, axis=-1, keepdims=True)
        grown = jnp.exp(scores - top)
        total = jnp.sum(grown, axis=-1, keepdims=True)
        mixed = nn(grown.astype(BF), v_ref[0 : start + size, :])
        o_ref[start : start + size, :] = (mixed / total).astype(BF)
    for d in range(GROUP):
        for e in range(2):
            left = o_ref[spot(((s ^ e) * GROUP + (z ^ d)) * 64, 64), :]
            right = o_ref[spot(((s ^ (e + 2)) * GROUP + (z ^ d)) * 64, 64), :]
            out_refs[d][e * 64 : (e + 1) * 64, :] = jnp.concatenate([left, right], axis=1)


def unpacked(piece):
    return jnp.concatenate([piece[:, :DH], piece[:, DH:]], axis=0)


def head_rows(w_ref, z):
    return jnp.concatenate([w_ref[z ^ d, 0:64, :] for d in range(GROUP)], axis=0)


def output_kernel(ids, *refs):
    pieces, own_ref, oth_ref = refs[:4], refs[4], refs[5]
    out_refs, att_ref = refs[6:10], refs[10]
    z, c = ids[1], ids[2]
    att = jnp.concatenate([unpacked(pieces[d][...]) for d in range(GROUP)], axis=1)
    att_ref[...] = att
    for w_ref, half in ((own_ref, c), (oth_ref, 1 - c)):
        part = nn(att, head_rows(w_ref, z)).astype(BF)
        for d in range(GROUP):
            out_refs[d][:, spot(half * 512, 512)] = part[d * 64 : (d + 1) * 64, :]


def summed(refs):
    total = refs[0][...].astype(F32)
    for ref in refs[1:]:
        total = total + ref[...].astype(F32)
    return total


def residual_kernel(ids, *refs):
    x_ref, vec = refs[4], refs[5]
    res_ref, n_ref = refs[6], refs[7]
    res = x_ref[...].astype(F32) + summed(refs[:4]) + vec[4:5, :]
    res_ref[...] = res
    n_ref[...] = normed_rows(res, vec[5:6, :], vec[6:7, :]).astype(BF)


ROOT = math.sqrt(2.0 / math.pi)


def hidden_bias(vec, half):
    return jnp.concatenate(
        [vec[8:9, spot(j * 256 + half * 128, 128)] for j in range(GROUP)], axis=1
    )


def feed_kernel(ids, *refs):
    n_refs, a_refs, p_refs, vec = refs[:4], refs[4:6], refs[6:8], refs[8]
    out_refs = refs[9:13]
    slope_ref, act_ref, nf_ref = refs[13:16]
    c = ids[2]
    for d in range(GROUP):
        nf_ref[d * 64 : (d + 1) * 64, :] = n_refs[d][...]
    part = jnp.zeros(nf_ref.shape, F32)
    for place, half in ((0, c), (1, 1 - c)):
        cols = slice(place * 512, (place + 1) * 512)
        pre = jnp.zeros((GROUP * 64, 512), F32)
        for k in range(GROUP):
            pre = pre + nn(nf_ref[:, k * 256 : (k + 1) * 256], a_refs[place][k, 64:320, :])
        pre = pre + hidden_bias(vec, half)
        square = pre * pre
        bend = jnp.tanh(ROOT * pre * (1.0 + 0.044715 * square))
        act = (0.5 * pre * (1.0 + bend)).astype(BF)
        slope_ref[:, cols] = 0.5 * (1.0 + bend) + (0.5 * ROOT) * pre * (1.0 - bend * bend) * (
            1.0 + (3.0 * 0.044715) * square
        )
        act_ref[:, cols] = act
        w_back = p_refs[place][...].reshape(512, nf_ref.shape[1])
        part = part + nn(act, w_back)
    for d in range(GROUP):
        out_refs[d][...] = part[d * 64 : (d + 1) * 64, :].astype(BF)


def close_kernel(ids, *refs):
    res_ref, vec = refs[4], refs[5]
    out_ref, low_ref = refs[6], refs[7]
    out = res_ref[...] + summed(refs[:4]) + vec[7:8, :]
    out_ref[...] = out
    low_ref[...] = out.astype(BF)


def feed_back_kernel(ids, *refs):
    g_refs, a_refs, p_refs, slope_ref = refs[:4], refs[4:6], refs[6:8], refs[8]
    out_refs = refs[9:13]
    d_pre_ref, gf_ref = refs[13:15]
    for d in range(GROUP):
        gf_ref[d * 64 : (d + 1) * 64, :] = g_refs[d][...]
    for place in range(2):
        cols = slice(place * 512, (place + 1) * 512)
        w_back = p_refs[place][...].reshape(512, gf_ref.shape[1])
        d_pre_ref[:, cols] = (nt(gf_ref[...], w_back) * slope_ref[:, cols]).astype(BF)
    for k in range(GROUP):
        part = nt(d_pre_ref[:, 0:512], a_refs[0][k, 64:320, :])
        part = (part + nt(d_pre_ref[:, 512:1024], a_refs[1][k, 64:320, :])).astype(BF)
        for d in range(GROUP):
            out_refs[d][:, k * 256 : (k + 1) * 256] = part[d * 64 : (d + 1) * 64, :]


def norm_two_back_kernel(ids, *refs):
    res_ref, g_ref, vec = refs[4], refs[5], refs[6]
    d_res_ref, ga_ref, rows_ref = refs[7:10]
    grad = g_ref[...].astype(F32)
    pulled, d_gain, d_bias = norm_pull(res_ref[...], vec[5:6, :], summed(refs[:4]))
    d_res = grad + pulled
    low = d_res.astype(BF)
    d_res_ref[...] = d_res
    ga_ref[...] = low
    rows_ref[0:1, :] = jnp.sum(low.astype(F32), axis=0, keepdims=True)
    rows_ref[1:2, :] = d_gain
    rows_ref[2:3, :] = d_bias
    rows_ref[3:4, :] = jnp.sum(grad.astype(BF).astype(F32), axis=0, keepdims=True)
    rows_ref[4:8, :] = jnp.zeros((4, grad.shape[1]), F32)


def output_back_kernel(ids, *refs):
    g_refs, own_ref, oth_ref = refs[:4], refs[4], refs[5]
    out_refs, gf_ref = refs[6:10], refs[10]
    z, c = ids[1], ids[2]
    for d in range(GROUP):
        gf_ref[d * 64 : (d + 1) * 64, :] = g_refs[d][...]
    d_att = nt(gf_ref[:, spot(c * 512, 512)], head_rows(own_ref, z))
    d_att = d_att + nt(gf_ref[:, spot((1 - c) * 512, 512)], head_rows(oth_ref, z))
    for d in range(GROUP):
        cols = d_att[:, d * DH : (d + 1) * DH]
        out_refs[d][...] = jnp.concatenate([cols[:128], cols[128:]], axis=1).astype(BF)


def feed_grads_kernel(ids, *refs):
    act_ref, gb_ref, nf_ref, d_pre_ref, att_ref, ga_ref = refs[:6]
    keep_ref, send_ref, sums_ref = refs[6:9]
    z, c = ids[1], ids[2]
    width = gb_ref.shape[1]
    for place, out_ref, half in ((0, keep_ref, c), (1, send_ref, 1 - c)):
        cols = slice(place * 512, (place + 1) * 512)
        d_fc = tn(nf_ref[...], d_pre_ref[:, cols]).astype(BF)
        for o in range(width // 64):
            out_ref[o % GROUP, (o // GROUP) * 64 : (o // GROUP) * 64 + 64, :] = d_fc[
                o * 64 : (o + 1) * 64, :
            ]
        d_proj = tn(act_ref[:, cols], gb_ref[...]).astype(BF)
        for j in range(GROUP):
            rows = d_proj[j * 128 : (j + 1) * 128, :]
            out_ref[j, 256:384, :] = rows[:, 0:512]
            out_ref[j, 384:512, :] = rows[:, 512:1024]
        d_out = tn(att_ref[...], ga_ref[:, spot(half * 512, 512)]).astype(BF)
        for d in range(GROUP):
            out_ref[z ^ d, 512:576, :] = d_out[d * 64 : (d + 1) * 64, :]
    sums_ref[...] = jnp.sum(d_pre_ref[...].astype(F32), axis=0, keepdims=True)


def attend_back_kernel(ids, *refs):
    pieces, d_pieces, seg_col, seg_row = refs[:4], refs[4:8], refs[8], refs[9]
    out_refs = refs[10:14]
    qk_ref, v_ref, do_ref, dq_ref, dk_ref, dv_ref = refs[14:20]
    s, z = ids[0], ids[1]
    spread(ids, pieces, qk_ref, v_ref)
    for d in range(GROUP):
        for e in range(GROUP):
            rows = spot(((s ^ e) * GROUP + (z ^ d)) * 64, 64)
            lanes = slice(0, DH) if e < 2 else slice(DH, 128)
            start = (e & 1) * 64
            do_ref[rows, :] = d_pieces[d][start : start + 64, lanes]
    count = qk_ref.shape[0]
    size = 256
    for start in range(0, count, size):
        stop = start + size
        scores = block_scores(qk_ref, seg_col, seg_row, start, size)
        top = jnp.max(scores, axis=-1, keepdims=True)
        grown = jnp.exp(scores - top)
        probs = grown * (1.0 / jnp.sum(grown, axis=-1, keepdims=True))
        d_out = do_ref[start:stop, :]
        d_weights = nt(d_out, v_ref[0:stop, :])
        row_dot = jnp.sum(probs * d_weights, axis=-1, keepdims=True)
        d_scores = (probs * (d_weights - row_dot) * DH ** (-0.5)).astype(BF)
        dq_ref[start:stop, :] = nn(d_scores, qk_ref[0:stop, DH:128])
        dk = tn(d_scores, qk_ref[start:stop, 0:DH])
        dv = tn(probs.astype(BF), d_out)
        if start:
            dk_ref[0:start, :] += dk[0:start]
            dv_ref[0:start, :] += dv[0:start]
        dk_ref[start:stop, :] = dk[start:stop]
        dv_ref[start:stop, :] = dv[start:stop]
    for d in range(GROUP):
        for e in range(GROUP):
            rows = spot(((s ^ e) * GROUP + (z ^ d)) * 64, 64)
            out_refs[d][e * 64 : (e + 1) * 64, :] = jnp.concatenate(
                [dq_ref[rows, :], dk_ref[rows, :]], axis=1
            ).astype(BF)
        for e in range(2):
            left = dv_ref[spot(((s ^ e) * GROUP + (z ^ d)) * 64, 64), :]
            right = dv_ref[spot(((s ^ (e + 2)) * GROUP + (z ^ d)) * 64, 64), :]
            out_refs[d][256 + e * 64 : 320 + e * 64, :] = jnp.concatenate(
                [left, right], axis=1
            ).astype(BF)


def mixed_back_kernel(ids, *refs):
    pieces, own_refs, oth_refs = refs[:4], refs[4:8], refs[8:12]
    out_refs, dm_ref = refs[12:16], refs[16]
    held = refs[17]
    z, c = ids[1], ids[2]
    for d in range(GROUP):
        held[d] = pieces[d][...]
    for place, half in ((0, c), (1, 1 - c)):
        base = place * 384
        values = []
        for i in range(2):
            d = (2 * half + i) ^ z
            dm_ref[:, base + i * 128 : base + (i + 1) * 128] = held[d, 0:256, :]
            values.append(unpacked(held[d, 256:384, :]))
        dm_ref[:, base + 256 : base + 384] = jnp.concatenate(values, axis=1)
    for k in range(GROUP):
        part = nt(dm_ref[:, 0:384], own_refs[k][...])
        part = (part + nt(dm_ref[:, 384:768], oth_refs[k][...])).astype(BF)
        for d in range(GROUP):
            out_refs[d][:, spot((z ^ k) * 256, 256)] = part[d * 64 : (d + 1) * 64, :]


def mixed_grads_kernel(ids, *refs):
    nf_ref, dm_ref = refs[:2]
    keep_refs, send_refs, sums_ref = refs[2:6], refs[6:10], refs[10]
    held = refs[11]
    z = ids[1]
    for out_refs, cols in ((keep_refs, slice(0, 384)), (send_refs, slice(384, 768))):
        d_w = tn(nf_ref[...], dm_ref[:, cols]).astype(BF)
        for o in range(nf_ref.shape[1] // 64):
            held[o % GROUP, (o // GROUP) * 64 : (o // GROUP) * 64 + 64, :] = d_w[
                o * 64 : (o + 1) * 64, :
            ]
        for d in range(GROUP):
            out_refs[d][...] = held[z ^ d]
    sums_ref[...] = jnp.sum(dm_ref[...].astype(F32), axis=0, keepdims=True)


def norm_one_back_kernel(ids, *refs):
    x_ref, d_res_ref, vec = refs[4], refs[5], refs[6]
    d_in_ref, low_ref, rows_ref = refs[7:10]
    pulled, d_gain, d_bias = norm_pull(x_ref[...].astype(F32), vec[0:1, :], summed(refs[:4]))
    d_in = d_res_ref[...] + pulled
    d_in_ref[...] = d_in
    low_ref[...] = d_in.astype(BF)
    rows_ref[0:1, :] = d_gain
    rows_ref[1:2, :] = d_bias
    rows_ref[2:8, :] = jnp.zeros((6, d_in.shape[1]), F32)


def add_kernel(ids, *refs):
    count = len(refs) // 3
    for k in range(count):
        left, right = refs[k][...], refs[count + k][...]
        refs[2 * count + k][...] = (left.astype(F32) + right.astype(F32)).astype(BF)


def split_mixed_kernel(ids, *refs):
    out_refs, held = refs[4:8], refs[8]
    held[...] = summed(refs[:4]).astype(BF)
    for d in range(GROUP):
        out_refs[d][...] = held[spot((ids[0] ^ d) * 64, 64), :]


def split_feed_kernel(ids, got_ref, o0, o1, o2, o3, po_ref):
    for d, ref in enumerate((o0, o1, o2, o3)):
        ref[...] = got_ref[spot((ids[0] ^ d) * 64, 64), :]
    po_ref[...] = got_ref[256:576, :]


def pack_kernel(ids, *refs):
    fc, mixed, out_ref = refs[:4], refs[4:8], refs[8]
    for d in range(GROUP):
        source = ids[0] ^ d
        out_ref[:, spot(source * 512, 512)] = fc[d][...]
        start = pl.multiple_of(2048 + source * 384, 128)
        out_ref[:, pl.ds(start, 384)] = mixed[d][...]


def rows_kernel(ids, *refs):
    layers, keep_ref, send_ref = (refs[:4], refs[4:8]), refs[8], refs[9]
    held = refs[10]
    s, c = ids[0], ids[2]
    for index, (two_ref, one_ref, fc_ref, mixed_ref) in enumerate(layers):
        held[index] = jnp.zeros(held.shape[1:], F32)
        held[index, 0:2, :] = one_ref[0:2, :]
        held[index, 2:6, :] = two_ref[0:4, :]
        for place, half in ((0, c), (1, 1 - c)):
            for j in range(GROUP):
                start = place * 512 + j * 128
                held[index, 8 + j : 9 + j, spot(s * 256 + half * 128, 128)] = fc_ref[
                    :, start : start + 128
                ]
            base = place * 384
            for i in range(2):
                tile = mixed_ref[:, base + i * 128 : base + (i + 1) * 128]
                query = tile[:, :DH]
                value = mixed_ref[:, base + 256 + i * DH : base + 256 + (i + 1) * DH]
                where = spot((2 * half + i) * 256 + (s >> 1) * 128, 128)
                empty = jnp.zeros((1, DH), F32)
                odd = (s & 1) == 1
                for row, vector in ((6, query), (7, value)):
                    held[index, row : row + 1, where] = jnp.where(
                        odd,
                        jnp.concatenate([empty, vector], axis=1),
                        jnp.concatenate([vector, empty], axis=1),
                    )
    keep_ref[...] = held[c]
    send_ref[...] = held[1 - c]


def sum_kernel(ids, *refs):
    refs[-1][...] = summed(refs[:-1])


def final_kernel(ids, own_ref, oth_ref, po_own_ref, po_oth_ref, *refs):
    rows = refs[:4]
    mixed_out, fc_out, proj_out, out_out, vec_out, bfc_out = refs[4:10]
    s, z, c = ids[0], ids[1], ids[2]
    width = out_out.shape[2]
    for ref, po_ref, half in ((own_ref, po_own_ref, c), (oth_ref, po_oth_ref, 1 - c)):
        for source in range(GROUP):
            for j in range(GROUP):
                start = source * 512 + j * 128
                fc_out[0, :, spot(j * 1024 + source * 256 + half * 128, 128)] = ref[
                    :, start : start + 128
                ].astype(F32)
        for pair in range(2):
            for i in range(2):
                tiles = []
                for source in (2 * pair, 2 * pair + 1):
                    base = 2048 + source * 384
                    qk = ref[:, base + i * 128 : base + (i + 1) * 128].astype(F32)
                    v = ref[:, base + 256 + i * DH : base + 256 + (i + 1) * DH].astype(F32)
                    tiles.append((qk[:, :DH], qk[:, DH:], v))
                for t in range(3):
                    start = t * width + (2 * half + i) * 256 + pair * 128
                    mixed_out[0, :, spot(start, 128)] = jnp.concatenate(
                        [tiles[0][t], tiles[1][t]], axis=1
                    )
        proj_out[0, spot(half * 128, 128), 0:512] = po_ref[0:128, :].astype(F32)
        proj_out[0, spot(half * 128, 128), 512:1024] = po_ref[128:256, :].astype(F32)
        out_out[0, :, spot(half * 512, 512)] = po_ref[256:320, :].astype(F32)
    total = summed(rows)
    vec_out[...] = total
    bfc_out[...] = total


def fast_body(
    inputs,
    cotangent,
    segment_ids,
    ln1_gain,
    ln1_bias,
    w_qkv,
    b_query,
    b_value,
    w_out,
    b_out,
    ln2_gain,
    ln2_bias,
    w_fc,
    b_fc,
    w_proj,
    b_proj,
):
    s, z, c = lax.axis_index("seq"), lax.axis_index("fsdp"), lax.axis_index("section")
    first = c == 0
    ids = jnp.stack([s, z, c]).astype(jnp.int32)
    micro, tok, width = inputs.shape
    count = segment_ids.shape[1]
    tall = GROUP * tok

    q_mine, q_send = call(
        pick_mixed_kernel,
        "pick_mixed",
        ids,
        [w_qkv],
        [((256, 384), BF)] * 2,
        [pltpu.VMEM((3, GROUP, 256, 128), BF), pltpu.SemaphoreType.DMA((12,))],
        anywhere=(0,),
    )
    q_got = swap(q_send)
    q_half = [jnp.where(first, q_mine, q_got), jnp.where(first, q_got, q_mine)]

    def both(block):
        own = gather(block, "fsdp")
        return own, [swap(piece) for piece in own]

    vectors = jnp.concatenate(
        [ln1_gain, ln1_bias, b_query, b_value, b_out, ln2_gain, ln2_bias, b_proj]
        + [lax.dynamic_slice(b_fc, (0, s * 256), (1, 256))],
        axis=0,
    )
    vectors = lax.all_gather(vectors, ("section", "fsdp"), axis=0)
    vectors = vectors.reshape(2, GROUP, 9, 256).transpose(0, 2, 1, 3).reshape(2, 9, width)
    vectors = vectors.astype(F32)
    vec = [vectors[0], vectors[1]]

    a_mine, a_send, p_mine, p_send = call(
        pick_rest_kernel,
        "pick_rest",
        ids,
        [w_fc, w_proj, w_out],
        [((320, 512), BF)] * 2 + [((128, 1024), BF)] * 2,
        [pltpu.SemaphoreType.DMA((12,))],
        anywhere=(0, 1, 2),
    )
    a_got, p_got = swap(a_send), swap(p_send)
    a_half = [jnp.where(first, a_mine, a_got), jnp.where(first, a_got, a_mine)]
    p_half = [jnp.where(first, p_mine, p_got), jnp.where(first, p_got, p_mine)]

    my_segs = lax.dynamic_index_in_dim(segment_ids, c, 0, keepdims=False)
    seg_col, seg_row = my_segs.reshape(count, 1), my_segs.reshape(1, count)

    w_mixed = [both(q_half[0]), None]
    feed_own = [lax.all_gather(a_half[0], "fsdp", axis=0), None]
    back_own = [lax.all_gather(p_half[0], "fsdp", axis=0), None]
    w_mixed[1] = both(q_half[1])
    feed_own[1] = lax.all_gather(a_half[1], "fsdp", axis=0)
    back_own[1] = lax.all_gather(p_half[1], "fsdp", axis=0)
    feed_w = [[w, swap(w)] for w in feed_own]
    back_w = [[w, swap(w)] for w in back_own]

    x = lax.dynamic_index_in_dim(inputs, c, 0, keepdims=False)
    piece = ((384, 128), BF)
    small = ((128, 128), BF)
    part = ((tok, width), BF)
    kept = []
    top = None
    for layer in range(2):
        own, oth = w_mixed[layer]
        *packed, normed = call(
            mixed_kernel,
            "mixed",
            ids,
            gather(x, "seq") + own + oth + [vec[layer]],
            [piece] * 4 + [((tall, width), BF)],
            [pltpu.VMEM((GROUP, 384, 128), BF)],
            cost=(2 * tall * width * 768, 0),
        )
        qkv = trade(packed, "fsdp")
        heads = call(
            attend_kernel,
            "attend",
            ids,
            qkv + [seg_col, seg_row],
            [small] * 4,
            [pltpu.VMEM((count, 128), BF), pltpu.VMEM((count, DH), BF), pltpu.VMEM((count, DH), BF)],
            cost=(4 * count * count * 256, 0),
        )
        heads = trade(heads, "fsdp")
        *parts, att = call(
            output_kernel,
            "output",
            ids,
            heads + feed_w[layer],
            [part] * 4 + [((tall, 256), BF)],
            cost=(2 * tall * width * 256, 0),
        )
        res, n_two = call(
            residual_kernel,
            "residual",
            ids,
            trade(parts, "seq") + [x, vec[layer]],
            [((tok, width), F32), part],
        )
        *parts, slope, act, n_full = call(
            feed_kernel,
            "feed",
            ids,
            gather(n_two, "seq") + feed_w[layer] + back_w[layer] + [vec[layer]],
            [part] * 4 + [((tall, 1024), F32), ((tall, 1024), BF), ((tall, width), BF)],
            cost=(4 * tall * width * 1024, 0),
        )
        top, low = call(
            close_kernel,
            "close",
            ids,
            trade(parts, "seq") + [res, vec[layer]],
            [((tok, width), F32), part],
        )
        kept.append((x, normed, qkv, att, res, slope, act, n_full))
        x = low

    grad = lax.dynamic_index_in_dim(cotangent, c, 0, keepdims=False)
    row_terms = [None, None]
    fc_parts, mixed_parts, proj_parts = [None, None], [None, None], [None, None]
    turned = [
        (i * GROUP + j, j * GROUP + i) for i in range(GROUP) for j in range(GROUP)
    ]
    bottom = None
    for layer in (1, 0):
        x, normed, qkv, att, res, slope, act, n_full = kept[layer]
        own, oth = w_mixed[layer]
        *parts, d_pre, gb_full = call(
            feed_back_kernel,
            "feed_back",
            ids,
            gather(grad, "seq") + feed_w[layer] + back_w[layer] + [slope],
            [part] * 4 + [((tall, 1024), BF), ((tall, width), BF)],
            cost=(4 * tall * width * 1024, 0),
        )
        d_res, ga, two_rows = call(
            norm_two_back_kernel,
            "norm_two_back",
            ids,
            trade(parts, "seq") + [res, grad, vec[layer]],
            [((tok, width), F32), part, ((8, width), F32)],
        )
        *d_heads, ga_full = call(
            output_back_kernel,
            "output_back",
            ids,
            gather(ga, "seq") + feed_w[layer],
            [small] * 4 + [((tall, width), BF)],
            cost=(2 * tall * width * 256, 0),
        )
        d_heads = trade(d_heads, "fsdp")
        keep, send, fc_sums = call(
            feed_grads_kernel,
            "feed_grads",
            ids,
            [act, gb_full, n_full, d_pre, att, ga_full],
            [((GROUP, 576, 512), BF)] * 2 + [((1, 1024), F32)],
            cost=(4 * tall * width * 1152, 0),
        )
        (feed_sum,) = call(
            add_kernel, "add", ids, [keep, swap(send)], [((GROUP, 576, 512), BF)]
        )
        feed_got = lax.psum_scatter(feed_sum, "fsdp", scatter_dimension=0)
        d_pieces = call(
            attend_back_kernel,
            "attend_back",
            ids,
            qkv + d_heads + [seg_col, seg_row],
            [piece] * 4,
            [
                pltpu.VMEM((count, 128), BF),
                pltpu.VMEM((count, DH), BF),
                pltpu.VMEM((count, DH), BF),
                pltpu.VMEM((count, DH), F32),
                pltpu.VMEM((count, DH), F32),
                pltpu.VMEM((count, DH), F32),
            ],
            cost=(10 * count * count * 256, 0),
        )
        *parts, d_mixed = call(
            mixed_back_kernel,
            "mixed_back",
            ids,
            trade(d_pieces, "fsdp") + own + oth,
            [part] * 4 + [((tall, 768), BF)],
            [pltpu.VMEM((GROUP, 384, 128), BF)],
            cost=(2 * tall * width * 768, 0),
        )
        d_in, low, one_rows = call(
            norm_one_back_kernel,
            "norm_one_back",
            ids,
            trade(parts, "seq") + [x, d_res, vec[layer]],
            [((tok, width), F32), part, ((8, width), F32)],
        )
        *terms, mixed_sums = call(
            mixed_grads_kernel,
            "mixed_grads",
            ids,
            [normed, d_mixed],
            [((256, 384), BF)] * 8 + [((1, 768), F32)],
            [pltpu.VMEM((GROUP, 256, 384), BF)],
            cost=(2 * tall * width * 768, 0),
        )
        keeps, sends = terms[:4], terms[4:]
        sums = call(
            add_kernel,
            "add",
            ids,
            list(keeps) + [swap(block) for block in sends],
            [((256, 384), BF)] * 4,
        )
        blocks = call(
            split_mixed_kernel,
            "split_mixed",
            ids,
            trade(sums, "fsdp"),
            [((64, 384), BF)] * 4,
            [pltpu.VMEM((256, 384), BF)],
        )
        mixed_parts[layer] = trade(blocks, "seq")
        *blocks, proj_out = call(
            split_feed_kernel,
            "split_feed",
            ids,
            [feed_got],
            [((64, 512), BF)] * 4 + [((320, 512), BF)],
        )
        fc_parts[layer] = trade(blocks, "seq")
        proj_parts[layer] = lax.ppermute(proj_out, ("seq", "fsdp"), turned)
        row_terms[layer] = (two_rows, one_rows, fc_sums, mixed_sums)
        bottom = d_in
        grad = low

    keep, send = call(
        rows_kernel,
        "rows",
        ids,
        list(row_terms[0]) + list(row_terms[1]),
        [((16, width), F32)] * 2,
        [pltpu.VMEM((2, 16, width), F32)],
    )
    (rows,) = call(sum_kernel, "sum", ids, [keep, swap(send)], [((16, width), F32)])
    (rows,) = call(sum_kernel, "sum", ids, gather(rows, "fsdp"), [((16, width), F32)])
    rows = gather(rows, "seq")

    packs = [
        call(pack_kernel, "pack", ids, fc_parts[k] + mixed_parts[k], [((64, 3584), BF)])[0]
        for k in range(2)
    ]
    mine, theirs = jnp.where(first, packs[0], packs[1]), jnp.where(first, packs[1], packs[0])
    po_mine = jnp.where(first, proj_parts[0], proj_parts[1])
    po_theirs = jnp.where(first, proj_parts[1], proj_parts[0])
    g_mixed, g_fc, g_proj, g_out, totals, _ = call(
        final_kernel,
        "final",
        ids,
        [mine, swap(theirs), po_mine, swap(po_theirs)] + rows,
        [
            ((1, 64, 3 * width), F32),
            ((1, 64, 4096), F32),
            ((1, 256, width), F32),
            ((1, 64, width), F32),
            ((16, width), F32),
            ((16, width), F32),
        ],
    )
    place = (s * GROUP + z) * 64
    mine = lax.dynamic_slice(totals, (0, place), (8, 64))
    g_bfc = lax.dynamic_slice(totals, (8 + s, z * 256), (1, 256))

    ends_mine = jnp.where(first, bottom, top)
    ends_other = swap(jnp.where(first, top, bottom))
    relay = jnp.where(
        first, jnp.stack([ends_mine, ends_other]), jnp.stack([ends_other, ends_mine])
    )[None]

    def row(index):
        return mine[index : index + 1]

    return (
        relay,
        row(0),
        row(1),
        g_mixed,
        row(6),
        row(7),
        g_out,
        row(2),
        row(3),
        row(4),
        g_fc,
        g_bfc,
        g_proj,
        row(5),
    )


def plan(mesh):
    fits = mesh.shape["section"] == 2 and mesh.shape["seq"] == mesh.shape["fsdp"] == GROUP
    return fast_body if fits else body


def solution(mesh):
    placed = (
        P(None, ("seq", "fsdp"), None),
        P(None, ("seq", "fsdp"), None),
        P(),
        P("section", "fsdp"),
        P("section", "fsdp"),
        P("section", "fsdp", None),
        P("section", "fsdp"),
        P("section", "fsdp"),
        P("section", "fsdp", None),
        P("section", "fsdp"),
        P("section", "fsdp"),
        P("section", "fsdp"),
        P("section", "fsdp", None),
        P("section", "fsdp"),
        P("section", "fsdp", None),
        P("section", "fsdp"),
    )
    return jax.shard_map(
        plan(mesh),
        mesh=mesh,
        in_specs=placed,
        out_specs=(
            P("section", None, ("seq", "fsdp"), None),
            P("section", ("seq", "fsdp")),
            P("section", ("seq", "fsdp")),
            P("section", ("seq", "fsdp"), None),
            P("section", ("seq", "fsdp")),
            P("section", ("seq", "fsdp")),
            P("section", ("seq", "fsdp"), None),
            P("section", ("seq", "fsdp")),
            P("section", ("seq", "fsdp")),
            P("section", ("seq", "fsdp")),
            P("section", ("seq", "fsdp"), None),
            P("section", ("seq", "fsdp")),
            P("section", ("seq", "fsdp"), None),
            P("section", ("seq", "fsdp")),
        ),
        check_vma=False,
    )
```

```python
import math

import jax
import jax.numpy as jnp
from jax import lax
from jax.experimental import pallas as pl
from jax.experimental.pallas import tpu as pltpu
from jax.sharding import PartitionSpec as P

DH = 64


EPSILON = 1e-05
NEGATIVE = -1e30


def shifted(block, axis, distance):
    devices = range(lax.axis_size(axis))
    route = [(i - distance, i) for i in devices if i - distance in devices]
    return lax.ppermute(block, axis, route)


def layer_norm(values, gain_vec, bias_vec):
    average = jnp.mean(values, axis=-1, keepdims=True)
    centred = values - average
    variance = jnp.mean(centred * centred, axis=-1, keepdims=True)
    return centred * lax.rsqrt(variance + EPSILON) * gain_vec + bias_vec


def gelu_tanh(values):
    return jax.nn.gelu(values, approximate=True)


def mask_rows(seg_row, fsdp_index, n_seq, n_fsdp, tok_rows):
    places = jnp.arange(seg_row.shape[0], dtype=jnp.int32)
    seg_grid = seg_row.reshape(n_seq, n_fsdp, tok_rows)
    place_grid = places.reshape(n_seq, n_fsdp, tok_rows)
    query_ids = lax.dynamic_index_in_dim(seg_grid, fsdp_index, 1, keepdims=False).reshape(-1)
    query_places = lax.dynamic_index_in_dim(place_grid, fsdp_index, 1, keepdims=False).reshape(-1)
    key_ids = jnp.transpose(seg_grid, (1, 0, 2)).reshape(-1)
    key_places = jnp.transpose(place_grid, (1, 0, 2)).reshape(-1)
    same_doc = (query_ids[:, None] == key_ids[None, :]) & (query_ids[:, None] > 0)
    itself = query_places[:, None] == key_places[None, :]
    return (key_places[None, :] <= query_places[:, None]) & (same_doc | itself)


def split_heads(matrix):
    return matrix.reshape(matrix.shape[0], matrix.shape[1] // DH, DH)


def block_rows(matrix, block_len):
    return matrix.reshape((matrix.shape[0] // block_len, block_len) + matrix.shape[1:])


def masked_scores(queries, key_rows, allowed):
    raw_scores = jnp.einsum(
        "qhd,khd->hqk",
        split_heads(queries),
        split_heads(key_rows),
        preferred_element_type=jnp.float32,
    )
    return jnp.where(allowed[None], raw_scores * DH ** (-0.5), NEGATIVE)


def body(
    inputs,
    cotangent,
    segment_ids,
    ln1_gain,
    ln1_bias,
    w_qkv,
    b_query,
    b_value,
    w_out,
    b_out,
    ln2_gain,
    ln2_bias,
    w_fc,
    b_fc,
    w_proj,
    b_proj,
):
    n_seq = lax.axis_size("seq")
    n_fsdp = lax.axis_size("fsdp")
    section_index = lax.axis_index("section")
    fsdp_index = lax.axis_index("fsdp")
    last_section = section_index == 1
    micro, tok_rows, width = inputs.shape
    score_scale = DH ** (-0.5)
    query_count = tok_rows * n_seq
    block_len = math.gcd(query_count, 512)

    def fetch_params():
        return (
            lax.all_gather(ln1_gain[0], "fsdp", axis=0, tiled=True),
            lax.all_gather(ln1_bias[0], "fsdp", axis=0, tiled=True),
            lax.all_gather(w_qkv[0], "fsdp", axis=0, tiled=True),
            lax.all_gather(b_query[0], "fsdp", axis=0, tiled=True),
            lax.all_gather(b_value[0], "fsdp", axis=0, tiled=True),
            lax.all_gather(w_out[0], "fsdp", axis=0, tiled=True),
            lax.all_gather(b_out[0], "fsdp", axis=0, tiled=True),
            lax.all_gather(ln2_gain[0], "fsdp", axis=0, tiled=True),
            lax.all_gather(ln2_bias[0], "fsdp", axis=0, tiled=True),
            lax.all_gather(w_fc[0], "fsdp", axis=0, tiled=True),
            lax.all_gather(b_fc[0], "fsdp", axis=0, tiled=True),
            lax.all_gather(w_proj[0], "fsdp", axis=0, tiled=True),
            lax.all_gather(b_proj[0], "fsdp", axis=0, tiled=True),
        )

    received = jnp.zeros((tok_rows, width), jnp.bfloat16)
    kept_ticks = []
    layer_outs = []
    for tick_index in range(micro + 1):
        params = fetch_params()
        batch_index = jnp.clip(tick_index - section_index, 0, micro - 1)
        seg_row = lax.dynamic_index_in_dim(segment_ids, batch_index, 0, keepdims=False)
        allowed = mask_rows(seg_row, fsdp_index, n_seq, n_fsdp, tok_rows)
        if tick_index < micro:
            first_in = inputs[tick_index].astype(jnp.float32)
        else:
            first_in = jnp.zeros((tok_rows, width), jnp.float32)
        layer_in = jnp.where(last_section, received.astype(jnp.float32), first_in)
        (
            forward_gain_one,
            forward_bias_one,
            forward_w_mixed,
            forward_bias_query,
            forward_bias_value,
            forward_w_output,
            forward_bias_output,
            forward_gain_two,
            forward_bias_two,
            forward_w_hidden,
            forward_bias_hidden,
            forward_w_back,
            forward_bias_back,
        ) = params
        forward_normed = layer_norm(
            layer_in, forward_gain_one.astype(jnp.float32), forward_bias_one.astype(jnp.float32)
        ).astype(jnp.bfloat16)
        mixed_proj = jnp.dot(forward_normed, forward_w_mixed, preferred_element_type=jnp.float32)
        bias_row = jnp.concatenate(
            [forward_bias_query, jnp.zeros_like(forward_bias_query), forward_bias_value]
        ).astype(jnp.float32)
        mixed_tok = (mixed_proj + bias_row).astype(jnp.bfloat16).reshape(tok_rows, 3, width)
        head_rows = lax.all_to_all(mixed_tok, "seq", split_axis=2, concat_axis=0, tiled=True)
        forward_queries = head_rows[:, 0]
        forward_key_rows = lax.all_gather(head_rows[:, 1], "fsdp", axis=0, tiled=True)
        forward_value_rows = lax.all_gather(head_rows[:, 2], "fsdp", axis=0, tiled=True)

        def attend_block(operands):
            query_block, allowed_block = operands
            scores = masked_scores(query_block, forward_key_rows, allowed_block)
            row_top = jnp.max(scores, axis=-1, keepdims=True)
            log_block = row_top + jnp.log(
                jnp.sum(jnp.exp(scores - row_top), axis=-1, keepdims=True)
            )
            attn_weights = jnp.exp(scores - log_block).astype(jnp.bfloat16)
            head_block = jnp.einsum(
                "hqk,khd->qhd",
                attn_weights,
                split_heads(forward_value_rows),
                preferred_element_type=jnp.float32,
            )
            return (head_block.reshape(query_block.shape).astype(jnp.bfloat16), log_block)

        head_blocks, forward_log_total = lax.map(
            attend_block, (block_rows(forward_queries, block_len), block_rows(allowed, block_len))
        )
        head_out = head_blocks.reshape(forward_queries.shape)
        forward_attended = lax.all_to_all(head_out, "seq", split_axis=0, concat_axis=1, tiled=True)
        forward_residual = (
            layer_in
            + jnp.dot(forward_attended, forward_w_output, preferred_element_type=jnp.float32)
            + forward_bias_output.astype(jnp.float32)
        )
        forward_normed_two = layer_norm(
            forward_residual,
            forward_gain_two.astype(jnp.float32),
            forward_bias_two.astype(jnp.float32),
        ).astype(jnp.bfloat16)
        forward_pre_act = jnp.dot(
            forward_normed_two, forward_w_hidden, preferred_element_type=jnp.float32
        ) + forward_bias_hidden.astype(jnp.float32)
        forward_activated = gelu_tanh(forward_pre_act).astype(jnp.bfloat16)
        layer_out = (
            forward_residual
            + jnp.dot(forward_activated, forward_w_back, preferred_element_type=jnp.float32)
            + forward_bias_back.astype(jnp.float32)
        )
        forward_kept = (
            layer_in,
            forward_normed,
            forward_queries,
            forward_key_rows,
            forward_value_rows,
            forward_log_total,
            allowed,
            forward_attended,
            forward_residual,
            forward_normed_two,
            forward_pre_act,
            forward_activated,
        )
        layer_out, kept = (layer_out, forward_kept)
        kept_ticks.append(kept)
        layer_outs.append(layer_out)
        if tick_index < micro:
            received = shifted(layer_out.astype(jnp.bfloat16), "section", 1)
    sent_back = jnp.zeros((tok_rows, width), jnp.bfloat16)
    input_grads = []
    totals = None
    for tick_index in range(micro + 1):
        params = fetch_params()
        later = kept_ticks[min(tick_index + 1, micro)]
        earlier = kept_ticks[max(tick_index - 1, 0)]
        kept = jax.tree.map(
            lambda upper, lower: jnp.where(last_section, upper, lower), later, earlier
        )
        if tick_index < micro:
            top_grad = cotangent[tick_index].astype(jnp.float32)
        else:
            top_grad = jnp.zeros((tok_rows, width), jnp.float32)
        grad_out = jnp.where(last_section, top_grad, sent_back.astype(jnp.float32))
        (
            gain_one,
            bias_one,
            w_mixed,
            bias_query,
            bias_value,
            w_output,
            bias_output,
            gain_two,
            bias_two,
            w_hidden,
            bias_hidden,
            w_back,
            bias_back,
        ) = params
        (
            backward_layer_in,
            normed,
            queries,
            key_rows,
            value_rows,
            log_total,
            backward_allowed,
            attended,
            residual,
            normed_two,
            pre_act,
            activated,
        ) = kept
        grad_back = grad_out.astype(jnp.bfloat16)
        d_w_back = jnp.einsum("cf,cd->fd", activated, grad_back, preferred_element_type=jnp.float32)
        d_bias_back = jnp.sum(grad_back.astype(jnp.float32), axis=0)
        d_activated = jnp.einsum("cd,fd->cf", grad_back, w_back, preferred_element_type=jnp.float32)
        gelu_pull = jax.vjp(gelu_tanh, pre_act)[1]
        d_pre = gelu_pull(d_activated)[0].astype(jnp.bfloat16)
        d_w_hidden = jnp.einsum("cm,cf->mf", normed_two, d_pre, preferred_element_type=jnp.float32)
        d_bias_hidden = jnp.sum(d_pre.astype(jnp.float32), axis=0)
        d_normed_two = jnp.einsum("cf,mf->cm", d_pre, w_hidden, preferred_element_type=jnp.float32)
        norm_pull_two = jax.vjp(
            layer_norm, residual, gain_two.astype(jnp.float32), bias_two.astype(jnp.float32)
        )[1]
        d_resid_part, d_gain_two, d_bias_two = norm_pull_two(d_normed_two)
        d_residual = grad_out + d_resid_part
        grad_attn = d_residual.astype(jnp.bfloat16)
        d_w_output = jnp.einsum(
            "cm,cd->md", attended, grad_attn, preferred_element_type=jnp.float32
        )
        d_bias_output = jnp.sum(grad_attn.astype(jnp.float32), axis=0)
        d_attended = jnp.einsum(
            "cd,md->cm", grad_attn, w_output, preferred_element_type=jnp.float32
        ).astype(jnp.bfloat16)
        d_head = lax.all_to_all(d_attended, "seq", split_axis=1, concat_axis=0, tiled=True)

        def grad_block(carry, operands):
            key_acc, value_acc = carry
            query_block, head_grad_block, allowed_block, log_block = operands
            scores = masked_scores(query_block, key_rows, allowed_block)
            attn_probs = jnp.exp(scores - log_block)
            d_weights = jnp.einsum(
                "qhd,khd->hqk",
                split_heads(head_grad_block),
                split_heads(value_rows),
                preferred_element_type=jnp.float32,
            )
            row_dot = jnp.sum(attn_probs * d_weights, axis=-1, keepdims=True)
            d_scores = (attn_probs * (d_weights - row_dot) * score_scale).astype(jnp.bfloat16)
            d_query_block = (
                jnp.einsum(
                    "hqk,khd->qhd",
                    d_scores,
                    split_heads(key_rows),
                    preferred_element_type=jnp.float32,
                )
                .reshape(query_block.shape)
                .astype(jnp.bfloat16)
            )
            key_acc = key_acc + jnp.einsum(
                "hqk,qhd->khd",
                d_scores,
                split_heads(query_block),
                preferred_element_type=jnp.float32,
            ).reshape(key_rows.shape)
            value_acc = value_acc + jnp.einsum(
                "hqk,qhd->khd",
                attn_probs.astype(jnp.bfloat16),
                split_heads(head_grad_block),
                preferred_element_type=jnp.float32,
            ).reshape(value_rows.shape)
            return ((key_acc, value_acc), d_query_block)

        empty_terms = (
            jnp.zeros(key_rows.shape, jnp.float32),
            jnp.zeros(value_rows.shape, jnp.float32),
        )
        (key_term, value_term), query_blocks = lax.scan(
            grad_block,
            empty_terms,
            (
                block_rows(queries, block_len),
                block_rows(d_head, block_len),
                block_rows(backward_allowed, block_len),
                log_total,
            ),
        )
        d_query = query_blocks.reshape(queries.shape)
        d_key = lax.psum_scatter(key_term, "fsdp", scatter_dimension=0, tiled=True)
        d_value = lax.psum_scatter(value_term, "fsdp", scatter_dimension=0, tiled=True)
        d_heads = jnp.stack(
            [d_query, d_key.astype(jnp.bfloat16), d_value.astype(jnp.bfloat16)], axis=1
        )
        d_mixed = lax.all_to_all(d_heads, "seq", split_axis=0, concat_axis=2, tiled=True)
        d_flat = d_mixed.reshape(tok_rows, 3 * width)
        d_w_mixed = jnp.einsum("cm,cn->mn", normed, d_flat, preferred_element_type=jnp.float32)
        d_bias_query = jnp.sum(d_mixed[:, 0].astype(jnp.float32), axis=0)
        d_bias_value = jnp.sum(d_mixed[:, 2].astype(jnp.float32), axis=0)
        d_normed = jnp.einsum("cn,mn->cm", d_flat, w_mixed, preferred_element_type=jnp.float32)
        norm_pull_one = jax.vjp(
            layer_norm,
            backward_layer_in,
            gain_one.astype(jnp.float32),
            bias_one.astype(jnp.float32),
        )[1]
        d_in_part, d_gain_one, d_bias_one = norm_pull_one(d_normed)
        d_in = d_residual + d_in_part
        d_in, local_grads = (
            d_in,
            (
                d_gain_one,
                d_bias_one,
                d_w_mixed,
                d_bias_query,
                d_bias_value,
                d_w_output,
                d_bias_output,
                d_gain_two,
                d_bias_two,
                d_w_hidden,
                d_bias_hidden,
                d_w_back,
                d_bias_back,
            ),
        )
        input_grads.append(d_in)
        shared = (
            lax.psum_scatter(local_grads[0], ("seq", "fsdp"), scatter_dimension=0, tiled=True),
            lax.psum_scatter(local_grads[1], ("seq", "fsdp"), scatter_dimension=0, tiled=True),
            lax.psum_scatter(local_grads[2], ("seq", "fsdp"), scatter_dimension=0, tiled=True),
            lax.psum_scatter(local_grads[3], ("seq", "fsdp"), scatter_dimension=0, tiled=True),
            lax.psum_scatter(local_grads[4], ("seq", "fsdp"), scatter_dimension=0, tiled=True),
            lax.psum_scatter(local_grads[5], ("seq", "fsdp"), scatter_dimension=0, tiled=True),
            lax.psum_scatter(local_grads[6], ("seq", "fsdp"), scatter_dimension=0, tiled=True),
            lax.psum_scatter(local_grads[7], ("seq", "fsdp"), scatter_dimension=0, tiled=True),
            lax.psum_scatter(local_grads[8], ("seq", "fsdp"), scatter_dimension=0, tiled=True),
            lax.psum_scatter(local_grads[9], ("seq", "fsdp"), scatter_dimension=0, tiled=True),
            lax.psum_scatter(local_grads[10], ("seq", "fsdp"), scatter_dimension=0, tiled=True),
            lax.psum_scatter(local_grads[11], ("seq", "fsdp"), scatter_dimension=0, tiled=True),
            lax.psum_scatter(local_grads[12], ("seq", "fsdp"), scatter_dimension=0, tiled=True),
        )
        totals = shared if totals is None else jax.tree.map(jnp.add, totals, shared)
        if tick_index < micro:
            sent_back = shifted(d_in.astype(jnp.bfloat16), "section", -1)
    section_tops = jnp.stack(layer_outs[1:])
    bottom_grads = jnp.stack(input_grads[1:])
    relay_ends = jnp.where(last_section, section_tops, bottom_grads)[None]
    return (relay_ends,) + tuple((grad_part[None] for grad_part in totals))


BF = jnp.bfloat16
F32 = jnp.float32
GROUP = 4
SECTION, SEQ, FSDP = "section", "seq", "fsdp"


def nt(left, right):
    return lax.dot_general(left, right, (((1,), (1,)), ((), ())), preferred_element_type=F32)


def tn(left, right):
    return lax.dot_general(left, right, (((0,), (0,)), ((), ())), preferred_element_type=F32)


def nn(left, right):
    return jnp.dot(left, right, preferred_element_type=F32)


def spot(start, size):
    return pl.ds(pl.multiple_of(start, size), size)


def call(kernel, ids, args, outs, scratch, anywhere, mib):
    places = [pltpu.HBM if i in anywhere else pltpu.VMEM for i in range(len(args))]
    args = [
        pltpu.with_memory_space_constraint(a, pltpu.HBM) if i in anywhere else a
        for i, a in enumerate(args)
    ]
    return pl.pallas_call(
        kernel,
        name=kernel.__name__.removesuffix("_kernel"),
        out_shape=[jax.ShapeDtypeStruct(shape, dtype) for shape, dtype in outs],
        in_specs=[pl.BlockSpec(memory_space=pltpu.SMEM)]
        + [pl.BlockSpec(memory_space=place) for place in places],
        out_specs=[pl.BlockSpec(memory_space=pltpu.VMEM)] * len(outs),
        scratch_shapes=list(scratch),
        compiler_params=pltpu.CompilerParams(vmem_limit_bytes=mib * 1024 * 1024),
        cost_estimate=pl.CostEstimate(flops=0, bytes_accessed=0, transcendentals=0),
    )(ids, *args)


def after(value, *earlier):
    return lax.optimization_barrier((value, earlier))[0]


def exchange(block, axis, d):
    return lax.ppermute(block, axis, [(i, i ^ d) for i in range(GROUP)])


def trade(blocks, axis):
    return [blocks[0]] + [exchange(blocks[d], axis, d) for d in range(1, GROUP)]


def gather(block, axis):
    return trade([block] * GROUP, axis)


def swap(block):
    return lax.ppermute(block, SECTION, [(0, 1), (1, 0)])


def normed_rows(values, gain_vec, bias_vec):
    average = jnp.mean(values, axis=-1, keepdims=True)
    centred = values - average
    variance = jnp.mean(centred * centred, axis=-1, keepdims=True)
    return centred * lax.rsqrt(variance + EPSILON) * gain_vec + bias_vec


def norm_pull(values, gain_vec, grad):
    average = jnp.mean(values, axis=-1, keepdims=True)
    centred = values - average
    variance = jnp.mean(centred * centred, axis=-1, keepdims=True)
    inverse = lax.rsqrt(variance + EPSILON)
    unit = centred * inverse
    scaled = grad * gain_vec
    first = jnp.mean(scaled, axis=-1, keepdims=True)
    second = jnp.mean(scaled * unit, axis=-1, keepdims=True)
    pulled = inverse * (scaled - first - unit * second)
    return (
        pulled,
        jnp.sum(grad * unit, axis=0, keepdims=True),
        jnp.sum(grad, axis=0, keepdims=True),
    )


def pick_heads_kernel(ids, w_ref, out_ref, vec_ref, mine_ref, send_ref, held, rows_held, sem):
    s, c = ids[0], ids[2]
    width = w_ref.shape[2] // 3
    copies = [pltpu.make_async_copy(w_ref.at[0, spot(s * 64, 64), :], held, sem.at[GROUP])]
    for k in range(GROUP):
        source = out_ref.at[0, pl.ds(pl.multiple_of(k * 64 + s * 16, 16), 16), :]
        copies.append(pltpu.make_async_copy(source, rows_held.at[k], sem.at[k]))
    for copy in copies:
        copy.start()
    for copy in copies:
        copy.wait()

    def head(t, j, k):
        tile = held[:, spot(t * width + j * 256 + (k >> 1) * 128, 128)].astype(F32)
        return tile[:, DH:] if k & 1 else tile[:, :DH]

    foot = jnp.concatenate([vec_ref[...], jnp.zeros((16, 256), BF)], axis=1)
    for ref, half in ((mine_ref, c), (send_ref, 1 - c)):
        for k in range(GROUP):
            for i in range(2):
                j = 2 * half + i
                pair = jnp.concatenate([head(0, j, k), head(1, j, k)], axis=1)
                ref[k, 0:64, i * 128 : (i + 1) * 128] = pair.astype(BF)
            pair = jnp.concatenate([head(2, 2 * half, k), head(2, 2 * half + 1, k)], axis=1)
            ref[k, 0:64, 256:384] = pair.astype(BF)
            for q in range(GROUP):
                ref[k, q * 16 : (q + 1) * 16, 384:512] = rows_held[
                    k, :, spot(half * 512 + q * 128, 128)
                ]
            ref[k, 64:80, :] = foot


def pick_feed_kernel(ids, fc_ref, proj_ref, mine_ref, send_ref, sem):
    s, c = ids[0], ids[2]
    copies = []

    def begin(source, target):
        copy = pltpu.make_async_copy(source, target, sem.at[len(copies)])
        copy.start()
        copies.append(copy)

    for ref, half in ((mine_ref, c), (send_ref, 1 - c)):
        for k in range(GROUP):
            for j in range(GROUP):
                begin(
                    fc_ref.at[0, spot(s * 64, 64), spot(j * 1024 + k * 256 + half * 128, 128)],
                    ref.at[k, 0:64, j * 128 : (j + 1) * 128],
                )
            rows = spot(k * 256 + half * 128 + s * 32, 32)
            begin(proj_ref.at[0, rows, 0:512], ref.at[k, 64:96, :])
            begin(proj_ref.at[0, rows, 512:1024], ref.at[k, 96:128, :])
    for copy in copies:
        copy.wait()


def settle_heads_kernel(ids, mine_ref, got_ref, x_ref, *refs):
    first, z = ids[2] == 0, ids[1]
    for d in range(GROUP):
        mine, got = mine_ref[z ^ d], got_ref[z ^ d]
        lower, upper = jnp.where(first, mine, got), jnp.where(first, got, mine)
        refs[d][0:64, :] = lower[0:64]
        refs[d][64:80, 0:256] = lower[64:80, 0:256]
        refs[d][64:80, 256:512] = upper[64:80, 0:256]
        refs[d][80:144, :] = x_ref[:, 0:512]
        refs[d][144:208, :] = x_ref[:, 512:1024]
        refs[GROUP][d] = upper[0:64]


def settle_feed_kernel(ids, mine_ref, got_ref, heads_ref, *refs):
    first, z = ids[2] == 0, ids[1]
    for d in range(GROUP):
        mine, got = mine_ref[z ^ d], got_ref[z ^ d]
        refs[d][0:128, :] = jnp.where(first, mine, got)
        refs[d][128:192, :] = heads_ref[d]
        refs[GROUP + d][...] = jnp.where(first, got, mine)


def first_heads_kernel(ids, *refs):
    z = ids[1]
    heads_ref, x_refs, vec_refs = refs[GROUP], refs[5:9], refs[9:11]
    for d in range(GROUP):
        block = refs[d][...]
        x_refs[d][:, 0:512] = block[80:144]
        x_refs[d][:, 512:1024] = block[144:208]
        heads_ref[z ^ d] = block[0:64]
        lanes = spot((z ^ d) * 256, 256)
        for layer in range(2):
            rows = block[64:80, layer * 256 : (layer + 1) * 256].astype(F32)
            row = rows[8:9, :]
            for k in range(1, GROUP):
                row = jnp.where(z == k, rows[8 + k : 9 + k, :], row)
            vec_refs[layer][0:8, lanes] = rows[0:8, :]
            vec_refs[layer][8:9, lanes] = row


def part_kernel(ids, *refs):
    for d in range(GROUP):
        refs[GROUP][ids[1] ^ d] = refs[d][0:128, :]
        refs[GROUP + 1][ids[1] ^ d] = refs[d][128:192, :]


def place_kernel(axis, ids, *refs):
    for d in range(GROUP):
        refs[GROUP][ids[axis] ^ d] = refs[d][...]


def start_kernel(ids, seg_ref, x_ref, g_ref, seg_col, seg_row, x_out, g_out, sem):
    c = ids[2]
    copies = [
        pltpu.make_async_copy(x_ref.at[c], x_out, sem.at[0]),
        pltpu.make_async_copy(g_ref.at[c], g_out, sem.at[1]),
    ]
    for copy in copies:
        copy.start()
    numbers = jnp.where(c == 0, seg_ref[0:1, :], seg_ref[1:2, :]).astype(F32)
    seg_row[...] = numbers
    seg_col[...] = jnp.broadcast_to(numbers, (128, numbers.shape[1])).T[:, 0:1]
    for copy in copies:
        copy.wait()


def mixed_piece(ref, level):
    return jnp.concatenate([ref[k, level, :, 0:384] for k in range(GROUP)], axis=0)


def head_rows(ref, s):
    rows = []
    for d in range(GROUP):
        for k in range(GROUP):
            tiles = [ref[k, s ^ d, q * 16 : (q + 1) * 16, 384:512] for q in range(GROUP)]
            rows.append(jnp.concatenate(tiles, axis=1))
    return jnp.concatenate(rows, axis=0)


def hidden_piece(ref, level):
    return jnp.concatenate([ref[k, level, 0:64, :] for k in range(GROUP)], axis=0)


def back_share(ref):
    rows = []
    for j in range(GROUP):
        for k in range(GROUP):
            rows.append(jnp.concatenate([ref[k, j, 64:96, :], ref[k, j, 96:128, :]], axis=1))
    return jnp.concatenate(rows, axis=0)


def mixed_kernel(ids, *refs):
    x_refs, own_ref, oth_ref, vec = refs[:4], refs[4], refs[5], refs[6]
    out_refs, nf_ref, packed = refs[7:11], refs[11], refs[12]
    s, z, c = ids[0], ids[1], ids[2]
    gain_vec, bias_vec = vec[0:1, :], vec[1:2, :]
    for d in range(GROUP):
        nf_ref[d * 64 : (d + 1) * 64, :] = normed_rows(
            x_refs[d][...].astype(F32), gain_vec, bias_vec
        ).astype(BF)

    def bias_of(row, j):
        tile = vec[row : row + 1, spot(j * 256 + (z >> 1) * 128, 128)]
        return jnp.where((z & 1) == 1, tile[:, DH:], tile[:, :DH])

    empty = jnp.zeros((1, DH), F32)
    for ref, half in ((own_ref, c), (oth_ref, 1 - c)):
        total = jnp.zeros((GROUP * 64, 384), F32)
        for k in range(GROUP):
            total = total + nn(nf_ref[:, k * 256 : (k + 1) * 256], mixed_piece(ref, k))
        j = 2 * half
        row = jnp.concatenate(
            [
                bias_of(2, j),
                empty,
                bias_of(2, j + 1),
                empty,
                bias_of(3, j),
                bias_of(3, j + 1),
            ],
            axis=1,
        )
        total = total + row
        for i in range(2):
            packed[j + i, 0:256, :] = total[:, i * 128 : (i + 1) * 128].astype(BF)
            values = total[:, 256 + i * DH : 256 + (i + 1) * DH]
            packed[j + i, 256:384, :] = jnp.concatenate(
                [values[:128], values[128:]], axis=1
            ).astype(BF)
    for d in range(GROUP):
        out_refs[d][...] = packed[s ^ d]


def spread(ids, pieces, qk_ref, v_ref):
    s, z = ids[0], ids[1]
    for d in range(GROUP):
        for e in range(GROUP):
            rows = spot(((s ^ d) * GROUP + (z ^ e)) * 64, 64)
            qk_ref[rows, :] = pieces[d][e * 64 : (e + 1) * 64, :]
            lanes = slice(0, DH) if e < 2 else slice(DH, 128)
            start = 256 + (e & 1) * 64
            v_ref[rows, :] = pieces[d][start : start + 64, lanes]


def block_scores(qk_ref, seg_col, seg_row, start, size):
    stop = start + size
    queries = qk_ref[start:stop, 0:DH] * jnp.asarray(DH ** (-0.5), BF)
    scores = nt(queries, qk_ref[0:stop, DH:128])
    q_place = lax.broadcasted_iota(jnp.int32, (size, stop), 0) + start
    k_place = lax.broadcasted_iota(jnp.int32, (size, stop), 1)
    q_doc, k_doc = seg_col[start:stop, :], seg_row[:, 0:stop]
    same = (q_doc == k_doc) & (q_doc > 0.0)
    allowed = ((k_place <= q_place) & same) | (k_place == q_place)
    return jnp.where(allowed, scores, NEGATIVE)


def attend_kernel(ids, *refs):
    pieces, seg_col, seg_row = refs[:4], refs[4], refs[5]
    out_refs, qk_out, v_out = refs[6:10], refs[10], refs[11]
    qk_ref, v_ref, o_ref = refs[12:15]
    s, z = ids[0], ids[1]
    spread(ids, pieces, qk_ref, v_ref)
    qk_out[...] = qk_ref[...]
    v_out[...] = v_ref[...]
    count = qk_ref.shape[0]
    size = 256
    for start in range(0, count, size):
        scores = block_scores(qk_ref, seg_col, seg_row, start, size)
        top = jnp.max(scores, axis=-1, keepdims=True)
        grown = jnp.exp(scores - top)
        total = jnp.sum(grown, axis=-1, keepdims=True)
        mixed = nn(grown.astype(BF), v_ref[0 : start + size, :])
        o_ref[start : start + size, :] = (mixed / total).astype(BF)
    for d in range(GROUP):
        for e in range(2):
            left = o_ref[spot(((s ^ d) * GROUP + (z ^ e)) * 64, 64), :]
            right = o_ref[spot(((s ^ d) * GROUP + (z ^ (e + 2))) * 64, 64), :]
            out_refs[d][e * 64 : (e + 1) * 64, :] = jnp.concatenate([left, right], axis=1)


def unpacked(piece):
    return jnp.concatenate([piece[:, :DH], piece[:, DH:]], axis=0)


def output_kernel(ids, *refs):
    pieces, own_ref, oth_ref = refs[:4], refs[4], refs[5]
    out_refs, att_ref = refs[6:10], refs[10]
    s, c = ids[0], ids[2]
    att = jnp.concatenate([unpacked(pieces[d][...]) for d in range(GROUP)], axis=1)
    att_ref[...] = att
    for w_ref, half in ((own_ref, c), (oth_ref, 1 - c)):
        part = nn(att, head_rows(w_ref, s)).astype(BF)
        for d in range(GROUP):
            out_refs[d][:, spot(half * 512, 512)] = part[d * 64 : (d + 1) * 64, :]


def summed(refs):
    blocks = []
    for ref in refs:
        blocks += [ref[...]] if len(ref.shape) == 2 else [ref[k] for k in range(GROUP)]
    total = blocks[0].astype(F32)
    for block in blocks[1:]:
        total = total + block.astype(F32)
    return total


def residual_kernel(ids, *refs):
    x_ref, vec = refs[4], refs[5]
    res_ref, n_ref = refs[6], refs[7]
    res = x_ref[...].astype(F32) + summed(refs[:4]) + vec[4:5, :]
    res_ref[...] = res
    n_ref[...] = normed_rows(res, vec[5:6, :], vec[6:7, :]).astype(BF)


ROOT = math.sqrt(2.0 / math.pi)


def hidden_bias(vec, half):
    return jnp.concatenate(
        [vec[8:9, spot(j * 256 + half * 128, 128)] for j in range(GROUP)], axis=1
    )


def feed_forward(n_refs, shares, vec, c, nf_ref, keep):
    for d in range(GROUP):
        nf_ref[d * 64 : (d + 1) * 64, :] = n_refs[d][...]
    part = jnp.zeros(nf_ref.shape, F32)
    for place, half in ((0, c), (1, 1 - c)):
        cols = slice(place * 512, (place + 1) * 512)
        pre = jnp.zeros((GROUP * 64, 512), F32)
        for d in range(GROUP):
            pre = pre + nn(nf_ref[:, d * 256 : (d + 1) * 256], hidden_piece(shares[place], d))
        pre = pre + hidden_bias(vec, half)
        square = pre * pre
        bend = jnp.tanh(ROOT * pre * (1.0 + 0.044715 * square))
        act = (0.5 * pre * (1.0 + bend)).astype(BF)
        slope = 0.5 * (1.0 + bend) + (0.5 * ROOT) * pre * (1.0 - bend * bend) * (
            1.0 + (3.0 * 0.044715) * square
        )
        keep(cols, act, slope)
        part = part + nn(act, back_share(shares[place]))
    return part.astype(BF)


def feed_backward(g_blocks, shares, slope_ref, out_refs, d_pre_ref, gf_ref):
    for d in range(GROUP):
        gf_ref[d * 64 : (d + 1) * 64, :] = g_blocks[d]
    for place in range(2):
        cols = slice(place * 512, (place + 1) * 512)
        d_act = nt(gf_ref[...], back_share(shares[place]))
        d_pre_ref[:, cols] = (d_act * slope_ref[:, cols]).astype(BF)
    for d in range(GROUP):
        part = nt(d_pre_ref[:, 0:512], hidden_piece(shares[0], d))
        part = (part + nt(d_pre_ref[:, 512:1024], hidden_piece(shares[1], d))).astype(BF)
        for e in range(GROUP):
            out_refs[e][:, d * 256 : (d + 1) * 256] = part[e * 64 : (e + 1) * 64, :]


def feed_kernel(ids, *refs):
    slope_ref, act_ref, nf_ref = refs[11:14]

    def keep(cols, act, slope):
        act_ref[:, cols] = act
        slope_ref[:, cols] = slope

    part = feed_forward(refs[:4], refs[4:6], refs[6], ids[2], nf_ref, keep)
    for d in range(GROUP):
        refs[7 + d][...] = part[d * 64 : (d + 1) * 64, :]


def feed_back_kernel(ids, *refs):
    blocks = [ref[...] for ref in refs[:4]]
    feed_backward(blocks, refs[4:6], refs[6], refs[7:11], refs[11], refs[12])


def feed_turn_kernel(ids, *refs):
    shares, vec, top_refs, outs = refs[8:10], refs[10], refs[11:15], refs[15:19]
    act_ref, nf_ref, d_pre_ref, gf_ref, slope_ref = refs[19:24]

    def keep(cols, act, slope):
        act_ref[:, cols] = act
        slope_ref[:, cols] = slope

    part = feed_forward(refs[:4], shares, vec, ids[2], nf_ref, keep)
    for d in range(GROUP):
        top_refs[d][...] = part[d * 64 : (d + 1) * 64, :]
    blocks = [ref[...] for ref in refs[4:8]]
    feed_backward(blocks, shares, slope_ref, outs, d_pre_ref, gf_ref)


def close_kernel(ids, *refs):
    res_ref, vec, out_ref = refs[4:]
    out = res_ref[...] + summed(refs[:4]) + vec[7:8, :]
    out_ref[...] = out.astype(out_ref.dtype)


def norm_two_back_kernel(ids, *refs):
    res_ref, g_ref, vec = refs[4], refs[5], refs[6]
    d_res_ref, ga_ref, rows_ref = refs[7:10]
    grad = g_ref[...].astype(F32)
    pulled, d_gain, d_bias = norm_pull(res_ref[...], vec[5:6, :], summed(refs[:4]))
    d_res = grad + pulled
    low = d_res.astype(BF)
    d_res_ref[...] = d_res
    ga_ref[...] = low
    rows_ref[0:1, :] = jnp.sum(low.astype(F32), axis=0, keepdims=True)
    rows_ref[1:2, :] = d_gain
    rows_ref[2:3, :] = d_bias
    rows_ref[3:4, :] = jnp.sum(grad.astype(BF).astype(F32), axis=0, keepdims=True)
    rows_ref[4:8, :] = jnp.zeros((4, grad.shape[1]), F32)


def output_back_kernel(ids, *refs):
    g_refs, own_ref, oth_ref = refs[:4], refs[4], refs[5]
    out_refs, gf_ref = refs[6:10], refs[10]
    s, c = ids[0], ids[2]
    for d in range(GROUP):
        gf_ref[d * 64 : (d + 1) * 64, :] = g_refs[d][...]
    d_att = nt(gf_ref[:, spot(c * 512, 512)], head_rows(own_ref, s))
    d_att = d_att + nt(gf_ref[:, spot((1 - c) * 512, 512)], head_rows(oth_ref, s))
    for d in range(GROUP):
        cols = d_att[:, d * DH : (d + 1) * DH]
        out_refs[d][...] = jnp.concatenate([cols[:128], cols[128:]], axis=1).astype(BF)


def feed_grads_kernel(ids, *refs):
    act_ref, gb_ref, nf_ref, d_pre_ref = refs[:4]
    keep_ref, send_ref, sums_ref = refs[4:7]
    for place, out_ref in ((0, keep_ref), (1, send_ref)):
        cols = slice(place * 512, (place + 1) * 512)
        d_fc = tn(nf_ref[...], d_pre_ref[:, cols]).astype(BF)
        for k in range(GROUP):
            out_ref[k, 0:256, :] = d_fc[k * 256 : (k + 1) * 256, :]
        d_proj = tn(act_ref[:, cols], gb_ref[...]).astype(BF)
        for j in range(GROUP):
            rows = d_proj[j * 128 : (j + 1) * 128, :]
            out_ref[j, 256:384, :] = rows[:, 0:512]
            out_ref[j, 384:512, :] = rows[:, 512:1024]
    sums_ref[...] = jnp.sum(d_pre_ref[...].astype(F32), axis=0, keepdims=True)


def attend_back_kernel(ids, *refs):
    d_pieces, qk_ref, v_ref, seg_col, seg_row = refs[0:4], refs[4], refs[5], refs[6], refs[7]
    out_refs = refs[8:12]
    do_ref, dq_ref, dk_ref, dv_ref = refs[12:16]
    s, z = ids[0], ids[1]
    for d in range(GROUP):
        for e in range(GROUP):
            rows = spot(((s ^ d) * GROUP + (z ^ e)) * 64, 64)
            lanes = slice(0, DH) if e < 2 else slice(DH, 128)
            start = (e & 1) * 64
            do_ref[rows, :] = d_pieces[d][start : start + 64, lanes]
    count = qk_ref.shape[0]
    size = 256
    for start in range(0, count, size):
        stop = start + size
        scores = block_scores(qk_ref, seg_col, seg_row, start, size)
        top = jnp.max(scores, axis=-1, keepdims=True)
        grown = jnp.exp(scores - top)
        probs = grown * (1.0 / jnp.sum(grown, axis=-1, keepdims=True))
        d_out = do_ref[start:stop, :]
        d_weights = nt(d_out, v_ref[0:stop, :])
        row_dot = jnp.sum(probs * d_weights, axis=-1, keepdims=True)
        d_scores = (probs * (d_weights - row_dot) * DH ** (-0.5)).astype(BF)
        dq_ref[start:stop, :] = nn(d_scores, qk_ref[0:stop, DH:128])
        dk = tn(d_scores, qk_ref[start:stop, 0:DH])
        dv = tn(probs.astype(BF), d_out)
        if start:
            dk_ref[0:start, :] += dk[0:start]
            dv_ref[0:start, :] += dv[0:start]
        dk_ref[start:stop, :] = dk[start:stop]
        dv_ref[start:stop, :] = dv[start:stop]
    for d in range(GROUP):
        for e in range(GROUP):
            rows = spot(((s ^ d) * GROUP + (z ^ e)) * 64, 64)
            out_refs[d][e * 64 : (e + 1) * 64, :] = jnp.concatenate(
                [dq_ref[rows, :], dk_ref[rows, :]], axis=1
            ).astype(BF)
        for e in range(2):
            left = dv_ref[spot(((s ^ d) * GROUP + (z ^ e)) * 64, 64), :]
            right = dv_ref[spot(((s ^ d) * GROUP + (z ^ (e + 2))) * 64, 64), :]
            out_refs[d][256 + e * 64 : 320 + e * 64, :] = jnp.concatenate(
                [left, right], axis=1
            ).astype(BF)


def mixed_back_kernel(ids, *refs):
    pieces, own_ref, oth_ref = refs[:4], refs[4], refs[5]
    out_refs, dm_ref, held = refs[6:10], refs[10], refs[11]
    s, c = ids[0], ids[2]
    for d in range(GROUP):
        held[d] = pieces[d][...]
    for place, half in ((0, c), (1, 1 - c)):
        base = place * 384
        values = []
        for i in range(2):
            d = (2 * half + i) ^ s
            dm_ref[:, base + i * 128 : base + (i + 1) * 128] = held[d, 0:256, :]
            values.append(unpacked(held[d, 256:384, :]))
        dm_ref[:, base + 256 : base + 384] = jnp.concatenate(values, axis=1)
    for k in range(GROUP):
        part = nt(dm_ref[:, 0:384], mixed_piece(own_ref, k))
        part = (part + nt(dm_ref[:, 384:768], mixed_piece(oth_ref, k))).astype(BF)
        for d in range(GROUP):
            out_refs[d][:, k * 256 : (k + 1) * 256] = part[d * 64 : (d + 1) * 64, :]


def attend_grads_kernel(ids, *refs):
    nf_ref, dm_ref, att_ref, ga_ref = refs[:4]
    keep_ref, send_ref, sums_ref = refs[4:7]
    s, c = ids[0], ids[2]
    for place, out_ref, half in ((0, keep_ref, c), (1, send_ref, 1 - c)):
        d_w = tn(nf_ref[...], dm_ref[:, place * 384 : (place + 1) * 384]).astype(BF)
        for k in range(GROUP):
            out_ref[k, :, 0:384] = d_w[k * 256 : (k + 1) * 256, :]
        d_out = tn(att_ref[...], ga_ref[:, spot(half * 512, 512)]).astype(BF)
        for d in range(GROUP):
            for q in range(GROUP):
                out_ref[s ^ d, q * 64 : (q + 1) * 64, 384:512] = d_out[
                    d * 64 : (d + 1) * 64, q * 128 : (q + 1) * 128
                ]
    sums_ref[...] = jnp.sum(dm_ref[...].astype(F32), axis=0, keepdims=True)


def norm_one_back_kernel(ids, *refs):
    x_ref, d_res_ref, vec = refs[4], refs[5], refs[6]
    d_in_ref, low_ref, rows_ref = refs[7:10]
    pulled, d_gain, d_bias = norm_pull(x_ref[...].astype(F32), vec[0:1, :], summed(refs[:4]))
    d_in = d_res_ref[...] + pulled
    d_in_ref[...] = d_in
    low_ref[...] = d_in.astype(BF)
    rows_ref[0:1, :] = d_gain
    rows_ref[1:2, :] = d_bias
    rows_ref[2:8, :] = jnp.zeros((6, d_in.shape[1]), F32)


def add_kernel(ids, left_ref, right_ref, *out_refs):
    for d in range(GROUP):
        k = ids[0] ^ d
        out_refs[d][...] = (left_ref[k].astype(F32) + right_ref[k].astype(F32)).astype(BF)


def join_kernel(ids, *refs):
    refs[-1][...] = summed(refs[:-1]).astype(BF)


def choose_kernel(ids, *refs):
    upper, mine_ref, theirs_ref = refs[-3][...], refs[-2], refs[-1]
    lower = summed(refs[:-3]).astype(BF)
    first = ids[2] == 0
    mine_ref[...] = jnp.where(first, lower, upper)
    theirs_ref[...] = jnp.where(first, upper, lower)


def split_feed_kernel(ids, own_ref, oth_ref, *refs):
    back_out = refs[GROUP]
    for d in range(GROUP):
        rows = spot((ids[1] ^ d) * 64, 64)
        refs[d][:, 0:512] = own_ref[rows, :]
        refs[d][:, 512:1024] = oth_ref[rows, :]
    for ref, half in ((own_ref, ids[2]), (oth_ref, 1 - ids[2])):
        rows = spot(half * 128, 128)
        back_out[0, rows, 0:512] = ref[256:384, :].astype(F32)
        back_out[0, rows, 512:1024] = ref[384:512, :].astype(F32)


def split_attend_kernel(ids, own_ref, oth_ref, *refs):
    for d in range(GROUP):
        rows = spot((ids[1] ^ d) * 64, 64)
        refs[d][:, 0:384] = own_ref[rows, 0:384]
        refs[d][:, 384:768] = oth_ref[rows, 0:384]
    for ref, half in ((own_ref, ids[2]), (oth_ref, 1 - ids[2])):
        for q in range(GROUP):
            refs[GROUP][0, :, spot(half * 512 + q * 128, 128)] = ref[
                q * 64 : (q + 1) * 64, 384:512
            ].astype(F32)


def rows_kernel(ids, *refs):
    layers, keep_ref, send_ref = (refs[:4], refs[4:8]), refs[8], refs[9]
    held = refs[10]
    z, c = ids[1], ids[2]
    for index, (two_ref, one_ref, fc_ref, mixed_ref) in enumerate(layers):
        held[index] = jnp.zeros(held.shape[1:], F32)
        held[index, 0:2, :] = one_ref[0:2, :]
        held[index, 2:6, :] = two_ref[0:4, :]
        for place, half in ((0, c), (1, 1 - c)):
            for j in range(GROUP):
                start = place * 512 + j * 128
                held[index, 8 + j : 9 + j, spot(z * 256 + half * 128, 128)] = fc_ref[
                    :, start : start + 128
                ]
            base = place * 384
            for i in range(2):
                tile = mixed_ref[:, base + i * 128 : base + (i + 1) * 128]
                query = tile[:, :DH]
                value = mixed_ref[:, base + 256 + i * DH : base + 256 + (i + 1) * DH]
                where = spot((2 * half + i) * 256 + (z >> 1) * 128, 128)
                empty = jnp.zeros((1, DH), F32)
                odd = (z & 1) == 1
                for row, vector in ((6, query), (7, value)):
                    held[index, row : row + 1, where] = jnp.where(
                        odd,
                        jnp.concatenate([empty, vector], axis=1),
                        jnp.concatenate([vector, empty], axis=1),
                    )
    keep_ref[...] = held[c]
    send_ref[...] = held[1 - c]


def sum_kernel(ids, *refs):
    refs[-1][...] = summed(refs[:-1])


def final_feed_kernel(ids, *refs):
    fc_out = refs[GROUP]
    for place, half in ((0, ids[2]), (1, 1 - ids[2])):
        for d in range(GROUP):
            for j in range(GROUP):
                start = place * 512 + j * 128
                lanes = spot(j * 1024 + (ids[1] ^ d) * 256 + half * 128, 128)
                fc_out[0, :, lanes] = refs[d][:, start : start + 128].astype(F32)


def final_attend_kernel(ids, *refs):
    mixed, rows, mixed_out, bfc_out = refs[:4], refs[4:6], refs[6], refs[7]
    vec_outs, total, held = refs[8:16], refs[16], refs[17]
    s, z, c = ids[0], ids[1], ids[2]
    width = mixed_out.shape[2] // 3
    for d in range(GROUP):
        held[z ^ d] = mixed[d][...]
    for place, half in ((0, c), (1, 1 - c)):
        base = place * 384
        for pair in range(2):
            for i in range(2):
                tiles = []
                for source in (2 * pair, 2 * pair + 1):
                    qk = held[source, :, base + i * 128 : base + (i + 1) * 128].astype(F32)
                    v = held[source, :, base + 256 + i * DH : base + 256 + (i + 1) * DH]
                    tiles.append((qk[:, :DH], qk[:, DH:], v.astype(F32)))
                for t in range(3):
                    start = t * width + (2 * half + i) * 256 + pair * 128
                    mixed_out[0, :, spot(start, 128)] = jnp.concatenate(
                        [tiles[0][t], tiles[1][t]], axis=1
                    )
    total[...] = summed(rows)
    tile = total[0:8, spot(s * 256 + (z >> 1) * 128, 128)]
    tile = jnp.where((z & 1) == 1, tile[:, DH:], tile[:, :DH])
    for row, ref in enumerate(vec_outs):
        ref[...] = tile[row : row + 1, :]
    bfc_out[...] = total[pl.ds(8 + s, 1), spot(z * 256, 256)]


def fast_body(
    inputs,
    cotangent,
    segment_ids,
    ln1_gain,
    ln1_bias,
    w_qkv,
    b_query,
    b_value,
    w_out,
    b_out,
    ln2_gain,
    ln2_bias,
    w_fc,
    b_fc,
    w_proj,
    b_proj,
):
    s, z, c = lax.axis_index(SEQ), lax.axis_index(FSDP), lax.axis_index(SECTION)
    first = c == 0
    ids = jnp.stack([s, z, c]).astype(jnp.int32)
    tok, width = inputs.shape[1:]
    count = segment_ids.shape[1]
    tall = GROUP * tok
    piece = ((384, 128), BF)
    small = ((128, 128), BF)
    part = ((tok, width), BF)
    wide = ((tall, width), BF)
    line = ((tok, width), F32)
    share = ((256, 512), BF)
    feed_share = ((512, 512), BF)
    rows_shape = ((16, width), F32)
    done, awaited, lagging = [], [], []

    def run(kernel, args, outs, *scratch, anywhere=(), mib=16, aside=False):
        args = list(args)
        earlier = done[-1:] + ([] if aside else list(awaited))
        if earlier:
            args[0] = after(args[0], *earlier)
        if not aside:
            awaited[:] = lagging
            lagging.clear()
        result = list(call(kernel, ids, args, outs, scratch, anywhere, mib))
        done.append(result[-1])
        return result

    def beside(blocks, got, axis, *which, lag=False):
        for d in which:
            got[d] = exchange(after(blocks[d], done[-1]), axis, d)
            (lagging if lag else awaited).append(got[d])

    def of(kernel, axis):
        def bound(*refs):
            kernel(axis, *refs)

        bound.__name__ = kernel.__name__
        return bound

    def shared(pieces, axis, shape, aside=False):
        (whole,) = run(of(place_kernel, axis), pieces, [(shape, BF)], aside=aside)
        return [whole, swap(whole)]

    seg_col, seg_row, x, grad = run(
        start_kernel,
        [segment_ids, inputs, cotangent],
        [((count, 1), F32), ((1, count), F32), part, part],
        pltpu.SemaphoreType.DMA((2,)),
        anywhere=(1, 2),
    )
    vectors = jnp.concatenate(
        [ln1_gain, ln1_bias, b_query, b_value, b_out, ln2_gain, ln2_bias, b_proj]
        + [b_fc[:, k * 256 : (k + 1) * 256] for k in range(GROUP)]
        + [jnp.zeros((4, 256), BF)],
        axis=0,
    )
    mine, send = run(
        pick_heads_kernel,
        [w_qkv, w_out, vectors],
        [((GROUP, 80, 512), BF)] * 2,
        pltpu.VMEM((64, 3 * width), BF),
        pltpu.VMEM((GROUP, 16, width), BF),
        pltpu.SemaphoreType.DMA((GROUP + 1,)),
        anywhere=(0, 1),
    )
    *heads, upper_heads = run(
        settle_heads_kernel,
        [mine, swap(send), x],
        [((208, 512), BF)] * 4 + [((GROUP, 64, 512), BF)],
    )
    heads = trade(heads, FSDP)
    mine, send = run(
        pick_feed_kernel,
        [w_fc, w_proj],
        [((GROUP, 128, 512), BF)] * 2,
        pltpu.SemaphoreType.DMA((48,)),
        anywhere=(0, 1),
    )
    got = swap(send)
    heads, *rest = run(
        first_heads_kernel,
        heads,
        [((GROUP, 64, 512), BF)] + [part] * 4 + [((16, width), F32)] * 2,
    )
    x_all, vec = rest[:4], rest[4:]
    heads = gather(heads, SEQ)
    grad_all = [grad] * GROUP
    beside([grad] * GROUP, grad_all, FSDP, 1, 3)
    rest = run(
        settle_feed_kernel,
        [mine, got, upper_heads],
        [((192, 512), BF)] * 4 + [((128, 512), BF)] * 4,
        aside=True,
    )
    rest, upper_feed = rest[:4], rest[4:]
    head_w = [shared(heads, 0, (GROUP, GROUP, 64, 512)), None]

    feed_w = [None, None]
    kept = []
    for layer in range(2):
        *packed, normed = run(
            mixed_kernel,
            x_all + head_w[layer] + [vec[layer]],
            [piece] * 4 + [wide],
            pltpu.VMEM((GROUP, 384, 128), BF),
        )
        qkv = trade(packed, SEQ)
        got = rest[:1] + [None] * 3
        beside(rest, got, FSDP, 1, 3)
        if layer == 1:
            beside([grad] * GROUP, grad_all, FSDP, 2, lag=True)
        *heads, qk_rows, v_rows = run(
            attend_kernel,
            qkv + [seg_col, seg_row],
            [small] * 4 + [((count, 128), BF), ((count, DH), BF)],
            pltpu.VMEM((count, 128), BF),
            pltpu.VMEM((count, DH), BF),
            pltpu.VMEM((count, DH), BF),
        )
        heads = trade(heads, SEQ)
        beside(rest, got, FSDP, 2)
        *parts, att = run(
            output_kernel,
            heads + head_w[layer],
            [part] * 4 + [((tall, 256), BF)],
        )
        parts = trade(parts, FSDP)
        if layer == 0:
            feed, heads_later = run(
                part_kernel,
                got,
                [((GROUP, 128, 512), BF), ((GROUP, 64, 512), BF)],
                aside=True,
            )
        else:
            (feed,) = run(
                of(place_kernel, 1), got, [((GROUP, 128, 512), BF)], aside=True
            )
        feeds = [feed] * GROUP
        beside(feeds, feeds, SEQ, 1, 2)
        res, n_two = run(
            residual_kernel, parts + [x, vec[layer]], [line, part]
        )
        n_all = gather(n_two, FSDP)
        beside([feed] * GROUP, feeds, SEQ, 3)
        feeds[0] = after(feeds[0], *n_all)
        feed_w[layer] = shared(feeds, 0, (GROUP, GROUP, 128, 512))
        kept.append((x, normed, qk_rows, v_rows, att, res))
        if layer == 0:
            *parts, slope, act, n_full = run(
                feed_kernel,
                n_all + feed_w[0] + [vec[0]],
                [part] * 4 + [((tall, 1024), F32), ((tall, 1024), BF), wide],
            )
            parts = trade(parts, FSDP)
            heads = [heads_later] * GROUP
            beside(heads, heads, SEQ, 1, 2)
            (x,) = run(close_kernel, parts + [res, vec[0]], [part])
            x_all = gather(x, FSDP)
            beside([heads_later] * GROUP, heads, SEQ, 3)
            heads[0] = after(heads[0], *x_all)
            head_w[1] = shared(heads, 0, (GROUP, GROUP, 64, 512))
            rest = upper_feed
        else:
            turn = run(
                feed_turn_kernel,
                n_all + grad_all + feed_w[1] + [vec[1]],
                [part] * 8 + [((tall, 1024), BF), wide, ((tall, 1024), BF), wide],
                pltpu.VMEM((tall, 1024), F32),
                mib=20,
            )

    def feed_terms(act, gb_full, n_full, d_pre):
        keep, send, sums = run(
            feed_grads_kernel,
            [act, gb_full, n_full, d_pre],
            [((GROUP, 512, 512), BF)] * 2 + [((1, 1024), F32)],
            aside=True,
        )
        return keep, swap(send), sums

    def attend_terms(normed, d_mixed, att, ga_full):
        keep, send, sums = run(
            attend_grads_kernel,
            [normed, d_mixed, att, ga_full],
            [((GROUP, 256, 512), BF)] * 2 + [((1, 768), F32)],
            aside=True,
        )
        return keep, swap(send), sums

    def total(keep, got, shape):
        return run(add_kernel, [keep, got], [shape] * 4, aside=True)

    def join(blocks, shape):
        return run(join_kernel, blocks, [shape], aside=True)[0]

    def norm_two_back(layer, parts, grad):
        return run(
            norm_two_back_kernel,
            parts + [kept[layer][5], grad, vec[layer]],
            [line, part, ((8, width), F32)],
        )

    def output_back(layer, ga_all):
        return run(
            output_back_kernel,
            ga_all + head_w[layer],
            [small] * 4 + [wide],
        )

    def attend_back(layer, d_heads):
        return run(
            attend_back_kernel,
            d_heads + list(kept[layer][2:4]) + [seg_col, seg_row],
            [piece] * 4,
            pltpu.VMEM((count, DH), BF),
            *[pltpu.VMEM((count, DH), F32)] * 3,
        )

    def mixed_back(layer, d_pieces):
        return run(
            mixed_back_kernel,
            d_pieces + head_w[layer],
            [part] * 4 + [((tall, 768), BF)],
            pltpu.VMEM((GROUP, 384, 128), BF),
        )

    def norm_one_back(layer, parts, d_res):
        return run(
            norm_one_back_kernel,
            parts + [kept[layer][0], d_res, vec[layer]],
            [line, part, ((8, width), F32)],
        )

    row_terms = [None, None]
    top_parts, parts = turn[:4], trade(turn[4:8], FSDP)
    keep, got, fc_sums = feed_terms(turn[8], turn[11], turn[9], turn[10])
    d_res, ga, two_rows = norm_two_back(1, parts, grad)
    ga_all = gather(ga, FSDP)
    terms = total(keep, got, feed_share)
    upper_feed = list(terms)
    beside(terms, upper_feed, SEQ, 1, 2)
    *d_heads, ga_full = output_back(1, ga_all)
    d_heads = trade(d_heads, SEQ)
    tops = list(top_parts)
    beside(top_parts, tops, FSDP, 1, 3)
    d_pieces = trade(attend_back(1, d_heads), SEQ)
    beside(top_parts, tops, FSDP, 2)
    *parts, d_mixed = mixed_back(1, d_pieces)
    parts = trade(parts, FSDP)
    beside(terms, upper_feed, SEQ, 3)
    keep, got, mixed_sums = attend_terms(kept[1][1], d_mixed, kept[1][4], ga_full)
    (top,) = run(close_kernel, tops + [kept[1][5], vec[1]], [line], aside=True)
    _, low, one_rows = norm_one_back(1, parts, d_res)
    row_terms[1] = (two_rows, one_rows, fc_sums, mixed_sums)
    g_all = gather(low, FSDP)
    terms = total(keep, got, share)
    upper_attend = list(terms)
    beside(terms, upper_attend, SEQ, 1, 2)
    upper_feed = join(upper_feed, feed_share)

    *parts, d_pre, gb_full = run(
        feed_back_kernel,
        g_all + feed_w[0] + [slope],
        [part] * 4 + [((tall, 1024), BF), wide],
    )
    parts = trade(parts, FSDP)
    beside(terms, upper_attend, SEQ, 3)
    keep, got, fc_sums = feed_terms(act, gb_full, n_full, d_pre)
    terms = total(keep, got, feed_share)
    lower_feed = list(terms)
    beside(terms, lower_feed, SEQ, 1, 2, lag=True)
    d_res, ga, two_rows = norm_two_back(0, parts, low)
    ga_all = gather(ga, FSDP)
    upper_attend = join(upper_attend, share)
    beside(terms, lower_feed, SEQ, 3)
    *d_heads, ga_full = output_back(0, ga_all)
    d_heads = trade(d_heads, SEQ)
    mine, theirs = run(
        choose_kernel, lower_feed + [upper_feed], [feed_share] * 2, aside=True
    )
    got = swap(theirs)
    d_pieces = trade(attend_back(0, d_heads), SEQ)
    *blocks, g_proj = run(
        split_feed_kernel,
        [mine, got],
        [((64, 1024), BF)] * 4 + [((1, 256, width), F32)],
        aside=True,
    )
    fc_parts = list(blocks)
    beside(blocks, fc_parts, FSDP, 3, 2)
    *parts, d_mixed = mixed_back(0, d_pieces)
    parts = trade(parts, FSDP)
    keep, got, mixed_sums = attend_terms(kept[0][1], d_mixed, kept[0][4], ga_full)
    lower_attend = trade(total(keep, got, share), SEQ)
    bottom, _, one_rows = norm_one_back(0, parts, d_res)
    row_terms[0] = (two_rows, one_rows, fc_sums, mixed_sums)

    keep, send = run(
        rows_kernel,
        list(row_terms[0]) + list(row_terms[1]),
        [rows_shape] * 2,
        pltpu.VMEM((2, 16, width), F32),
    )
    rows_got = swap(send)

    def folded(rows, axis, d):
        return run(sum_kernel, [rows, exchange(rows, axis, d)], [rows_shape])[0]

    mine, theirs = run(choose_kernel, lower_attend + [upper_attend], [share] * 2)
    got = swap(theirs)
    (rows,) = run(sum_kernel, [keep, rows_got], [rows_shape])
    *blocks, g_out = run(
        split_attend_kernel,
        [mine, got],
        [((64, 768), BF)] * 4 + [((1, 64, width), F32)],
    )
    mixed_parts = trade(blocks, FSDP)
    fc_parts[1] = exchange(after(fc_parts[1], g_out), FSDP, 1)
    rows = folded(rows, SEQ, 1)
    rows = folded(rows, SEQ, 2)
    (g_fc,) = run(final_feed_kernel, fc_parts, [((1, 64, 4096), F32)])
    rows = folded(rows, FSDP, 1)
    last = exchange(rows, FSDP, 2)
    g_mixed, g_bfc, *vec_grads = run(
        final_attend_kernel,
        mixed_parts + [rows, last],
        [((1, 64, 3 * width), F32), ((1, 256), F32)] + [((1, 64), F32)] * 8,
        pltpu.VMEM((16, width), F32),
        pltpu.VMEM((GROUP, 64, 768), BF),
    )

    ends_mine = jnp.where(first, bottom, top)
    ends_other = swap(jnp.where(first, top, bottom))
    relay = jnp.where(
        first, jnp.stack([ends_mine, ends_other]), jnp.stack([ends_other, ends_mine])
    )[None]

    return (
        relay,
        vec_grads[0],
        vec_grads[1],
        g_mixed,
        vec_grads[6],
        vec_grads[7],
        g_out,
        vec_grads[2],
        vec_grads[3],
        vec_grads[4],
        g_fc,
        g_bfc,
        g_proj,
        vec_grads[5],
    )


def plan(mesh):
    fits = mesh.shape[SECTION] == 2 and mesh.shape[SEQ] == mesh.shape[FSDP] == GROUP
    return fast_body if fits else body


def solution(mesh):
    placed = (
        P(None, ("seq", "fsdp"), None),
        P(None, ("seq", "fsdp"), None),
        P(),
        P("section", "fsdp"),
        P("section", "fsdp"),
        P("section", "fsdp", None),
        P("section", "fsdp"),
        P("section", "fsdp"),
        P("section", "fsdp", None),
        P("section", "fsdp"),
        P("section", "fsdp"),
        P("section", "fsdp"),
        P("section", "fsdp", None),
        P("section", "fsdp"),
        P("section", "fsdp", None),
        P("section", "fsdp"),
    )
    return jax.shard_map(
        plan(mesh),
        mesh=mesh,
        in_specs=placed,
        out_specs=(
            P("section", None, ("seq", "fsdp"), None),
            P("section", ("seq", "fsdp")),
            P("section", ("seq", "fsdp")),
            P("section", ("seq", "fsdp"), None),
            P("section", ("seq", "fsdp")),
            P("section", ("seq", "fsdp")),
            P("section", ("seq", "fsdp"), None),
            P("section", ("seq", "fsdp")),
            P("section", ("seq", "fsdp")),
            P("section", ("seq", "fsdp")),
            P("section", ("seq", "fsdp"), None),
            P("section", ("seq", "fsdp")),
            P("section", ("seq", "fsdp"), None),
            P("section", ("seq", "fsdp")),
        ),
        check_vma=False,
    )
```

```python
import math

import jax
import jax.numpy as jnp
from jax import lax
from jax.experimental import pallas as pl
from jax.experimental.pallas import tpu as pltpu
from jax.sharding import PartitionSpec as P

DH = 64


EPSILON = 1e-05
NEGATIVE = -1e30


def shifted(block, axis, distance):
    devices = range(lax.axis_size(axis))
    route = [(i - distance, i) for i in devices if i - distance in devices]
    return lax.ppermute(block, axis, route)


def layer_norm(values, gain_vec, bias_vec):
    average = jnp.mean(values, axis=-1, keepdims=True)
    centred = values - average
    variance = jnp.mean(centred * centred, axis=-1, keepdims=True)
    return centred * lax.rsqrt(variance + EPSILON) * gain_vec + bias_vec


def gelu_tanh(values):
    return jax.nn.gelu(values, approximate=True)


def mask_rows(seg_row, fsdp_index, n_seq, n_fsdp, tok_rows):
    places = jnp.arange(seg_row.shape[0], dtype=jnp.int32)
    seg_grid = seg_row.reshape(n_seq, n_fsdp, tok_rows)
    place_grid = places.reshape(n_seq, n_fsdp, tok_rows)
    query_ids = lax.dynamic_index_in_dim(seg_grid, fsdp_index, 1, keepdims=False).reshape(-1)
    query_places = lax.dynamic_index_in_dim(place_grid, fsdp_index, 1, keepdims=False).reshape(-1)
    key_ids = jnp.transpose(seg_grid, (1, 0, 2)).reshape(-1)
    key_places = jnp.transpose(place_grid, (1, 0, 2)).reshape(-1)
    same_doc = (query_ids[:, None] == key_ids[None, :]) & (query_ids[:, None] > 0)
    itself = query_places[:, None] == key_places[None, :]
    return (key_places[None, :] <= query_places[:, None]) & (same_doc | itself)


def split_heads(matrix):
    return matrix.reshape(matrix.shape[0], matrix.shape[1] // DH, DH)


def block_rows(matrix, block_len):
    return matrix.reshape((matrix.shape[0] // block_len, block_len) + matrix.shape[1:])


def masked_scores(queries, key_rows, allowed):
    raw_scores = jnp.einsum(
        "qhd,khd->hqk",
        split_heads(queries),
        split_heads(key_rows),
        preferred_element_type=jnp.float32,
    )
    return jnp.where(allowed[None], raw_scores * DH ** (-0.5), NEGATIVE)


def body(
    inputs,
    cotangent,
    segment_ids,
    ln1_gain,
    ln1_bias,
    w_qkv,
    b_query,
    b_value,
    w_out,
    b_out,
    ln2_gain,
    ln2_bias,
    w_fc,
    b_fc,
    w_proj,
    b_proj,
):
    n_seq = lax.axis_size("seq")
    n_fsdp = lax.axis_size("fsdp")
    section_index = lax.axis_index("section")
    fsdp_index = lax.axis_index("fsdp")
    last_section = section_index == 1
    micro, tok_rows, width = inputs.shape
    score_scale = DH ** (-0.5)
    query_count = tok_rows * n_seq
    block_len = math.gcd(query_count, 512)

    def fetch_params():
        return (
            lax.all_gather(ln1_gain[0], "fsdp", axis=0, tiled=True),
            lax.all_gather(ln1_bias[0], "fsdp", axis=0, tiled=True),
            lax.all_gather(w_qkv[0], "fsdp", axis=0, tiled=True),
            lax.all_gather(b_query[0], "fsdp", axis=0, tiled=True),
            lax.all_gather(b_value[0], "fsdp", axis=0, tiled=True),
            lax.all_gather(w_out[0], "fsdp", axis=0, tiled=True),
            lax.all_gather(b_out[0], "fsdp", axis=0, tiled=True),
            lax.all_gather(ln2_gain[0], "fsdp", axis=0, tiled=True),
            lax.all_gather(ln2_bias[0], "fsdp", axis=0, tiled=True),
            lax.all_gather(w_fc[0], "fsdp", axis=0, tiled=True),
            lax.all_gather(b_fc[0], "fsdp", axis=0, tiled=True),
            lax.all_gather(w_proj[0], "fsdp", axis=0, tiled=True),
            lax.all_gather(b_proj[0], "fsdp", axis=0, tiled=True),
        )

    received = jnp.zeros((tok_rows, width), jnp.bfloat16)
    kept_ticks = []
    layer_outs = []
    for tick_index in range(micro + 1):
        params = fetch_params()
        batch_index = jnp.clip(tick_index - section_index, 0, micro - 1)
        seg_row = lax.dynamic_index_in_dim(segment_ids, batch_index, 0, keepdims=False)
        allowed = mask_rows(seg_row, fsdp_index, n_seq, n_fsdp, tok_rows)
        if tick_index < micro:
            first_in = inputs[tick_index].astype(jnp.float32)
        else:
            first_in = jnp.zeros((tok_rows, width), jnp.float32)
        layer_in = jnp.where(last_section, received.astype(jnp.float32), first_in)
        (
            forward_gain_one,
            forward_bias_one,
            forward_w_mixed,
            forward_bias_query,
            forward_bias_value,
            forward_w_output,
            forward_bias_output,
            forward_gain_two,
            forward_bias_two,
            forward_w_hidden,
            forward_bias_hidden,
            forward_w_back,
            forward_bias_back,
        ) = params
        forward_normed = layer_norm(
            layer_in, forward_gain_one.astype(jnp.float32), forward_bias_one.astype(jnp.float32)
        ).astype(jnp.bfloat16)
        mixed_proj = jnp.dot(forward_normed, forward_w_mixed, preferred_element_type=jnp.float32)
        bias_row = jnp.concatenate(
            [forward_bias_query, jnp.zeros_like(forward_bias_query), forward_bias_value]
        ).astype(jnp.float32)
        mixed_tok = (mixed_proj + bias_row).astype(jnp.bfloat16).reshape(tok_rows, 3, width)
        head_rows = lax.all_to_all(mixed_tok, "seq", split_axis=2, concat_axis=0, tiled=True)
        forward_queries = head_rows[:, 0]
        forward_key_rows = lax.all_gather(head_rows[:, 1], "fsdp", axis=0, tiled=True)
        forward_value_rows = lax.all_gather(head_rows[:, 2], "fsdp", axis=0, tiled=True)

        def attend_block(operands):
            query_block, allowed_block = operands
            scores = masked_scores(query_block, forward_key_rows, allowed_block)
            row_top = jnp.max(scores, axis=-1, keepdims=True)
            log_block = row_top + jnp.log(
                jnp.sum(jnp.exp(scores - row_top), axis=-1, keepdims=True)
            )
            attn_weights = jnp.exp(scores - log_block).astype(jnp.bfloat16)
            head_block = jnp.einsum(
                "hqk,khd->qhd",
                attn_weights,
                split_heads(forward_value_rows),
                preferred_element_type=jnp.float32,
            )
            return (head_block.reshape(query_block.shape).astype(jnp.bfloat16), log_block)

        head_blocks, forward_log_total = lax.map(
            attend_block, (block_rows(forward_queries, block_len), block_rows(allowed, block_len))
        )
        head_out = head_blocks.reshape(forward_queries.shape)
        forward_attended = lax.all_to_all(head_out, "seq", split_axis=0, concat_axis=1, tiled=True)
        forward_residual = (
            layer_in
            + jnp.dot(forward_attended, forward_w_output, preferred_element_type=jnp.float32)
            + forward_bias_output.astype(jnp.float32)
        )
        forward_normed_two = layer_norm(
            forward_residual,
            forward_gain_two.astype(jnp.float32),
            forward_bias_two.astype(jnp.float32),
        ).astype(jnp.bfloat16)
        forward_pre_act = jnp.dot(
            forward_normed_two, forward_w_hidden, preferred_element_type=jnp.float32
        ) + forward_bias_hidden.astype(jnp.float32)
        forward_activated = gelu_tanh(forward_pre_act).astype(jnp.bfloat16)
        layer_out = (
            forward_residual
            + jnp.dot(forward_activated, forward_w_back, preferred_element_type=jnp.float32)
            + forward_bias_back.astype(jnp.float32)
        )
        forward_kept = (
            layer_in,
            forward_normed,
            forward_queries,
            forward_key_rows,
            forward_value_rows,
            forward_log_total,
            allowed,
            forward_attended,
            forward_residual,
            forward_normed_two,
            forward_pre_act,
            forward_activated,
        )
        layer_out, kept = (layer_out, forward_kept)
        kept_ticks.append(kept)
        layer_outs.append(layer_out)
        if tick_index < micro:
            received = shifted(layer_out.astype(jnp.bfloat16), "section", 1)
    sent_back = jnp.zeros((tok_rows, width), jnp.bfloat16)
    input_grads = []
    totals = None
    for tick_index in range(micro + 1):
        params = fetch_params()
        later = kept_ticks[min(tick_index + 1, micro)]
        earlier = kept_ticks[max(tick_index - 1, 0)]
        kept = jax.tree.map(
            lambda upper, lower: jnp.where(last_section, upper, lower), later, earlier
        )
        if tick_index < micro:
            top_grad = cotangent[tick_index].astype(jnp.float32)
        else:
            top_grad = jnp.zeros((tok_rows, width), jnp.float32)
        grad_out = jnp.where(last_section, top_grad, sent_back.astype(jnp.float32))
        (
            gain_one,
            bias_one,
            w_mixed,
            bias_query,
            bias_value,
            w_output,
            bias_output,
            gain_two,
            bias_two,
            w_hidden,
            bias_hidden,
            w_back,
            bias_back,
        ) = params
        (
            backward_layer_in,
            normed,
            queries,
            key_rows,
            value_rows,
            log_total,
            backward_allowed,
            attended,
            residual,
            normed_two,
            pre_act,
            activated,
        ) = kept
        grad_back = grad_out.astype(jnp.bfloat16)
        d_w_back = jnp.einsum("cf,cd->fd", activated, grad_back, preferred_element_type=jnp.float32)
        d_bias_back = jnp.sum(grad_back.astype(jnp.float32), axis=0)
        d_activated = jnp.einsum("cd,fd->cf", grad_back, w_back, preferred_element_type=jnp.float32)
        gelu_pull = jax.vjp(gelu_tanh, pre_act)[1]
        d_pre = gelu_pull(d_activated)[0].astype(jnp.bfloat16)
        d_w_hidden = jnp.einsum("cm,cf->mf", normed_two, d_pre, preferred_element_type=jnp.float32)
        d_bias_hidden = jnp.sum(d_pre.astype(jnp.float32), axis=0)
        d_normed_two = jnp.einsum("cf,mf->cm", d_pre, w_hidden, preferred_element_type=jnp.float32)
        norm_pull_two = jax.vjp(
            layer_norm, residual, gain_two.astype(jnp.float32), bias_two.astype(jnp.float32)
        )[1]
        d_resid_part, d_gain_two, d_bias_two = norm_pull_two(d_normed_two)
        d_residual = grad_out + d_resid_part
        grad_attn = d_residual.astype(jnp.bfloat16)
        d_w_output = jnp.einsum(
            "cm,cd->md", attended, grad_attn, preferred_element_type=jnp.float32
        )
        d_bias_output = jnp.sum(grad_attn.astype(jnp.float32), axis=0)
        d_attended = jnp.einsum(
            "cd,md->cm", grad_attn, w_output, preferred_element_type=jnp.float32
        ).astype(jnp.bfloat16)
        d_head = lax.all_to_all(d_attended, "seq", split_axis=1, concat_axis=0, tiled=True)

        def grad_block(carry, operands):
            key_acc, value_acc = carry
            query_block, head_grad_block, allowed_block, log_block = operands
            scores = masked_scores(query_block, key_rows, allowed_block)
            attn_probs = jnp.exp(scores - log_block)
            d_weights = jnp.einsum(
                "qhd,khd->hqk",
                split_heads(head_grad_block),
                split_heads(value_rows),
                preferred_element_type=jnp.float32,
            )
            row_dot = jnp.sum(attn_probs * d_weights, axis=-1, keepdims=True)
            d_scores = (attn_probs * (d_weights - row_dot) * score_scale).astype(jnp.bfloat16)
            d_query_block = (
                jnp.einsum(
                    "hqk,khd->qhd",
                    d_scores,
                    split_heads(key_rows),
                    preferred_element_type=jnp.float32,
                )
                .reshape(query_block.shape)
                .astype(jnp.bfloat16)
            )
            key_acc = key_acc + jnp.einsum(
                "hqk,qhd->khd",
                d_scores,
                split_heads(query_block),
                preferred_element_type=jnp.float32,
            ).reshape(key_rows.shape)
            value_acc = value_acc + jnp.einsum(
                "hqk,qhd->khd",
                attn_probs.astype(jnp.bfloat16),
                split_heads(head_grad_block),
                preferred_element_type=jnp.float32,
            ).reshape(value_rows.shape)
            return ((key_acc, value_acc), d_query_block)

        empty_terms = (
            jnp.zeros(key_rows.shape, jnp.float32),
            jnp.zeros(value_rows.shape, jnp.float32),
        )
        (key_term, value_term), query_blocks = lax.scan(
            grad_block,
            empty_terms,
            (
                block_rows(queries, block_len),
                block_rows(d_head, block_len),
                block_rows(backward_allowed, block_len),
                log_total,
            ),
        )
        d_query = query_blocks.reshape(queries.shape)
        d_key = lax.psum_scatter(key_term, "fsdp", scatter_dimension=0, tiled=True)
        d_value = lax.psum_scatter(value_term, "fsdp", scatter_dimension=0, tiled=True)
        d_heads = jnp.stack(
            [d_query, d_key.astype(jnp.bfloat16), d_value.astype(jnp.bfloat16)], axis=1
        )
        d_mixed = lax.all_to_all(d_heads, "seq", split_axis=0, concat_axis=2, tiled=True)
        d_flat = d_mixed.reshape(tok_rows, 3 * width)
        d_w_mixed = jnp.einsum("cm,cn->mn", normed, d_flat, preferred_element_type=jnp.float32)
        d_bias_query = jnp.sum(d_mixed[:, 0].astype(jnp.float32), axis=0)
        d_bias_value = jnp.sum(d_mixed[:, 2].astype(jnp.float32), axis=0)
        d_normed = jnp.einsum("cn,mn->cm", d_flat, w_mixed, preferred_element_type=jnp.float32)
        norm_pull_one = jax.vjp(
            layer_norm,
            backward_layer_in,
            gain_one.astype(jnp.float32),
            bias_one.astype(jnp.float32),
        )[1]
        d_in_part, d_gain_one, d_bias_one = norm_pull_one(d_normed)
        d_in = d_residual + d_in_part
        d_in, local_grads = (
            d_in,
            (
                d_gain_one,
                d_bias_one,
                d_w_mixed,
                d_bias_query,
                d_bias_value,
                d_w_output,
                d_bias_output,
                d_gain_two,
                d_bias_two,
                d_w_hidden,
                d_bias_hidden,
                d_w_back,
                d_bias_back,
            ),
        )
        input_grads.append(d_in)
        shared = (
            lax.psum_scatter(local_grads[0], ("seq", "fsdp"), scatter_dimension=0, tiled=True),
            lax.psum_scatter(local_grads[1], ("seq", "fsdp"), scatter_dimension=0, tiled=True),
            lax.psum_scatter(local_grads[2], ("seq", "fsdp"), scatter_dimension=0, tiled=True),
            lax.psum_scatter(local_grads[3], ("seq", "fsdp"), scatter_dimension=0, tiled=True),
            lax.psum_scatter(local_grads[4], ("seq", "fsdp"), scatter_dimension=0, tiled=True),
            lax.psum_scatter(local_grads[5], ("seq", "fsdp"), scatter_dimension=0, tiled=True),
            lax.psum_scatter(local_grads[6], ("seq", "fsdp"), scatter_dimension=0, tiled=True),
            lax.psum_scatter(local_grads[7], ("seq", "fsdp"), scatter_dimension=0, tiled=True),
            lax.psum_scatter(local_grads[8], ("seq", "fsdp"), scatter_dimension=0, tiled=True),
            lax.psum_scatter(local_grads[9], ("seq", "fsdp"), scatter_dimension=0, tiled=True),
            lax.psum_scatter(local_grads[10], ("seq", "fsdp"), scatter_dimension=0, tiled=True),
            lax.psum_scatter(local_grads[11], ("seq", "fsdp"), scatter_dimension=0, tiled=True),
            lax.psum_scatter(local_grads[12], ("seq", "fsdp"), scatter_dimension=0, tiled=True),
        )
        totals = shared if totals is None else jax.tree.map(jnp.add, totals, shared)
        if tick_index < micro:
            sent_back = shifted(d_in.astype(jnp.bfloat16), "section", -1)
    section_tops = jnp.stack(layer_outs[1:])
    bottom_grads = jnp.stack(input_grads[1:])
    relay_ends = jnp.where(last_section, section_tops, bottom_grads)[None]
    return (relay_ends,) + tuple((grad_part[None] for grad_part in totals))


BF = jnp.bfloat16
F32 = jnp.float32
GROUP = 4
SECTION, SEQ, FSDP = "section", "seq", "fsdp"


def nt(left, right):
    return lax.dot_general(left, right, (((1,), (1,)), ((), ())), preferred_element_type=F32)


def tn(left, right):
    return lax.dot_general(left, right, (((0,), (0,)), ((), ())), preferred_element_type=F32)


def nn(left, right):
    return jnp.dot(left, right, preferred_element_type=F32)


def spot(start, size):
    return pl.ds(pl.multiple_of(start, size), size)


def call(kernel, ids, args, outs, scratch, anywhere, mib):
    places = [pltpu.HBM if i in anywhere else pltpu.VMEM for i in range(len(args))]
    args = [
        pltpu.with_memory_space_constraint(a, pltpu.HBM) if i in anywhere else a
        for i, a in enumerate(args)
    ]
    return pl.pallas_call(
        kernel,
        name=kernel.__name__.removesuffix("_kernel"),
        out_shape=[jax.ShapeDtypeStruct(shape, dtype) for shape, dtype in outs],
        in_specs=[pl.BlockSpec(memory_space=pltpu.SMEM)]
        + [pl.BlockSpec(memory_space=place) for place in places],
        out_specs=[pl.BlockSpec(memory_space=pltpu.VMEM)] * len(outs),
        scratch_shapes=list(scratch),
        compiler_params=pltpu.CompilerParams(vmem_limit_bytes=mib * 1024 * 1024),
        cost_estimate=pl.CostEstimate(flops=0, bytes_accessed=0, transcendentals=0),
    )(ids, *args)


def after(value, *earlier):
    return lax.optimization_barrier((value, earlier))[0]


def exchange(block, axis, d):
    return lax.ppermute(block, axis, [(i, i ^ d) for i in range(GROUP)])


def trade(blocks, axis):
    return [blocks[0]] + [exchange(blocks[d], axis, d) for d in range(1, GROUP)]


def gather(block, axis):
    return trade([block] * GROUP, axis)


def swap(block):
    return lax.ppermute(block, SECTION, [(0, 1), (1, 0)])


def normed_rows(values, gain_vec, bias_vec):
    average = jnp.mean(values, axis=-1, keepdims=True)
    centred = values - average
    variance = jnp.mean(centred * centred, axis=-1, keepdims=True)
    return centred * lax.rsqrt(variance + EPSILON) * gain_vec + bias_vec


def norm_pull(values, gain_vec, grad):
    average = jnp.mean(values, axis=-1, keepdims=True)
    centred = values - average
    variance = jnp.mean(centred * centred, axis=-1, keepdims=True)
    inverse = lax.rsqrt(variance + EPSILON)
    unit = centred * inverse
    scaled = grad * gain_vec
    first = jnp.mean(scaled, axis=-1, keepdims=True)
    second = jnp.mean(scaled * unit, axis=-1, keepdims=True)
    pulled = inverse * (scaled - first - unit * second)
    return (
        pulled,
        jnp.sum(grad * unit, axis=0, keepdims=True),
        jnp.sum(grad, axis=0, keepdims=True),
    )


def pick_kernel(ids, w_ref, out_ref, *refs):
    vector_refs, fc_bias_ref, x_ref, g_ref, fc_ref, proj_ref = refs[:8], *refs[8:13]
    mine_ref, send_ref, feed_mine_ref, feed_send_ref, x_out, g_out = refs[13:19]
    held, rows_held, lines, fc_line, sem = refs[19:]
    s, c = ids[0], ids[2]
    width = w_ref.shape[2] // 3
    sources = [w_ref.at[0, spot(s * 64, 64), :]]
    targets = [held]
    for k in range(GROUP):
        sources.append(out_ref.at[0, pl.ds(pl.multiple_of(k * 64 + s * 16, 16), 16), :])
        targets.append(rows_held.at[k])
    for i, ref in enumerate(vector_refs):
        sources.append(ref)
        targets.append(lines.at[i])
    sources += [fc_bias_ref, x_ref.at[c], g_ref.at[c]]
    targets += [fc_line, x_out, g_out]
    first = len(sources)
    for ref, half in ((feed_send_ref, 1 - c), (feed_mine_ref, c)):
        for k in range(GROUP):
            for j in range(GROUP):
                lanes = spot(j * 1024 + k * 256 + half * 128, 128)
                sources.append(fc_ref.at[0, spot(s * 64, 64), lanes])
                targets.append(ref.at[k, 0:64, j * 128 : (j + 1) * 128])
            rows = spot(k * 256 + half * 128 + s * 32, 32)
            sources += [proj_ref.at[0, rows, 0:512], proj_ref.at[0, rows, 512:1024]]
            targets += [ref.at[k, 64:96, :], ref.at[k, 96:128, :]]
    copies = [
        pltpu.make_async_copy(source, target, sem.at[i])
        for i, (source, target) in enumerate(zip(sources, targets))
    ]
    for copy in copies:
        copy.start()
    for copy in copies[:first]:
        copy.wait()

    def head(t, j, k):
        tile = held[:, spot(t * width + j * 256 + (k >> 1) * 128, 128)].astype(F32)
        return tile[:, DH:] if k & 1 else tile[:, :DH]

    foot = [lines[i].astype(F32) for i in range(len(vector_refs))]
    foot += [fc_line[:, k * 256 : (k + 1) * 256].astype(F32) for k in range(GROUP)]
    foot.append(jnp.zeros((4, 256), F32))
    foot = jnp.concatenate(foot, axis=0).astype(BF)
    foot = jnp.concatenate([foot, jnp.zeros((16, 256), BF)], axis=1)
    for ref, half in ((mine_ref, c), (send_ref, 1 - c)):
        for k in range(GROUP):
            for i in range(2):
                j = 2 * half + i
                pair = jnp.concatenate([head(0, j, k), head(1, j, k)], axis=1)
                ref[k, 0:64, i * 128 : (i + 1) * 128] = pair.astype(BF)
            pair = jnp.concatenate([head(2, 2 * half, k), head(2, 2 * half + 1, k)], axis=1)
            ref[k, 0:64, 256:384] = pair.astype(BF)
            for q in range(GROUP):
                ref[k, q * 16 : (q + 1) * 16, 384:512] = rows_held[
                    k, :, spot(half * 512 + q * 128, 128)
                ]
            ref[k, 64:80, :] = foot
    for copy in copies[first:]:
        copy.wait()


def settle_heads_kernel(ids, mine_ref, got_ref, x_ref, *refs):
    first, z = ids[2] == 0, ids[1]
    for d in range(GROUP):
        mine, got = mine_ref[z ^ d], got_ref[z ^ d]
        lower, upper = jnp.where(first, mine, got), jnp.where(first, got, mine)
        refs[d][0:64, :] = lower[0:64]
        refs[d][64:80, 0:256] = lower[64:80, 0:256]
        refs[d][64:80, 256:512] = upper[64:80, 0:256]
        refs[d][80:144, :] = x_ref[:, 0:512]
        refs[d][144:208, :] = x_ref[:, 512:1024]
        refs[GROUP][d] = upper[0:64]


def settle_feed_kernel(ids, mine_ref, got_ref, heads_ref, seg_ref, *refs):
    first, z = ids[2] == 0, ids[1]
    numbers = jnp.where(first, seg_ref[0:1, :], seg_ref[1:2, :]).astype(F32)
    refs[8][...] = jnp.broadcast_to(numbers, (128, numbers.shape[1])).T[:, 0:1]
    refs[9][...] = numbers
    for d in range(GROUP):
        mine, got = mine_ref[z ^ d], got_ref[z ^ d]
        refs[d][0:128, :] = jnp.where(first, mine, got)
        refs[d][128:192, :] = heads_ref[d]
        refs[GROUP + d][...] = jnp.where(first, got, mine)


def first_heads_kernel(ids, *refs):
    z = ids[1]
    heads_ref, x_refs, vec_refs = refs[GROUP], refs[5:9], refs[9:11]
    for d in range(GROUP):
        block = refs[d][...]
        x_refs[d][:, 0:512] = block[80:144]
        x_refs[d][:, 512:1024] = block[144:208]
        heads_ref[z ^ d] = block[0:64]
        lanes = spot((z ^ d) * 256, 256)
        for layer in range(2):
            rows = block[64:80, layer * 256 : (layer + 1) * 256].astype(F32)
            row = rows[8:9, :]
            for k in range(1, GROUP):
                row = jnp.where(z == k, rows[8 + k : 9 + k, :], row)
            vec_refs[layer][0:8, lanes] = rows[0:8, :]
            vec_refs[layer][8:9, lanes] = row


def part_kernel(ids, *refs):
    for d in range(GROUP):
        refs[GROUP][ids[1] ^ d] = refs[d][0:128, :]
        refs[GROUP + 1][ids[1] ^ d] = refs[d][128:192, :]


def place_kernel(axis, ids, *refs):
    for d in range(GROUP):
        refs[GROUP][ids[axis] ^ d] = refs[d][...]


def mixed_piece(ref, level):
    return jnp.concatenate([ref[k, level, :, 0:384] for k in range(GROUP)], axis=0)


def head_rows(ref, s):
    rows = []
    for d in range(GROUP):
        for k in range(GROUP):
            tiles = [ref[k, s ^ d, q * 16 : (q + 1) * 16, 384:512] for q in range(GROUP)]
            rows.append(jnp.concatenate(tiles, axis=1))
    return jnp.concatenate(rows, axis=0)


def hidden_piece(ref, level):
    return jnp.concatenate([ref[k, level, 0:64, :] for k in range(GROUP)], axis=0)


def back_share(ref):
    rows = []
    for j in range(GROUP):
        for k in range(GROUP):
            rows.append(jnp.concatenate([ref[k, j, 64:96, :], ref[k, j, 96:128, :]], axis=1))
    return jnp.concatenate(rows, axis=0)


def mixed_kernel(ids, *refs):
    x_refs, own_ref, oth_ref, vec = refs[:4], refs[4], refs[5], refs[6]
    out_refs, nf_ref, packed = refs[7:11], refs[11], refs[12]
    s, z, c = ids[0], ids[1], ids[2]
    gain_vec, bias_vec = vec[0:1, :], vec[1:2, :]
    for d in range(GROUP):
        nf_ref[d * 64 : (d + 1) * 64, :] = normed_rows(
            x_refs[d][...].astype(F32), gain_vec, bias_vec
        ).astype(BF)

    def bias_of(row, j):
        tile = vec[row : row + 1, spot(j * 256 + (z >> 1) * 128, 128)]
        return jnp.where((z & 1) == 1, tile[:, DH:], tile[:, :DH])

    empty = jnp.zeros((1, DH), F32)
    for ref, half in ((own_ref, c), (oth_ref, 1 - c)):
        total = jnp.zeros((GROUP * 64, 384), F32)
        for k in range(GROUP):
            total = total + nn(nf_ref[:, k * 256 : (k + 1) * 256], mixed_piece(ref, k))
        j = 2 * half
        row = jnp.concatenate(
            [
                bias_of(2, j),
                empty,
                bias_of(2, j + 1),
                empty,
                bias_of(3, j),
                bias_of(3, j + 1),
            ],
            axis=1,
        )
        total = total + row
        for i in range(2):
            packed[j + i, 0:256, :] = total[:, i * 128 : (i + 1) * 128].astype(BF)
            values = total[:, 256 + i * DH : 256 + (i + 1) * DH]
            packed[j + i, 256:384, :] = jnp.concatenate(
                [values[:128], values[128:]], axis=1
            ).astype(BF)
    for d in range(GROUP):
        out_refs[d][...] = packed[s ^ d]


def spread(ids, pieces, qk_ref, v_ref):
    s, z = ids[0], ids[1]
    for d in range(GROUP):
        for e in range(GROUP):
            rows = spot(((s ^ d) * GROUP + (z ^ e)) * 64, 64)
            qk_ref[rows, :] = pieces[d][e * 64 : (e + 1) * 64, :]
            lanes = slice(0, DH) if e < 2 else slice(DH, 128)
            start = 256 + (e & 1) * 64
            v_ref[rows, :] = pieces[d][start : start + 64, lanes]


def block_scores(qk_ref, seg_col, seg_row, start, size):
    stop = start + size
    queries = qk_ref[start:stop, 0:DH] * jnp.asarray(DH ** (-0.5), BF)
    scores = nt(queries, qk_ref[0:stop, DH:128])
    q_place = lax.broadcasted_iota(jnp.int32, (size, stop), 0) + start
    k_place = lax.broadcasted_iota(jnp.int32, (size, stop), 1)
    q_doc, k_doc = seg_col[start:stop, :], seg_row[:, 0:stop]
    same = (q_doc == k_doc) & (q_doc > 0.0)
    allowed = ((k_place <= q_place) & same) | (k_place == q_place)
    return jnp.where(allowed, scores, NEGATIVE)


def attend_kernel(ids, *refs):
    pieces, seg_col, seg_row = refs[:4], refs[4], refs[5]
    out_refs, qk_out, v_out = refs[6:10], refs[10], refs[11]
    qk_ref, v_ref, o_ref = refs[12:15]
    s, z = ids[0], ids[1]
    spread(ids, pieces, qk_ref, v_ref)
    qk_out[...] = qk_ref[...]
    v_out[...] = v_ref[...]
    count = qk_ref.shape[0]
    size = 256
    for start in range(0, count, size):
        scores = block_scores(qk_ref, seg_col, seg_row, start, size)
        top = jnp.max(scores, axis=-1, keepdims=True)
        grown = jnp.exp(scores - top)
        total = jnp.sum(grown, axis=-1, keepdims=True)
        mixed = nn(grown.astype(BF), v_ref[0 : start + size, :])
        o_ref[start : start + size, :] = (mixed / total).astype(BF)
    for d in range(GROUP):
        for e in range(2):
            left = o_ref[spot(((s ^ d) * GROUP + (z ^ e)) * 64, 64), :]
            right = o_ref[spot(((s ^ d) * GROUP + (z ^ (e + 2))) * 64, 64), :]
            out_refs[d][e * 64 : (e + 1) * 64, :] = jnp.concatenate([left, right], axis=1)


def unpacked(piece):
    return jnp.concatenate([piece[:, :DH], piece[:, DH:]], axis=0)


def output_kernel(ids, *refs):
    pieces, own_ref, oth_ref = refs[:4], refs[4], refs[5]
    out_refs, att_ref = refs[6:10], refs[10]
    s, c = ids[0], ids[2]
    att = jnp.concatenate([unpacked(pieces[d][...]) for d in range(GROUP)], axis=1)
    att_ref[...] = att
    for w_ref, half in ((own_ref, c), (oth_ref, 1 - c)):
        part = nn(att, head_rows(w_ref, s)).astype(BF)
        for d in range(GROUP):
            out_refs[d][:, spot(half * 512, 512)] = part[d * 64 : (d + 1) * 64, :]


def summed(refs):
    blocks = []
    for ref in refs:
        blocks += [ref[...]] if len(ref.shape) == 2 else [ref[k] for k in range(GROUP)]
    total = blocks[0].astype(F32)
    for block in blocks[1:]:
        total = total + block.astype(F32)
    return total


def residual_kernel(ids, *refs):
    x_ref, vec = refs[4], refs[5]
    res_ref, n_ref = refs[6], refs[7]
    res = x_ref[...].astype(F32) + summed(refs[:4]) + vec[4:5, :]
    res_ref[...] = res
    n_ref[...] = normed_rows(res, vec[5:6, :], vec[6:7, :]).astype(BF)


ROOT = math.sqrt(2.0 / math.pi)


def hidden_bias(vec, half):
    return jnp.concatenate(
        [vec[8:9, spot(j * 256 + half * 128, 128)] for j in range(GROUP)], axis=1
    )


def feed_forward(n_refs, shares, vec, c, nf_ref, keep):
    for d in range(GROUP):
        nf_ref[d * 64 : (d + 1) * 64, :] = n_refs[d][...]
    part = jnp.zeros(nf_ref.shape, F32)
    for place, half in ((0, c), (1, 1 - c)):
        cols = slice(place * 512, (place + 1) * 512)
        pre = jnp.zeros((GROUP * 64, 512), F32)
        for d in range(GROUP):
            pre = pre + nn(nf_ref[:, d * 256 : (d + 1) * 256], hidden_piece(shares[place], d))
        pre = pre + hidden_bias(vec, half)
        square = pre * pre
        bend = jnp.tanh(ROOT * pre * (1.0 + 0.044715 * square))
        act = (0.5 * pre * (1.0 + bend)).astype(BF)
        slope = 0.5 * (1.0 + bend) + (0.5 * ROOT) * pre * (1.0 - bend * bend) * (
            1.0 + (3.0 * 0.044715) * square
        )
        keep(cols, act, slope)
        part = part + nn(act, back_share(shares[place]))
    return part.astype(BF)


def feed_backward(g_blocks, shares, slope_ref, out_refs, d_pre_ref, gf_ref):
    for d in range(GROUP):
        gf_ref[d * 64 : (d + 1) * 64, :] = g_blocks[d]
    for place in range(2):
        cols = slice(place * 512, (place + 1) * 512)
        d_act = nt(gf_ref[...], back_share(shares[place]))
        d_pre_ref[:, cols] = (d_act * slope_ref[:, cols]).astype(BF)
    for d in range(GROUP):
        part = nt(d_pre_ref[:, 0:512], hidden_piece(shares[0], d))
        part = (part + nt(d_pre_ref[:, 512:1024], hidden_piece(shares[1], d))).astype(BF)
        for e in range(GROUP):
            out_refs[e][:, d * 256 : (d + 1) * 256] = part[e * 64 : (e + 1) * 64, :]


def feed_kernel(ids, *refs):
    slope_ref, act_ref, nf_ref = refs[11:14]

    def keep(cols, act, slope):
        act_ref[:, cols] = act
        slope_ref[:, cols] = slope

    part = feed_forward(refs[:4], refs[4:6], refs[6], ids[2], nf_ref, keep)
    for d in range(GROUP):
        refs[7 + d][...] = part[d * 64 : (d + 1) * 64, :]


def feed_back_kernel(ids, *refs):
    blocks = [ref[...] for ref in refs[:4]]
    feed_backward(blocks, refs[4:6], refs[6], refs[7:11], refs[11], refs[12])


def feed_turn_kernel(ids, *refs):
    shares, vec, top_refs, outs = refs[8:10], refs[10], refs[11:15], refs[15:19]
    act_ref, nf_ref, d_pre_ref, gf_ref, slope_ref = refs[19:24]

    def keep(cols, act, slope):
        act_ref[:, cols] = act
        slope_ref[:, cols] = slope

    part = feed_forward(refs[:4], shares, vec, ids[2], nf_ref, keep)
    for d in range(GROUP):
        top_refs[d][...] = part[d * 64 : (d + 1) * 64, :]
    blocks = [ref[...] for ref in refs[4:8]]
    feed_backward(blocks, shares, slope_ref, outs, d_pre_ref, gf_ref)


def close_kernel(ids, *refs):
    res_ref, vec, out_ref = refs[4:]
    out = res_ref[...] + summed(refs[:4]) + vec[7:8, :]
    out_ref[...] = out.astype(out_ref.dtype)


def norm_two_back_kernel(ids, *refs):
    res_ref, g_ref, vec = refs[4], refs[5], refs[6]
    d_res_ref, ga_ref, rows_ref = refs[7:10]
    grad = g_ref[...].astype(F32)
    pulled, d_gain, d_bias = norm_pull(res_ref[...], vec[5:6, :], summed(refs[:4]))
    d_res = grad + pulled
    low = d_res.astype(BF)
    d_res_ref[...] = d_res
    ga_ref[...] = low
    rows_ref[0:1, :] = jnp.sum(low.astype(F32), axis=0, keepdims=True)
    rows_ref[1:2, :] = d_gain
    rows_ref[2:3, :] = d_bias
    rows_ref[3:4, :] = jnp.sum(grad.astype(BF).astype(F32), axis=0, keepdims=True)
    rows_ref[4:8, :] = jnp.zeros((4, grad.shape[1]), F32)


def output_back_kernel(ids, *refs):
    g_refs, own_ref, oth_ref = refs[:4], refs[4], refs[5]
    out_refs, gf_ref = refs[6:10], refs[10]
    s, c = ids[0], ids[2]
    for d in range(GROUP):
        gf_ref[d * 64 : (d + 1) * 64, :] = g_refs[d][...]
    d_att = nt(gf_ref[:, spot(c * 512, 512)], head_rows(own_ref, s))
    d_att = d_att + nt(gf_ref[:, spot((1 - c) * 512, 512)], head_rows(oth_ref, s))
    for d in range(GROUP):
        cols = d_att[:, d * DH : (d + 1) * DH]
        out_refs[d][...] = jnp.concatenate([cols[:128], cols[128:]], axis=1).astype(BF)


def feed_grads_kernel(ids, *refs):
    act_ref, gb_ref, nf_ref, d_pre_ref = refs[:4]
    keep_ref, send_ref, sums_ref = refs[4:7]
    for place, out_ref in ((0, keep_ref), (1, send_ref)):
        cols = slice(place * 512, (place + 1) * 512)
        d_fc = tn(nf_ref[...], d_pre_ref[:, cols]).astype(BF)
        for k in range(GROUP):
            out_ref[k, 0:256, :] = d_fc[k * 256 : (k + 1) * 256, :]
        d_proj = tn(act_ref[:, cols], gb_ref[...]).astype(BF)
        for j in range(GROUP):
            rows = d_proj[j * 128 : (j + 1) * 128, :]
            out_ref[j, 256:384, :] = rows[:, 0:512]
            out_ref[j, 384:512, :] = rows[:, 512:1024]
    sums_ref[...] = jnp.sum(d_pre_ref[...].astype(F32), axis=0, keepdims=True)


def attend_back_kernel(ids, *refs):
    d_pieces, qk_ref, v_ref, seg_col, seg_row = refs[0:4], refs[4], refs[5], refs[6], refs[7]
    out_refs = refs[8:12]
    do_ref, dq_ref, dk_ref, dv_ref = refs[12:16]
    s, z = ids[0], ids[1]
    for d in range(GROUP):
        for e in range(GROUP):
            rows = spot(((s ^ d) * GROUP + (z ^ e)) * 64, 64)
            lanes = slice(0, DH) if e < 2 else slice(DH, 128)
            start = (e & 1) * 64
            do_ref[rows, :] = d_pieces[d][start : start + 64, lanes]
    count = qk_ref.shape[0]
    size = 256
    for start in range(0, count, size):
        stop = start + size
        scores = block_scores(qk_ref, seg_col, seg_row, start, size)
        top = jnp.max(scores, axis=-1, keepdims=True)
        grown = jnp.exp(scores - top)
        probs = grown * (1.0 / jnp.sum(grown, axis=-1, keepdims=True))
        d_out = do_ref[start:stop, :]
        d_weights = nt(d_out, v_ref[0:stop, :])
        row_dot = jnp.sum(probs * d_weights, axis=-1, keepdims=True)
        d_scores = (probs * (d_weights - row_dot) * DH ** (-0.5)).astype(BF)
        dq_ref[start:stop, :] = nn(d_scores, qk_ref[0:stop, DH:128])
        dk = tn(d_scores, qk_ref[start:stop, 0:DH])
        dv = tn(probs.astype(BF), d_out)
        if start:
            dk_ref[0:start, :] += dk[0:start]
            dv_ref[0:start, :] += dv[0:start]
        dk_ref[start:stop, :] = dk[start:stop]
        dv_ref[start:stop, :] = dv[start:stop]
    for d in range(GROUP):
        for e in range(GROUP):
            rows = spot(((s ^ d) * GROUP + (z ^ e)) * 64, 64)
            out_refs[d][e * 64 : (e + 1) * 64, :] = jnp.concatenate(
                [dq_ref[rows, :], dk_ref[rows, :]], axis=1
            ).astype(BF)
        for e in range(2):
            left = dv_ref[spot(((s ^ d) * GROUP + (z ^ e)) * 64, 64), :]
            right = dv_ref[spot(((s ^ d) * GROUP + (z ^ (e + 2))) * 64, 64), :]
            out_refs[d][256 + e * 64 : 320 + e * 64, :] = jnp.concatenate(
                [left, right], axis=1
            ).astype(BF)


def mixed_back_kernel(ids, *refs):
    pieces, own_ref, oth_ref = refs[:4], refs[4], refs[5]
    out_refs, dm_ref, held = refs[6:10], refs[10], refs[11]
    s, c = ids[0], ids[2]
    for d in range(GROUP):
        held[d] = pieces[d][...]
    for place, half in ((0, c), (1, 1 - c)):
        base = place * 384
        values = []
        for i in range(2):
            d = (2 * half + i) ^ s
            dm_ref[:, base + i * 128 : base + (i + 1) * 128] = held[d, 0:256, :]
            values.append(unpacked(held[d, 256:384, :]))
        dm_ref[:, base + 256 : base + 384] = jnp.concatenate(values, axis=1)
    for k in range(GROUP):
        part = nt(dm_ref[:, 0:384], mixed_piece(own_ref, k))
        part = (part + nt(dm_ref[:, 384:768], mixed_piece(oth_ref, k))).astype(BF)
        for d in range(GROUP):
            out_refs[d][:, k * 256 : (k + 1) * 256] = part[d * 64 : (d + 1) * 64, :]


def attend_grads_kernel(ids, *refs):
    nf_ref, dm_ref, att_ref, ga_ref, two_ref, fc_ref = refs[:6]
    part_refs, x_refs = refs[6:10], refs[10:14]
    keep_ref, send_ref, lines = refs[14:17]
    s, c = ids[0], ids[2]
    d_gain = d_bias = 0.0
    for d in range(GROUP):
        grad = part_refs[d][...].astype(F32)
        values = x_refs[d][...].astype(F32)
        average = jnp.mean(values, axis=-1, keepdims=True)
        centred = values - average
        variance = jnp.mean(centred * centred, axis=-1, keepdims=True)
        unit = centred * lax.rsqrt(variance + EPSILON)
        d_gain = d_gain + jnp.sum(grad * unit, axis=0, keepdims=True)
        d_bias = d_bias + jnp.sum(grad, axis=0, keepdims=True)
    lines[0:1, :] = d_gain
    lines[1:2, :] = d_bias
    lines[2:6, :] = two_ref[0:4, :]
    lines[6:8, :] = jnp.zeros((2, d_gain.shape[1]), F32)
    for place, out_ref, half in ((0, keep_ref, c), (1, send_ref, 1 - c)):
        base = place * 384
        d_w = tn(nf_ref[...], dm_ref[:, base : base + 384]).astype(BF)
        sums = jnp.sum(dm_ref[:, base : base + 384].astype(F32), axis=0, keepdims=True)
        for k in range(GROUP):
            out_ref[k, 0:256, 0:384] = d_w[k * 256 : (k + 1) * 256, :]
            mine = (k >> 1) == half
            i = k & 1
            query = sums[:, i * 128 : i * 128 + DH]
            value = sums[:, 256 + i * DH : 256 + (i + 1) * DH]
            first = place * 512 + k * 128
            line = jnp.concatenate(
                [
                    fc_ref[:, first : first + 128],
                    jnp.where(mine, query, 0.0),
                    jnp.where(mine, value, 0.0),
                    jnp.zeros((1, 128), F32),
                ],
                axis=1,
            )
            foot = jnp.concatenate([line, jnp.zeros((7, 384), F32)], axis=0)
            foot = jnp.concatenate([lines[:, spot(k * 256 + half * 128, 128)], foot], axis=1)
            foot = jnp.concatenate([foot, jnp.zeros((8, 512), F32)], axis=0)
            out_ref[k, 256:272, :] = foot.astype(BF)
        d_out = tn(att_ref[...], ga_ref[:, spot(half * 512, 512)]).astype(BF)
        for d in range(GROUP):
            for q in range(GROUP):
                out_ref[s ^ d, q * 64 : (q + 1) * 64, 384:512] = d_out[
                    d * 64 : (d + 1) * 64, q * 128 : (q + 1) * 128
                ]


def norm_one_back_kernel(ids, *refs):
    x_ref, d_res_ref, vec = refs[4], refs[5], refs[6]
    pulled, _, _ = norm_pull(x_ref[...].astype(F32), vec[0:1, :], summed(refs[:4]))
    d_in = d_res_ref[...] + pulled
    refs[7][...] = d_in
    refs[8][...] = d_in.astype(BF)


def add_kernel(ids, left_ref, right_ref, *out_refs):
    for d in range(GROUP):
        k = ids[0] ^ d
        out_refs[d][...] = (left_ref[k].astype(F32) + right_ref[k].astype(F32)).astype(BF)


def choose_kernel(ids, *refs):
    lower, upper = summed(refs[:4]).astype(BF), summed(refs[4:8]).astype(BF)
    first = ids[2] == 0
    refs[8][...] = jnp.where(first, lower, upper)
    refs[9][...] = jnp.where(first, upper, lower)


def split_feed_kernel(ids, own_ref, oth_ref, *refs):
    back_out = refs[GROUP]
    for d in range(GROUP):
        rows = spot((ids[1] ^ d) * 64, 64)
        refs[d][:, 0:512] = own_ref[rows, :]
        refs[d][:, 512:1024] = oth_ref[rows, :]
    for ref, half in ((own_ref, ids[2]), (oth_ref, 1 - ids[2])):
        rows = spot(half * 128, 128)
        back_out[0, rows, 0:512] = ref[256:384, :].astype(F32)
        back_out[0, rows, 512:1024] = ref[384:512, :].astype(F32)


def split_attend_kernel(ids, own_ref, oth_ref, *refs):
    out_ref, bfc_ref, query_ref, value_ref = refs[GROUP:]
    s, z, c = ids[0], ids[1], ids[2]
    foots = (own_ref[256:272, :], oth_ref[256:272, :])
    for d in range(GROUP):
        rows = spot((z ^ d) * 64, 64)
        refs[d][0:64, 0:384] = own_ref[rows, 0:384]
        refs[d][0:64, 384:768] = oth_ref[rows, 0:384]
        lines = jnp.where(((z ^ d) >> 1) == c, foots[0][:, 0:128], foots[1][:, 0:128])
        refs[d][64:80, :] = jnp.concatenate([lines, jnp.zeros((16, 640), BF)], axis=1)
    for ref, half in ((own_ref, c), (oth_ref, 1 - c)):
        for q in range(GROUP):
            out_ref[0, :, spot(half * 512 + q * 128, 128)] = ref[
                q * 64 : (q + 1) * 64, 384:512
            ].astype(F32)
    own, oth = foots[0][0:1, :].astype(F32), foots[1][0:1, :].astype(F32)
    lower, upper = jnp.where(c == 0, own, oth), jnp.where(c == 0, oth, own)
    bfc_ref[:, 0:128] = lower[:, 128:256]
    bfc_ref[:, 128:256] = upper[:, 128:256]
    line = jnp.where((s >> 1) == 0, lower, upper)
    query_ref[...] = line[:, 256 : 256 + DH]
    value_ref[...] = line[:, 256 + DH : 384]


def final_feed_kernel(ids, *refs):
    fc_out = refs[GROUP]
    for place, half in ((0, ids[2]), (1, 1 - ids[2])):
        for d in range(GROUP):
            for j in range(GROUP):
                start = place * 512 + j * 128
                lanes = spot(j * 1024 + (ids[1] ^ d) * 256 + half * 128, 128)
                fc_out[0, :, lanes] = refs[d][:, start : start + 128].astype(F32)


def final_attend_kernel(ids, *refs):
    mixed, mixed_out, line_outs, held = refs[:4], refs[4], refs[5:11], refs[11]
    z, c = ids[1], ids[2]
    width = mixed_out.shape[2] // 3
    lines = 0.0
    for d in range(GROUP):
        held[z ^ d] = mixed[d][0:64, :]
        lines = lines + mixed[d][64:80, 0:128].astype(F32)
    lines = jnp.where((z & 1) == 1, lines[:, DH:], lines[:, :DH])
    for i, ref in enumerate(line_outs):
        ref[...] = lines[i : i + 1, :]
    for place, half in ((0, c), (1, 1 - c)):
        base = place * 384
        for pair in range(2):
            for i in range(2):
                tiles = []
                for source in (2 * pair, 2 * pair + 1):
                    qk = held[source, :, base + i * 128 : base + (i + 1) * 128].astype(F32)
                    v = held[source, :, base + 256 + i * DH : base + 256 + (i + 1) * DH]
                    tiles.append((qk[:, :DH], qk[:, DH:], v.astype(F32)))
                for t in range(3):
                    start = t * width + (2 * half + i) * 256 + pair * 128
                    mixed_out[0, :, spot(start, 128)] = jnp.concatenate(
                        [tiles[0][t], tiles[1][t]], axis=1
                    )


def fast_body(
    inputs,
    cotangent,
    segment_ids,
    ln1_gain,
    ln1_bias,
    w_qkv,
    b_query,
    b_value,
    w_out,
    b_out,
    ln2_gain,
    ln2_bias,
    w_fc,
    b_fc,
    w_proj,
    b_proj,
):
    s, z, c = lax.axis_index(SEQ), lax.axis_index(FSDP), lax.axis_index("section")
    first = c == 0
    ids = jnp.stack([s, z, c]).astype(jnp.int32)
    tok, width = inputs.shape[1:]
    count = segment_ids.shape[1]
    tall = GROUP * tok
    piece = ((384, 128), BF)
    small = ((128, 128), BF)
    part = ((tok, width), BF)
    wide = ((tall, width), BF)
    line = ((tok, width), F32)
    share = ((272, 512), BF)
    feed_share = ((512, 512), BF)
    done, awaited, lagging = [], [], []

    def run(kernel, args, outs, *scratch, anywhere=(), mib=16, aside=False):
        args = list(args)
        earlier = done[-1:] + ([] if aside else list(awaited))
        if earlier:
            args[0] = after(args[0], *earlier)
        if not aside:
            awaited[:] = lagging
            lagging.clear()
        result = list(call(kernel, ids, args, outs, scratch, anywhere, mib))
        done.append(result[-1])
        return result

    def beside(blocks, got, axis, *which, lag=False):
        for d in which:
            got[d] = exchange(after(blocks[d], done[-1]), axis, d)
            (lagging if lag else awaited).append(got[d])

    def now(blocks):
        return [after(block, done[-1]) for block in blocks]

    def of(kernel, axis):
        def bound(*refs):
            kernel(axis, *refs)

        bound.__name__ = kernel.__name__
        return bound

    def shared(pieces, axis, shape, aside=False):
        (whole,) = run(of(place_kernel, axis), pieces, [(shape, BF)], aside=aside)
        return [whole, swap(whole)]

    mine, send, feed_mine, feed_send, x, grad = run(
        pick_kernel,
        [w_qkv, w_out]
        + [ln1_gain, ln1_bias, b_query, b_value, b_out, ln2_gain, ln2_bias, b_proj, b_fc]
        + [inputs, cotangent, w_fc, w_proj],
        [((GROUP, 80, 512), BF)] * 2 + [((GROUP, 128, 512), BF)] * 2 + [part] * 2,
        pltpu.VMEM((64, 3 * width), BF),
        pltpu.VMEM((GROUP, 16, width), BF),
        pltpu.VMEM((8, 1, 256), BF),
        pltpu.VMEM((1, 1024), BF),
        pltpu.SemaphoreType.DMA((64,)),
        anywhere=range(15),
    )
    *heads, upper_heads = run(
        settle_heads_kernel,
        [mine, swap(send), x],
        [((208, 512), BF)] * 4 + [((GROUP, 64, 512), BF)],
    )
    heads = trade(heads, FSDP)
    feed_got = swap(feed_send)
    heads, *rest = run(
        first_heads_kernel,
        heads,
        [((GROUP, 64, 512), BF)] + [part] * 4 + [((16, width), F32)] * 2,
    )
    x_all, vec = rest[:4], rest[4:]
    heads = gather(heads, SEQ)
    grad_all = [grad] * GROUP
    beside([grad] * GROUP, grad_all, FSDP, 1, 3)
    *rest, seg_col, seg_row = run(
        settle_feed_kernel,
        [feed_mine, feed_got, upper_heads, segment_ids],
        [((192, 512), BF)] * 4
        + [((128, 512), BF)] * 4
        + [((count, 1), F32), ((1, count), F32)],
        aside=True,
    )
    rest, upper_feed = rest[:4], rest[4:]
    head_w = [shared(heads, 0, (GROUP, GROUP, 64, 512)), None]

    feed_w = [None, None]
    kept = []
    for layer in range(2):
        *packed, normed = run(
            mixed_kernel,
            x_all + head_w[layer] + [vec[layer]],
            [piece] * 4 + [wide],
            pltpu.VMEM((GROUP, 384, 128), BF),
        )
        qkv = trade(packed, SEQ)
        got = rest[:1] + [None] * 3
        beside(rest, got, FSDP, 1, 3)
        if layer == 1:
            beside([grad] * GROUP, grad_all, FSDP, 2, lag=True)
        *heads, qk_rows, v_rows = run(
            attend_kernel,
            qkv + [seg_col, seg_row],
            [small] * 4 + [((count, 128), BF), ((count, DH), BF)],
            pltpu.VMEM((count, 128), BF),
            pltpu.VMEM((count, DH), BF),
            pltpu.VMEM((count, DH), BF),
        )
        heads = trade(heads, SEQ)
        beside(rest, got, FSDP, 2)
        *parts, att = run(
            output_kernel,
            heads + head_w[layer],
            [part] * 4 + [((tall, 256), BF)],
        )
        parts = trade(parts, FSDP)
        if layer == 0:
            feed, heads_later = run(
                part_kernel,
                got,
                [((GROUP, 128, 512), BF), ((GROUP, 64, 512), BF)],
                aside=True,
            )
        else:
            (feed,) = run(
                of(place_kernel, 1), got, [((GROUP, 128, 512), BF)], aside=True
            )
        feeds = [feed] * GROUP
        beside(feeds, feeds, SEQ, 1, 2)
        res, n_two = run(
            residual_kernel, parts + [x, vec[layer]], [line, part]
        )
        n_all = gather(n_two, FSDP)
        beside([feed] * GROUP, feeds, SEQ, 3)
        feeds[0] = after(feeds[0], *n_all)
        feed_w[layer] = shared(feeds, 0, (GROUP, GROUP, 128, 512))
        kept.append((x, normed, qk_rows, v_rows, att, res, x_all))
        if layer == 0:
            *parts, slope, act, n_full = run(
                feed_kernel,
                n_all + feed_w[0] + [vec[0]],
                [part] * 4 + [((tall, 1024), F32), ((tall, 1024), BF), wide],
            )
            parts = trade(parts, FSDP)
            heads = [heads_later] * GROUP
            beside(heads, heads, SEQ, 1, 2)
            (x,) = run(close_kernel, parts + [res, vec[0]], [part])
            x_all = gather(x, FSDP)
            beside([heads_later] * GROUP, heads, SEQ, 3)
            heads[0] = after(heads[0], *x_all)
            head_w[1] = shared(heads, 0, (GROUP, GROUP, 64, 512))
            rest = upper_feed
        else:
            turn = run(
                feed_turn_kernel,
                n_all + grad_all + feed_w[1] + [vec[1]],
                [part] * 8 + [((tall, 1024), BF), wide, ((tall, 1024), BF), wide],
                pltpu.VMEM((tall, 1024), F32),
                mib=20,
            )

    def feed_terms(act, gb_full, n_full, d_pre):
        keep, send, sums = run(
            feed_grads_kernel,
            [act, gb_full, n_full, d_pre],
            [((GROUP, 512, 512), BF)] * 2 + [((1, 1024), F32)],
            aside=True,
        )
        return keep, swap(send), sums

    def attend_terms(layer, two_rows, fc_sums, parts, d_mixed, ga_full):
        x, normed, _, _, att, _, x_all = kept[layer]
        keep, send = run(
            attend_grads_kernel,
            [normed, d_mixed, att, ga_full, two_rows, fc_sums] + parts + x_all,
            [((GROUP,) + share[0], BF)] * 2,
            pltpu.VMEM((8, width), F32),
            aside=True,
        )
        return keep, swap(send)

    def total(keep, got, shape):
        return run(add_kernel, [keep, got], [shape] * 4, aside=True)

    def norm_two_back(layer, parts, grad):
        return run(
            norm_two_back_kernel,
            parts + [kept[layer][5], grad, vec[layer]],
            [line, part, ((8, width), F32)],
        )

    def output_back(layer, ga_all):
        return run(
            output_back_kernel,
            ga_all + head_w[layer],
            [small] * 4 + [wide],
        )

    def attend_back(layer, d_heads):
        return run(
            attend_back_kernel,
            d_heads + list(kept[layer][2:4]) + [seg_col, seg_row],
            [piece] * 4,
            pltpu.VMEM((count, DH), BF),
            *[pltpu.VMEM((count, DH), F32)] * 3,
        )

    def mixed_back(layer, d_pieces):
        return run(
            mixed_back_kernel,
            d_pieces + head_w[layer],
            [part] * 4 + [((tall, 768), BF)],
            pltpu.VMEM((GROUP, 384, 128), BF),
        )

    def norm_one_back(layer, parts, d_res):
        return run(
            norm_one_back_kernel,
            parts + [kept[layer][0], d_res, vec[layer]],
            [line, part],
        )

    top_parts, parts = turn[:4], trade(turn[4:8], FSDP)
    keep, got, fc_sums = feed_terms(turn[8], turn[11], turn[9], turn[10])
    terms = total(keep, got, feed_share)
    d_res, ga, two_rows = norm_two_back(1, parts, grad)
    ga_all = gather(ga, FSDP)
    upper_feed = list(terms)
    beside(terms, upper_feed, SEQ, 1, 2)
    *d_heads, ga_full = output_back(1, ga_all)
    d_heads = trade(d_heads, SEQ)
    tops = list(top_parts)
    beside(top_parts, tops, FSDP, 1, 3)
    d_pieces = trade(attend_back(1, d_heads), SEQ)
    beside(top_parts, tops, FSDP, 2)
    *sent, d_mixed = mixed_back(1, d_pieces)
    parts = trade(sent, FSDP)
    beside(terms, upper_feed, SEQ, 3)
    keep, got = attend_terms(1, two_rows, fc_sums, sent, d_mixed, ga_full)
    (top,) = run(close_kernel, tops + [kept[1][5], vec[1]], [line], aside=True)
    upper_terms = total(keep, got, share)
    _, low = norm_one_back(1, parts, d_res)
    g_all = gather(low, FSDP)
    upper_attend = list(upper_terms)
    beside(upper_terms, upper_attend, SEQ, 1, 2)

    *parts, d_pre, gb_full = run(
        feed_back_kernel,
        g_all + feed_w[0] + [slope],
        [part] * 4 + [((tall, 1024), BF), wide],
    )
    parts = trade(parts, FSDP)
    keep, got, fc_sums = feed_terms(act, gb_full, n_full, d_pre)
    terms = total(keep, got, feed_share)
    lower_feed = list(terms)
    beside(terms, lower_feed, SEQ, 1, 2)
    d_res, ga, two_rows = norm_two_back(0, parts, low)
    ga_all = gather(ga, FSDP)
    beside(terms, lower_feed, SEQ, 3)
    beside(upper_terms, upper_attend, SEQ, 3)
    *d_heads, ga_full = output_back(0, ga_all)
    d_heads = trade(d_heads, SEQ)
    mine, theirs = run(choose_kernel, lower_feed + upper_feed, [feed_share] * 2, aside=True)
    got = swap(theirs)
    d_pieces = trade(attend_back(0, d_heads), SEQ)
    *blocks, g_proj = run(
        split_feed_kernel,
        [mine, got],
        [((64, 1024), BF)] * 4 + [((1, 256, width), F32)],
        aside=True,
    )
    fc_parts = list(blocks)
    beside(blocks, fc_parts, FSDP, 3, 2)
    *sent, d_mixed = mixed_back(0, d_pieces)
    keep, got = attend_terms(0, two_rows, fc_sums, sent, d_mixed, ga_full)
    lower_attend = trade(total(keep, got, share), SEQ)

    parts = trade(now(sent), FSDP)
    mine, theirs = run(choose_kernel, lower_attend + upper_attend, [share] * 2)
    got = swap(theirs)
    bottom, _ = norm_one_back(0, parts, d_res)
    *blocks, g_out, g_bfc, g_query, g_value = run(
        split_attend_kernel,
        [mine, got],
        [((80, 768), BF)] * 4
        + [((1, 64, width), F32), ((1, 256), F32), ((1, 64), F32), ((1, 64), F32)],
    )
    mixed_parts = trade(blocks, FSDP)
    fc_parts[1] = exchange(after(fc_parts[1], g_out), FSDP, 1)
    (g_fc,) = run(final_feed_kernel, fc_parts, [((1, 64, 4096), F32)])
    g_mixed, *lines = run(
        final_attend_kernel,
        mixed_parts,
        [((1, 64, 3 * width), F32)] + [((1, 64), F32)] * 6,
        pltpu.VMEM((GROUP, 64, 768), BF),
    )

    ends_mine = jnp.where(first, bottom, top)
    ends_other = swap(jnp.where(first, top, bottom))
    relay = jnp.where(
        first, jnp.stack([ends_mine, ends_other]), jnp.stack([ends_other, ends_mine])
    )[None]

    return (
        relay,
        lines[0],
        lines[1],
        g_mixed,
        g_query,
        g_value,
        g_out,
        lines[2],
        lines[3],
        lines[4],
        g_fc,
        g_bfc,
        g_proj,
        lines[5],
    )


def plan(mesh):
    fits = mesh.shape[SECTION] == 2 and mesh.shape[SEQ] == mesh.shape[FSDP] == GROUP
    return fast_body if fits else body


def solution(mesh):
    placed = (
        P(None, ("seq", "fsdp"), None),
        P(None, ("seq", "fsdp"), None),
        P(),
        P("section", "fsdp"),
        P("section", "fsdp"),
        P("section", "fsdp", None),
        P("section", "fsdp"),
        P("section", "fsdp"),
        P("section", "fsdp", None),
        P("section", "fsdp"),
        P("section", "fsdp"),
        P("section", "fsdp"),
        P("section", "fsdp", None),
        P("section", "fsdp"),
        P("section", "fsdp", None),
        P("section", "fsdp"),
    )
    return jax.shard_map(
        plan(mesh),
        mesh=mesh,
        in_specs=placed,
        out_specs=(
            P("section", None, ("seq", "fsdp"), None),
            P("section", ("seq", "fsdp")),
            P("section", ("seq", "fsdp")),
            P("section", ("seq", "fsdp"), None),
            P("section", ("seq", "fsdp")),
            P("section", ("seq", "fsdp")),
            P("section", ("seq", "fsdp"), None),
            P("section", ("seq", "fsdp")),
            P("section", ("seq", "fsdp")),
            P("section", ("seq", "fsdp")),
            P("section", ("seq", "fsdp"), None),
            P("section", ("seq", "fsdp")),
            P("section", ("seq", "fsdp"), None),
            P("section", ("seq", "fsdp")),
        ),
        check_vma=False,
    )
```

```python
import math

import jax
import jax.numpy as jnp
from jax import lax
from jax.experimental import pallas as pl
from jax.experimental.pallas import tpu as pltpu
from jax.sharding import PartitionSpec as P

DH = 64


EPSILON = 1e-05
NEGATIVE = -1e30


def shifted(block, axis, distance):
    devices = range(lax.axis_size(axis))
    route = [(i - distance, i) for i in devices if i - distance in devices]
    return lax.ppermute(block, axis, route)


def layer_norm(values, gain_vec, bias_vec):
    average = jnp.mean(values, axis=-1, keepdims=True)
    centred = values - average
    variance = jnp.mean(centred * centred, axis=-1, keepdims=True)
    return centred * lax.rsqrt(variance + EPSILON) * gain_vec + bias_vec


def gelu_tanh(values):
    return jax.nn.gelu(values, approximate=True)


def mask_rows(seg_row, fsdp_index, n_seq, n_fsdp, tok_rows):
    places = jnp.arange(seg_row.shape[0], dtype=jnp.int32)
    seg_grid = seg_row.reshape(n_seq, n_fsdp, tok_rows)
    place_grid = places.reshape(n_seq, n_fsdp, tok_rows)
    query_ids = lax.dynamic_index_in_dim(seg_grid, fsdp_index, 1, keepdims=False).reshape(-1)
    query_places = lax.dynamic_index_in_dim(place_grid, fsdp_index, 1, keepdims=False).reshape(-1)
    key_ids = jnp.transpose(seg_grid, (1, 0, 2)).reshape(-1)
    key_places = jnp.transpose(place_grid, (1, 0, 2)).reshape(-1)
    same_doc = (query_ids[:, None] == key_ids[None, :]) & (query_ids[:, None] > 0)
    itself = query_places[:, None] == key_places[None, :]
    return (key_places[None, :] <= query_places[:, None]) & (same_doc | itself)


def split_heads(matrix):
    return matrix.reshape(matrix.shape[0], matrix.shape[1] // DH, DH)


def block_rows(matrix, block_len):
    return matrix.reshape((matrix.shape[0] // block_len, block_len) + matrix.shape[1:])


def masked_scores(queries, key_rows, allowed):
    raw_scores = jnp.einsum(
        "qhd,khd->hqk",
        split_heads(queries),
        split_heads(key_rows),
        preferred_element_type=jnp.float32,
    )
    return jnp.where(allowed[None], raw_scores * DH ** (-0.5), NEGATIVE)


def body(
    inputs,
    cotangent,
    segment_ids,
    ln1_gain,
    ln1_bias,
    w_qkv,
    b_query,
    b_value,
    w_out,
    b_out,
    ln2_gain,
    ln2_bias,
    w_fc,
    b_fc,
    w_proj,
    b_proj,
):
    n_seq = lax.axis_size("seq")
    n_fsdp = lax.axis_size("fsdp")
    section_index = lax.axis_index("section")
    fsdp_index = lax.axis_index("fsdp")
    last_section = section_index == 1
    micro, tok_rows, width = inputs.shape
    score_scale = DH ** (-0.5)
    query_count = tok_rows * n_seq
    block_len = math.gcd(query_count, 512)

    def fetch_params():
        return (
            lax.all_gather(ln1_gain[0], "fsdp", axis=0, tiled=True),
            lax.all_gather(ln1_bias[0], "fsdp", axis=0, tiled=True),
            lax.all_gather(w_qkv[0], "fsdp", axis=0, tiled=True),
            lax.all_gather(b_query[0], "fsdp", axis=0, tiled=True),
            lax.all_gather(b_value[0], "fsdp", axis=0, tiled=True),
            lax.all_gather(w_out[0], "fsdp", axis=0, tiled=True),
            lax.all_gather(b_out[0], "fsdp", axis=0, tiled=True),
            lax.all_gather(ln2_gain[0], "fsdp", axis=0, tiled=True),
            lax.all_gather(ln2_bias[0], "fsdp", axis=0, tiled=True),
            lax.all_gather(w_fc[0], "fsdp", axis=0, tiled=True),
            lax.all_gather(b_fc[0], "fsdp", axis=0, tiled=True),
            lax.all_gather(w_proj[0], "fsdp", axis=0, tiled=True),
            lax.all_gather(b_proj[0], "fsdp", axis=0, tiled=True),
        )

    received = jnp.zeros((tok_rows, width), jnp.bfloat16)
    kept_ticks = []
    layer_outs = []
    for tick_index in range(micro + 1):
        params = fetch_params()
        batch_index = jnp.clip(tick_index - section_index, 0, micro - 1)
        seg_row = lax.dynamic_index_in_dim(segment_ids, batch_index, 0, keepdims=False)
        allowed = mask_rows(seg_row, fsdp_index, n_seq, n_fsdp, tok_rows)
        if tick_index < micro:
            first_in = inputs[tick_index].astype(jnp.float32)
        else:
            first_in = jnp.zeros((tok_rows, width), jnp.float32)
        layer_in = jnp.where(last_section, received.astype(jnp.float32), first_in)
        (
            forward_gain_one,
            forward_bias_one,
            forward_w_mixed,
            forward_bias_query,
            forward_bias_value,
            forward_w_output,
            forward_bias_output,
            forward_gain_two,
            forward_bias_two,
            forward_w_hidden,
            forward_bias_hidden,
            forward_w_back,
            forward_bias_back,
        ) = params
        forward_normed = layer_norm(
            layer_in, forward_gain_one.astype(jnp.float32), forward_bias_one.astype(jnp.float32)
        ).astype(jnp.bfloat16)
        mixed_proj = jnp.dot(forward_normed, forward_w_mixed, preferred_element_type=jnp.float32)
        bias_row = jnp.concatenate(
            [forward_bias_query, jnp.zeros_like(forward_bias_query), forward_bias_value]
        ).astype(jnp.float32)
        mixed_tok = (mixed_proj + bias_row).astype(jnp.bfloat16).reshape(tok_rows, 3, width)
        head_rows = lax.all_to_all(mixed_tok, "seq", split_axis=2, concat_axis=0, tiled=True)
        forward_queries = head_rows[:, 0]
        forward_key_rows = lax.all_gather(head_rows[:, 1], "fsdp", axis=0, tiled=True)
        forward_value_rows = lax.all_gather(head_rows[:, 2], "fsdp", axis=0, tiled=True)

        def attend_block(operands):
            query_block, allowed_block = operands
            scores = masked_scores(query_block, forward_key_rows, allowed_block)
            row_top = jnp.max(scores, axis=-1, keepdims=True)
            log_block = row_top + jnp.log(
                jnp.sum(jnp.exp(scores - row_top), axis=-1, keepdims=True)
            )
            attn_weights = jnp.exp(scores - log_block).astype(jnp.bfloat16)
            head_block = jnp.einsum(
                "hqk,khd->qhd",
                attn_weights,
                split_heads(forward_value_rows),
                preferred_element_type=jnp.float32,
            )
            return (head_block.reshape(query_block.shape).astype(jnp.bfloat16), log_block)

        head_blocks, forward_log_total = lax.map(
            attend_block, (block_rows(forward_queries, block_len), block_rows(allowed, block_len))
        )
        head_out = head_blocks.reshape(forward_queries.shape)
        forward_attended = lax.all_to_all(head_out, "seq", split_axis=0, concat_axis=1, tiled=True)
        forward_residual = (
            layer_in
            + jnp.dot(forward_attended, forward_w_output, preferred_element_type=jnp.float32)
            + forward_bias_output.astype(jnp.float32)
        )
        forward_normed_two = layer_norm(
            forward_residual,
            forward_gain_two.astype(jnp.float32),
            forward_bias_two.astype(jnp.float32),
        ).astype(jnp.bfloat16)
        forward_pre_act = jnp.dot(
            forward_normed_two, forward_w_hidden, preferred_element_type=jnp.float32
        ) + forward_bias_hidden.astype(jnp.float32)
        forward_activated = gelu_tanh(forward_pre_act).astype(jnp.bfloat16)
        layer_out = (
            forward_residual
            + jnp.dot(forward_activated, forward_w_back, preferred_element_type=jnp.float32)
            + forward_bias_back.astype(jnp.float32)
        )
        forward_kept = (
            layer_in,
            forward_normed,
            forward_queries,
            forward_key_rows,
            forward_value_rows,
            forward_log_total,
            allowed,
            forward_attended,
            forward_residual,
            forward_normed_two,
            forward_pre_act,
            forward_activated,
        )
        layer_out, kept = (layer_out, forward_kept)
        kept_ticks.append(kept)
        layer_outs.append(layer_out)
        if tick_index < micro:
            received = shifted(layer_out.astype(jnp.bfloat16), "section", 1)
    sent_back = jnp.zeros((tok_rows, width), jnp.bfloat16)
    input_grads = []
    totals = None
    for tick_index in range(micro + 1):
        params = fetch_params()
        later = kept_ticks[min(tick_index + 1, micro)]
        earlier = kept_ticks[max(tick_index - 1, 0)]
        kept = jax.tree.map(
            lambda upper, lower: jnp.where(last_section, upper, lower), later, earlier
        )
        if tick_index < micro:
            top_grad = cotangent[tick_index].astype(jnp.float32)
        else:
            top_grad = jnp.zeros((tok_rows, width), jnp.float32)
        grad_out = jnp.where(last_section, top_grad, sent_back.astype(jnp.float32))
        (
            gain_one,
            bias_one,
            w_mixed,
            bias_query,
            bias_value,
            w_output,
            bias_output,
            gain_two,
            bias_two,
            w_hidden,
            bias_hidden,
            w_back,
            bias_back,
        ) = params
        (
            backward_layer_in,
            normed,
            queries,
            key_rows,
            value_rows,
            log_total,
            backward_allowed,
            attended,
            residual,
            normed_two,
            pre_act,
            activated,
        ) = kept
        grad_back = grad_out.astype(jnp.bfloat16)
        d_w_back = jnp.einsum("cf,cd->fd", activated, grad_back, preferred_element_type=jnp.float32)
        d_bias_back = jnp.sum(grad_back.astype(jnp.float32), axis=0)
        d_activated = jnp.einsum("cd,fd->cf", grad_back, w_back, preferred_element_type=jnp.float32)
        gelu_pull = jax.vjp(gelu_tanh, pre_act)[1]
        d_pre = gelu_pull(d_activated)[0].astype(jnp.bfloat16)
        d_w_hidden = jnp.einsum("cm,cf->mf", normed_two, d_pre, preferred_element_type=jnp.float32)
        d_bias_hidden = jnp.sum(d_pre.astype(jnp.float32), axis=0)
        d_normed_two = jnp.einsum("cf,mf->cm", d_pre, w_hidden, preferred_element_type=jnp.float32)
        norm_pull_two = jax.vjp(
            layer_norm, residual, gain_two.astype(jnp.float32), bias_two.astype(jnp.float32)
        )[1]
        d_resid_part, d_gain_two, d_bias_two = norm_pull_two(d_normed_two)
        d_residual = grad_out + d_resid_part
        grad_attn = d_residual.astype(jnp.bfloat16)
        d_w_output = jnp.einsum(
            "cm,cd->md", attended, grad_attn, preferred_element_type=jnp.float32
        )
        d_bias_output = jnp.sum(grad_attn.astype(jnp.float32), axis=0)
        d_attended = jnp.einsum(
            "cd,md->cm", grad_attn, w_output, preferred_element_type=jnp.float32
        ).astype(jnp.bfloat16)
        d_head = lax.all_to_all(d_attended, "seq", split_axis=1, concat_axis=0, tiled=True)

        def grad_block(carry, operands):
            key_acc, value_acc = carry
            query_block, head_grad_block, allowed_block, log_block = operands
            scores = masked_scores(query_block, key_rows, allowed_block)
            attn_probs = jnp.exp(scores - log_block)
            d_weights = jnp.einsum(
                "qhd,khd->hqk",
                split_heads(head_grad_block),
                split_heads(value_rows),
                preferred_element_type=jnp.float32,
            )
            row_dot = jnp.sum(attn_probs * d_weights, axis=-1, keepdims=True)
            d_scores = (attn_probs * (d_weights - row_dot) * score_scale).astype(jnp.bfloat16)
            d_query_block = (
                jnp.einsum(
                    "hqk,khd->qhd",
                    d_scores,
                    split_heads(key_rows),
                    preferred_element_type=jnp.float32,
                )
                .reshape(query_block.shape)
                .astype(jnp.bfloat16)
            )
            key_acc = key_acc + jnp.einsum(
                "hqk,qhd->khd",
                d_scores,
                split_heads(query_block),
                preferred_element_type=jnp.float32,
            ).reshape(key_rows.shape)
            value_acc = value_acc + jnp.einsum(
                "hqk,qhd->khd",
                attn_probs.astype(jnp.bfloat16),
                split_heads(head_grad_block),
                preferred_element_type=jnp.float32,
            ).reshape(value_rows.shape)
            return ((key_acc, value_acc), d_query_block)

        empty_terms = (
            jnp.zeros(key_rows.shape, jnp.float32),
            jnp.zeros(value_rows.shape, jnp.float32),
        )
        (key_term, value_term), query_blocks = lax.scan(
            grad_block,
            empty_terms,
            (
                block_rows(queries, block_len),
                block_rows(d_head, block_len),
                block_rows(backward_allowed, block_len),
                log_total,
            ),
        )
        d_query = query_blocks.reshape(queries.shape)
        d_key = lax.psum_scatter(key_term, "fsdp", scatter_dimension=0, tiled=True)
        d_value = lax.psum_scatter(value_term, "fsdp", scatter_dimension=0, tiled=True)
        d_heads = jnp.stack(
            [d_query, d_key.astype(jnp.bfloat16), d_value.astype(jnp.bfloat16)], axis=1
        )
        d_mixed = lax.all_to_all(d_heads, "seq", split_axis=0, concat_axis=2, tiled=True)
        d_flat = d_mixed.reshape(tok_rows, 3 * width)
        d_w_mixed = jnp.einsum("cm,cn->mn", normed, d_flat, preferred_element_type=jnp.float32)
        d_bias_query = jnp.sum(d_mixed[:, 0].astype(jnp.float32), axis=0)
        d_bias_value = jnp.sum(d_mixed[:, 2].astype(jnp.float32), axis=0)
        d_normed = jnp.einsum("cn,mn->cm", d_flat, w_mixed, preferred_element_type=jnp.float32)
        norm_pull_one = jax.vjp(
            layer_norm,
            backward_layer_in,
            gain_one.astype(jnp.float32),
            bias_one.astype(jnp.float32),
        )[1]
        d_in_part, d_gain_one, d_bias_one = norm_pull_one(d_normed)
        d_in = d_residual + d_in_part
        d_in, local_grads = (
            d_in,
            (
                d_gain_one,
                d_bias_one,
                d_w_mixed,
                d_bias_query,
                d_bias_value,
                d_w_output,
                d_bias_output,
                d_gain_two,
                d_bias_two,
                d_w_hidden,
                d_bias_hidden,
                d_w_back,
                d_bias_back,
            ),
        )
        input_grads.append(d_in)
        shared = (
            lax.psum_scatter(local_grads[0], ("seq", "fsdp"), scatter_dimension=0, tiled=True),
            lax.psum_scatter(local_grads[1], ("seq", "fsdp"), scatter_dimension=0, tiled=True),
            lax.psum_scatter(local_grads[2], ("seq", "fsdp"), scatter_dimension=0, tiled=True),
            lax.psum_scatter(local_grads[3], ("seq", "fsdp"), scatter_dimension=0, tiled=True),
            lax.psum_scatter(local_grads[4], ("seq", "fsdp"), scatter_dimension=0, tiled=True),
            lax.psum_scatter(local_grads[5], ("seq", "fsdp"), scatter_dimension=0, tiled=True),
            lax.psum_scatter(local_grads[6], ("seq", "fsdp"), scatter_dimension=0, tiled=True),
            lax.psum_scatter(local_grads[7], ("seq", "fsdp"), scatter_dimension=0, tiled=True),
            lax.psum_scatter(local_grads[8], ("seq", "fsdp"), scatter_dimension=0, tiled=True),
            lax.psum_scatter(local_grads[9], ("seq", "fsdp"), scatter_dimension=0, tiled=True),
            lax.psum_scatter(local_grads[10], ("seq", "fsdp"), scatter_dimension=0, tiled=True),
            lax.psum_scatter(local_grads[11], ("seq", "fsdp"), scatter_dimension=0, tiled=True),
            lax.psum_scatter(local_grads[12], ("seq", "fsdp"), scatter_dimension=0, tiled=True),
        )
        totals = shared if totals is None else jax.tree.map(jnp.add, totals, shared)
        if tick_index < micro:
            sent_back = shifted(d_in.astype(jnp.bfloat16), "section", -1)
    section_tops = jnp.stack(layer_outs[1:])
    bottom_grads = jnp.stack(input_grads[1:])
    relay_ends = jnp.where(last_section, section_tops, bottom_grads)[None]
    return (relay_ends,) + tuple((grad_part[None] for grad_part in totals))


BF = jnp.bfloat16
F32 = jnp.float32
GROUP = 4
SECTION, SEQ, FSDP = "section", "seq", "fsdp"


def nt(left, right):
    return lax.dot_general(left, right, (((1,), (1,)), ((), ())), preferred_element_type=F32)


def tn(left, right):
    return lax.dot_general(left, right, (((0,), (0,)), ((), ())), preferred_element_type=F32)


def nn(left, right):
    return jnp.dot(left, right, preferred_element_type=F32)


def spot(start, size):
    return pl.ds(pl.multiple_of(start, size), size)


def call(kernel, ids, args, outs, scratch, anywhere, mib):
    places = [pltpu.HBM if i in anywhere else pltpu.VMEM for i in range(len(args))]
    args = [
        pltpu.with_memory_space_constraint(a, pltpu.HBM) if i in anywhere else a
        for i, a in enumerate(args)
    ]
    return pl.pallas_call(
        kernel,
        name=kernel.__name__.removesuffix("_kernel"),
        out_shape=[jax.ShapeDtypeStruct(shape, dtype) for shape, dtype in outs],
        in_specs=[pl.BlockSpec(memory_space=pltpu.SMEM)]
        + [pl.BlockSpec(memory_space=place) for place in places],
        out_specs=[pl.BlockSpec(memory_space=pltpu.VMEM)] * len(outs),
        scratch_shapes=list(scratch),
        compiler_params=pltpu.CompilerParams(vmem_limit_bytes=mib * 1024 * 1024),
        cost_estimate=pl.CostEstimate(flops=0, bytes_accessed=0, transcendentals=0),
    )(ids, *args)


def after(value, *earlier):
    return lax.optimization_barrier((value, earlier))[0]


def exchange(block, axis, d):
    return lax.ppermute(block, axis, [(i, i ^ d) for i in range(GROUP)])


def trade(blocks, axis):
    return [blocks[0]] + [exchange(blocks[d], axis, d) for d in range(1, GROUP)]


def gather(block, axis):
    return trade([block] * GROUP, axis)


def swap(block):
    return lax.ppermute(block, SECTION, [(0, 1), (1, 0)])


def normed_rows(values, gain_vec, bias_vec):
    average = jnp.mean(values, axis=-1, keepdims=True)
    centred = values - average
    variance = jnp.mean(centred * centred, axis=-1, keepdims=True)
    return centred * lax.rsqrt(variance + EPSILON) * gain_vec + bias_vec


def norm_pull(values, gain_vec, grad):
    average = jnp.mean(values, axis=-1, keepdims=True)
    centred = values - average
    variance = jnp.mean(centred * centred, axis=-1, keepdims=True)
    inverse = lax.rsqrt(variance + EPSILON)
    unit = centred * inverse
    scaled = grad * gain_vec
    first = jnp.mean(scaled, axis=-1, keepdims=True)
    second = jnp.mean(scaled * unit, axis=-1, keepdims=True)
    pulled = inverse * (scaled - first - unit * second)
    return (
        pulled,
        jnp.sum(grad * unit, axis=0, keepdims=True),
        jnp.sum(grad, axis=0, keepdims=True),
    )


def pick_kernel(ids, w_ref, out_ref, *refs):
    vector_refs, fc_bias_ref, x_ref, g_ref, fc_ref, proj_ref = refs[:8], *refs[8:13]
    mine_ref, send_ref, feed_mine_ref, feed_send_ref, x_out, g_out = refs[13:19]
    held, rows_held, lines, fc_line, sem = refs[19:]
    s, c = ids[0], ids[2]
    width = w_ref.shape[2] // 3
    sources = [w_ref.at[0, spot(s * 64, 64), :]]
    targets = [held]
    for k in range(GROUP):
        sources.append(out_ref.at[0, pl.ds(pl.multiple_of(k * 64 + s * 16, 16), 16), :])
        targets.append(rows_held.at[k])
    for i, ref in enumerate(vector_refs):
        sources.append(ref)
        targets.append(lines.at[i])
    sources += [fc_bias_ref, x_ref.at[c], g_ref.at[c]]
    targets += [fc_line, x_out, g_out]
    first = len(sources)
    for ref, half in ((feed_send_ref, 1 - c), (feed_mine_ref, c)):
        for k in range(GROUP):
            for j in range(GROUP):
                lanes = spot(j * 1024 + k * 256 + half * 128, 128)
                sources.append(fc_ref.at[0, spot(s * 64, 64), lanes])
                targets.append(ref.at[k, 0:64, j * 128 : (j + 1) * 128])
            rows = spot(k * 256 + half * 128 + s * 32, 32)
            sources += [proj_ref.at[0, rows, 0:512], proj_ref.at[0, rows, 512:1024]]
            targets += [ref.at[k, 64:96, :], ref.at[k, 96:128, :]]
    copies = [
        pltpu.make_async_copy(source, target, sem.at[i])
        for i, (source, target) in enumerate(zip(sources, targets))
    ]
    for copy in copies:
        copy.start()
    for copy in copies[:first]:
        copy.wait()

    def head(t, j, k):
        tile = held[:, spot(t * width + j * 256 + (k >> 1) * 128, 128)].astype(F32)
        return tile[:, DH:] if k & 1 else tile[:, :DH]

    foot = [lines[i].astype(F32) for i in range(len(vector_refs))]
    foot += [fc_line[:, k * 256 : (k + 1) * 256].astype(F32) for k in range(GROUP)]
    foot.append(jnp.zeros((4, 256), F32))
    foot = jnp.concatenate(foot, axis=0).astype(BF)
    foot = jnp.concatenate([foot, jnp.zeros((16, 256), BF)], axis=1)
    for ref, half in ((mine_ref, c), (send_ref, 1 - c)):
        for k in range(GROUP):
            for i in range(2):
                j = 2 * half + i
                pair = jnp.concatenate([head(0, j, k), head(1, j, k)], axis=1)
                ref[k, 0:64, i * 128 : (i + 1) * 128] = pair.astype(BF)
            pair = jnp.concatenate([head(2, 2 * half, k), head(2, 2 * half + 1, k)], axis=1)
            ref[k, 0:64, 256:384] = pair.astype(BF)
            for q in range(GROUP):
                ref[k, q * 16 : (q + 1) * 16, 384:512] = rows_held[
                    k, :, spot(half * 512 + q * 128, 128)
                ]
            ref[k, 64:80, :] = foot
    for copy in copies[first:]:
        copy.wait()


def settle_heads_kernel(ids, mine_ref, got_ref, x_ref, *refs):
    first, z = ids[2] == 0, ids[1]
    for d in range(GROUP):
        mine, got = mine_ref[z ^ d], got_ref[z ^ d]
        lower, upper = jnp.where(first, mine, got), jnp.where(first, got, mine)
        refs[d][0:64, :] = lower[0:64]
        refs[d][64:80, 0:256] = lower[64:80, 0:256]
        refs[d][64:80, 256:512] = upper[64:80, 0:256]
        refs[d][80:144, :] = x_ref[:, 0:512]
        refs[d][144:208, :] = x_ref[:, 512:1024]
        refs[GROUP][d] = upper[0:64]


def settle_feed_kernel(ids, mine_ref, got_ref, heads_ref, seg_ref, g_ref, *refs):
    first, z = ids[2] == 0, ids[1]
    numbers = jnp.where(first, seg_ref[0:1, :], seg_ref[1:2, :]).astype(F32)
    marked = jnp.where(numbers > 0.0, numbers, -1.0)
    refs[8][...] = jnp.broadcast_to(marked, (128, numbers.shape[1])).T[:, 0:1]
    refs[9][...] = numbers
    for d in range(GROUP):
        mine, got = mine_ref[z ^ d], got_ref[z ^ d]
        refs[d][0:128, :] = jnp.where(first, mine, got)
        refs[d][128:192, :] = heads_ref[d]
        refs[GROUP + d][0:128, :] = jnp.where(first, got, mine)
        refs[GROUP + d][128:192, :] = g_ref[:, 0:512]
        refs[GROUP + d][192:256, :] = g_ref[:, 512:1024]


def first_heads_kernel(ids, *refs):
    z = ids[1]
    heads_ref, x_refs, vec_refs = refs[GROUP], refs[5:9], refs[9:11]
    for d in range(GROUP):
        block = refs[d][...]
        x_refs[d][:, 0:512] = block[80:144]
        x_refs[d][:, 512:1024] = block[144:208]
        heads_ref[z ^ d] = block[0:64]
        lanes = spot((z ^ d) * 256, 256)
        for layer in range(2):
            rows = block[64:80, layer * 256 : (layer + 1) * 256].astype(F32)
            row = rows[8:9, :]
            for k in range(1, GROUP):
                row = jnp.where(z == k, rows[8 + k : 9 + k, :], row)
            vec_refs[layer][0:8, lanes] = rows[0:8, :]
            vec_refs[layer][8:9, lanes] = row


def part_kernel(ids, *refs):
    for d in range(GROUP):
        refs[GROUP][ids[1] ^ d] = refs[d][0:128, :]
        refs[GROUP + 1][ids[1] ^ d] = refs[d][128:192, :]


def turn_part_kernel(ids, *refs):
    for d in range(GROUP):
        refs[GROUP][ids[1] ^ d] = refs[d][0:128, :]
        refs[GROUP + 1 + d][:, 0:512] = refs[d][128:192, :]
        refs[GROUP + 1 + d][:, 512:1024] = refs[d][192:256, :]


def place_kernel(axis, ids, *refs):
    for d in range(GROUP):
        refs[GROUP][ids[axis] ^ d] = refs[d][...]


def mixed_piece(ref, level):
    return jnp.concatenate([ref[k, level, :, 0:384] for k in range(GROUP)], axis=0)


def head_rows(ref, s):
    rows = []
    for d in range(GROUP):
        for k in range(GROUP):
            tiles = [ref[k, s ^ d, q * 16 : (q + 1) * 16, 384:512] for q in range(GROUP)]
            rows.append(jnp.concatenate(tiles, axis=1))
    return jnp.concatenate(rows, axis=0)


def hidden_piece(ref, level):
    return jnp.concatenate([ref[k, level, 0:64, :] for k in range(GROUP)], axis=0)


def back_share(ref):
    rows = []
    for j in range(GROUP):
        for k in range(GROUP):
            rows.append(jnp.concatenate([ref[k, j, 64:96, :], ref[k, j, 96:128, :]], axis=1))
    return jnp.concatenate(rows, axis=0)


def mixed_kernel(ids, *refs):
    x_refs, own_ref, oth_ref, vec = refs[:4], refs[4], refs[5], refs[6]
    out_refs, nf_ref, packed = refs[7:11], refs[11], refs[12]
    s, z, c = ids[0], ids[1], ids[2]
    gain_vec, bias_vec = vec[0:1, :], vec[1:2, :]
    for d in range(GROUP):
        nf_ref[d * 64 : (d + 1) * 64, :] = normed_rows(
            x_refs[d][...].astype(F32), gain_vec, bias_vec
        ).astype(BF)

    def bias_of(row, j):
        tile = vec[row : row + 1, spot(j * 256 + (z >> 1) * 128, 128)]
        return jnp.where((z & 1) == 1, tile[:, DH:], tile[:, :DH])

    empty = jnp.zeros((1, DH), F32)
    for ref, half in ((own_ref, c), (oth_ref, 1 - c)):
        total = jnp.zeros((GROUP * 64, 384), F32)
        for k in range(GROUP):
            total = total + nn(nf_ref[:, k * 256 : (k + 1) * 256], mixed_piece(ref, k))
        j = 2 * half
        row = jnp.concatenate(
            [
                bias_of(2, j),
                empty,
                bias_of(2, j + 1),
                empty,
                bias_of(3, j),
                bias_of(3, j + 1),
            ],
            axis=1,
        )
        total = total + row
        for i in range(2):
            packed[j + i, 0:256, :] = total[:, i * 128 : (i + 1) * 128].astype(BF)
            values = total[:, 256 + i * DH : 256 + (i + 1) * DH]
            packed[j + i, 256:384, :] = jnp.concatenate(
                [values[:128], values[128:]], axis=1
            ).astype(BF)
    for d in range(GROUP):
        out_refs[d][...] = packed[s ^ d]


def spread(ids, pieces, qk_ref, v_ref):
    s, z = ids[0], ids[1]
    for d in range(GROUP):
        for e in range(GROUP):
            rows = spot(((s ^ d) * GROUP + (z ^ e)) * 64, 64)
            qk_ref[rows, :] = pieces[d][e * 64 : (e + 1) * 64, :]
            lanes = slice(0, DH) if e < 2 else slice(DH, 128)
            start = 256 + (e & 1) * 64
            v_ref[rows, :] = pieces[d][start : start + 64, lanes]


def block_scores(qk_ref, seg_col, seg_row, start, size):
    stop = start + size
    queries = qk_ref[start:stop, 0:DH] * jnp.asarray(DH ** (-0.5), BF)
    scores = nt(queries, qk_ref[0:stop, DH:128])
    same = seg_col[start:stop, :] == seg_row[:, 0:stop]
    q_place = lax.broadcasted_iota(jnp.int32, (size, size), 0)
    k_place = lax.broadcasted_iota(jnp.int32, (size, size), 1)
    near = ((k_place <= q_place) & same[:, start:stop]) | (k_place == q_place)
    near = jnp.where(near, scores[:, start:stop], NEGATIVE)
    if start == 0:
        return near
    return jnp.concatenate([jnp.where(same[:, :start], scores[:, :start], NEGATIVE), near], axis=1)


def attend_kernel(ids, *refs):
    pieces, seg_col, seg_row = refs[:4], refs[4], refs[5]
    out_refs, qk_ref, v_ref, probs_ref, o_ref = refs[6:10], *refs[10:14]
    s, z = ids[0], ids[1]
    spread(ids, pieces, qk_ref, v_ref)
    count = qk_ref.shape[0]
    size = 256
    for start in range(0, count, size):
        scores = block_scores(qk_ref, seg_col, seg_row, start, size)
        top = jnp.max(scores, axis=-1, keepdims=True)
        grown = jnp.exp(scores - top)
        total = jnp.sum(grown, axis=-1, keepdims=True)
        probs = grown * (1.0 / total)
        probs_ref[start : start + size, 0 : start + size] = probs
        o_ref[start : start + size, :] = nn(
            probs.astype(BF), v_ref[0 : start + size, :]
        ).astype(BF)
    for d in range(GROUP):
        for e in range(2):
            left = o_ref[spot(((s ^ d) * GROUP + (z ^ e)) * 64, 64), :]
            right = o_ref[spot(((s ^ d) * GROUP + (z ^ (e + 2))) * 64, 64), :]
            out_refs[d][e * 64 : (e + 1) * 64, :] = jnp.concatenate([left, right], axis=1)


def unpacked(piece):
    return jnp.concatenate([piece[:, :DH], piece[:, DH:]], axis=0)


def output_kernel(ids, *refs):
    pieces, own_ref, oth_ref = refs[:4], refs[4], refs[5]
    out_refs, att_ref = refs[6:10], refs[10]
    s, c = ids[0], ids[2]
    att = jnp.concatenate([unpacked(pieces[d][...]) for d in range(GROUP)], axis=1)
    att_ref[...] = att
    for w_ref, half in ((own_ref, c), (oth_ref, 1 - c)):
        part = nn(att, head_rows(w_ref, s)).astype(BF)
        for d in range(GROUP):
            out_refs[d][:, spot(half * 512, 512)] = part[d * 64 : (d + 1) * 64, :]


def summed(refs):
    blocks = []
    for ref in refs:
        blocks += [ref[...]] if len(ref.shape) == 2 else [ref[k] for k in range(GROUP)]
    total = blocks[0].astype(F32)
    for block in blocks[1:]:
        total = total + block.astype(F32)
    return total


def residual_kernel(ids, *refs):
    x_ref, vec = refs[4], refs[5]
    res_ref, n_ref = refs[6], refs[7]
    res = x_ref[...].astype(F32) + summed(refs[:4]) + vec[4:5, :]
    res_ref[...] = res
    n_ref[...] = normed_rows(res, vec[5:6, :], vec[6:7, :]).astype(BF)


ROOT = math.sqrt(2.0 / math.pi)


def hidden_bias(vec, half):
    return jnp.concatenate(
        [vec[8:9, spot(j * 256 + half * 128, 128)] for j in range(GROUP)], axis=1
    )


def feed_forward(n_refs, shares, vec, c, nf_ref, keep):
    for d in range(GROUP):
        nf_ref[d * 64 : (d + 1) * 64, :] = n_refs[d][...]
    part = jnp.zeros(nf_ref.shape, F32)
    for place, half in ((0, c), (1, 1 - c)):
        cols = slice(place * 512, (place + 1) * 512)
        pre = jnp.zeros((GROUP * 64, 512), F32)
        for d in range(GROUP):
            pre = pre + nn(nf_ref[:, d * 256 : (d + 1) * 256], hidden_piece(shares[place], d))
        pre = pre + hidden_bias(vec, half)
        square = pre * pre
        bend = jnp.tanh(ROOT * pre * (1.0 + 0.044715 * square))
        act = (0.5 * pre * (1.0 + bend)).astype(BF)
        slope = 0.5 * (1.0 + bend) + (0.5 * ROOT) * pre * (1.0 - bend * bend) * (
            1.0 + (3.0 * 0.044715) * square
        )
        keep(cols, act, slope)
        part = part + nn(act, back_share(shares[place]))
    return part.astype(BF)


def feed_backward(g_blocks, shares, slope_ref, out_refs, d_pre_ref, gf_ref):
    for d in range(GROUP):
        gf_ref[d * 64 : (d + 1) * 64, :] = g_blocks[d]
    for place in range(2):
        cols = slice(place * 512, (place + 1) * 512)
        d_act = nt(gf_ref[...], back_share(shares[place]))
        d_pre_ref[:, cols] = (d_act * slope_ref[:, cols]).astype(BF)
    for d in range(GROUP):
        part = nt(d_pre_ref[:, 0:512], hidden_piece(shares[0], d))
        part = (part + nt(d_pre_ref[:, 512:1024], hidden_piece(shares[1], d))).astype(BF)
        for e in range(GROUP):
            out_refs[e][:, d * 256 : (d + 1) * 256] = part[e * 64 : (e + 1) * 64, :]


def feed_kernel(ids, *refs):
    slope_ref, act_ref, nf_ref = refs[11:14]

    def keep(cols, act, slope):
        act_ref[:, cols] = act
        slope_ref[:, cols] = slope

    part = feed_forward(refs[:4], refs[4:6], refs[6], ids[2], nf_ref, keep)
    for d in range(GROUP):
        refs[7 + d][...] = part[d * 64 : (d + 1) * 64, :]


def feed_back_kernel(ids, *refs):
    blocks = [ref[...] for ref in refs[:4]]
    feed_backward(blocks, refs[4:6], refs[6], refs[7:11], refs[11], refs[12])


def feed_turn_kernel(ids, *refs):
    shares, vec, top_refs, outs = refs[8:10], refs[10], refs[11:15], refs[15:19]
    act_ref, nf_ref, d_pre_ref, gf_ref, slope_ref = refs[19:24]

    def keep(cols, act, slope):
        act_ref[:, cols] = act
        slope_ref[:, cols] = slope

    part = feed_forward(refs[:4], shares, vec, ids[2], nf_ref, keep)
    for d in range(GROUP):
        top_refs[d][...] = part[d * 64 : (d + 1) * 64, :]
    blocks = [ref[...] for ref in refs[4:8]]
    feed_backward(blocks, shares, slope_ref, outs, d_pre_ref, gf_ref)


def close_kernel(ids, *refs):
    res_ref, vec, out_ref = refs[4:]
    out = res_ref[...] + summed(refs[:4]) + vec[7:8, :]
    out_ref[...] = out.astype(out_ref.dtype)


def norm_two_back_kernel(ids, *refs):
    res_ref, g_ref, vec = refs[4], refs[5], refs[6]
    d_res_ref, ga_ref, rows_ref = refs[7:10]
    grad = g_ref[...].astype(F32)
    pulled, d_gain, d_bias = norm_pull(res_ref[...], vec[5:6, :], summed(refs[:4]))
    d_res = grad + pulled
    low = d_res.astype(BF)
    d_res_ref[...] = d_res
    ga_ref[...] = low
    rows_ref[0:1, :] = jnp.sum(low.astype(F32), axis=0, keepdims=True)
    rows_ref[1:2, :] = d_gain
    rows_ref[2:3, :] = d_bias
    rows_ref[3:4, :] = jnp.sum(grad.astype(BF).astype(F32), axis=0, keepdims=True)
    rows_ref[4:8, :] = jnp.zeros((4, grad.shape[1]), F32)


def output_back_kernel(ids, *refs):
    g_refs, own_ref, oth_ref = refs[:4], refs[4], refs[5]
    out_refs, gf_ref = refs[6:10], refs[10]
    s, c = ids[0], ids[2]
    for d in range(GROUP):
        gf_ref[d * 64 : (d + 1) * 64, :] = g_refs[d][...]
    d_att = nt(gf_ref[:, spot(c * 512, 512)], head_rows(own_ref, s))
    d_att = d_att + nt(gf_ref[:, spot((1 - c) * 512, 512)], head_rows(oth_ref, s))
    for d in range(GROUP):
        cols = d_att[:, d * DH : (d + 1) * DH]
        out_refs[d][...] = jnp.concatenate([cols[:128], cols[128:]], axis=1).astype(BF)


def feed_grads_kernel(ids, *refs):
    act_ref, gb_ref, nf_ref, d_pre_ref = refs[:4]
    keep_ref, send_ref, sums_ref = refs[4:7]
    for place, out_ref in ((0, keep_ref), (1, send_ref)):
        cols = slice(place * 512, (place + 1) * 512)
        d_fc = tn(nf_ref[...], d_pre_ref[:, cols]).astype(BF)
        for k in range(GROUP):
            out_ref[k, 0:256, :] = d_fc[k * 256 : (k + 1) * 256, :]
        d_proj = tn(act_ref[:, cols], gb_ref[...]).astype(BF)
        for j in range(GROUP):
            rows = d_proj[j * 128 : (j + 1) * 128, :]
            out_ref[j, 256:384, :] = rows[:, 0:512]
            out_ref[j, 384:512, :] = rows[:, 512:1024]
    sums_ref[...] = jnp.sum(d_pre_ref[...].astype(F32), axis=0, keepdims=True)


def attend_back_kernel(ids, *refs):
    d_pieces, qk_ref, v_ref, probs_ref, out_refs = refs[0:4], *refs[4:7], refs[7:11]
    do_ref, dq_ref, dk_ref, dv_ref = refs[11:15]
    s, z = ids[0], ids[1]
    for d in range(GROUP):
        for e in range(GROUP):
            rows = spot(((s ^ d) * GROUP + (z ^ e)) * 64, 64)
            lanes = slice(0, DH) if e < 2 else slice(DH, 128)
            start = (e & 1) * 64
            do_ref[rows, :] = d_pieces[d][start : start + 64, lanes]
    count = qk_ref.shape[0]
    size = 256
    for start in range(0, count, size):
        stop = start + size
        probs = probs_ref[start:stop, 0:stop]
        d_out = do_ref[start:stop, :]
        d_weights = nt(d_out, v_ref[0:stop, :])
        row_dot = jnp.sum(probs * d_weights, axis=-1, keepdims=True)
        d_scores = (probs * (d_weights - row_dot) * DH ** (-0.5)).astype(BF)
        dq_ref[start:stop, :] = nn(d_scores, qk_ref[0:stop, DH:128])
        dk = tn(d_scores, qk_ref[start:stop, 0:DH])
        dv = tn(probs.astype(BF), d_out)
        if start:
            dk_ref[0:start, :] += dk[0:start]
            dv_ref[0:start, :] += dv[0:start]
        dk_ref[start:stop, :] = dk[start:stop]
        dv_ref[start:stop, :] = dv[start:stop]
    for d in range(GROUP):
        for e in range(GROUP):
            rows = spot(((s ^ d) * GROUP + (z ^ e)) * 64, 64)
            out_refs[d][e * 64 : (e + 1) * 64, :] = jnp.concatenate(
                [dq_ref[rows, :], dk_ref[rows, :]], axis=1
            ).astype(BF)
        for e in range(2):
            left = dv_ref[spot(((s ^ d) * GROUP + (z ^ e)) * 64, 64), :]
            right = dv_ref[spot(((s ^ d) * GROUP + (z ^ (e + 2))) * 64, 64), :]
            out_refs[d][256 + e * 64 : 320 + e * 64, :] = jnp.concatenate(
                [left, right], axis=1
            ).astype(BF)


def mixed_back_kernel(ids, *refs):
    pieces, own_ref, oth_ref = refs[:4], refs[4], refs[5]
    out_refs, dm_ref, held = refs[6:10], refs[10], refs[11]
    s, c = ids[0], ids[2]
    for d in range(GROUP):
        held[d] = pieces[d][...]
    for place, half in ((0, c), (1, 1 - c)):
        base = place * 384
        values = []
        for i in range(2):
            d = (2 * half + i) ^ s
            dm_ref[:, base + i * 128 : base + (i + 1) * 128] = held[d, 0:256, :]
            values.append(unpacked(held[d, 256:384, :]))
        dm_ref[:, base + 256 : base + 384] = jnp.concatenate(values, axis=1)
    for k in range(GROUP):
        part = nt(dm_ref[:, 0:384], mixed_piece(own_ref, k))
        part = (part + nt(dm_ref[:, 384:768], mixed_piece(oth_ref, k))).astype(BF)
        for d in range(GROUP):
            out_refs[d][:, k * 256 : (k + 1) * 256] = part[d * 64 : (d + 1) * 64, :]


def attend_grads_kernel(ids, *refs):
    nf_ref, dm_ref, att_ref, ga_ref, two_ref, fc_ref = refs[:6]
    part_refs, x_refs = refs[6:10], refs[10:14]
    keep_ref, send_ref, lines = refs[14:17]
    s, c = ids[0], ids[2]
    d_gain = d_bias = 0.0
    for d in range(GROUP):
        grad = part_refs[d][...].astype(F32)
        values = x_refs[d][...].astype(F32)
        average = jnp.mean(values, axis=-1, keepdims=True)
        centred = values - average
        variance = jnp.mean(centred * centred, axis=-1, keepdims=True)
        unit = centred * lax.rsqrt(variance + EPSILON)
        d_gain = d_gain + jnp.sum(grad * unit, axis=0, keepdims=True)
        d_bias = d_bias + jnp.sum(grad, axis=0, keepdims=True)
    lines[0:1, :] = d_gain
    lines[1:2, :] = d_bias
    lines[2:6, :] = two_ref[0:4, :]
    lines[6:8, :] = jnp.zeros((2, d_gain.shape[1]), F32)
    for place, out_ref, half in ((0, keep_ref, c), (1, send_ref, 1 - c)):
        base = place * 384
        d_w = tn(nf_ref[...], dm_ref[:, base : base + 384]).astype(BF)
        sums = jnp.sum(dm_ref[:, base : base + 384].astype(F32), axis=0, keepdims=True)
        for k in range(GROUP):
            out_ref[k, 0:256, 0:384] = d_w[k * 256 : (k + 1) * 256, :]
            mine = (k >> 1) == half
            i = k & 1
            query = sums[:, i * 128 : i * 128 + DH]
            value = sums[:, 256 + i * DH : 256 + (i + 1) * DH]
            first = place * 512 + k * 128
            line = jnp.concatenate(
                [
                    fc_ref[:, first : first + 128],
                    jnp.where(mine, query, 0.0),
                    jnp.where(mine, value, 0.0),
                    jnp.zeros((1, 128), F32),
                ],
                axis=1,
            )
            foot = jnp.concatenate([line, jnp.zeros((7, 384), F32)], axis=0)
            foot = jnp.concatenate([lines[:, spot(k * 256 + half * 128, 128)], foot], axis=1)
            foot = jnp.concatenate([foot, jnp.zeros((8, 512), F32)], axis=0)
            out_ref[k, 256:272, :] = foot.astype(BF)
        d_out = tn(att_ref[...], ga_ref[:, spot(half * 512, 512)]).astype(BF)
        for d in range(GROUP):
            for q in range(GROUP):
                out_ref[s ^ d, q * 64 : (q + 1) * 64, 384:512] = d_out[
                    d * 64 : (d + 1) * 64, q * 128 : (q + 1) * 128
                ]


def norm_one_back_kernel(ids, *refs):
    x_ref, d_res_ref, vec = refs[4], refs[5], refs[6]
    pulled, _, _ = norm_pull(x_ref[...].astype(F32), vec[0:1, :], summed(refs[:4]))
    d_in = d_res_ref[...] + pulled
    refs[7][...] = d_in
    refs[8][...] = d_in.astype(BF)


def add_kernel(ids, left_ref, right_ref, *out_refs):
    for d in range(GROUP):
        k = ids[0] ^ d
        out_refs[d][...] = (left_ref[k].astype(F32) + right_ref[k].astype(F32)).astype(BF)


def choose_kernel(ids, *refs):
    lower, upper = summed(refs[:4]).astype(BF), summed(refs[4:8]).astype(BF)
    first = ids[2] == 0
    refs[8][...] = jnp.where(first, lower, upper)
    refs[9][...] = jnp.where(first, upper, lower)


def split_feed_kernel(ids, own_ref, oth_ref, *refs):
    back_out = refs[GROUP]
    for d in range(GROUP):
        rows = spot((ids[1] ^ d) * 64, 64)
        refs[d][:, 0:512] = own_ref[rows, :]
        refs[d][:, 512:1024] = oth_ref[rows, :]
    for ref, half in ((own_ref, ids[2]), (oth_ref, 1 - ids[2])):
        rows = spot(half * 128, 128)
        back_out[0, rows, 0:512] = ref[256:384, :].astype(F32)
        back_out[0, rows, 512:1024] = ref[384:512, :].astype(F32)


def split_attend_kernel(ids, own_ref, oth_ref, *refs):
    out_ref, bfc_ref, query_ref, value_ref = refs[GROUP:]
    s, z, c = ids[0], ids[1], ids[2]
    foots = (own_ref[256:272, :], oth_ref[256:272, :])
    for d in range(GROUP):
        rows = spot((z ^ d) * 64, 64)
        refs[d][0:64, 0:384] = own_ref[rows, 0:384]
        refs[d][0:64, 384:768] = oth_ref[rows, 0:384]
        lines = jnp.where(((z ^ d) >> 1) == c, foots[0][:, 0:128], foots[1][:, 0:128])
        refs[d][64:80, :] = jnp.concatenate([lines, jnp.zeros((16, 640), BF)], axis=1)
    for ref, half in ((own_ref, c), (oth_ref, 1 - c)):
        for q in range(GROUP):
            out_ref[0, :, spot(half * 512 + q * 128, 128)] = ref[
                q * 64 : (q + 1) * 64, 384:512
            ].astype(F32)
    own, oth = foots[0][0:1, :].astype(F32), foots[1][0:1, :].astype(F32)
    lower, upper = jnp.where(c == 0, own, oth), jnp.where(c == 0, oth, own)
    bfc_ref[:, 0:128] = lower[:, 128:256]
    bfc_ref[:, 128:256] = upper[:, 128:256]
    line = jnp.where((s >> 1) == 0, lower, upper)
    query_ref[...] = line[:, 256 : 256 + DH]
    value_ref[...] = line[:, 256 + DH : 384]


def final_feed_kernel(ids, *refs):
    fc_out = refs[GROUP]
    for place, half in ((0, ids[2]), (1, 1 - ids[2])):
        for d in range(GROUP):
            for j in range(GROUP):
                start = place * 512 + j * 128
                lanes = spot(j * 1024 + (ids[1] ^ d) * 256 + half * 128, 128)
                fc_out[0, :, lanes] = refs[d][:, start : start + 128].astype(F32)


def final_attend_kernel(ids, *refs):
    mixed, mixed_out, line_outs, held = refs[:4], refs[4], refs[5:11], refs[11]
    z, c = ids[1], ids[2]
    width = mixed_out.shape[2] // 3
    lines = 0.0
    for d in range(GROUP):
        held[z ^ d] = mixed[d][0:64, :]
        lines = lines + mixed[d][64:80, 0:128].astype(F32)
    lines = jnp.where((z & 1) == 1, lines[:, DH:], lines[:, :DH])
    for i, ref in enumerate(line_outs):
        ref[...] = lines[i : i + 1, :]
    for place, half in ((0, c), (1, 1 - c)):
        base = place * 384
        for pair in range(2):
            for i in range(2):
                tiles = []
                for source in (2 * pair, 2 * pair + 1):
                    qk = held[source, :, base + i * 128 : base + (i + 1) * 128].astype(F32)
                    v = held[source, :, base + 256 + i * DH : base + 256 + (i + 1) * DH]
                    tiles.append((qk[:, :DH], qk[:, DH:], v.astype(F32)))
                for t in range(3):
                    start = t * width + (2 * half + i) * 256 + pair * 128
                    mixed_out[0, :, spot(start, 128)] = jnp.concatenate(
                        [tiles[0][t], tiles[1][t]], axis=1
                    )


def fast_body(
    inputs,
    cotangent,
    segment_ids,
    ln1_gain,
    ln1_bias,
    w_qkv,
    b_query,
    b_value,
    w_out,
    b_out,
    ln2_gain,
    ln2_bias,
    w_fc,
    b_fc,
    w_proj,
    b_proj,
):
    s, z, c = lax.axis_index(SEQ), lax.axis_index(FSDP), lax.axis_index("section")
    first = c == 0
    ids = jnp.stack([s, z, c]).astype(jnp.int32)
    tok, width = inputs.shape[1:]
    count = segment_ids.shape[1]
    tall = GROUP * tok
    piece = ((384, 128), BF)
    small = ((128, 128), BF)
    part = ((tok, width), BF)
    wide = ((tall, width), BF)
    line = ((tok, width), F32)
    share = ((272, 512), BF)
    feed_share = ((512, 512), BF)
    done, awaited, lagging = [], [], []

    def run(kernel, args, outs, *scratch, anywhere=(), mib=16, aside=False):
        args = list(args)
        earlier = done[-1:] + ([] if aside else list(awaited))
        if earlier:
            args[0] = after(args[0], *earlier)
        if not aside:
            awaited[:] = lagging
            lagging.clear()
        result = list(call(kernel, ids, args, outs, scratch, anywhere, mib))
        done.append(result[-1])
        return result

    def beside(blocks, got, axis, *which, lag=False):
        for d in which:
            got[d] = exchange(after(blocks[d], done[-1]), axis, d)
            (lagging if lag else awaited).append(got[d])

    def now(blocks):
        return [after(block, done[-1]) for block in blocks]

    def of(kernel, axis):
        def bound(*refs):
            kernel(axis, *refs)

        bound.__name__ = kernel.__name__
        return bound

    def shared(pieces, axis, shape, aside=False):
        (whole,) = run(of(place_kernel, axis), pieces, [(shape, BF)], aside=aside)
        return [whole, swap(whole)]

    mine, send, feed_mine, feed_send, x, grad = run(
        pick_kernel,
        [w_qkv, w_out]
        + [ln1_gain, ln1_bias, b_query, b_value, b_out, ln2_gain, ln2_bias, b_proj, b_fc]
        + [inputs, cotangent, w_fc, w_proj],
        [((GROUP, 80, 512), BF)] * 2 + [((GROUP, 128, 512), BF)] * 2 + [part] * 2,
        pltpu.VMEM((64, 3 * width), BF),
        pltpu.VMEM((GROUP, 16, width), BF),
        pltpu.VMEM((8, 1, 256), BF),
        pltpu.VMEM((1, 1024), BF),
        pltpu.SemaphoreType.DMA((64,)),
        anywhere=range(15),
    )
    *heads, upper_heads = run(
        settle_heads_kernel,
        [mine, swap(send), x],
        [((208, 512), BF)] * 4 + [((GROUP, 64, 512), BF)],
    )
    heads = trade(heads, FSDP)
    feed_got = swap(feed_send)
    *rest, seg_col, seg_row = run(
        settle_feed_kernel,
        [feed_mine, feed_got, upper_heads, segment_ids, grad],
        [((192, 512), BF)] * 4
        + [((256, 512), BF)] * 4
        + [((count, 1), F32), ((1, count), F32)],
        aside=True,
    )
    rests = [rest[:4], rest[4:]]
    rest_got = [list(blocks) for blocks in rests]
    heads, *rest = run(
        first_heads_kernel,
        heads,
        [((GROUP, 64, 512), BF)] + [part] * 4 + [((16, width), F32)] * 2,
    )
    x_all, vec = rest[:4], rest[4:]
    heads = gather(heads, SEQ)
    for blocks, got in zip(rests, rest_got):
        beside(blocks, got, FSDP, 1)
    head_w = [shared(heads, 0, (GROUP, GROUP, 64, 512)), None]

    feed_w = [None, None]
    kept = []
    for layer in range(2):
        *packed, normed = run(
            mixed_kernel,
            x_all + head_w[layer] + [vec[layer]],
            [piece] * 4 + [wide],
            pltpu.VMEM((GROUP, 384, 128), BF),
        )
        qkv = trade(packed, SEQ)
        got = rest_got[layer]
        beside(rests[layer], got, FSDP, 3, 2, lag=True)
        *heads, qk_rows, v_rows, probs = run(
            attend_kernel,
            qkv + [seg_col, seg_row],
            [small] * 4 + [((count, 128), BF), ((count, DH), BF), ((count, count), F32)],
            pltpu.VMEM((count, DH), BF),
        )
        heads = trade(heads, SEQ)
        *parts, att = run(
            output_kernel,
            heads + head_w[layer],
            [part] * 4 + [((tall, 256), BF)],
        )
        parts = trade(parts, FSDP)
        if layer == 0:
            feed, heads_later = run(
                part_kernel,
                got,
                [((GROUP, 128, 512), BF), ((GROUP, 64, 512), BF)],
                aside=True,
            )
        else:
            feed, *grad_all = run(
                turn_part_kernel, got, [((GROUP, 128, 512), BF)] + [part] * 4, aside=True
            )
        feeds = [feed] * GROUP
        beside(feeds, feeds, SEQ, 1, 2)
        res, n_two = run(
            residual_kernel, parts + [x, vec[layer]], [line, part]
        )
        n_all = gather(n_two, FSDP)
        beside([feed] * GROUP, feeds, SEQ, 3)
        feeds[0] = after(feeds[0], *n_all)
        feed_w[layer] = shared(feeds, 0, (GROUP, GROUP, 128, 512))
        kept.append((x, normed, (qk_rows, v_rows, probs), att, res, x_all))
        if layer == 0:
            *parts, slope, act, n_full = run(
                feed_kernel,
                n_all + feed_w[0] + [vec[0]],
                [part] * 4 + [((tall, 1024), F32), ((tall, 1024), BF), wide],
            )
            parts = trade(parts, FSDP)
            heads = [heads_later] * GROUP
            beside(heads, heads, SEQ, 1, 2)
            (x,) = run(close_kernel, parts + [res, vec[0]], [part])
            x_all = gather(x, FSDP)
            beside([heads_later] * GROUP, heads, SEQ, 3)
            heads[0] = after(heads[0], *x_all)
            head_w[1] = shared(heads, 0, (GROUP, GROUP, 64, 512))
        else:
            turn = run(
                feed_turn_kernel,
                n_all + grad_all + feed_w[1] + [vec[1]],
                [part] * 8 + [((tall, 1024), BF), wide, ((tall, 1024), BF), wide],
                pltpu.VMEM((tall, 1024), F32),
                mib=20,
            )

    def feed_terms(act, gb_full, n_full, d_pre):
        keep, send, sums = run(
            feed_grads_kernel,
            [act, gb_full, n_full, d_pre],
            [((GROUP, 512, 512), BF)] * 2 + [((1, 1024), F32)],
            aside=True,
        )
        return keep, swap(send), sums

    def attend_terms(layer, two_rows, fc_sums, parts, d_mixed, ga_full):
        x, normed, _, att, _, x_all = kept[layer]
        keep, send = run(
            attend_grads_kernel,
            [normed, d_mixed, att, ga_full, two_rows, fc_sums] + parts + x_all,
            [((GROUP,) + share[0], BF)] * 2,
            pltpu.VMEM((8, width), F32),
            aside=True,
        )
        return keep, swap(send)

    def total(keep, got, shape):
        return run(add_kernel, [keep, got], [shape] * 4, aside=True)

    def norm_two_back(layer, parts, grad):
        return run(
            norm_two_back_kernel,
            parts + [kept[layer][4], grad, vec[layer]],
            [line, part, ((8, width), F32)],
        )

    def output_back(layer, ga_all):
        return run(
            output_back_kernel,
            ga_all + head_w[layer],
            [small] * 4 + [wide],
        )

    def attend_back(layer, d_heads):
        return run(
            attend_back_kernel,
            d_heads + list(kept[layer][2]),
            [piece] * 4,
            pltpu.VMEM((count, DH), BF),
            *[pltpu.VMEM((count, DH), F32)] * 3,
        )

    def mixed_back(layer, d_pieces):
        return run(
            mixed_back_kernel,
            d_pieces + head_w[layer],
            [part] * 4 + [((tall, 768), BF)],
            pltpu.VMEM((GROUP, 384, 128), BF),
        )

    def norm_one_back(layer, parts, d_res):
        return run(
            norm_one_back_kernel,
            parts + [kept[layer][0], d_res, vec[layer]],
            [line, part],
        )

    top_parts, parts = turn[:4], trade(turn[4:8], FSDP)
    keep, got, fc_sums = feed_terms(turn[8], turn[11], turn[9], turn[10])
    terms = total(keep, got, feed_share)
    d_res, ga, two_rows = norm_two_back(1, parts, grad)
    ga_all = gather(ga, FSDP)
    upper_feed = list(terms)
    beside(terms, upper_feed, SEQ, 1, 2)
    *d_heads, ga_full = output_back(1, ga_all)
    d_heads = trade(d_heads, SEQ)
    tops = list(top_parts)
    beside(top_parts, tops, FSDP, 1, 3)
    d_pieces = trade(attend_back(1, d_heads), SEQ)
    beside(top_parts, tops, FSDP, 2)
    *sent, d_mixed = mixed_back(1, d_pieces)
    parts = trade(sent, FSDP)
    beside(terms, upper_feed, SEQ, 3)
    keep, got = attend_terms(1, two_rows, fc_sums, sent, d_mixed, ga_full)
    (top,) = run(close_kernel, tops + [kept[1][4], vec[1]], [line], aside=True)
    upper_terms = total(keep, got, share)
    _, low = norm_one_back(1, parts, d_res)
    g_all = gather(low, FSDP)
    upper_attend = list(upper_terms)
    beside(upper_terms, upper_attend, SEQ, 1, 2)

    *parts, d_pre, gb_full = run(
        feed_back_kernel,
        g_all + feed_w[0] + [slope],
        [part] * 4 + [((tall, 1024), BF), wide],
    )
    parts = trade(parts, FSDP)
    beside(upper_terms, upper_attend, SEQ, 3)
    keep, got, fc_sums = feed_terms(act, gb_full, n_full, d_pre)
    terms = total(keep, got, feed_share)
    d_res, ga, two_rows = norm_two_back(0, parts, low)
    ga_all = gather(ga, FSDP)
    lower_feed = list(terms)
    beside(terms, lower_feed, SEQ, 1, 2)
    *d_heads, ga_full = output_back(0, ga_all)
    d_heads = trade(d_heads, SEQ)
    beside(terms, lower_feed, SEQ, 3)
    d_pieces = trade(attend_back(0, d_heads), SEQ)
    mine, theirs = run(choose_kernel, lower_feed + upper_feed, [feed_share] * 2, aside=True)
    got = swap(theirs)
    *blocks, g_proj = run(
        split_feed_kernel,
        [mine, got],
        [((64, 1024), BF)] * 4 + [((1, 256, width), F32)],
        aside=True,
    )
    fc_parts = list(blocks)
    beside(blocks, fc_parts, FSDP, 3, 2)
    *sent, d_mixed = mixed_back(0, d_pieces)
    keep, got = attend_terms(0, two_rows, fc_sums, sent, d_mixed, ga_full)
    lower_attend = trade(total(keep, got, share), SEQ)

    parts = trade(now(sent), FSDP)
    mine, theirs = run(choose_kernel, lower_attend + upper_attend, [share] * 2)
    got = swap(theirs)
    bottom, _ = norm_one_back(0, parts, d_res)
    *blocks, g_out, g_bfc, g_query, g_value = run(
        split_attend_kernel,
        [mine, got],
        [((80, 768), BF)] * 4
        + [((1, 64, width), F32), ((1, 256), F32), ((1, 64), F32), ((1, 64), F32)],
    )
    mixed_parts = trade(blocks, FSDP)
    fc_parts[1] = exchange(after(fc_parts[1], g_out), FSDP, 1)
    (g_fc,) = run(final_feed_kernel, fc_parts, [((1, 64, 4096), F32)])
    g_mixed, *lines = run(
        final_attend_kernel,
        mixed_parts,
        [((1, 64, 3 * width), F32)] + [((1, 64), F32)] * 6,
        pltpu.VMEM((GROUP, 64, 768), BF),
    )

    ends_mine = jnp.where(first, bottom, top)
    ends_other = swap(jnp.where(first, top, bottom))
    relay = jnp.where(
        first, jnp.stack([ends_mine, ends_other]), jnp.stack([ends_other, ends_mine])
    )[None]

    return (
        relay,
        lines[0],
        lines[1],
        g_mixed,
        g_query,
        g_value,
        g_out,
        lines[2],
        lines[3],
        lines[4],
        g_fc,
        g_bfc,
        g_proj,
        lines[5],
    )


def plan(mesh):
    fits = mesh.shape[SECTION] == 2 and mesh.shape[SEQ] == mesh.shape[FSDP] == GROUP
    return fast_body if fits else body


def solution(mesh):
    placed = (
        P(None, ("seq", "fsdp"), None),
        P(None, ("seq", "fsdp"), None),
        P(),
        P("section", "fsdp"),
        P("section", "fsdp"),
        P("section", "fsdp", None),
        P("section", "fsdp"),
        P("section", "fsdp"),
        P("section", "fsdp", None),
        P("section", "fsdp"),
        P("section", "fsdp"),
        P("section", "fsdp"),
        P("section", "fsdp", None),
        P("section", "fsdp"),
        P("section", "fsdp", None),
        P("section", "fsdp"),
    )
    return jax.shard_map(
        plan(mesh),
        mesh=mesh,
        in_specs=placed,
        out_specs=(
            P("section", None, ("seq", "fsdp"), None),
            P("section", ("seq", "fsdp")),
            P("section", ("seq", "fsdp")),
            P("section", ("seq", "fsdp"), None),
            P("section", ("seq", "fsdp")),
            P("section", ("seq", "fsdp")),
            P("section", ("seq", "fsdp"), None),
            P("section", ("seq", "fsdp")),
            P("section", ("seq", "fsdp")),
            P("section", ("seq", "fsdp")),
            P("section", ("seq", "fsdp"), None),
            P("section", ("seq", "fsdp")),
            P("section", ("seq", "fsdp"), None),
            P("section", ("seq", "fsdp")),
        ),
        check_vma=False,
    )
```

```python
import math

import jax
import jax.numpy as jnp
from jax import lax
from jax.experimental import pallas as pl
from jax.experimental.pallas import tpu as pltpu
from jax.sharding import PartitionSpec as P

DH = 64


EPSILON = 1e-05
NEGATIVE = -1e30


def shifted(block, axis, distance):
    devices = range(lax.axis_size(axis))
    route = [(i - distance, i) for i in devices if i - distance in devices]
    return lax.ppermute(block, axis, route)


def layer_norm(values, gain_vec, bias_vec):
    average = jnp.mean(values, axis=-1, keepdims=True)
    centred = values - average
    variance = jnp.mean(centred * centred, axis=-1, keepdims=True)
    return centred * lax.rsqrt(variance + EPSILON) * gain_vec + bias_vec


def gelu_tanh(values):
    return jax.nn.gelu(values, approximate=True)


def mask_rows(seg_row, fsdp_index, n_seq, n_fsdp, tok_rows):
    places = jnp.arange(seg_row.shape[0], dtype=jnp.int32)
    seg_grid = seg_row.reshape(n_seq, n_fsdp, tok_rows)
    place_grid = places.reshape(n_seq, n_fsdp, tok_rows)
    query_ids = lax.dynamic_index_in_dim(seg_grid, fsdp_index, 1, keepdims=False).reshape(-1)
    query_places = lax.dynamic_index_in_dim(place_grid, fsdp_index, 1, keepdims=False).reshape(-1)
    key_ids = jnp.transpose(seg_grid, (1, 0, 2)).reshape(-1)
    key_places = jnp.transpose(place_grid, (1, 0, 2)).reshape(-1)
    same_doc = (query_ids[:, None] == key_ids[None, :]) & (query_ids[:, None] > 0)
    itself = query_places[:, None] == key_places[None, :]
    return (key_places[None, :] <= query_places[:, None]) & (same_doc | itself)


def split_heads(matrix):
    return matrix.reshape(matrix.shape[0], matrix.shape[1] // DH, DH)


def block_rows(matrix, block_len):
    return matrix.reshape((matrix.shape[0] // block_len, block_len) + matrix.shape[1:])


def masked_scores(queries, key_rows, allowed):
    raw_scores = jnp.einsum(
        "qhd,khd->hqk",
        split_heads(queries),
        split_heads(key_rows),
        preferred_element_type=jnp.float32,
    )
    return jnp.where(allowed[None], raw_scores * DH ** (-0.5), NEGATIVE)


def body(
    inputs,
    cotangent,
    segment_ids,
    ln1_gain,
    ln1_bias,
    w_qkv,
    b_query,
    b_value,
    w_out,
    b_out,
    ln2_gain,
    ln2_bias,
    w_fc,
    b_fc,
    w_proj,
    b_proj,
):
    n_seq = lax.axis_size("seq")
    n_fsdp = lax.axis_size("fsdp")
    section_index = lax.axis_index("section")
    fsdp_index = lax.axis_index("fsdp")
    last_section = section_index == 1
    micro, tok_rows, width = inputs.shape
    score_scale = DH ** (-0.5)
    query_count = tok_rows * n_seq
    block_len = math.gcd(query_count, 512)

    def fetch_params():
        return (
            lax.all_gather(ln1_gain[0], "fsdp", axis=0, tiled=True),
            lax.all_gather(ln1_bias[0], "fsdp", axis=0, tiled=True),
            lax.all_gather(w_qkv[0], "fsdp", axis=0, tiled=True),
            lax.all_gather(b_query[0], "fsdp", axis=0, tiled=True),
            lax.all_gather(b_value[0], "fsdp", axis=0, tiled=True),
            lax.all_gather(w_out[0], "fsdp", axis=0, tiled=True),
            lax.all_gather(b_out[0], "fsdp", axis=0, tiled=True),
            lax.all_gather(ln2_gain[0], "fsdp", axis=0, tiled=True),
            lax.all_gather(ln2_bias[0], "fsdp", axis=0, tiled=True),
            lax.all_gather(w_fc[0], "fsdp", axis=0, tiled=True),
            lax.all_gather(b_fc[0], "fsdp", axis=0, tiled=True),
            lax.all_gather(w_proj[0], "fsdp", axis=0, tiled=True),
            lax.all_gather(b_proj[0], "fsdp", axis=0, tiled=True),
        )

    received = jnp.zeros((tok_rows, width), jnp.bfloat16)
    kept_ticks = []
    layer_outs = []
    for tick_index in range(micro + 1):
        params = fetch_params()
        batch_index = jnp.clip(tick_index - section_index, 0, micro - 1)
        seg_row = lax.dynamic_index_in_dim(segment_ids, batch_index, 0, keepdims=False)
        allowed = mask_rows(seg_row, fsdp_index, n_seq, n_fsdp, tok_rows)
        if tick_index < micro:
            first_in = inputs[tick_index].astype(jnp.float32)
        else:
            first_in = jnp.zeros((tok_rows, width), jnp.float32)
        layer_in = jnp.where(last_section, received.astype(jnp.float32), first_in)
        (
            forward_gain_one,
            forward_bias_one,
            forward_w_mixed,
            forward_bias_query,
            forward_bias_value,
            forward_w_output,
            forward_bias_output,
            forward_gain_two,
            forward_bias_two,
            forward_w_hidden,
            forward_bias_hidden,
            forward_w_back,
            forward_bias_back,
        ) = params
        forward_normed = layer_norm(
            layer_in, forward_gain_one.astype(jnp.float32), forward_bias_one.astype(jnp.float32)
        ).astype(jnp.bfloat16)
        mixed_proj = jnp.dot(forward_normed, forward_w_mixed, preferred_element_type=jnp.float32)
        bias_row = jnp.concatenate(
            [forward_bias_query, jnp.zeros_like(forward_bias_query), forward_bias_value]
        ).astype(jnp.float32)
        mixed_tok = (mixed_proj + bias_row).astype(jnp.bfloat16).reshape(tok_rows, 3, width)
        head_rows = lax.all_to_all(mixed_tok, "seq", split_axis=2, concat_axis=0, tiled=True)
        forward_queries = head_rows[:, 0]
        forward_key_rows = lax.all_gather(head_rows[:, 1], "fsdp", axis=0, tiled=True)
        forward_value_rows = lax.all_gather(head_rows[:, 2], "fsdp", axis=0, tiled=True)

        def attend_block(operands):
            query_block, allowed_block = operands
            scores = masked_scores(query_block, forward_key_rows, allowed_block)
            row_top = jnp.max(scores, axis=-1, keepdims=True)
            log_block = row_top + jnp.log(
                jnp.sum(jnp.exp(scores - row_top), axis=-1, keepdims=True)
            )
            attn_weights = jnp.exp(scores - log_block).astype(jnp.bfloat16)
            head_block = jnp.einsum(
                "hqk,khd->qhd",
                attn_weights,
                split_heads(forward_value_rows),
                preferred_element_type=jnp.float32,
            )
            return (head_block.reshape(query_block.shape).astype(jnp.bfloat16), log_block)

        head_blocks, forward_log_total = lax.map(
            attend_block, (block_rows(forward_queries, block_len), block_rows(allowed, block_len))
        )
        head_out = head_blocks.reshape(forward_queries.shape)
        forward_attended = lax.all_to_all(head_out, "seq", split_axis=0, concat_axis=1, tiled=True)
        forward_residual = (
            layer_in
            + jnp.dot(forward_attended, forward_w_output, preferred_element_type=jnp.float32)
            + forward_bias_output.astype(jnp.float32)
        )
        forward_normed_two = layer_norm(
            forward_residual,
            forward_gain_two.astype(jnp.float32),
            forward_bias_two.astype(jnp.float32),
        ).astype(jnp.bfloat16)
        forward_pre_act = jnp.dot(
            forward_normed_two, forward_w_hidden, preferred_element_type=jnp.float32
        ) + forward_bias_hidden.astype(jnp.float32)
        forward_activated = gelu_tanh(forward_pre_act).astype(jnp.bfloat16)
        layer_out = (
            forward_residual
            + jnp.dot(forward_activated, forward_w_back, preferred_element_type=jnp.float32)
            + forward_bias_back.astype(jnp.float32)
        )
        forward_kept = (
            layer_in,
            forward_normed,
            forward_queries,
            forward_key_rows,
            forward_value_rows,
            forward_log_total,
            allowed,
            forward_attended,
            forward_residual,
            forward_normed_two,
            forward_pre_act,
            forward_activated,
        )
        layer_out, kept = (layer_out, forward_kept)
        kept_ticks.append(kept)
        layer_outs.append(layer_out)
        if tick_index < micro:
            received = shifted(layer_out.astype(jnp.bfloat16), "section", 1)
    sent_back = jnp.zeros((tok_rows, width), jnp.bfloat16)
    input_grads = []
    totals = None
    for tick_index in range(micro + 1):
        params = fetch_params()
        later = kept_ticks[min(tick_index + 1, micro)]
        earlier = kept_ticks[max(tick_index - 1, 0)]
        kept = jax.tree.map(
            lambda upper, lower: jnp.where(last_section, upper, lower), later, earlier
        )
        if tick_index < micro:
            top_grad = cotangent[tick_index].astype(jnp.float32)
        else:
            top_grad = jnp.zeros((tok_rows, width), jnp.float32)
        grad_out = jnp.where(last_section, top_grad, sent_back.astype(jnp.float32))
        (
            gain_one,
            bias_one,
            w_mixed,
            bias_query,
            bias_value,
            w_output,
            bias_output,
            gain_two,
            bias_two,
            w_hidden,
            bias_hidden,
            w_back,
            bias_back,
        ) = params
        (
            backward_layer_in,
            normed,
            queries,
            key_rows,
            value_rows,
            log_total,
            backward_allowed,
            attended,
            residual,
            normed_two,
            pre_act,
            activated,
        ) = kept
        grad_back = grad_out.astype(jnp.bfloat16)
        d_w_back = jnp.einsum("cf,cd->fd", activated, grad_back, preferred_element_type=jnp.float32)
        d_bias_back = jnp.sum(grad_back.astype(jnp.float32), axis=0)
        d_activated = jnp.einsum("cd,fd->cf", grad_back, w_back, preferred_element_type=jnp.float32)
        gelu_pull = jax.vjp(gelu_tanh, pre_act)[1]
        d_pre = gelu_pull(d_activated)[0].astype(jnp.bfloat16)
        d_w_hidden = jnp.einsum("cm,cf->mf", normed_two, d_pre, preferred_element_type=jnp.float32)
        d_bias_hidden = jnp.sum(d_pre.astype(jnp.float32), axis=0)
        d_normed_two = jnp.einsum("cf,mf->cm", d_pre, w_hidden, preferred_element_type=jnp.float32)
        norm_pull_two = jax.vjp(
            layer_norm, residual, gain_two.astype(jnp.float32), bias_two.astype(jnp.float32)
        )[1]
        d_resid_part, d_gain_two, d_bias_two = norm_pull_two(d_normed_two)
        d_residual = grad_out + d_resid_part
        grad_attn = d_residual.astype(jnp.bfloat16)
        d_w_output = jnp.einsum(
            "cm,cd->md", attended, grad_attn, preferred_element_type=jnp.float32
        )
        d_bias_output = jnp.sum(grad_attn.astype(jnp.float32), axis=0)
        d_attended = jnp.einsum(
            "cd,md->cm", grad_attn, w_output, preferred_element_type=jnp.float32
        ).astype(jnp.bfloat16)
        d_head = lax.all_to_all(d_attended, "seq", split_axis=1, concat_axis=0, tiled=True)

        def grad_block(carry, operands):
            key_acc, value_acc = carry
            query_block, head_grad_block, allowed_block, log_block = operands
            scores = masked_scores(query_block, key_rows, allowed_block)
            attn_probs = jnp.exp(scores - log_block)
            d_weights = jnp.einsum(
                "qhd,khd->hqk",
                split_heads(head_grad_block),
                split_heads(value_rows),
                preferred_element_type=jnp.float32,
            )
            row_dot = jnp.sum(attn_probs * d_weights, axis=-1, keepdims=True)
            d_scores = (attn_probs * (d_weights - row_dot) * score_scale).astype(jnp.bfloat16)
            d_query_block = (
                jnp.einsum(
                    "hqk,khd->qhd",
                    d_scores,
                    split_heads(key_rows),
                    preferred_element_type=jnp.float32,
                )
                .reshape(query_block.shape)
                .astype(jnp.bfloat16)
            )
            key_acc = key_acc + jnp.einsum(
                "hqk,qhd->khd",
                d_scores,
                split_heads(query_block),
                preferred_element_type=jnp.float32,
            ).reshape(key_rows.shape)
            value_acc = value_acc + jnp.einsum(
                "hqk,qhd->khd",
                attn_probs.astype(jnp.bfloat16),
                split_heads(head_grad_block),
                preferred_element_type=jnp.float32,
            ).reshape(value_rows.shape)
            return ((key_acc, value_acc), d_query_block)

        empty_terms = (
            jnp.zeros(key_rows.shape, jnp.float32),
            jnp.zeros(value_rows.shape, jnp.float32),
        )
        (key_term, value_term), query_blocks = lax.scan(
            grad_block,
            empty_terms,
            (
                block_rows(queries, block_len),
                block_rows(d_head, block_len),
                block_rows(backward_allowed, block_len),
                log_total,
            ),
        )
        d_query = query_blocks.reshape(queries.shape)
        d_key = lax.psum_scatter(key_term, "fsdp", scatter_dimension=0, tiled=True)
        d_value = lax.psum_scatter(value_term, "fsdp", scatter_dimension=0, tiled=True)
        d_heads = jnp.stack(
            [d_query, d_key.astype(jnp.bfloat16), d_value.astype(jnp.bfloat16)], axis=1
        )
        d_mixed = lax.all_to_all(d_heads, "seq", split_axis=0, concat_axis=2, tiled=True)
        d_flat = d_mixed.reshape(tok_rows, 3 * width)
        d_w_mixed = jnp.einsum("cm,cn->mn", normed, d_flat, preferred_element_type=jnp.float32)
        d_bias_query = jnp.sum(d_mixed[:, 0].astype(jnp.float32), axis=0)
        d_bias_value = jnp.sum(d_mixed[:, 2].astype(jnp.float32), axis=0)
        d_normed = jnp.einsum("cn,mn->cm", d_flat, w_mixed, preferred_element_type=jnp.float32)
        norm_pull_one = jax.vjp(
            layer_norm,
            backward_layer_in,
            gain_one.astype(jnp.float32),
            bias_one.astype(jnp.float32),
        )[1]
        d_in_part, d_gain_one, d_bias_one = norm_pull_one(d_normed)
        d_in = d_residual + d_in_part
        d_in, local_grads = (
            d_in,
            (
                d_gain_one,
                d_bias_one,
                d_w_mixed,
                d_bias_query,
                d_bias_value,
                d_w_output,
                d_bias_output,
                d_gain_two,
                d_bias_two,
                d_w_hidden,
                d_bias_hidden,
                d_w_back,
                d_bias_back,
            ),
        )
        input_grads.append(d_in)
        shared = (
            lax.psum_scatter(local_grads[0], ("seq", "fsdp"), scatter_dimension=0, tiled=True),
            lax.psum_scatter(local_grads[1], ("seq", "fsdp"), scatter_dimension=0, tiled=True),
            lax.psum_scatter(local_grads[2], ("seq", "fsdp"), scatter_dimension=0, tiled=True),
            lax.psum_scatter(local_grads[3], ("seq", "fsdp"), scatter_dimension=0, tiled=True),
            lax.psum_scatter(local_grads[4], ("seq", "fsdp"), scatter_dimension=0, tiled=True),
            lax.psum_scatter(local_grads[5], ("seq", "fsdp"), scatter_dimension=0, tiled=True),
            lax.psum_scatter(local_grads[6], ("seq", "fsdp"), scatter_dimension=0, tiled=True),
            lax.psum_scatter(local_grads[7], ("seq", "fsdp"), scatter_dimension=0, tiled=True),
            lax.psum_scatter(local_grads[8], ("seq", "fsdp"), scatter_dimension=0, tiled=True),
            lax.psum_scatter(local_grads[9], ("seq", "fsdp"), scatter_dimension=0, tiled=True),
            lax.psum_scatter(local_grads[10], ("seq", "fsdp"), scatter_dimension=0, tiled=True),
            lax.psum_scatter(local_grads[11], ("seq", "fsdp"), scatter_dimension=0, tiled=True),
            lax.psum_scatter(local_grads[12], ("seq", "fsdp"), scatter_dimension=0, tiled=True),
        )
        totals = shared if totals is None else jax.tree.map(jnp.add, totals, shared)
        if tick_index < micro:
            sent_back = shifted(d_in.astype(jnp.bfloat16), "section", -1)
    section_tops = jnp.stack(layer_outs[1:])
    bottom_grads = jnp.stack(input_grads[1:])
    relay_ends = jnp.where(last_section, section_tops, bottom_grads)[None]
    return (relay_ends,) + tuple((grad_part[None] for grad_part in totals))


BF = jnp.bfloat16
F32 = jnp.float32
GROUP = 4
SECTION, SEQ, FSDP = "section", "seq", "fsdp"


def nt(left, right):
    return lax.dot_general(left, right, (((1,), (1,)), ((), ())), preferred_element_type=F32)


def tn(left, right):
    return lax.dot_general(left, right, (((0,), (0,)), ((), ())), preferred_element_type=F32)


def nn(left, right):
    return jnp.dot(left, right, preferred_element_type=F32)


def spot(start, size):
    return pl.ds(pl.multiple_of(start, size), size)


def call(kernel, ids, args, outs, scratch, anywhere, mib):
    places = [pltpu.HBM if i in anywhere else pltpu.VMEM for i in range(len(args))]
    args = [
        pltpu.with_memory_space_constraint(a, pltpu.HBM) if i in anywhere else a
        for i, a in enumerate(args)
    ]
    return pl.pallas_call(
        kernel,
        name=kernel.__name__.removesuffix("_kernel"),
        out_shape=[jax.ShapeDtypeStruct(shape, dtype) for shape, dtype in outs],
        in_specs=[pl.BlockSpec(memory_space=pltpu.SMEM)]
        + [pl.BlockSpec(memory_space=place) for place in places],
        out_specs=[pl.BlockSpec(memory_space=pltpu.VMEM)] * len(outs),
        scratch_shapes=list(scratch),
        compiler_params=pltpu.CompilerParams(vmem_limit_bytes=mib * 1024 * 1024),
        cost_estimate=pl.CostEstimate(flops=0, bytes_accessed=0, transcendentals=0),
    )(ids, *args)


def after(value, *earlier):
    return lax.optimization_barrier((value, earlier))[0]


def exchange(block, axis, d):
    return lax.ppermute(block, axis, [(i, i ^ d) for i in range(GROUP)])


def trade(blocks, axis):
    return [blocks[0]] + [exchange(blocks[d], axis, d) for d in range(1, GROUP)]


def gather(block, axis):
    return trade([block] * GROUP, axis)


def swap(block):
    return lax.ppermute(block, SECTION, [(0, 1), (1, 0)])


def normed_rows(values, gain_vec, bias_vec):
    average = jnp.mean(values, axis=-1, keepdims=True)
    centred = values - average
    variance = jnp.mean(centred * centred, axis=-1, keepdims=True)
    return centred * lax.rsqrt(variance + EPSILON) * gain_vec + bias_vec


def norm_pull(values, gain_vec, grad):
    average = jnp.mean(values, axis=-1, keepdims=True)
    centred = values - average
    variance = jnp.mean(centred * centred, axis=-1, keepdims=True)
    inverse = lax.rsqrt(variance + EPSILON)
    unit = centred * inverse
    scaled = grad * gain_vec
    first = jnp.mean(scaled, axis=-1, keepdims=True)
    second = jnp.mean(scaled * unit, axis=-1, keepdims=True)
    pulled = inverse * (scaled - first - unit * second)
    return (
        pulled,
        jnp.sum(grad * unit, axis=0, keepdims=True),
        jnp.sum(grad, axis=0, keepdims=True),
    )


def pick_kernel(ids, w_ref, out_ref, *refs):
    vector_refs, fc_bias_ref, x_ref, g_ref, fc_ref, proj_ref = refs[:8], *refs[8:13]
    mine_ref, send_ref, feed_mine_ref, feed_send_ref, x_out, g_out = refs[13:19]
    held, rows_held, lines, fc_line, sem = refs[19:]
    s, c = ids[0], ids[2]
    width = w_ref.shape[2] // 3
    sources = [w_ref.at[0, spot(s * 64, 64), :]]
    targets = [held]
    for k in range(GROUP):
        sources.append(out_ref.at[0, pl.ds(pl.multiple_of(k * 64 + s * 16, 16), 16), :])
        targets.append(rows_held.at[k])
    for i, ref in enumerate(vector_refs):
        sources.append(ref)
        targets.append(lines.at[i])
    sources += [fc_bias_ref, x_ref.at[c], g_ref.at[c]]
    targets += [fc_line, x_out, g_out]
    first = len(sources)
    for ref, half in ((feed_send_ref, 1 - c), (feed_mine_ref, c)):
        for k in range(GROUP):
            for j in range(GROUP):
                lanes = spot(j * 1024 + k * 256 + half * 128, 128)
                sources.append(fc_ref.at[0, spot(s * 64, 64), lanes])
                targets.append(ref.at[k, 0:64, j * 128 : (j + 1) * 128])
            rows = spot(k * 256 + half * 128 + s * 32, 32)
            sources += [proj_ref.at[0, rows, 0:512], proj_ref.at[0, rows, 512:1024]]
            targets += [ref.at[k, 64:96, :], ref.at[k, 96:128, :]]
    copies = [
        pltpu.make_async_copy(source, target, sem.at[i])
        for i, (source, target) in enumerate(zip(sources, targets))
    ]
    for copy in copies:
        copy.start()
    for copy in copies[:first]:
        copy.wait()

    def head(t, j, k):
        tile = held[:, spot(t * width + j * 256 + (k >> 1) * 128, 128)].astype(F32)
        return tile[:, DH:] if k & 1 else tile[:, :DH]

    foot = [lines[i].astype(F32) for i in range(len(vector_refs))]
    foot += [fc_line[:, k * 256 : (k + 1) * 256].astype(F32) for k in range(GROUP)]
    foot.append(jnp.zeros((4, 256), F32))
    foot = jnp.concatenate(foot, axis=0).astype(BF)
    foot = jnp.concatenate([foot, jnp.zeros((16, 256), BF)], axis=1)
    for ref, half in ((mine_ref, c), (send_ref, 1 - c)):
        for k in range(GROUP):
            for i in range(2):
                j = 2 * half + i
                pair = jnp.concatenate([head(0, j, k), head(1, j, k)], axis=1)
                ref[k, 0:64, i * 128 : (i + 1) * 128] = pair.astype(BF)
            pair = jnp.concatenate([head(2, 2 * half, k), head(2, 2 * half + 1, k)], axis=1)
            ref[k, 0:64, 256:384] = pair.astype(BF)
            for q in range(GROUP):
                ref[k, q * 16 : (q + 1) * 16, 384:512] = rows_held[
                    k, :, spot(half * 512 + q * 128, 128)
                ]
            ref[k, 64:80, :] = foot
    for copy in copies[first:]:
        copy.wait()


def settle_heads_kernel(ids, mine_ref, got_ref, x_ref, *refs):
    first, z = ids[2] == 0, ids[1]
    for d in range(GROUP):
        mine, got = mine_ref[z ^ d], got_ref[z ^ d]
        lower, upper = jnp.where(first, mine, got), jnp.where(first, got, mine)
        refs[d][0:64, :] = lower[0:64]
        refs[d][64:80, 0:256] = lower[64:80, 0:256]
        refs[d][64:80, 256:512] = upper[64:80, 0:256]
        refs[d][80:144, :] = x_ref[:, 0:512]
        refs[d][144:208, :] = x_ref[:, 512:1024]
        refs[GROUP][d] = upper[0:64]


def settle_feed_kernel(ids, mine_ref, got_ref, heads_ref, seg_ref, g_ref, *refs):
    first, z = ids[2] == 0, ids[1]
    numbers = jnp.where(first, seg_ref[0:1, :], seg_ref[1:2, :]).astype(F32)
    marked = jnp.where(numbers > 0.0, numbers, -1.0)
    refs[8][...] = jnp.broadcast_to(marked, (128, numbers.shape[1])).T[:, 0:1]
    refs[9][...] = numbers
    for d in range(GROUP):
        mine, got = mine_ref[z ^ d], got_ref[z ^ d]
        refs[d][0:128, :] = jnp.where(first, mine, got)
        refs[d][128:192, :] = heads_ref[d]
        refs[GROUP + d][0:128, :] = jnp.where(first, got, mine)
        refs[GROUP + d][128:192, :] = g_ref[:, 0:512]
        refs[GROUP + d][192:256, :] = g_ref[:, 512:1024]


def first_heads_kernel(ids, *refs):
    z = ids[1]
    heads_ref, x_refs, vec_refs = refs[GROUP], refs[5:9], refs[9:11]
    for d in range(GROUP):
        block = refs[d][...]
        x_refs[d][:, 0:512] = block[80:144]
        x_refs[d][:, 512:1024] = block[144:208]
        heads_ref[z ^ d] = block[0:64]
        lanes = spot((z ^ d) * 256, 256)
        for layer in range(2):
            rows = block[64:80, layer * 256 : (layer + 1) * 256].astype(F32)
            row = rows[8:9, :]
            for k in range(1, GROUP):
                row = jnp.where(z == k, rows[8 + k : 9 + k, :], row)
            vec_refs[layer][0:8, lanes] = rows[0:8, :]
            vec_refs[layer][8:9, lanes] = row


def part_kernel(ids, *refs):
    for d in range(GROUP):
        refs[GROUP][ids[1] ^ d] = refs[d][0:128, :]
        refs[GROUP + 1][ids[1] ^ d] = refs[d][128:192, :]


def turn_part_kernel(ids, *refs):
    for d in range(GROUP):
        refs[GROUP][ids[1] ^ d] = refs[d][0:128, :]
        refs[GROUP + 1 + d][:, 0:512] = refs[d][128:192, :]
        refs[GROUP + 1 + d][:, 512:1024] = refs[d][192:256, :]


def place_kernel(axis, ids, *refs):
    for d in range(GROUP):
        refs[GROUP][ids[axis] ^ d] = refs[d][...]


def mixed_piece(ref, level):
    return jnp.concatenate([ref[k, level, :, 0:384] for k in range(GROUP)], axis=0)


def head_rows(ref, s):
    rows = []
    for d in range(GROUP):
        for k in range(GROUP):
            tiles = [ref[k, s ^ d, q * 16 : (q + 1) * 16, 384:512] for q in range(GROUP)]
            rows.append(jnp.concatenate(tiles, axis=1))
    return jnp.concatenate(rows, axis=0)


def hidden_piece(ref, level):
    return jnp.concatenate([ref[k, level, 0:64, :] for k in range(GROUP)], axis=0)


def back_share(ref):
    rows = []
    for j in range(GROUP):
        for k in range(GROUP):
            rows.append(jnp.concatenate([ref[k, j, 64:96, :], ref[k, j, 96:128, :]], axis=1))
    return jnp.concatenate(rows, axis=0)


def mixed_kernel(ids, *refs):
    x_refs, own_ref, oth_ref, vec = refs[:4], refs[4], refs[5], refs[6]
    out_refs, nf_ref, packed = refs[7:11], refs[11], refs[12]
    s, z, c = ids[0], ids[1], ids[2]
    gain_vec, bias_vec = vec[0:1, :], vec[1:2, :]
    for d in range(GROUP):
        nf_ref[d * 64 : (d + 1) * 64, :] = normed_rows(
            x_refs[d][...].astype(F32), gain_vec, bias_vec
        ).astype(BF)

    def bias_of(row, j):
        tile = vec[row : row + 1, spot(j * 256 + (z >> 1) * 128, 128)]
        return jnp.where((z & 1) == 1, tile[:, DH:], tile[:, :DH])

    empty = jnp.zeros((1, DH), F32)
    for ref, half in ((own_ref, c), (oth_ref, 1 - c)):
        total = jnp.zeros((GROUP * 64, 384), F32)
        for k in range(GROUP):
            total = total + nn(nf_ref[:, k * 256 : (k + 1) * 256], mixed_piece(ref, k))
        j = 2 * half
        row = jnp.concatenate(
            [
                bias_of(2, j),
                empty,
                bias_of(2, j + 1),
                empty,
                bias_of(3, j),
                bias_of(3, j + 1),
            ],
            axis=1,
        )
        total = total + row
        for i in range(2):
            packed[j + i, 0:256, :] = total[:, i * 128 : (i + 1) * 128].astype(BF)
            values = total[:, 256 + i * DH : 256 + (i + 1) * DH]
            packed[j + i, 256:384, :] = jnp.concatenate(
                [values[:128], values[128:]], axis=1
            ).astype(BF)
    for d in range(GROUP):
        out_refs[d][...] = packed[s ^ d]


def spread(ids, pieces, qk_ref, v_ref):
    s, z = ids[0], ids[1]
    for d in range(GROUP):
        for e in range(GROUP):
            rows = spot(((s ^ d) * GROUP + (z ^ e)) * 64, 64)
            qk_ref[rows, :] = pieces[d][e * 64 : (e + 1) * 64, :]
            lanes = slice(0, DH) if e < 2 else slice(DH, 128)
            start = 256 + (e & 1) * 64
            v_ref[rows, :] = pieces[d][start : start + 64, lanes]


def block_scores(qk_ref, seg_col, seg_row, start, size):
    stop = start + size
    queries = qk_ref[start:stop, 0:DH] * jnp.asarray(DH ** (-0.5), BF)
    scores = nt(queries, qk_ref[0:stop, DH:128])
    same = seg_col[start:stop, :] == seg_row[:, 0:stop]
    q_place = lax.broadcasted_iota(jnp.int32, (size, size), 0)
    k_place = lax.broadcasted_iota(jnp.int32, (size, size), 1)
    near = ((k_place <= q_place) & same[:, start:stop]) | (k_place == q_place)
    near = jnp.where(near, scores[:, start:stop], NEGATIVE)
    if start == 0:
        return near
    return jnp.concatenate([jnp.where(same[:, :start], scores[:, :start], NEGATIVE), near], axis=1)


def attend_kernel(ids, *refs):
    pieces, seg_col, seg_row = refs[:4], refs[4], refs[5]
    out_refs, qk_ref, v_ref, probs_ref, o_ref = refs[6:10], *refs[10:14]
    s, z = ids[0], ids[1]
    spread(ids, pieces, qk_ref, v_ref)
    count = qk_ref.shape[0]
    size = 256
    for start in range(0, count, size):
        scores = block_scores(qk_ref, seg_col, seg_row, start, size)
        top = jnp.max(scores, axis=-1, keepdims=True)
        grown = jnp.exp(scores - top)
        total = jnp.sum(grown, axis=-1, keepdims=True)
        probs = grown * (1.0 / total)
        probs_ref[start : start + size, 0 : start + size] = probs
        o_ref[start : start + size, :] = nn(
            probs.astype(BF), v_ref[0 : start + size, :]
        ).astype(BF)
    for d in range(GROUP):
        for e in range(2):
            left = o_ref[spot(((s ^ d) * GROUP + (z ^ e)) * 64, 64), :]
            right = o_ref[spot(((s ^ d) * GROUP + (z ^ (e + 2))) * 64, 64), :]
            out_refs[d][e * 64 : (e + 1) * 64, :] = jnp.concatenate([left, right], axis=1)


def unpacked(piece):
    return jnp.concatenate([piece[:, :DH], piece[:, DH:]], axis=0)


def output_kernel(ids, *refs):
    pieces, own_ref, oth_ref = refs[:4], refs[4], refs[5]
    out_refs, att_ref = refs[6:10], refs[10]
    s, c = ids[0], ids[2]
    att = jnp.concatenate([unpacked(pieces[d][...]) for d in range(GROUP)], axis=1)
    att_ref[...] = att
    for w_ref, half in ((own_ref, c), (oth_ref, 1 - c)):
        part = nn(att, head_rows(w_ref, s)).astype(BF)
        for d in range(GROUP):
            out_refs[d][:, spot(half * 512, 512)] = part[d * 64 : (d + 1) * 64, :]


def summed(refs):
    blocks = []
    for ref in refs:
        blocks += [ref[...]] if len(ref.shape) == 2 else [ref[k] for k in range(GROUP)]
    total = blocks[0].astype(F32)
    for block in blocks[1:]:
        total = total + block.astype(F32)
    return total


def residual_kernel(ids, *refs):
    x_ref, vec = refs[4], refs[5]
    res_ref, n_ref = refs[6], refs[7]
    res = x_ref[...].astype(F32) + summed(refs[:4]) + vec[4:5, :]
    res_ref[...] = res
    n_ref[...] = normed_rows(res, vec[5:6, :], vec[6:7, :]).astype(BF)


ROOT = math.sqrt(2.0 / math.pi)


def hidden_bias(vec, half):
    return jnp.concatenate(
        [vec[8:9, spot(j * 256 + half * 128, 128)] for j in range(GROUP)], axis=1
    )


def feed_forward(n_refs, shares, vec, c, nf_ref, keep):
    for d in range(GROUP):
        nf_ref[d * 64 : (d + 1) * 64, :] = n_refs[d][...]
    part = jnp.zeros(nf_ref.shape, F32)
    for place, half in ((0, c), (1, 1 - c)):
        cols = slice(place * 512, (place + 1) * 512)
        pre = jnp.zeros((GROUP * 64, 512), F32)
        for d in range(GROUP):
            pre = pre + nn(nf_ref[:, d * 256 : (d + 1) * 256], hidden_piece(shares[place], d))
        pre = pre + hidden_bias(vec, half)
        square = pre * pre
        bend = jnp.tanh(ROOT * pre * (1.0 + 0.044715 * square))
        act = (0.5 * pre * (1.0 + bend)).astype(BF)
        slope = 0.5 * (1.0 + bend) + (0.5 * ROOT) * pre * (1.0 - bend * bend) * (
            1.0 + (3.0 * 0.044715) * square
        )
        keep(cols, act, slope)
        part = part + nn(act, back_share(shares[place]))
    return part.astype(BF)


def feed_backward(g_blocks, shares, slope_ref, out_refs, d_pre_ref, gf_ref):
    for d in range(GROUP):
        gf_ref[d * 64 : (d + 1) * 64, :] = g_blocks[d]
    for place in range(2):
        cols = slice(place * 512, (place + 1) * 512)
        d_act = nt(gf_ref[...], back_share(shares[place]))
        d_pre_ref[:, cols] = (d_act * slope_ref[:, cols]).astype(BF)
    for d in range(GROUP):
        part = nt(d_pre_ref[:, 0:512], hidden_piece(shares[0], d))
        part = (part + nt(d_pre_ref[:, 512:1024], hidden_piece(shares[1], d))).astype(BF)
        for e in range(GROUP):
            out_refs[e][:, d * 256 : (d + 1) * 256] = part[e * 64 : (e + 1) * 64, :]


def feed_kernel(ids, *refs):
    slope_ref, act_ref, nf_ref = refs[11:14]

    def keep(cols, act, slope):
        act_ref[:, cols] = act
        slope_ref[:, cols] = slope

    part = feed_forward(refs[:4], refs[4:6], refs[6], ids[2], nf_ref, keep)
    for d in range(GROUP):
        refs[7 + d][...] = part[d * 64 : (d + 1) * 64, :]


def feed_back_kernel(ids, *refs):
    blocks = [ref[...] for ref in refs[:4]]
    feed_backward(blocks, refs[4:6], refs[6], refs[7:11], refs[11], refs[12])


def feed_turn_kernel(ids, *refs):
    shares, vec, top_refs, outs = refs[8:10], refs[10], refs[11:15], refs[15:19]
    act_ref, nf_ref, d_pre_ref, gf_ref, slope_ref = refs[19:24]

    def keep(cols, act, slope):
        act_ref[:, cols] = act
        slope_ref[:, cols] = slope

    part = feed_forward(refs[:4], shares, vec, ids[2], nf_ref, keep)
    for d in range(GROUP):
        top_refs[d][...] = part[d * 64 : (d + 1) * 64, :]
    blocks = [ref[...] for ref in refs[4:8]]
    feed_backward(blocks, shares, slope_ref, outs, d_pre_ref, gf_ref)


def close_kernel(ids, *refs):
    res_ref, vec, out_ref = refs[4:]
    out = res_ref[...] + summed(refs[:4]) + vec[7:8, :]
    out_ref[...] = out.astype(out_ref.dtype)


def norm_two_back_kernel(ids, *refs):
    res_ref, g_ref, vec = refs[4], refs[5], refs[6]
    d_res_ref, ga_ref, rows_ref = refs[7:10]
    grad = g_ref[...].astype(F32)
    pulled, d_gain, d_bias = norm_pull(res_ref[...], vec[5:6, :], summed(refs[:4]))
    d_res = grad + pulled
    low = d_res.astype(BF)
    d_res_ref[...] = d_res
    ga_ref[...] = low
    rows_ref[0:1, :] = jnp.sum(low.astype(F32), axis=0, keepdims=True)
    rows_ref[1:2, :] = d_gain
    rows_ref[2:3, :] = d_bias
    rows_ref[3:4, :] = jnp.sum(grad.astype(BF).astype(F32), axis=0, keepdims=True)
    rows_ref[4:8, :] = jnp.zeros((4, grad.shape[1]), F32)


def output_back_kernel(ids, *refs):
    g_refs, own_ref, oth_ref = refs[:4], refs[4], refs[5]
    out_refs, gf_ref = refs[6:10], refs[10]
    s, c = ids[0], ids[2]
    for d in range(GROUP):
        gf_ref[d * 64 : (d + 1) * 64, :] = g_refs[d][...]
    d_att = nt(gf_ref[:, spot(c * 512, 512)], head_rows(own_ref, s))
    d_att = d_att + nt(gf_ref[:, spot((1 - c) * 512, 512)], head_rows(oth_ref, s))
    for d in range(GROUP):
        cols = d_att[:, d * DH : (d + 1) * DH]
        out_refs[d][...] = jnp.concatenate([cols[:128], cols[128:]], axis=1).astype(BF)


def feed_grads_kernel(ids, *refs):
    act_ref, gb_ref, nf_ref, d_pre_ref = refs[:4]
    keep_ref, send_ref, sums_ref = refs[4:7]
    for place, out_ref in ((0, keep_ref), (1, send_ref)):
        cols = slice(place * 512, (place + 1) * 512)
        d_fc = tn(nf_ref[...], d_pre_ref[:, cols]).astype(BF)
        for k in range(GROUP):
            out_ref[k, 0:256, :] = d_fc[k * 256 : (k + 1) * 256, :]
        d_proj = tn(act_ref[:, cols], gb_ref[...]).astype(BF)
        for j in range(GROUP):
            rows = d_proj[j * 128 : (j + 1) * 128, :]
            out_ref[j, 256:384, :] = rows[:, 0:512]
            out_ref[j, 384:512, :] = rows[:, 512:1024]
    sums_ref[...] = jnp.sum(d_pre_ref[...].astype(F32), axis=0, keepdims=True)


def attend_back_kernel(ids, *refs):
    d_pieces, qk_ref, v_ref, probs_ref, out_refs = refs[0:4], *refs[4:7], refs[7:11]
    do_ref, dq_ref, dk_ref, dv_ref = refs[11:15]
    s, z = ids[0], ids[1]
    for d in range(GROUP):
        for e in range(GROUP):
            rows = spot(((s ^ d) * GROUP + (z ^ e)) * 64, 64)
            lanes = slice(0, DH) if e < 2 else slice(DH, 128)
            start = (e & 1) * 64
            do_ref[rows, :] = d_pieces[d][start : start + 64, lanes]
    count = qk_ref.shape[0]
    size = 256
    for start in range(0, count, size):
        stop = start + size
        probs = probs_ref[start:stop, 0:stop]
        d_out = do_ref[start:stop, :]
        d_weights = nt(d_out, v_ref[0:stop, :])
        row_dot = jnp.sum(probs * d_weights, axis=-1, keepdims=True)
        d_scores = (probs * (d_weights - row_dot) * DH ** (-0.5)).astype(BF)
        dq_ref[start:stop, :] = nn(d_scores, qk_ref[0:stop, DH:128])
        dk = tn(d_scores, qk_ref[start:stop, 0:DH])
        dv = tn(probs.astype(BF), d_out)
        if start:
            dk_ref[0:start, :] += dk[0:start]
            dv_ref[0:start, :] += dv[0:start]
        dk_ref[start:stop, :] = dk[start:stop]
        dv_ref[start:stop, :] = dv[start:stop]
    for d in range(GROUP):
        for e in range(GROUP):
            rows = spot(((s ^ d) * GROUP + (z ^ e)) * 64, 64)
            out_refs[d][e * 64 : (e + 1) * 64, :] = jnp.concatenate(
                [dq_ref[rows, :], dk_ref[rows, :]], axis=1
            ).astype(BF)
        for e in range(2):
            left = dv_ref[spot(((s ^ d) * GROUP + (z ^ e)) * 64, 64), :]
            right = dv_ref[spot(((s ^ d) * GROUP + (z ^ (e + 2))) * 64, 64), :]
            out_refs[d][256 + e * 64 : 320 + e * 64, :] = jnp.concatenate(
                [left, right], axis=1
            ).astype(BF)


def mixed_back_kernel(ids, *refs):
    pieces, own_ref, oth_ref = refs[:4], refs[4], refs[5]
    out_refs, dm_ref, held = refs[6:10], refs[10], refs[11]
    s, c = ids[0], ids[2]
    for d in range(GROUP):
        held[d] = pieces[d][...]
    for place, half in ((0, c), (1, 1 - c)):
        base = place * 384
        values = []
        for i in range(2):
            d = (2 * half + i) ^ s
            dm_ref[:, base + i * 128 : base + (i + 1) * 128] = held[d, 0:256, :]
            values.append(unpacked(held[d, 256:384, :]))
        dm_ref[:, base + 256 : base + 384] = jnp.concatenate(values, axis=1)
    for k in range(GROUP):
        part = nt(dm_ref[:, 0:384], mixed_piece(own_ref, k))
        part = (part + nt(dm_ref[:, 384:768], mixed_piece(oth_ref, k))).astype(BF)
        for d in range(GROUP):
            out_refs[d][:, k * 256 : (k + 1) * 256] = part[d * 64 : (d + 1) * 64, :]


def attend_grads_kernel(ids, *refs):
    nf_ref, dm_ref, att_ref, ga_ref, two_ref, fc_ref = refs[:6]
    part_refs, x_refs = refs[6:10], refs[10:14]
    keep_ref, send_ref, lines = refs[14:17]
    s, c = ids[0], ids[2]
    d_gain = d_bias = 0.0
    for d in range(GROUP):
        grad = part_refs[d][...].astype(F32)
        values = x_refs[d][...].astype(F32)
        average = jnp.mean(values, axis=-1, keepdims=True)
        centred = values - average
        variance = jnp.mean(centred * centred, axis=-1, keepdims=True)
        unit = centred * lax.rsqrt(variance + EPSILON)
        d_gain = d_gain + jnp.sum(grad * unit, axis=0, keepdims=True)
        d_bias = d_bias + jnp.sum(grad, axis=0, keepdims=True)
    lines[0:1, :] = d_gain
    lines[1:2, :] = d_bias
    lines[2:6, :] = two_ref[0:4, :]
    lines[6:8, :] = jnp.zeros((2, d_gain.shape[1]), F32)
    for place, out_ref, half in ((0, keep_ref, c), (1, send_ref, 1 - c)):
        base = place * 384
        d_w = tn(nf_ref[...], dm_ref[:, base : base + 384]).astype(BF)
        sums = jnp.sum(dm_ref[:, base : base + 384].astype(F32), axis=0, keepdims=True)
        for k in range(GROUP):
            out_ref[k, 0:256, 0:384] = d_w[k * 256 : (k + 1) * 256, :]
            mine = (k >> 1) == half
            i = k & 1
            query = sums[:, i * 128 : i * 128 + DH]
            value = sums[:, 256 + i * DH : 256 + (i + 1) * DH]
            first = place * 512 + k * 128
            line = jnp.concatenate(
                [
                    fc_ref[:, first : first + 128],
                    jnp.where(mine, query, 0.0),
                    jnp.where(mine, value, 0.0),
                    jnp.zeros((1, 128), F32),
                ],
                axis=1,
            )
            foot = jnp.concatenate([line, jnp.zeros((7, 384), F32)], axis=0)
            foot = jnp.concatenate([lines[:, spot(k * 256 + half * 128, 128)], foot], axis=1)
            foot = jnp.concatenate([foot, jnp.zeros((8, 512), F32)], axis=0)
            out_ref[k, 256:272, :] = foot.astype(BF)
        d_out = tn(att_ref[...], ga_ref[:, spot(half * 512, 512)]).astype(BF)
        for d in range(GROUP):
            for q in range(GROUP):
                out_ref[s ^ d, q * 64 : (q + 1) * 64, 384:512] = d_out[
                    d * 64 : (d + 1) * 64, q * 128 : (q + 1) * 128
                ]


def norm_one_back_kernel(ids, *refs):
    x_ref, d_res_ref, vec = refs[4], refs[5], refs[6]
    pulled, _, _ = norm_pull(x_ref[...].astype(F32), vec[0:1, :], summed(refs[:4]))
    refs[7][...] = (d_res_ref[...] + pulled).astype(BF)


def ends_kernel(ids, *refs):
    x_ref, d_res_ref, vec, top_ref = refs[4:8]
    pulled, _, _ = norm_pull(x_ref[...].astype(F32), vec[0:1, :], summed(refs[:4]))
    bottom, top = d_res_ref[...] + pulled, top_ref[...]
    first = ids[2] == 0
    refs[8][...] = jnp.where(first, bottom, top)
    refs[9][...] = jnp.where(first, top, bottom)


def add_kernel(ids, left_ref, right_ref, *out_refs):
    for d in range(GROUP):
        k = ids[0] ^ d
        out_refs[d][...] = (left_ref[k].astype(F32) + right_ref[k].astype(F32)).astype(BF)


def choose_kernel(ids, *refs):
    lower, upper = summed(refs[:4]).astype(BF), summed(refs[4:8]).astype(BF)
    first = ids[2] == 0
    refs[8][...] = jnp.where(first, lower, upper)
    refs[9][...] = jnp.where(first, upper, lower)


def split_feed_kernel(ids, own_ref, oth_ref, *refs):
    back_out = refs[GROUP]
    for d in range(GROUP):
        rows = spot((ids[1] ^ d) * 64, 64)
        refs[d][:, 0:512] = own_ref[rows, :]
        refs[d][:, 512:1024] = oth_ref[rows, :]
    for ref, half in ((own_ref, ids[2]), (oth_ref, 1 - ids[2])):
        rows = spot(half * 128, 128)
        back_out[0, rows, 0:512] = ref[256:384, :].astype(F32)
        back_out[0, rows, 512:1024] = ref[384:512, :].astype(F32)


def split_attend_kernel(ids, own_ref, oth_ref, *refs):
    out_ref, bfc_ref, query_ref, value_ref = refs[GROUP:]
    s, z, c = ids[0], ids[1], ids[2]
    foots = (own_ref[256:272, :], oth_ref[256:272, :])
    for d in range(GROUP):
        rows = spot((z ^ d) * 64, 64)
        refs[d][0:64, 0:384] = own_ref[rows, 0:384]
        refs[d][0:64, 384:768] = oth_ref[rows, 0:384]
        lines = jnp.where(((z ^ d) >> 1) == c, foots[0][:, 0:128], foots[1][:, 0:128])
        refs[d][64:80, :] = jnp.concatenate([lines, jnp.zeros((16, 640), BF)], axis=1)
    for ref, half in ((own_ref, c), (oth_ref, 1 - c)):
        for q in range(GROUP):
            out_ref[0, :, spot(half * 512 + q * 128, 128)] = ref[
                q * 64 : (q + 1) * 64, 384:512
            ].astype(F32)
    own, oth = foots[0][0:1, :].astype(F32), foots[1][0:1, :].astype(F32)
    lower, upper = jnp.where(c == 0, own, oth), jnp.where(c == 0, oth, own)
    bfc_ref[:, 0:128] = lower[:, 128:256]
    bfc_ref[:, 128:256] = upper[:, 128:256]
    line = jnp.where((s >> 1) == 0, lower, upper)
    query_ref[...] = line[:, 256 : 256 + DH]
    value_ref[...] = line[:, 256 + DH : 384]


def final_feed_kernel(ids, *refs):
    mine_ref, got_ref, fc_out, relay_out = refs[GROUP:]
    first = ids[2] == 0
    mine, got = mine_ref[...], got_ref[...]
    relay_out[0, 0] = jnp.where(first, mine, got)
    relay_out[0, 1] = jnp.where(first, got, mine)
    for place, half in ((0, ids[2]), (1, 1 - ids[2])):
        for d in range(GROUP):
            for j in range(GROUP):
                start = place * 512 + j * 128
                lanes = spot(j * 1024 + (ids[1] ^ d) * 256 + half * 128, 128)
                fc_out[0, :, lanes] = refs[d][:, start : start + 128].astype(F32)


def final_attend_kernel(ids, *refs):
    mixed, mixed_out, line_outs, held = refs[:4], refs[4], refs[5:11], refs[11]
    z, c = ids[1], ids[2]
    width = mixed_out.shape[2] // 3
    lines = 0.0
    for d in range(GROUP):
        held[z ^ d] = mixed[d][0:64, :]
        lines = lines + mixed[d][64:80, 0:128].astype(F32)
    lines = jnp.where((z & 1) == 1, lines[:, DH:], lines[:, :DH])
    for i, ref in enumerate(line_outs):
        ref[...] = lines[i : i + 1, :]
    for place, half in ((0, c), (1, 1 - c)):
        base = place * 384
        for pair in range(2):
            for i in range(2):
                tiles = []
                for source in (2 * pair, 2 * pair + 1):
                    qk = held[source, :, base + i * 128 : base + (i + 1) * 128].astype(F32)
                    v = held[source, :, base + 256 + i * DH : base + 256 + (i + 1) * DH]
                    tiles.append((qk[:, :DH], qk[:, DH:], v.astype(F32)))
                for t in range(3):
                    start = t * width + (2 * half + i) * 256 + pair * 128
                    mixed_out[0, :, spot(start, 128)] = jnp.concatenate(
                        [tiles[0][t], tiles[1][t]], axis=1
                    )


def fast_body(
    inputs,
    cotangent,
    segment_ids,
    ln1_gain,
    ln1_bias,
    w_qkv,
    b_query,
    b_value,
    w_out,
    b_out,
    ln2_gain,
    ln2_bias,
    w_fc,
    b_fc,
    w_proj,
    b_proj,
):
    s, z, c = lax.axis_index(SEQ), lax.axis_index(FSDP), lax.axis_index("section")
    ids = jnp.stack([s, z, c]).astype(jnp.int32)
    tok, width = inputs.shape[1:]
    count = segment_ids.shape[1]
    tall = GROUP * tok
    piece = ((384, 128), BF)
    small = ((128, 128), BF)
    part = ((tok, width), BF)
    wide = ((tall, width), BF)
    line = ((tok, width), F32)
    share = ((272, 512), BF)
    feed_share = ((512, 512), BF)
    done, awaited, lagging = [], [], []

    def run(kernel, args, outs, *scratch, anywhere=(), mib=16, aside=False):
        args = list(args)
        earlier = done[-1:] + ([] if aside else list(awaited))
        if earlier:
            args[0] = after(args[0], *earlier)
        if not aside:
            awaited[:] = lagging
            lagging.clear()
        result = list(call(kernel, ids, args, outs, scratch, anywhere, mib))
        done.append(result[-1])
        return result

    def beside(blocks, got, axis, *which, lag=False):
        for d in which:
            got[d] = exchange(after(blocks[d], done[-1]), axis, d)
            (lagging if lag else awaited).append(got[d])

    def now(blocks):
        return [after(block, done[-1]) for block in blocks]

    def of(kernel, axis):
        def bound(*refs):
            kernel(axis, *refs)

        bound.__name__ = kernel.__name__
        return bound

    def shared(pieces, axis, shape, aside=False):
        (whole,) = run(of(place_kernel, axis), pieces, [(shape, BF)], aside=aside)
        return [whole, swap(whole)]

    mine, send, feed_mine, feed_send, x, grad = run(
        pick_kernel,
        [w_qkv, w_out]
        + [ln1_gain, ln1_bias, b_query, b_value, b_out, ln2_gain, ln2_bias, b_proj, b_fc]
        + [inputs, cotangent, w_fc, w_proj],
        [((GROUP, 80, 512), BF)] * 2 + [((GROUP, 128, 512), BF)] * 2 + [part] * 2,
        pltpu.VMEM((64, 3 * width), BF),
        pltpu.VMEM((GROUP, 16, width), BF),
        pltpu.VMEM((8, 1, 256), BF),
        pltpu.VMEM((1, 1024), BF),
        pltpu.SemaphoreType.DMA((64,)),
        anywhere=range(15),
    )
    *heads, upper_heads = run(
        settle_heads_kernel,
        [mine, swap(send), x],
        [((208, 512), BF)] * 4 + [((GROUP, 64, 512), BF)],
    )
    heads = trade(heads, FSDP)
    feed_got = swap(feed_send)
    *rest, seg_col, seg_row = run(
        settle_feed_kernel,
        [feed_mine, feed_got, upper_heads, segment_ids, grad],
        [((192, 512), BF)] * 4
        + [((256, 512), BF)] * 4
        + [((count, 1), F32), ((1, count), F32)],
        aside=True,
    )
    rests = [rest[:4], rest[4:]]
    rest_got = [list(blocks) for blocks in rests]
    heads, *rest = run(
        first_heads_kernel,
        heads,
        [((GROUP, 64, 512), BF)] + [part] * 4 + [((16, width), F32)] * 2,
    )
    x_all, vec = rest[:4], rest[4:]
    heads = gather(heads, SEQ)
    for blocks, got in zip(rests, rest_got):
        beside(blocks, got, FSDP, 1)
    head_w = [shared(heads, 0, (GROUP, GROUP, 64, 512)), None]

    feed_w = [None, None]
    kept = []
    for layer in range(2):
        *packed, normed = run(
            mixed_kernel,
            x_all + head_w[layer] + [vec[layer]],
            [piece] * 4 + [wide],
            pltpu.VMEM((GROUP, 384, 128), BF),
        )
        qkv = trade(packed, SEQ)
        got = rest_got[layer]
        beside(rests[layer], got, FSDP, 3, 2, lag=True)
        *heads, qk_rows, v_rows, probs = run(
            attend_kernel,
            qkv + [seg_col, seg_row],
            [small] * 4 + [((count, 128), BF), ((count, DH), BF), ((count, count), F32)],
            pltpu.VMEM((count, DH), BF),
        )
        heads = trade(heads, SEQ)
        *parts, att = run(
            output_kernel,
            heads + head_w[layer],
            [part] * 4 + [((tall, 256), BF)],
        )
        parts = trade(parts, FSDP)
        if layer == 0:
            feed, heads_later = run(
                part_kernel,
                got,
                [((GROUP, 128, 512), BF), ((GROUP, 64, 512), BF)],
                aside=True,
            )
        else:
            feed, *grad_all = run(
                turn_part_kernel, got, [((GROUP, 128, 512), BF)] + [part] * 4, aside=True
            )
        feeds = [feed] * GROUP
        beside(feeds, feeds, SEQ, 1, 2)
        res, n_two = run(
            residual_kernel, parts + [x, vec[layer]], [line, part]
        )
        n_all = gather(n_two, FSDP)
        beside([feed] * GROUP, feeds, SEQ, 3)
        feeds[0] = after(feeds[0], *n_all)
        feed_w[layer] = shared(feeds, 0, (GROUP, GROUP, 128, 512))
        kept.append((x, normed, (qk_rows, v_rows, probs), att, res, x_all))
        if layer == 0:
            *parts, slope, act, n_full = run(
                feed_kernel,
                n_all + feed_w[0] + [vec[0]],
                [part] * 4 + [((tall, 1024), F32), ((tall, 1024), BF), wide],
            )
            parts = trade(parts, FSDP)
            heads = [heads_later] * GROUP
            beside(heads, heads, SEQ, 1, 2)
            (x,) = run(close_kernel, parts + [res, vec[0]], [part])
            x_all = gather(x, FSDP)
            beside([heads_later] * GROUP, heads, SEQ, 3)
            heads[0] = after(heads[0], *x_all)
            head_w[1] = shared(heads, 0, (GROUP, GROUP, 64, 512))
        else:
            turn = run(
                feed_turn_kernel,
                n_all + grad_all + feed_w[1] + [vec[1]],
                [part] * 8 + [((tall, 1024), BF), wide, ((tall, 1024), BF), wide],
                pltpu.VMEM((tall, 1024), F32),
                mib=20,
            )

    def feed_terms(act, gb_full, n_full, d_pre):
        keep, send, sums = run(
            feed_grads_kernel,
            [act, gb_full, n_full, d_pre],
            [((GROUP, 512, 512), BF)] * 2 + [((1, 1024), F32)],
            aside=True,
        )
        return keep, swap(send), sums

    def attend_terms(layer, two_rows, fc_sums, parts, d_mixed, ga_full):
        x, normed, _, att, _, x_all = kept[layer]
        keep, send = run(
            attend_grads_kernel,
            [normed, d_mixed, att, ga_full, two_rows, fc_sums] + parts + x_all,
            [((GROUP,) + share[0], BF)] * 2,
            pltpu.VMEM((8, width), F32),
            aside=True,
        )
        return keep, swap(send)

    def total(keep, got, shape):
        return run(add_kernel, [keep, got], [shape] * 4, aside=True)

    def norm_two_back(layer, parts, grad):
        return run(
            norm_two_back_kernel,
            parts + [kept[layer][4], grad, vec[layer]],
            [line, part, ((8, width), F32)],
        )

    def output_back(layer, ga_all):
        return run(
            output_back_kernel,
            ga_all + head_w[layer],
            [small] * 4 + [wide],
        )

    def attend_back(layer, d_heads):
        return run(
            attend_back_kernel,
            d_heads + list(kept[layer][2]),
            [piece] * 4,
            pltpu.VMEM((count, DH), BF),
            *[pltpu.VMEM((count, DH), F32)] * 3,
        )

    def mixed_back(layer, d_pieces):
        return run(
            mixed_back_kernel,
            d_pieces + head_w[layer],
            [part] * 4 + [((tall, 768), BF)],
            pltpu.VMEM((GROUP, 384, 128), BF),
        )

    def norm_one_back(layer, parts, d_res):
        return run(
            norm_one_back_kernel,
            parts + [kept[layer][0], d_res, vec[layer]],
            [part],
        )[0]

    top_parts, parts = turn[:4], trade(turn[4:8], FSDP)
    keep, got, fc_sums = feed_terms(turn[8], turn[11], turn[9], turn[10])
    terms = total(keep, got, feed_share)
    d_res, ga, two_rows = norm_two_back(1, parts, grad)
    ga_all = gather(ga, FSDP)
    upper_feed = list(terms)
    beside(terms, upper_feed, SEQ, 1, 2)
    *d_heads, ga_full = output_back(1, ga_all)
    d_heads = trade(d_heads, SEQ)
    tops = list(top_parts)
    beside(top_parts, tops, FSDP, 1, 3)
    d_pieces = trade(attend_back(1, d_heads), SEQ)
    beside(top_parts, tops, FSDP, 2)
    *sent, d_mixed = mixed_back(1, d_pieces)
    parts = trade(sent, FSDP)
    beside(terms, upper_feed, SEQ, 3)
    keep, got = attend_terms(1, two_rows, fc_sums, sent, d_mixed, ga_full)
    (top,) = run(close_kernel, tops + [kept[1][4], vec[1]], [line], aside=True)
    upper_terms = total(keep, got, share)
    low = norm_one_back(1, parts, d_res)
    g_all = gather(low, FSDP)
    upper_attend = list(upper_terms)
    beside(upper_terms, upper_attend, SEQ, 1, 2)

    *parts, d_pre, gb_full = run(
        feed_back_kernel,
        g_all + feed_w[0] + [slope],
        [part] * 4 + [((tall, 1024), BF), wide],
    )
    parts = trade(parts, FSDP)
    beside(upper_terms, upper_attend, SEQ, 3)
    keep, got, fc_sums = feed_terms(act, gb_full, n_full, d_pre)
    terms = total(keep, got, feed_share)
    d_res, ga, two_rows = norm_two_back(0, parts, low)
    ga_all = gather(ga, FSDP)
    lower_feed = list(terms)
    beside(terms, lower_feed, SEQ, 1, 2)
    *d_heads, ga_full = output_back(0, ga_all)
    d_heads = trade(d_heads, SEQ)
    beside(terms, lower_feed, SEQ, 3)
    d_pieces = trade(attend_back(0, d_heads), SEQ)
    mine, theirs = run(choose_kernel, lower_feed + upper_feed, [feed_share] * 2, aside=True)
    got = swap(theirs)
    *blocks, g_proj = run(
        split_feed_kernel,
        [mine, got],
        [((64, 1024), BF)] * 4 + [((1, 256, width), F32)],
        aside=True,
    )
    fc_parts = list(blocks)
    beside(blocks, fc_parts, FSDP, 3, 2)
    *sent, d_mixed = mixed_back(0, d_pieces)
    keep, got = attend_terms(0, two_rows, fc_sums, sent, d_mixed, ga_full)
    lower_attend = trade(total(keep, got, share), SEQ)

    parts = trade(now(sent), FSDP)
    lower_attend[0] = after(lower_attend[0], *parts)
    mine, theirs = run(choose_kernel, lower_attend + upper_attend, [share] * 2)
    got = swap(theirs)
    ends_mine, ends_theirs = run(
        ends_kernel, parts + [kept[0][0], d_res, vec[0], top], [line] * 2
    )
    ends_got = swap(ends_theirs)
    *blocks, g_out, g_bfc, g_query, g_value = run(
        split_attend_kernel,
        [mine, got],
        [((80, 768), BF)] * 4
        + [((1, 64, width), F32), ((1, 256), F32), ((1, 64), F32), ((1, 64), F32)],
    )
    mixed_parts = trade(blocks, FSDP)
    fc_parts[1] = exchange(after(fc_parts[1], g_out), FSDP, 1)
    g_fc, relay = run(
        final_feed_kernel,
        fc_parts + [ends_mine, ends_got],
        [((1, 64, 4096), F32), ((1, 2, tok, width), F32)],
    )
    g_mixed, *lines = run(
        final_attend_kernel,
        mixed_parts,
        [((1, 64, 3 * width), F32)] + [((1, 64), F32)] * 6,
        pltpu.VMEM((GROUP, 64, 768), BF),
    )

    return (
        relay,
        lines[0],
        lines[1],
        g_mixed,
        g_query,
        g_value,
        g_out,
        lines[2],
        lines[3],
        lines[4],
        g_fc,
        g_bfc,
        g_proj,
        lines[5],
    )


def plan(mesh):
    fits = mesh.shape[SECTION] == 2 and mesh.shape[SEQ] == mesh.shape[FSDP] == GROUP
    return fast_body if fits else body


def solution(mesh):
    placed = (
        P(None, ("seq", "fsdp"), None),
        P(None, ("seq", "fsdp"), None),
        P(),
        P("section", "fsdp"),
        P("section", "fsdp"),
        P("section", "fsdp", None),
        P("section", "fsdp"),
        P("section", "fsdp"),
        P("section", "fsdp", None),
        P("section", "fsdp"),
        P("section", "fsdp"),
        P("section", "fsdp"),
        P("section", "fsdp", None),
        P("section", "fsdp"),
        P("section", "fsdp", None),
        P("section", "fsdp"),
    )
    return jax.shard_map(
        plan(mesh),
        mesh=mesh,
        in_specs=placed,
        out_specs=(
            P("section", None, ("seq", "fsdp"), None),
            P("section", ("seq", "fsdp")),
            P("section", ("seq", "fsdp")),
            P("section", ("seq", "fsdp"), None),
            P("section", ("seq", "fsdp")),
            P("section", ("seq", "fsdp")),
            P("section", ("seq", "fsdp"), None),
            P("section", ("seq", "fsdp")),
            P("section", ("seq", "fsdp")),
            P("section", ("seq", "fsdp")),
            P("section", ("seq", "fsdp"), None),
            P("section", ("seq", "fsdp")),
            P("section", ("seq", "fsdp"), None),
            P("section", ("seq", "fsdp")),
        ),
        check_vma=False,
    )
```

```python
import math

import jax
import jax.numpy as jnp
from jax import lax
from jax.experimental import pallas as pl
from jax.experimental.pallas import tpu as pltpu
from jax.sharding import PartitionSpec as P

DH = 64


EPSILON = 1e-05
NEGATIVE = -1e30


def shifted(block, axis, distance):
    devices = range(lax.axis_size(axis))
    route = [(i - distance, i) for i in devices if i - distance in devices]
    return lax.ppermute(block, axis, route)


def layer_norm(values, gain_vec, bias_vec):
    average = jnp.mean(values, axis=-1, keepdims=True)
    centred = values - average
    variance = jnp.mean(centred * centred, axis=-1, keepdims=True)
    return centred * lax.rsqrt(variance + EPSILON) * gain_vec + bias_vec


def gelu_tanh(values):
    return jax.nn.gelu(values, approximate=True)


def mask_rows(seg_row, fsdp_index, n_seq, n_fsdp, tok_rows):
    places = jnp.arange(seg_row.shape[0], dtype=jnp.int32)
    seg_grid = seg_row.reshape(n_seq, n_fsdp, tok_rows)
    place_grid = places.reshape(n_seq, n_fsdp, tok_rows)
    query_ids = lax.dynamic_index_in_dim(seg_grid, fsdp_index, 1, keepdims=False).reshape(-1)
    query_places = lax.dynamic_index_in_dim(place_grid, fsdp_index, 1, keepdims=False).reshape(-1)
    key_ids = jnp.transpose(seg_grid, (1, 0, 2)).reshape(-1)
    key_places = jnp.transpose(place_grid, (1, 0, 2)).reshape(-1)
    same_doc = (query_ids[:, None] == key_ids[None, :]) & (query_ids[:, None] > 0)
    itself = query_places[:, None] == key_places[None, :]
    return (key_places[None, :] <= query_places[:, None]) & (same_doc | itself)


def split_heads(matrix):
    return matrix.reshape(matrix.shape[0], matrix.shape[1] // DH, DH)


def block_rows(matrix, block_len):
    return matrix.reshape((matrix.shape[0] // block_len, block_len) + matrix.shape[1:])


def masked_scores(queries, key_rows, allowed):
    raw_scores = jnp.einsum(
        "qhd,khd->hqk",
        split_heads(queries),
        split_heads(key_rows),
        preferred_element_type=jnp.float32,
    )
    return jnp.where(allowed[None], raw_scores * DH ** (-0.5), NEGATIVE)


def body(
    inputs,
    cotangent,
    segment_ids,
    ln1_gain,
    ln1_bias,
    w_qkv,
    b_query,
    b_value,
    w_out,
    b_out,
    ln2_gain,
    ln2_bias,
    w_fc,
    b_fc,
    w_proj,
    b_proj,
):
    n_seq = lax.axis_size("seq")
    n_fsdp = lax.axis_size("fsdp")
    section_index = lax.axis_index("section")
    fsdp_index = lax.axis_index("fsdp")
    last_section = section_index == 1
    micro, tok_rows, width = inputs.shape
    score_scale = DH ** (-0.5)
    query_count = tok_rows * n_seq
    block_len = math.gcd(query_count, 512)

    def fetch_params():
        return (
            lax.all_gather(ln1_gain[0], "fsdp", axis=0, tiled=True),
            lax.all_gather(ln1_bias[0], "fsdp", axis=0, tiled=True),
            lax.all_gather(w_qkv[0], "fsdp", axis=0, tiled=True),
            lax.all_gather(b_query[0], "fsdp", axis=0, tiled=True),
            lax.all_gather(b_value[0], "fsdp", axis=0, tiled=True),
            lax.all_gather(w_out[0], "fsdp", axis=0, tiled=True),
            lax.all_gather(b_out[0], "fsdp", axis=0, tiled=True),
            lax.all_gather(ln2_gain[0], "fsdp", axis=0, tiled=True),
            lax.all_gather(ln2_bias[0], "fsdp", axis=0, tiled=True),
            lax.all_gather(w_fc[0], "fsdp", axis=0, tiled=True),
            lax.all_gather(b_fc[0], "fsdp", axis=0, tiled=True),
            lax.all_gather(w_proj[0], "fsdp", axis=0, tiled=True),
            lax.all_gather(b_proj[0], "fsdp", axis=0, tiled=True),
        )

    received = jnp.zeros((tok_rows, width), jnp.bfloat16)
    kept_ticks = []
    layer_outs = []
    for tick_index in range(micro + 1):
        params = fetch_params()
        batch_index = jnp.clip(tick_index - section_index, 0, micro - 1)
        seg_row = lax.dynamic_index_in_dim(segment_ids, batch_index, 0, keepdims=False)
        allowed = mask_rows(seg_row, fsdp_index, n_seq, n_fsdp, tok_rows)
        if tick_index < micro:
            first_in = inputs[tick_index].astype(jnp.float32)
        else:
            first_in = jnp.zeros((tok_rows, width), jnp.float32)
        layer_in = jnp.where(last_section, received.astype(jnp.float32), first_in)
        (
            forward_gain_one,
            forward_bias_one,
            forward_w_mixed,
            forward_bias_query,
            forward_bias_value,
            forward_w_output,
            forward_bias_output,
            forward_gain_two,
            forward_bias_two,
            forward_w_hidden,
            forward_bias_hidden,
            forward_w_back,
            forward_bias_back,
        ) = params
        forward_normed = layer_norm(
            layer_in, forward_gain_one.astype(jnp.float32), forward_bias_one.astype(jnp.float32)
        ).astype(jnp.bfloat16)
        mixed_proj = jnp.dot(forward_normed, forward_w_mixed, preferred_element_type=jnp.float32)
        bias_row = jnp.concatenate(
            [forward_bias_query, jnp.zeros_like(forward_bias_query), forward_bias_value]
        ).astype(jnp.float32)
        mixed_tok = (mixed_proj + bias_row).astype(jnp.bfloat16).reshape(tok_rows, 3, width)
        head_rows = lax.all_to_all(mixed_tok, "seq", split_axis=2, concat_axis=0, tiled=True)
        forward_queries = head_rows[:, 0]
        forward_key_rows = lax.all_gather(head_rows[:, 1], "fsdp", axis=0, tiled=True)
        forward_value_rows = lax.all_gather(head_rows[:, 2], "fsdp", axis=0, tiled=True)

        def attend_block(operands):
            query_block, allowed_block = operands
            scores = masked_scores(query_block, forward_key_rows, allowed_block)
            row_top = jnp.max(scores, axis=-1, keepdims=True)
            log_block = row_top + jnp.log(
                jnp.sum(jnp.exp(scores - row_top), axis=-1, keepdims=True)
            )
            attn_weights = jnp.exp(scores - log_block).astype(jnp.bfloat16)
            head_block = jnp.einsum(
                "hqk,khd->qhd",
                attn_weights,
                split_heads(forward_value_rows),
                preferred_element_type=jnp.float32,
            )
            return (head_block.reshape(query_block.shape).astype(jnp.bfloat16), log_block)

        head_blocks, forward_log_total = lax.map(
            attend_block, (block_rows(forward_queries, block_len), block_rows(allowed, block_len))
        )
        head_out = head_blocks.reshape(forward_queries.shape)
        forward_attended = lax.all_to_all(head_out, "seq", split_axis=0, concat_axis=1, tiled=True)
        forward_residual = (
            layer_in
            + jnp.dot(forward_attended, forward_w_output, preferred_element_type=jnp.float32)
            + forward_bias_output.astype(jnp.float32)
        )
        forward_normed_two = layer_norm(
            forward_residual,
            forward_gain_two.astype(jnp.float32),
            forward_bias_two.astype(jnp.float32),
        ).astype(jnp.bfloat16)
        forward_pre_act = jnp.dot(
            forward_normed_two, forward_w_hidden, preferred_element_type=jnp.float32
        ) + forward_bias_hidden.astype(jnp.float32)
        forward_activated = gelu_tanh(forward_pre_act).astype(jnp.bfloat16)
        layer_out = (
            forward_residual
            + jnp.dot(forward_activated, forward_w_back, preferred_element_type=jnp.float32)
            + forward_bias_back.astype(jnp.float32)
        )
        forward_kept = (
            layer_in,
            forward_normed,
            forward_queries,
            forward_key_rows,
            forward_value_rows,
            forward_log_total,
            allowed,
            forward_attended,
            forward_residual,
            forward_normed_two,
            forward_pre_act,
            forward_activated,
        )
        layer_out, kept = (layer_out, forward_kept)
        kept_ticks.append(kept)
        layer_outs.append(layer_out)
        if tick_index < micro:
            received = shifted(layer_out.astype(jnp.bfloat16), "section", 1)
    sent_back = jnp.zeros((tok_rows, width), jnp.bfloat16)
    input_grads = []
    totals = None
    for tick_index in range(micro + 1):
        params = fetch_params()
        later = kept_ticks[min(tick_index + 1, micro)]
        earlier = kept_ticks[max(tick_index - 1, 0)]
        kept = jax.tree.map(
            lambda upper, lower: jnp.where(last_section, upper, lower), later, earlier
        )
        if tick_index < micro:
            top_grad = cotangent[tick_index].astype(jnp.float32)
        else:
            top_grad = jnp.zeros((tok_rows, width), jnp.float32)
        grad_out = jnp.where(last_section, top_grad, sent_back.astype(jnp.float32))
        (
            gain_one,
            bias_one,
            w_mixed,
            bias_query,
            bias_value,
            w_output,
            bias_output,
            gain_two,
            bias_two,
            w_hidden,
            bias_hidden,
            w_back,
            bias_back,
        ) = params
        (
            backward_layer_in,
            normed,
            queries,
            key_rows,
            value_rows,
            log_total,
            backward_allowed,
            attended,
            residual,
            normed_two,
            pre_act,
            activated,
        ) = kept
        grad_back = grad_out.astype(jnp.bfloat16)
        d_w_back = jnp.einsum("cf,cd->fd", activated, grad_back, preferred_element_type=jnp.float32)
        d_bias_back = jnp.sum(grad_back.astype(jnp.float32), axis=0)
        d_activated = jnp.einsum("cd,fd->cf", grad_back, w_back, preferred_element_type=jnp.float32)
        gelu_pull = jax.vjp(gelu_tanh, pre_act)[1]
        d_pre = gelu_pull(d_activated)[0].astype(jnp.bfloat16)
        d_w_hidden = jnp.einsum("cm,cf->mf", normed_two, d_pre, preferred_element_type=jnp.float32)
        d_bias_hidden = jnp.sum(d_pre.astype(jnp.float32), axis=0)
        d_normed_two = jnp.einsum("cf,mf->cm", d_pre, w_hidden, preferred_element_type=jnp.float32)
        norm_pull_two = jax.vjp(
            layer_norm, residual, gain_two.astype(jnp.float32), bias_two.astype(jnp.float32)
        )[1]
        d_resid_part, d_gain_two, d_bias_two = norm_pull_two(d_normed_two)
        d_residual = grad_out + d_resid_part
        grad_attn = d_residual.astype(jnp.bfloat16)
        d_w_output = jnp.einsum(
            "cm,cd->md", attended, grad_attn, preferred_element_type=jnp.float32
        )
        d_bias_output = jnp.sum(grad_attn.astype(jnp.float32), axis=0)
        d_attended = jnp.einsum(
            "cd,md->cm", grad_attn, w_output, preferred_element_type=jnp.float32
        ).astype(jnp.bfloat16)
        d_head = lax.all_to_all(d_attended, "seq", split_axis=1, concat_axis=0, tiled=True)

        def grad_block(carry, operands):
            key_acc, value_acc = carry
            query_block, head_grad_block, allowed_block, log_block = operands
            scores = masked_scores(query_block, key_rows, allowed_block)
            attn_probs = jnp.exp(scores - log_block)
            d_weights = jnp.einsum(
                "qhd,khd->hqk",
                split_heads(head_grad_block),
                split_heads(value_rows),
                preferred_element_type=jnp.float32,
            )
            row_dot = jnp.sum(attn_probs * d_weights, axis=-1, keepdims=True)
            d_scores = (attn_probs * (d_weights - row_dot) * score_scale).astype(jnp.bfloat16)
            d_query_block = (
                jnp.einsum(
                    "hqk,khd->qhd",
                    d_scores,
                    split_heads(key_rows),
                    preferred_element_type=jnp.float32,
                )
                .reshape(query_block.shape)
                .astype(jnp.bfloat16)
            )
            key_acc = key_acc + jnp.einsum(
                "hqk,qhd->khd",
                d_scores,
                split_heads(query_block),
                preferred_element_type=jnp.float32,
            ).reshape(key_rows.shape)
            value_acc = value_acc + jnp.einsum(
                "hqk,qhd->khd",
                attn_probs.astype(jnp.bfloat16),
                split_heads(head_grad_block),
                preferred_element_type=jnp.float32,
            ).reshape(value_rows.shape)
            return ((key_acc, value_acc), d_query_block)

        empty_terms = (
            jnp.zeros(key_rows.shape, jnp.float32),
            jnp.zeros(value_rows.shape, jnp.float32),
        )
        (key_term, value_term), query_blocks = lax.scan(
            grad_block,
            empty_terms,
            (
                block_rows(queries, block_len),
                block_rows(d_head, block_len),
                block_rows(backward_allowed, block_len),
                log_total,
            ),
        )
        d_query = query_blocks.reshape(queries.shape)
        d_key = lax.psum_scatter(key_term, "fsdp", scatter_dimension=0, tiled=True)
        d_value = lax.psum_scatter(value_term, "fsdp", scatter_dimension=0, tiled=True)
        d_heads = jnp.stack(
            [d_query, d_key.astype(jnp.bfloat16), d_value.astype(jnp.bfloat16)], axis=1
        )
        d_mixed = lax.all_to_all(d_heads, "seq", split_axis=0, concat_axis=2, tiled=True)
        d_flat = d_mixed.reshape(tok_rows, 3 * width)
        d_w_mixed = jnp.einsum("cm,cn->mn", normed, d_flat, preferred_element_type=jnp.float32)
        d_bias_query = jnp.sum(d_mixed[:, 0].astype(jnp.float32), axis=0)
        d_bias_value = jnp.sum(d_mixed[:, 2].astype(jnp.float32), axis=0)
        d_normed = jnp.einsum("cn,mn->cm", d_flat, w_mixed, preferred_element_type=jnp.float32)
        norm_pull_one = jax.vjp(
            layer_norm,
            backward_layer_in,
            gain_one.astype(jnp.float32),
            bias_one.astype(jnp.float32),
        )[1]
        d_in_part, d_gain_one, d_bias_one = norm_pull_one(d_normed)
        d_in = d_residual + d_in_part
        d_in, local_grads = (
            d_in,
            (
                d_gain_one,
                d_bias_one,
                d_w_mixed,
                d_bias_query,
                d_bias_value,
                d_w_output,
                d_bias_output,
                d_gain_two,
                d_bias_two,
                d_w_hidden,
                d_bias_hidden,
                d_w_back,
                d_bias_back,
            ),
        )
        input_grads.append(d_in)
        shared = (
            lax.psum_scatter(local_grads[0], ("seq", "fsdp"), scatter_dimension=0, tiled=True),
            lax.psum_scatter(local_grads[1], ("seq", "fsdp"), scatter_dimension=0, tiled=True),
            lax.psum_scatter(local_grads[2], ("seq", "fsdp"), scatter_dimension=0, tiled=True),
            lax.psum_scatter(local_grads[3], ("seq", "fsdp"), scatter_dimension=0, tiled=True),
            lax.psum_scatter(local_grads[4], ("seq", "fsdp"), scatter_dimension=0, tiled=True),
            lax.psum_scatter(local_grads[5], ("seq", "fsdp"), scatter_dimension=0, tiled=True),
            lax.psum_scatter(local_grads[6], ("seq", "fsdp"), scatter_dimension=0, tiled=True),
            lax.psum_scatter(local_grads[7], ("seq", "fsdp"), scatter_dimension=0, tiled=True),
            lax.psum_scatter(local_grads[8], ("seq", "fsdp"), scatter_dimension=0, tiled=True),
            lax.psum_scatter(local_grads[9], ("seq", "fsdp"), scatter_dimension=0, tiled=True),
            lax.psum_scatter(local_grads[10], ("seq", "fsdp"), scatter_dimension=0, tiled=True),
            lax.psum_scatter(local_grads[11], ("seq", "fsdp"), scatter_dimension=0, tiled=True),
            lax.psum_scatter(local_grads[12], ("seq", "fsdp"), scatter_dimension=0, tiled=True),
        )
        totals = shared if totals is None else jax.tree.map(jnp.add, totals, shared)
        if tick_index < micro:
            sent_back = shifted(d_in.astype(jnp.bfloat16), "section", -1)
    section_tops = jnp.stack(layer_outs[1:])
    bottom_grads = jnp.stack(input_grads[1:])
    relay_ends = jnp.where(last_section, section_tops, bottom_grads)[None]
    return (relay_ends,) + tuple((grad_part[None] for grad_part in totals))


BF = jnp.bfloat16
F32 = jnp.float32
GROUP = 4
SECTION, SEQ, FSDP = "section", "seq", "fsdp"


def nt(left, right):
    return lax.dot_general(left, right, (((1,), (1,)), ((), ())), preferred_element_type=F32)


def tn(left, right):
    return lax.dot_general(left, right, (((0,), (0,)), ((), ())), preferred_element_type=F32)


def nn(left, right):
    return jnp.dot(left, right, preferred_element_type=F32)


def spot(start, size):
    return pl.ds(pl.multiple_of(start, size), size)


def call(kernel, ids, args, outs, scratch, anywhere, mib):
    places = [pltpu.HBM if i in anywhere else pltpu.VMEM for i in range(len(args))]
    args = [
        pltpu.with_memory_space_constraint(a, pltpu.HBM) if i in anywhere else a
        for i, a in enumerate(args)
    ]
    return pl.pallas_call(
        kernel,
        name=kernel.__name__.removesuffix("_kernel"),
        out_shape=[jax.ShapeDtypeStruct(shape, dtype) for shape, dtype in outs],
        in_specs=[pl.BlockSpec(memory_space=pltpu.SMEM)]
        + [pl.BlockSpec(memory_space=place) for place in places],
        out_specs=[pl.BlockSpec(memory_space=pltpu.VMEM)] * len(outs),
        scratch_shapes=list(scratch),
        compiler_params=pltpu.CompilerParams(vmem_limit_bytes=mib * 1024 * 1024),
        cost_estimate=pl.CostEstimate(flops=0, bytes_accessed=0, transcendentals=0),
    )(ids, *args)


def after(value, *earlier):
    return lax.optimization_barrier((value, earlier))[0]


def exchange(block, axis, d):
    return lax.ppermute(block, axis, [(i, i ^ d) for i in range(GROUP)])


def trade(blocks, axis):
    return [blocks[0]] + [exchange(blocks[d], axis, d) for d in range(1, GROUP)]


def far_first(blocks):
    return blocks[:1] + blocks[:0:-1]


def gather(block, axis):
    return trade([block] * GROUP, axis)


def swap(block):
    return lax.ppermute(block, SECTION, [(0, 1), (1, 0)])


def normed_rows(values, gain_vec, bias_vec):
    average = jnp.mean(values, axis=-1, keepdims=True)
    centred = values - average
    variance = jnp.mean(centred * centred, axis=-1, keepdims=True)
    return centred * lax.rsqrt(variance + EPSILON) * gain_vec + bias_vec


def norm_pull(values, gain_vec, grad):
    average = jnp.mean(values, axis=-1, keepdims=True)
    centred = values - average
    variance = jnp.mean(centred * centred, axis=-1, keepdims=True)
    inverse = lax.rsqrt(variance + EPSILON)
    unit = centred * inverse
    scaled = grad * gain_vec
    first = jnp.mean(scaled, axis=-1, keepdims=True)
    second = jnp.mean(scaled * unit, axis=-1, keepdims=True)
    pulled = inverse * (scaled - first - unit * second)
    return (
        pulled,
        jnp.sum(grad * unit, axis=0, keepdims=True),
        jnp.sum(grad, axis=0, keepdims=True),
    )


def pick_kernel(ids, w_ref, out_ref, *refs):
    vector_refs, fc_bias_ref, x_ref, g_ref, fc_ref, proj_ref = refs[:8], *refs[8:13]
    mine_ref, send_ref, feed_mine_ref, feed_send_ref, x_out, g_out = refs[13:19]
    held, rows_held, lines, fc_line, sem = refs[19:]
    s, c = ids[0], ids[2]
    width = w_ref.shape[2] // 3
    sources = [w_ref.at[0, spot(s * 64, 64), :]]
    targets = [held]
    for k in range(GROUP):
        sources.append(out_ref.at[0, pl.ds(pl.multiple_of(k * 64 + s * 16, 16), 16), :])
        targets.append(rows_held.at[k])
    for i, ref in enumerate(vector_refs):
        sources.append(ref)
        targets.append(lines.at[i])
    sources += [fc_bias_ref, x_ref.at[c], g_ref.at[c]]
    targets += [fc_line, x_out, g_out]
    first = len(sources)
    for ref, half in ((feed_send_ref, 1 - c), (feed_mine_ref, c)):
        for k in range(GROUP):
            for j in range(GROUP):
                lanes = spot(j * 1024 + k * 256 + half * 128, 128)
                sources.append(fc_ref.at[0, spot(s * 64, 64), lanes])
                targets.append(ref.at[k, 0:64, j * 128 : (j + 1) * 128])
            rows = spot(k * 256 + half * 128 + s * 32, 32)
            sources += [proj_ref.at[0, rows, 0:512], proj_ref.at[0, rows, 512:1024]]
            targets += [ref.at[k, 64:96, :], ref.at[k, 96:128, :]]
    copies = [
        pltpu.make_async_copy(source, target, sem.at[i])
        for i, (source, target) in enumerate(zip(sources, targets))
    ]
    for copy in copies:
        copy.start()
    for copy in copies[:first]:
        copy.wait()

    def head(t, j, k):
        tile = held[:, spot(t * width + j * 256 + (k >> 1) * 128, 128)].astype(F32)
        return tile[:, DH:] if k & 1 else tile[:, :DH]

    foot = [lines[i].astype(F32) for i in range(len(vector_refs))]
    foot += [fc_line[:, k * 256 : (k + 1) * 256].astype(F32) for k in range(GROUP)]
    foot.append(jnp.zeros((4, 256), F32))
    foot = jnp.concatenate(foot, axis=0).astype(BF)
    foot = jnp.concatenate([foot, jnp.zeros((16, 256), BF)], axis=1)
    for ref, half in ((mine_ref, c), (send_ref, 1 - c)):
        for k in range(GROUP):
            for i in range(2):
                j = 2 * half + i
                pair = jnp.concatenate([head(0, j, k), head(1, j, k)], axis=1)
                ref[k, 0:64, i * 128 : (i + 1) * 128] = pair.astype(BF)
            pair = jnp.concatenate([head(2, 2 * half, k), head(2, 2 * half + 1, k)], axis=1)
            ref[k, 0:64, 256:384] = pair.astype(BF)
            for q in range(GROUP):
                ref[k, q * 16 : (q + 1) * 16, 384:512] = rows_held[
                    k, :, spot(half * 512 + q * 128, 128)
                ]
            ref[k, 64:80, :] = foot
    for copy in copies[first:]:
        copy.wait()


def settle_heads_kernel(ids, mine_ref, got_ref, x_ref, *refs):
    first, z = ids[2] == 0, ids[1]
    for d in range(GROUP):
        mine, got = mine_ref[z ^ d], got_ref[z ^ d]
        lower, upper = jnp.where(first, mine, got), jnp.where(first, got, mine)
        refs[d][0:64, :] = lower[0:64]
        refs[d][64:80, 0:256] = lower[64:80, 0:256]
        refs[d][64:80, 256:512] = upper[64:80, 0:256]
        refs[d][80:144, :] = x_ref[:, 0:512]
        refs[d][144:208, :] = x_ref[:, 512:1024]
        refs[GROUP][d] = upper[0:64]


def settle_feed_kernel(ids, mine_ref, got_ref, heads_ref, seg_ref, g_ref, *refs):
    first, z = ids[2] == 0, ids[1]
    numbers = jnp.where(first, seg_ref[0:1, :], seg_ref[1:2, :]).astype(F32)
    marked = jnp.where(numbers > 0.0, numbers, -1.0)
    refs[8][...] = jnp.broadcast_to(marked, (128, numbers.shape[1])).T[:, 0:1]
    refs[9][...] = numbers
    for d in range(GROUP):
        mine, got = mine_ref[z ^ d], got_ref[z ^ d]
        refs[d][0:128, :] = jnp.where(first, mine, got)
        refs[d][128:192, :] = heads_ref[d]
        refs[GROUP + d][0:128, :] = jnp.where(first, got, mine)
        refs[GROUP + d][128:192, :] = g_ref[:, 0:512]
        refs[GROUP + d][192:256, :] = g_ref[:, 512:1024]


def first_heads_kernel(ids, *refs):
    z = ids[1]
    heads_ref, x_refs, vec_refs = refs[GROUP], refs[5:9], refs[9:11]
    for d in range(GROUP):
        block = refs[d][...]
        x_refs[d][:, 0:512] = block[80:144]
        x_refs[d][:, 512:1024] = block[144:208]
        heads_ref[z ^ d] = block[0:64]
        lanes = spot((z ^ d) * 256, 256)
        for layer in range(2):
            rows = block[64:80, layer * 256 : (layer + 1) * 256].astype(F32)
            row = rows[8:9, :]
            for k in range(1, GROUP):
                row = jnp.where(z == k, rows[8 + k : 9 + k, :], row)
            vec_refs[layer][0:8, lanes] = rows[0:8, :]
            vec_refs[layer][8:9, lanes] = row


def part_kernel(ids, *refs):
    for d in range(GROUP):
        refs[GROUP][ids[1] ^ d] = refs[d][0:128, :]
        refs[GROUP + 1][ids[1] ^ d] = refs[d][128:192, :]


def turn_part_kernel(ids, *refs):
    for d in range(GROUP):
        refs[GROUP][ids[1] ^ d] = refs[d][0:128, :]
        refs[GROUP + 1 + d][:, 0:512] = refs[d][128:192, :]
        refs[GROUP + 1 + d][:, 512:1024] = refs[d][192:256, :]


def place_kernel(axis, ids, *refs):
    for d in range(GROUP):
        refs[GROUP][ids[axis] ^ d] = refs[d][...]


def mixed_piece(ref, level):
    return jnp.concatenate([ref[k, level, :, 0:384] for k in range(GROUP)], axis=0)


def head_rows(ref, s):
    rows = []
    for d in range(GROUP):
        for k in range(GROUP):
            tiles = [ref[k, s ^ d, q * 16 : (q + 1) * 16, 384:512] for q in range(GROUP)]
            rows.append(jnp.concatenate(tiles, axis=1))
    return jnp.concatenate(rows, axis=0)


def hidden_piece(ref, level):
    return jnp.concatenate([ref[k, level, 0:64, :] for k in range(GROUP)], axis=0)


def back_share(ref):
    rows = []
    for j in range(GROUP):
        for k in range(GROUP):
            rows.append(jnp.concatenate([ref[k, j, 64:96, :], ref[k, j, 96:128, :]], axis=1))
    return jnp.concatenate(rows, axis=0)


def mixed_kernel(ids, *refs):
    x_refs, own_ref, oth_ref, vec = refs[:4], refs[4], refs[5], refs[6]
    out_refs, nf_ref, packed = refs[7:11], refs[11], refs[12]
    s, z, c = ids[0], ids[1], ids[2]
    gain_vec, bias_vec = vec[0:1, :], vec[1:2, :]
    for d in range(GROUP):
        nf_ref[d * 64 : (d + 1) * 64, :] = normed_rows(
            x_refs[d][...].astype(F32), gain_vec, bias_vec
        ).astype(BF)

    def bias_of(row, j):
        tile = vec[row : row + 1, spot(j * 256 + (z >> 1) * 128, 128)]
        return jnp.where((z & 1) == 1, tile[:, DH:], tile[:, :DH])

    empty = jnp.zeros((1, DH), F32)
    for ref, half in ((own_ref, c), (oth_ref, 1 - c)):
        total = jnp.zeros((GROUP * 64, 384), F32)
        for k in range(GROUP):
            total = total + nn(nf_ref[:, k * 256 : (k + 1) * 256], mixed_piece(ref, k))
        j = 2 * half
        row = jnp.concatenate(
            [
                bias_of(2, j),
                empty,
                bias_of(2, j + 1),
                empty,
                bias_of(3, j),
                bias_of(3, j + 1),
            ],
            axis=1,
        )
        total = total + row
        for i in range(2):
            packed[j + i, 0:256, :] = total[:, i * 128 : (i + 1) * 128].astype(BF)
            values = total[:, 256 + i * DH : 256 + (i + 1) * DH]
            packed[j + i, 256:384, :] = jnp.concatenate(
                [values[:128], values[128:]], axis=1
            ).astype(BF)
    for d in range(GROUP):
        out_refs[d][...] = packed[s ^ d]


def spread(ids, pieces, qk_ref, v_ref):
    s, z = ids[0], ids[1]
    for d in range(GROUP):
        for e in range(GROUP):
            rows = spot(((s ^ d) * GROUP + (z ^ e)) * 64, 64)
            qk_ref[rows, :] = pieces[d][e * 64 : (e + 1) * 64, :]
            lanes = slice(0, DH) if e < 2 else slice(DH, 128)
            start = 256 + (e & 1) * 64
            v_ref[rows, :] = pieces[d][start : start + 64, lanes]


def block_scores(qk_ref, seg_col, seg_row, start, size):
    stop = start + size
    queries = qk_ref[start:stop, 0:DH] * jnp.asarray(DH ** (-0.5), BF)
    scores = nt(queries, qk_ref[0:stop, DH:128])
    same = seg_col[start:stop, :] == seg_row[:, 0:stop]
    q_place = lax.broadcasted_iota(jnp.int32, (size, size), 0)
    k_place = lax.broadcasted_iota(jnp.int32, (size, size), 1)
    near = ((k_place <= q_place) & same[:, start:stop]) | (k_place == q_place)
    near = jnp.where(near, scores[:, start:stop], NEGATIVE)
    if start == 0:
        return near
    return jnp.concatenate([jnp.where(same[:, :start], scores[:, :start], NEGATIVE), near], axis=1)


def attend_kernel(ids, *refs):
    pieces, seg_col, seg_row = refs[:4], refs[4], refs[5]
    out_refs, qk_ref, v_ref, probs_ref, o_ref = refs[6:10], *refs[10:14]
    s, z = ids[0], ids[1]
    spread(ids, pieces, qk_ref, v_ref)
    count = qk_ref.shape[0]
    size = 256
    for start in range(0, count, size):
        scores = block_scores(qk_ref, seg_col, seg_row, start, size)
        top = jnp.max(scores, axis=-1, keepdims=True)
        grown = jnp.exp(scores - top)
        total = jnp.sum(grown, axis=-1, keepdims=True)
        probs = grown * (1.0 / total)
        probs_ref[start : start + size, 0 : start + size] = probs
        o_ref[start : start + size, :] = nn(
            probs.astype(BF), v_ref[0 : start + size, :]
        ).astype(BF)
    for d in range(GROUP):
        for e in range(2):
            left = o_ref[spot(((s ^ d) * GROUP + (z ^ e)) * 64, 64), :]
            right = o_ref[spot(((s ^ d) * GROUP + (z ^ (e + 2))) * 64, 64), :]
            out_refs[d][e * 64 : (e + 1) * 64, :] = jnp.concatenate([left, right], axis=1)


def unpacked(piece):
    return jnp.concatenate([piece[:, :DH], piece[:, DH:]], axis=0)


def output_kernel(ids, *refs):
    pieces, own_ref, oth_ref = refs[:4], refs[4], refs[5]
    out_refs, att_ref = refs[6:10], refs[10]
    s, c = ids[0], ids[2]
    att = jnp.concatenate([unpacked(pieces[d][...]) for d in range(GROUP)], axis=1)
    att_ref[...] = att
    for w_ref, half in ((own_ref, c), (oth_ref, 1 - c)):
        part = nn(att, head_rows(w_ref, s)).astype(BF)
        for d in range(GROUP):
            out_refs[d][:, spot(half * 512, 512)] = part[d * 64 : (d + 1) * 64, :]


def summed(refs):
    blocks = []
    for ref in refs:
        blocks += [ref[...]] if len(ref.shape) == 2 else [ref[k] for k in range(GROUP)]
    total = blocks[0].astype(F32)
    for block in blocks[1:]:
        total = total + block.astype(F32)
    return total


def residual_kernel(ids, *refs):
    x_ref, vec = refs[4], refs[5]
    res_ref, n_ref = refs[6], refs[7]
    res = x_ref[...].astype(F32) + summed(refs[:4]) + vec[4:5, :]
    res_ref[...] = res
    n_ref[...] = normed_rows(res, vec[5:6, :], vec[6:7, :]).astype(BF)


ROOT = math.sqrt(2.0 / math.pi)


def hidden_bias(vec, half):
    return jnp.concatenate(
        [vec[8:9, spot(j * 256 + half * 128, 128)] for j in range(GROUP)], axis=1
    )


def feed_forward(n_refs, shares, vec, c, nf_ref, keep):
    for d in range(GROUP):
        nf_ref[d * 64 : (d + 1) * 64, :] = n_refs[d][...]
    part = jnp.zeros(nf_ref.shape, F32)
    for place, half in ((0, c), (1, 1 - c)):
        cols = slice(place * 512, (place + 1) * 512)
        pre = jnp.zeros((GROUP * 64, 512), F32)
        for d in range(GROUP):
            pre = pre + nn(nf_ref[:, d * 256 : (d + 1) * 256], hidden_piece(shares[place], d))
        pre = pre + hidden_bias(vec, half)
        square = pre * pre
        bend = jnp.tanh(ROOT * pre * (1.0 + 0.044715 * square))
        act = (0.5 * pre * (1.0 + bend)).astype(BF)
        slope = 0.5 * (1.0 + bend) + (0.5 * ROOT) * pre * (1.0 - bend * bend) * (
            1.0 + (3.0 * 0.044715) * square
        )
        keep(cols, act, slope)
        part = part + nn(act, back_share(shares[place]))
    return part.astype(BF)


def feed_backward(g_blocks, shares, slope_ref, out_refs, d_pre_ref, gf_ref):
    for d in range(GROUP):
        gf_ref[d * 64 : (d + 1) * 64, :] = g_blocks[d]
    for place in range(2):
        cols = slice(place * 512, (place + 1) * 512)
        d_act = nt(gf_ref[...], back_share(shares[place]))
        d_pre_ref[:, cols] = (d_act * slope_ref[:, cols]).astype(BF)
    for d in range(GROUP):
        part = nt(d_pre_ref[:, 0:512], hidden_piece(shares[0], d))
        part = (part + nt(d_pre_ref[:, 512:1024], hidden_piece(shares[1], d))).astype(BF)
        for e in range(GROUP):
            out_refs[e][:, d * 256 : (d + 1) * 256] = part[e * 64 : (e + 1) * 64, :]


def feed_kernel(ids, *refs):
    slope_ref, act_ref, nf_ref = refs[11:14]

    def keep(cols, act, slope):
        act_ref[:, cols] = act
        slope_ref[:, cols] = slope

    part = feed_forward(refs[:4], refs[4:6], refs[6], ids[2], nf_ref, keep)
    for d in range(GROUP):
        refs[7 + d][...] = part[d * 64 : (d + 1) * 64, :]


def feed_back_kernel(ids, *refs):
    blocks = [ref[...] for ref in refs[:4]]
    feed_backward(blocks, refs[4:6], refs[6], refs[7:11], refs[11], refs[12])


def feed_turn_kernel(ids, *refs):
    shares, vec, top_refs, outs = refs[8:10], refs[10], refs[11:15], refs[15:19]
    act_ref, nf_ref, d_pre_ref, gf_ref, slope_ref = refs[19:24]

    def keep(cols, act, slope):
        act_ref[:, cols] = act
        slope_ref[:, cols] = slope

    part = feed_forward(refs[:4], shares, vec, ids[2], nf_ref, keep)
    for d in range(GROUP):
        top_refs[d][...] = part[d * 64 : (d + 1) * 64, :]
    blocks = [ref[...] for ref in refs[4:8]]
    feed_backward(blocks, shares, slope_ref, outs, d_pre_ref, gf_ref)


def close_kernel(ids, *refs):
    res_ref, vec, out_ref = refs[4:]
    out = res_ref[...] + summed(refs[:4]) + vec[7:8, :]
    out_ref[...] = out.astype(out_ref.dtype)


def norm_two_back_kernel(ids, *refs):
    res_ref, g_ref, vec = refs[4], refs[5], refs[6]
    d_res_ref, ga_ref, rows_ref = refs[7:10]
    grad = g_ref[...].astype(F32)
    pulled, d_gain, d_bias = norm_pull(res_ref[...], vec[5:6, :], summed(refs[:4]))
    d_res = grad + pulled
    low = d_res.astype(BF)
    d_res_ref[...] = d_res
    ga_ref[...] = low
    rows_ref[0:1, :] = jnp.sum(low.astype(F32), axis=0, keepdims=True)
    rows_ref[1:2, :] = d_gain
    rows_ref[2:3, :] = d_bias
    rows_ref[3:4, :] = jnp.sum(grad.astype(BF).astype(F32), axis=0, keepdims=True)
    rows_ref[4:8, :] = jnp.zeros((4, grad.shape[1]), F32)


def output_back_kernel(ids, *refs):
    g_refs, own_ref, oth_ref = refs[:4], refs[4], refs[5]
    out_refs, gf_ref = refs[6:10], refs[10]
    s, c = ids[0], ids[2]
    for d in range(GROUP):
        gf_ref[d * 64 : (d + 1) * 64, :] = g_refs[d][...]
    d_att = nt(gf_ref[:, spot(c * 512, 512)], head_rows(own_ref, s))
    d_att = d_att + nt(gf_ref[:, spot((1 - c) * 512, 512)], head_rows(oth_ref, s))
    for d in range(GROUP):
        cols = d_att[:, d * DH : (d + 1) * DH]
        out_refs[d][...] = jnp.concatenate([cols[:128], cols[128:]], axis=1).astype(BF)


def feed_grads_kernel(ids, *refs):
    act_ref, gb_ref, nf_ref, d_pre_ref = refs[:4]
    keep_ref, send_ref, sums_ref = refs[4:7]
    for place, out_ref in ((0, keep_ref), (1, send_ref)):
        cols = slice(place * 512, (place + 1) * 512)
        d_fc = tn(nf_ref[...], d_pre_ref[:, cols]).astype(BF)
        for k in range(GROUP):
            out_ref[k, 0:256, :] = d_fc[k * 256 : (k + 1) * 256, :]
        d_proj = tn(act_ref[:, cols], gb_ref[...]).astype(BF)
        for j in range(GROUP):
            rows = d_proj[j * 128 : (j + 1) * 128, :]
            out_ref[j, 256:384, :] = rows[:, 0:512]
            out_ref[j, 384:512, :] = rows[:, 512:1024]
    sums_ref[...] = jnp.sum(d_pre_ref[...].astype(F32), axis=0, keepdims=True)


def attend_back_kernel(ids, *refs):
    d_pieces, qk_ref, v_ref, probs_ref, out_refs = refs[0:4], *refs[4:7], refs[7:11]
    do_ref, dq_ref, dk_ref, dv_ref = refs[11:15]
    s, z = ids[0], ids[1]
    for d in range(GROUP):
        for e in range(GROUP):
            rows = spot(((s ^ d) * GROUP + (z ^ e)) * 64, 64)
            lanes = slice(0, DH) if e < 2 else slice(DH, 128)
            start = (e & 1) * 64
            do_ref[rows, :] = d_pieces[d][start : start + 64, lanes]
    count = qk_ref.shape[0]
    size = 256
    for start in range(0, count, size):
        stop = start + size
        probs = probs_ref[start:stop, 0:stop]
        d_out = do_ref[start:stop, :]
        d_weights = nt(d_out, v_ref[0:stop, :])
        row_dot = jnp.sum(probs * d_weights, axis=-1, keepdims=True)
        d_scores = (probs * (d_weights - row_dot) * DH ** (-0.5)).astype(BF)
        dq_ref[start:stop, :] = nn(d_scores, qk_ref[0:stop, DH:128])
        dk = tn(d_scores, qk_ref[start:stop, 0:DH])
        dv = tn(probs.astype(BF), d_out)
        if start:
            dk_ref[0:start, :] += dk[0:start]
            dv_ref[0:start, :] += dv[0:start]
        dk_ref[start:stop, :] = dk[start:stop]
        dv_ref[start:stop, :] = dv[start:stop]
    for d in range(GROUP):
        for e in range(GROUP):
            rows = spot(((s ^ d) * GROUP + (z ^ e)) * 64, 64)
            out_refs[d][e * 64 : (e + 1) * 64, :] = jnp.concatenate(
                [dq_ref[rows, :], dk_ref[rows, :]], axis=1
            ).astype(BF)
        for e in range(2):
            left = dv_ref[spot(((s ^ d) * GROUP + (z ^ e)) * 64, 64), :]
            right = dv_ref[spot(((s ^ d) * GROUP + (z ^ (e + 2))) * 64, 64), :]
            out_refs[d][256 + e * 64 : 320 + e * 64, :] = jnp.concatenate(
                [left, right], axis=1
            ).astype(BF)


def mixed_back_kernel(ids, *refs):
    pieces, own_ref, oth_ref = refs[:4], refs[4], refs[5]
    out_refs, dm_ref, held = refs[6:10], refs[10], refs[11]
    s, c = ids[0], ids[2]
    for d in range(GROUP):
        held[d] = pieces[d][...]
    for place, half in ((0, c), (1, 1 - c)):
        base = place * 384
        values = []
        for i in range(2):
            d = (2 * half + i) ^ s
            dm_ref[:, base + i * 128 : base + (i + 1) * 128] = held[d, 0:256, :]
            values.append(unpacked(held[d, 256:384, :]))
        dm_ref[:, base + 256 : base + 384] = jnp.concatenate(values, axis=1)
    for k in range(GROUP):
        part = nt(dm_ref[:, 0:384], mixed_piece(own_ref, k))
        part = (part + nt(dm_ref[:, 384:768], mixed_piece(oth_ref, k))).astype(BF)
        for d in range(GROUP):
            out_refs[d][:, k * 256 : (k + 1) * 256] = part[d * 64 : (d + 1) * 64, :]


def attend_grads_kernel(ids, *refs):
    nf_ref, dm_ref, att_ref, ga_ref, two_ref, fc_ref = refs[:6]
    part_refs, x_refs = refs[6:10], refs[10:14]
    keep_ref, send_ref, lines = refs[14:17]
    s, c = ids[0], ids[2]
    d_gain = d_bias = 0.0
    for d in range(GROUP):
        grad = part_refs[d][...].astype(F32)
        values = x_refs[d][...].astype(F32)
        average = jnp.mean(values, axis=-1, keepdims=True)
        centred = values - average
        variance = jnp.mean(centred * centred, axis=-1, keepdims=True)
        unit = centred * lax.rsqrt(variance + EPSILON)
        d_gain = d_gain + jnp.sum(grad * unit, axis=0, keepdims=True)
        d_bias = d_bias + jnp.sum(grad, axis=0, keepdims=True)
    lines[0:1, :] = d_gain
    lines[1:2, :] = d_bias
    lines[2:6, :] = two_ref[0:4, :]
    lines[6:8, :] = jnp.zeros((2, d_gain.shape[1]), F32)
    for place, out_ref, half in ((0, keep_ref, c), (1, send_ref, 1 - c)):
        base = place * 384
        d_w = tn(nf_ref[...], dm_ref[:, base : base + 384]).astype(BF)
        sums = jnp.sum(dm_ref[:, base : base + 384].astype(F32), axis=0, keepdims=True)
        for k in range(GROUP):
            out_ref[k, 0:256, 0:384] = d_w[k * 256 : (k + 1) * 256, :]
            mine = (k >> 1) == half
            i = k & 1
            query = sums[:, i * 128 : i * 128 + DH]
            value = sums[:, 256 + i * DH : 256 + (i + 1) * DH]
            first = place * 512 + k * 128
            line = jnp.concatenate(
                [
                    fc_ref[:, first : first + 128],
                    jnp.where(mine, query, 0.0),
                    jnp.where(mine, value, 0.0),
                    jnp.zeros((1, 128), F32),
                ],
                axis=1,
            )
            foot = jnp.concatenate([line, jnp.zeros((7, 384), F32)], axis=0)
            foot = jnp.concatenate([lines[:, spot(k * 256 + half * 128, 128)], foot], axis=1)
            foot = jnp.concatenate([foot, jnp.zeros((8, 512), F32)], axis=0)
            out_ref[k, 256:272, :] = foot.astype(BF)
        d_out = tn(att_ref[...], ga_ref[:, spot(half * 512, 512)]).astype(BF)
        for d in range(GROUP):
            for q in range(GROUP):
                out_ref[s ^ d, q * 64 : (q + 1) * 64, 384:512] = d_out[
                    d * 64 : (d + 1) * 64, q * 128 : (q + 1) * 128
                ]


def norm_one_back_kernel(ids, *refs):
    x_ref, d_res_ref, vec = refs[4], refs[5], refs[6]
    pulled, _, _ = norm_pull(x_ref[...].astype(F32), vec[0:1, :], summed(refs[:4]))
    refs[7][...] = (d_res_ref[...] + pulled).astype(BF)


def ends_kernel(ids, *refs):
    x_ref, d_res_ref, vec, top_ref = refs[4:8]
    pulled, _, _ = norm_pull(x_ref[...].astype(F32), vec[0:1, :], summed(refs[:4]))
    bottom, top = d_res_ref[...] + pulled, top_ref[...]
    first = ids[2] == 0
    refs[8][...] = jnp.where(first, bottom, top)
    refs[9][...] = jnp.where(first, top, bottom)


def add_kernel(ids, left_ref, right_ref, *out_refs):
    for d in range(GROUP):
        k = ids[0] ^ d
        out_refs[d][...] = (left_ref[k].astype(F32) + right_ref[k].astype(F32)).astype(BF)


def choose_kernel(ids, *refs):
    lower, upper = summed(refs[:4]).astype(BF), summed(refs[4:8]).astype(BF)
    first = ids[2] == 0
    refs[8][...] = jnp.where(first, lower, upper)
    refs[9][...] = jnp.where(first, upper, lower)


def split_feed_kernel(ids, own_ref, oth_ref, *refs):
    back_out = refs[GROUP]
    for d in range(GROUP):
        rows = spot((ids[1] ^ d) * 64, 64)
        refs[d][:, 0:512] = own_ref[rows, :]
        refs[d][:, 512:1024] = oth_ref[rows, :]
    for ref, half in ((own_ref, ids[2]), (oth_ref, 1 - ids[2])):
        rows = spot(half * 128, 128)
        back_out[0, rows, 0:512] = ref[256:384, :].astype(F32)
        back_out[0, rows, 512:1024] = ref[384:512, :].astype(F32)


def split_attend_kernel(ids, own_ref, oth_ref, *refs):
    out_ref, bfc_ref, query_ref, value_ref = refs[GROUP:]
    s, z, c = ids[0], ids[1], ids[2]
    foots = (own_ref[256:272, :], oth_ref[256:272, :])
    for d in range(GROUP):
        rows = spot((z ^ d) * 64, 64)
        refs[d][0:64, 0:384] = own_ref[rows, 0:384]
        refs[d][0:64, 384:768] = oth_ref[rows, 0:384]
        lines = jnp.where(((z ^ d) >> 1) == c, foots[0][:, 0:128], foots[1][:, 0:128])
        refs[d][64:80, :] = jnp.concatenate([lines, jnp.zeros((16, 640), BF)], axis=1)
    for ref, half in ((own_ref, c), (oth_ref, 1 - c)):
        for q in range(GROUP):
            out_ref[0, :, spot(half * 512 + q * 128, 128)] = ref[
                q * 64 : (q + 1) * 64, 384:512
            ].astype(F32)
    own, oth = foots[0][0:1, :].astype(F32), foots[1][0:1, :].astype(F32)
    lower, upper = jnp.where(c == 0, own, oth), jnp.where(c == 0, oth, own)
    bfc_ref[:, 0:128] = lower[:, 128:256]
    bfc_ref[:, 128:256] = upper[:, 128:256]
    line = jnp.where((s >> 1) == 0, lower, upper)
    query_ref[...] = line[:, 256 : 256 + DH]
    value_ref[...] = line[:, 256 + DH : 384]


def final_feed_kernel(ids, *refs):
    mine_ref, got_ref, fc_out, relay_out = refs[GROUP:]
    first = ids[2] == 0
    mine, got = mine_ref[...], got_ref[...]
    relay_out[0, 0] = jnp.where(first, mine, got)
    relay_out[0, 1] = jnp.where(first, got, mine)
    for place, half in ((0, ids[2]), (1, 1 - ids[2])):
        for d in range(GROUP):
            for j in range(GROUP):
                start = place * 512 + j * 128
                lanes = spot(j * 1024 + (ids[1] ^ d) * 256 + half * 128, 128)
                fc_out[0, :, lanes] = refs[d][:, start : start + 128].astype(F32)


def final_attend_kernel(ids, *refs):
    mixed, mixed_out, line_outs, held = refs[:4], refs[4], refs[5:11], refs[11]
    z, c = ids[1], ids[2]
    width = mixed_out.shape[2] // 3
    lines = 0.0
    for d in range(GROUP):
        held[z ^ d] = mixed[d][0:64, :]
        lines = lines + mixed[d][64:80, 0:128].astype(F32)
    lines = jnp.where((z & 1) == 1, lines[:, DH:], lines[:, :DH])
    for i, ref in enumerate(line_outs):
        ref[...] = lines[i : i + 1, :]
    for place, half in ((0, c), (1, 1 - c)):
        base = place * 384
        for pair in range(2):
            for i in range(2):
                tiles = []
                for source in (2 * pair, 2 * pair + 1):
                    qk = held[source, :, base + i * 128 : base + (i + 1) * 128].astype(F32)
                    v = held[source, :, base + 256 + i * DH : base + 256 + (i + 1) * DH]
                    tiles.append((qk[:, :DH], qk[:, DH:], v.astype(F32)))
                for t in range(3):
                    start = t * width + (2 * half + i) * 256 + pair * 128
                    mixed_out[0, :, spot(start, 128)] = jnp.concatenate(
                        [tiles[0][t], tiles[1][t]], axis=1
                    )


def fast_body(
    inputs,
    cotangent,
    segment_ids,
    ln1_gain,
    ln1_bias,
    w_qkv,
    b_query,
    b_value,
    w_out,
    b_out,
    ln2_gain,
    ln2_bias,
    w_fc,
    b_fc,
    w_proj,
    b_proj,
):
    s, z, c = lax.axis_index(SEQ), lax.axis_index(FSDP), lax.axis_index("section")
    ids = jnp.stack([s, z, c]).astype(jnp.int32)
    tok, width = inputs.shape[1:]
    count = segment_ids.shape[1]
    tall = GROUP * tok
    piece = ((384, 128), BF)
    small = ((128, 128), BF)
    part = ((tok, width), BF)
    wide = ((tall, width), BF)
    line = ((tok, width), F32)
    share = ((272, 512), BF)
    feed_share = ((512, 512), BF)
    done, awaited, lagging = [], [], []

    def run(kernel, args, outs, *scratch, anywhere=(), mib=16, aside=False):
        args = list(args)
        earlier = done[-1:] + ([] if aside else list(awaited))
        if earlier:
            args[0] = after(args[0], *earlier)
        if not aside:
            awaited[:] = lagging
            lagging.clear()
        result = list(call(kernel, ids, args, outs, scratch, anywhere, mib))
        done.append(result[-1])
        return result

    def beside(blocks, got, axis, *which, lag=False):
        for d in which:
            got[d] = exchange(after(blocks[d], done[-1]), axis, d)
            (lagging if lag else awaited).append(got[d])

    def now(blocks):
        return [after(block, done[-1]) for block in blocks]

    def of(kernel, axis):
        def bound(*refs):
            kernel(axis, *refs)

        bound.__name__ = kernel.__name__
        return bound

    def shared(pieces, axis, shape, aside=False):
        (whole,) = run(of(place_kernel, axis), pieces, [(shape, BF)], aside=aside)
        return [whole, swap(whole)]

    mine, send, feed_mine, feed_send, x, grad = run(
        pick_kernel,
        [w_qkv, w_out]
        + [ln1_gain, ln1_bias, b_query, b_value, b_out, ln2_gain, ln2_bias, b_proj, b_fc]
        + [inputs, cotangent, w_fc, w_proj],
        [((GROUP, 80, 512), BF)] * 2 + [((GROUP, 128, 512), BF)] * 2 + [part] * 2,
        pltpu.VMEM((64, 3 * width), BF),
        pltpu.VMEM((GROUP, 16, width), BF),
        pltpu.VMEM((8, 1, 256), BF),
        pltpu.VMEM((1, 1024), BF),
        pltpu.SemaphoreType.DMA((64,)),
        anywhere=range(15),
    )
    *heads, upper_heads = run(
        settle_heads_kernel,
        [mine, swap(send), x],
        [((208, 512), BF)] * 4 + [((GROUP, 64, 512), BF)],
    )
    heads = trade(heads, FSDP)
    feed_got = swap(feed_send)
    *rest, seg_col, seg_row = run(
        settle_feed_kernel,
        [feed_mine, feed_got, upper_heads, segment_ids, grad],
        [((192, 512), BF)] * 4
        + [((256, 512), BF)] * 4
        + [((count, 1), F32), ((1, count), F32)],
        aside=True,
    )
    rests = [rest[:4], rest[4:]]
    rest_got = [list(blocks) for blocks in rests]
    heads, *rest = run(
        first_heads_kernel,
        heads,
        [((GROUP, 64, 512), BF)] + [part] * 4 + [((16, width), F32)] * 2,
    )
    x_all, vec = rest[:4], rest[4:]
    heads = gather(heads, SEQ)
    for blocks, got in zip(rests, rest_got):
        beside(blocks, got, FSDP, 1)
    head_w = [shared(heads, 0, (GROUP, GROUP, 64, 512)), None]

    feed_w = [None, None]
    kept = []
    for layer in range(2):
        *packed, normed = run(
            mixed_kernel,
            x_all + head_w[layer] + [vec[layer]],
            [piece] * 4 + [wide],
            pltpu.VMEM((GROUP, 384, 128), BF),
        )
        qkv = trade(packed, SEQ)
        got = rest_got[layer]
        beside(rests[layer], got, FSDP, 3, 2, lag=True)
        *heads, qk_rows, v_rows, probs = run(
            attend_kernel,
            qkv + [seg_col, seg_row],
            [small] * 4 + [((count, 128), BF), ((count, DH), BF), ((count, count), F32)],
            pltpu.VMEM((count, DH), BF),
        )
        heads = trade(heads, SEQ)
        *parts, att = run(
            output_kernel,
            heads + head_w[layer],
            [part] * 4 + [((tall, 256), BF)],
        )
        parts = trade(parts, FSDP)
        if layer == 0:
            feed, heads_later = run(
                part_kernel,
                got,
                [((GROUP, 128, 512), BF), ((GROUP, 64, 512), BF)],
                aside=True,
            )
        else:
            feed, *grad_all = run(
                turn_part_kernel, got, [((GROUP, 128, 512), BF)] + [part] * 4, aside=True
            )
        feeds = [feed] * GROUP
        beside(feeds, feeds, SEQ, 1, 2)
        res, n_two = run(
            residual_kernel, far_first(parts) + [x, vec[layer]], [line, part]
        )
        n_all = gather(n_two, FSDP)
        beside([feed] * GROUP, feeds, SEQ, 3)
        feeds[0] = after(feeds[0], *n_all)
        feed_w[layer] = shared(feeds, 0, (GROUP, GROUP, 128, 512))
        kept.append((x, normed, (qk_rows, v_rows, probs), att, res, x_all))
        if layer == 0:
            *parts, slope, act, n_full = run(
                feed_kernel,
                n_all + feed_w[0] + [vec[0]],
                [part] * 4 + [((tall, 1024), F32), ((tall, 1024), BF), wide],
            )
            parts = trade(parts, FSDP)
            heads = [heads_later] * GROUP
            beside(heads, heads, SEQ, 1, 2)
            (x,) = run(close_kernel, far_first(parts) + [res, vec[0]], [part])
            x_all = gather(x, FSDP)
            beside([heads_later] * GROUP, heads, SEQ, 3)
            heads[0] = after(heads[0], *x_all)
            head_w[1] = shared(heads, 0, (GROUP, GROUP, 64, 512))
        else:
            turn = run(
                feed_turn_kernel,
                n_all + grad_all + feed_w[1] + [vec[1]],
                [part] * 8 + [((tall, 1024), BF), wide, ((tall, 1024), BF), wide],
                pltpu.VMEM((tall, 1024), F32),
                mib=20,
            )

    def feed_terms(act, gb_full, n_full, d_pre):
        keep, send, sums = run(
            feed_grads_kernel,
            [act, gb_full, n_full, d_pre],
            [((GROUP, 512, 512), BF)] * 2 + [((1, 1024), F32)],
            aside=True,
        )
        return keep, swap(send), sums

    def attend_terms(layer, two_rows, fc_sums, parts, d_mixed, ga_full):
        x, normed, _, att, _, x_all = kept[layer]
        keep, send = run(
            attend_grads_kernel,
            [normed, d_mixed, att, ga_full, two_rows, fc_sums] + parts + x_all,
            [((GROUP,) + share[0], BF)] * 2,
            pltpu.VMEM((8, width), F32),
            aside=True,
        )
        return keep, swap(send)

    def total(keep, got, shape):
        return run(add_kernel, [keep, got], [shape] * 4, aside=True)

    def norm_two_back(layer, parts, grad):
        return run(
            norm_two_back_kernel,
            far_first(parts) + [kept[layer][4], grad, vec[layer]],
            [line, part, ((8, width), F32)],
        )

    def output_back(layer, ga_all):
        return run(
            output_back_kernel,
            ga_all + head_w[layer],
            [small] * 4 + [wide],
        )

    def attend_back(layer, d_heads):
        return run(
            attend_back_kernel,
            d_heads + list(kept[layer][2]),
            [piece] * 4,
            pltpu.VMEM((count, DH), BF),
            *[pltpu.VMEM((count, DH), F32)] * 3,
        )

    def mixed_back(layer, d_pieces):
        return run(
            mixed_back_kernel,
            d_pieces + head_w[layer],
            [part] * 4 + [((tall, 768), BF)],
            pltpu.VMEM((GROUP, 384, 128), BF),
        )

    def norm_one_back(layer, parts, d_res):
        return run(
            norm_one_back_kernel,
            far_first(parts) + [kept[layer][0], d_res, vec[layer]],
            [part],
        )[0]

    top_parts, parts = turn[:4], trade(turn[4:8], FSDP)
    tops = list(top_parts)
    beside(top_parts, tops, FSDP, 1)
    keep, got, fc_sums = feed_terms(turn[8], turn[11], turn[9], turn[10])
    terms = total(keep, got, feed_share)
    d_res, ga, two_rows = norm_two_back(1, parts, grad)
    ga_all = gather(ga, FSDP)
    upper_feed = list(terms)
    beside(terms, upper_feed, SEQ, 1, 2)
    *d_heads, ga_full = output_back(1, ga_all)
    d_heads = trade(d_heads, SEQ)
    beside(top_parts, tops, FSDP, 3, 2, lag=True)
    d_pieces = trade(attend_back(1, d_heads), SEQ)
    *sent, d_mixed = mixed_back(1, d_pieces)
    parts = trade(sent, FSDP)
    beside(terms, upper_feed, SEQ, 3)
    keep, got = attend_terms(1, two_rows, fc_sums, sent, d_mixed, ga_full)
    (top,) = run(close_kernel, tops + [kept[1][4], vec[1]], [line], aside=True)
    upper_terms = total(keep, got, share)
    low = norm_one_back(1, parts, d_res)
    g_all = gather(low, FSDP)
    upper_attend = list(upper_terms)
    beside(upper_terms, upper_attend, SEQ, 1, 2)

    *parts, d_pre, gb_full = run(
        feed_back_kernel,
        g_all + feed_w[0] + [slope],
        [part] * 4 + [((tall, 1024), BF), wide],
    )
    parts = trade(parts, FSDP)
    beside(upper_terms, upper_attend, SEQ, 3)
    keep, got, fc_sums = feed_terms(act, gb_full, n_full, d_pre)
    terms = total(keep, got, feed_share)
    d_res, ga, two_rows = norm_two_back(0, parts, low)
    ga_all = gather(ga, FSDP)
    lower_feed = list(terms)
    beside(terms, lower_feed, SEQ, 1, 2)
    *d_heads, ga_full = output_back(0, ga_all)
    d_heads = trade(d_heads, SEQ)
    beside(terms, lower_feed, SEQ, 3)
    d_pieces = trade(attend_back(0, d_heads), SEQ)
    mine, theirs = run(choose_kernel, lower_feed + upper_feed, [feed_share] * 2, aside=True)
    got = swap(theirs)
    *blocks, g_proj = run(
        split_feed_kernel,
        [mine, got],
        [((64, 1024), BF)] * 4 + [((1, 256, width), F32)],
        aside=True,
    )
    fc_parts = list(blocks)
    beside(blocks, fc_parts, FSDP, 3, 2)
    *sent, d_mixed = mixed_back(0, d_pieces)
    keep, got = attend_terms(0, two_rows, fc_sums, sent, d_mixed, ga_full)
    lower_attend = trade(total(keep, got, share), SEQ)

    parts = trade(now(sent), FSDP)
    lower_attend[0] = after(lower_attend[0], *parts)
    mine, theirs = run(choose_kernel, lower_attend + upper_attend, [share] * 2)
    got = swap(theirs)
    ends_mine, ends_theirs = run(
        ends_kernel, far_first(parts) + [kept[0][0], d_res, vec[0], top], [line] * 2
    )
    ends_got = swap(ends_theirs)
    *blocks, g_out, g_bfc, g_query, g_value = run(
        split_attend_kernel,
        [mine, got],
        [((80, 768), BF)] * 4
        + [((1, 64, width), F32), ((1, 256), F32), ((1, 64), F32), ((1, 64), F32)],
    )
    mixed_parts = trade(blocks, FSDP)
    fc_parts[1] = exchange(after(fc_parts[1], g_out), FSDP, 1)
    g_fc, relay = run(
        final_feed_kernel,
        fc_parts + [ends_mine, ends_got],
        [((1, 64, 4096), F32), ((1, 2, tok, width), F32)],
    )
    g_mixed, *lines = run(
        final_attend_kernel,
        mixed_parts,
        [((1, 64, 3 * width), F32)] + [((1, 64), F32)] * 6,
        pltpu.VMEM((GROUP, 64, 768), BF),
    )

    return (
        relay,
        lines[0],
        lines[1],
        g_mixed,
        g_query,
        g_value,
        g_out,
        lines[2],
        lines[3],
        lines[4],
        g_fc,
        g_bfc,
        g_proj,
        lines[5],
    )


def plan(mesh):
    fits = mesh.shape[SECTION] == 2 and mesh.shape[SEQ] == mesh.shape[FSDP] == GROUP
    return fast_body if fits else body


def solution(mesh):
    placed = (
        P(None, ("seq", "fsdp"), None),
        P(None, ("seq", "fsdp"), None),
        P(),
        P("section", "fsdp"),
        P("section", "fsdp"),
        P("section", "fsdp", None),
        P("section", "fsdp"),
        P("section", "fsdp"),
        P("section", "fsdp", None),
        P("section", "fsdp"),
        P("section", "fsdp"),
        P("section", "fsdp"),
        P("section", "fsdp", None),
        P("section", "fsdp"),
        P("section", "fsdp", None),
        P("section", "fsdp"),
    )
    return jax.shard_map(
        plan(mesh),
        mesh=mesh,
        in_specs=placed,
        out_specs=(
            P("section", None, ("seq", "fsdp"), None),
            P("section", ("seq", "fsdp")),
            P("section", ("seq", "fsdp")),
            P("section", ("seq", "fsdp"), None),
            P("section", ("seq", "fsdp")),
            P("section", ("seq", "fsdp")),
            P("section", ("seq", "fsdp"), None),
            P("section", ("seq", "fsdp")),
            P("section", ("seq", "fsdp")),
            P("section", ("seq", "fsdp")),
            P("section", ("seq", "fsdp"), None),
            P("section", ("seq", "fsdp")),
            P("section", ("seq", "fsdp"), None),
            P("section", ("seq", "fsdp")),
        ),
        check_vma=False,
    )
```

```python
import math

import jax
import jax.numpy as jnp
from jax import lax
from jax.experimental import pallas as pl
from jax.experimental.pallas import tpu as pltpu
from jax.sharding import PartitionSpec as P

DH = 64


EPSILON = 1e-05
NEGATIVE = -1e30


def shifted(block, axis, distance):
    devices = range(lax.axis_size(axis))
    route = [(i - distance, i) for i in devices if i - distance in devices]
    return lax.ppermute(block, axis, route)


def layer_norm(values, gain_vec, bias_vec):
    average = jnp.mean(values, axis=-1, keepdims=True)
    centred = values - average
    variance = jnp.mean(centred * centred, axis=-1, keepdims=True)
    return centred * lax.rsqrt(variance + EPSILON) * gain_vec + bias_vec


def gelu_tanh(values):
    return jax.nn.gelu(values, approximate=True)


def mask_rows(seg_row, fsdp_index, n_seq, n_fsdp, tok_rows):
    places = jnp.arange(seg_row.shape[0], dtype=jnp.int32)
    seg_grid = seg_row.reshape(n_seq, n_fsdp, tok_rows)
    place_grid = places.reshape(n_seq, n_fsdp, tok_rows)
    query_ids = lax.dynamic_index_in_dim(seg_grid, fsdp_index, 1, keepdims=False).reshape(-1)
    query_places = lax.dynamic_index_in_dim(place_grid, fsdp_index, 1, keepdims=False).reshape(-1)
    key_ids = jnp.transpose(seg_grid, (1, 0, 2)).reshape(-1)
    key_places = jnp.transpose(place_grid, (1, 0, 2)).reshape(-1)
    same_doc = (query_ids[:, None] == key_ids[None, :]) & (query_ids[:, None] > 0)
    itself = query_places[:, None] == key_places[None, :]
    return (key_places[None, :] <= query_places[:, None]) & (same_doc | itself)


def split_heads(matrix):
    return matrix.reshape(matrix.shape[0], matrix.shape[1] // DH, DH)


def block_rows(matrix, block_len):
    return matrix.reshape((matrix.shape[0] // block_len, block_len) + matrix.shape[1:])


def masked_scores(queries, key_rows, allowed):
    raw_scores = jnp.einsum(
        "qhd,khd->hqk",
        split_heads(queries),
        split_heads(key_rows),
        preferred_element_type=jnp.float32,
    )
    return jnp.where(allowed[None], raw_scores * DH ** (-0.5), NEGATIVE)


def body(
    inputs,
    cotangent,
    segment_ids,
    ln1_gain,
    ln1_bias,
    w_qkv,
    b_query,
    b_value,
    w_out,
    b_out,
    ln2_gain,
    ln2_bias,
    w_fc,
    b_fc,
    w_proj,
    b_proj,
):
    n_seq = lax.axis_size("seq")
    n_fsdp = lax.axis_size("fsdp")
    section_index = lax.axis_index("section")
    fsdp_index = lax.axis_index("fsdp")
    last_section = section_index == 1
    micro, tok_rows, width = inputs.shape
    score_scale = DH ** (-0.5)
    query_count = tok_rows * n_seq
    block_len = math.gcd(query_count, 512)

    def fetch_params():
        return (
            lax.all_gather(ln1_gain[0], "fsdp", axis=0, tiled=True),
            lax.all_gather(ln1_bias[0], "fsdp", axis=0, tiled=True),
            lax.all_gather(w_qkv[0], "fsdp", axis=0, tiled=True),
            lax.all_gather(b_query[0], "fsdp", axis=0, tiled=True),
            lax.all_gather(b_value[0], "fsdp", axis=0, tiled=True),
            lax.all_gather(w_out[0], "fsdp", axis=0, tiled=True),
            lax.all_gather(b_out[0], "fsdp", axis=0, tiled=True),
            lax.all_gather(ln2_gain[0], "fsdp", axis=0, tiled=True),
            lax.all_gather(ln2_bias[0], "fsdp", axis=0, tiled=True),
            lax.all_gather(w_fc[0], "fsdp", axis=0, tiled=True),
            lax.all_gather(b_fc[0], "fsdp", axis=0, tiled=True),
            lax.all_gather(w_proj[0], "fsdp", axis=0, tiled=True),
            lax.all_gather(b_proj[0], "fsdp", axis=0, tiled=True),
        )

    received = jnp.zeros((tok_rows, width), jnp.bfloat16)
    kept_ticks = []
    layer_outs = []
    for tick_index in range(micro + 1):
        params = fetch_params()
        batch_index = jnp.clip(tick_index - section_index, 0, micro - 1)
        seg_row = lax.dynamic_index_in_dim(segment_ids, batch_index, 0, keepdims=False)
        allowed = mask_rows(seg_row, fsdp_index, n_seq, n_fsdp, tok_rows)
        if tick_index < micro:
            first_in = inputs[tick_index].astype(jnp.float32)
        else:
            first_in = jnp.zeros((tok_rows, width), jnp.float32)
        layer_in = jnp.where(last_section, received.astype(jnp.float32), first_in)
        (
            forward_gain_one,
            forward_bias_one,
            forward_w_mixed,
            forward_bias_query,
            forward_bias_value,
            forward_w_output,
            forward_bias_output,
            forward_gain_two,
            forward_bias_two,
            forward_w_hidden,
            forward_bias_hidden,
            forward_w_back,
            forward_bias_back,
        ) = params
        forward_normed = layer_norm(
            layer_in, forward_gain_one.astype(jnp.float32), forward_bias_one.astype(jnp.float32)
        ).astype(jnp.bfloat16)
        mixed_proj = jnp.dot(forward_normed, forward_w_mixed, preferred_element_type=jnp.float32)
        bias_row = jnp.concatenate(
            [forward_bias_query, jnp.zeros_like(forward_bias_query), forward_bias_value]
        ).astype(jnp.float32)
        mixed_tok = (mixed_proj + bias_row).astype(jnp.bfloat16).reshape(tok_rows, 3, width)
        head_rows = lax.all_to_all(mixed_tok, "seq", split_axis=2, concat_axis=0, tiled=True)
        forward_queries = head_rows[:, 0]
        forward_key_rows = lax.all_gather(head_rows[:, 1], "fsdp", axis=0, tiled=True)
        forward_value_rows = lax.all_gather(head_rows[:, 2], "fsdp", axis=0, tiled=True)

        def attend_block(operands):
            query_block, allowed_block = operands
            scores = masked_scores(query_block, forward_key_rows, allowed_block)
            row_top = jnp.max(scores, axis=-1, keepdims=True)
            log_block = row_top + jnp.log(
                jnp.sum(jnp.exp(scores - row_top), axis=-1, keepdims=True)
            )
            attn_weights = jnp.exp(scores - log_block).astype(jnp.bfloat16)
            head_block = jnp.einsum(
                "hqk,khd->qhd",
                attn_weights,
                split_heads(forward_value_rows),
                preferred_element_type=jnp.float32,
            )
            return (head_block.reshape(query_block.shape).astype(jnp.bfloat16), log_block)

        head_blocks, forward_log_total = lax.map(
            attend_block, (block_rows(forward_queries, block_len), block_rows(allowed, block_len))
        )
        head_out = head_blocks.reshape(forward_queries.shape)
        forward_attended = lax.all_to_all(head_out, "seq", split_axis=0, concat_axis=1, tiled=True)
        forward_residual = (
            layer_in
            + jnp.dot(forward_attended, forward_w_output, preferred_element_type=jnp.float32)
            + forward_bias_output.astype(jnp.float32)
        )
        forward_normed_two = layer_norm(
            forward_residual,
            forward_gain_two.astype(jnp.float32),
            forward_bias_two.astype(jnp.float32),
        ).astype(jnp.bfloat16)
        forward_pre_act = jnp.dot(
            forward_normed_two, forward_w_hidden, preferred_element_type=jnp.float32
        ) + forward_bias_hidden.astype(jnp.float32)
        forward_activated = gelu_tanh(forward_pre_act).astype(jnp.bfloat16)
        layer_out = (
            forward_residual
            + jnp.dot(forward_activated, forward_w_back, preferred_element_type=jnp.float32)
            + forward_bias_back.astype(jnp.float32)
        )
        forward_kept = (
            layer_in,
            forward_normed,
            forward_queries,
            forward_key_rows,
            forward_value_rows,
            forward_log_total,
            allowed,
            forward_attended,
            forward_residual,
            forward_normed_two,
            forward_pre_act,
            forward_activated,
        )
        layer_out, kept = (layer_out, forward_kept)
        kept_ticks.append(kept)
        layer_outs.append(layer_out)
        if tick_index < micro:
            received = shifted(layer_out.astype(jnp.bfloat16), "section", 1)
    sent_back = jnp.zeros((tok_rows, width), jnp.bfloat16)
    input_grads = []
    totals = None
    for tick_index in range(micro + 1):
        params = fetch_params()
        later = kept_ticks[min(tick_index + 1, micro)]
        earlier = kept_ticks[max(tick_index - 1, 0)]
        kept = jax.tree.map(
            lambda upper, lower: jnp.where(last_section, upper, lower), later, earlier
        )
        if tick_index < micro:
            top_grad = cotangent[tick_index].astype(jnp.float32)
        else:
            top_grad = jnp.zeros((tok_rows, width), jnp.float32)
        grad_out = jnp.where(last_section, top_grad, sent_back.astype(jnp.float32))
        (
            gain_one,
            bias_one,
            w_mixed,
            bias_query,
            bias_value,
            w_output,
            bias_output,
            gain_two,
            bias_two,
            w_hidden,
            bias_hidden,
            w_back,
            bias_back,
        ) = params
        (
            backward_layer_in,
            normed,
            queries,
            key_rows,
            value_rows,
            log_total,
            backward_allowed,
            attended,
            residual,
            normed_two,
            pre_act,
            activated,
        ) = kept
        grad_back = grad_out.astype(jnp.bfloat16)
        d_w_back = jnp.einsum("cf,cd->fd", activated, grad_back, preferred_element_type=jnp.float32)
        d_bias_back = jnp.sum(grad_back.astype(jnp.float32), axis=0)
        d_activated = jnp.einsum("cd,fd->cf", grad_back, w_back, preferred_element_type=jnp.float32)
        gelu_pull = jax.vjp(gelu_tanh, pre_act)[1]
        d_pre = gelu_pull(d_activated)[0].astype(jnp.bfloat16)
        d_w_hidden = jnp.einsum("cm,cf->mf", normed_two, d_pre, preferred_element_type=jnp.float32)
        d_bias_hidden = jnp.sum(d_pre.astype(jnp.float32), axis=0)
        d_normed_two = jnp.einsum("cf,mf->cm", d_pre, w_hidden, preferred_element_type=jnp.float32)
        norm_pull_two = jax.vjp(
            layer_norm, residual, gain_two.astype(jnp.float32), bias_two.astype(jnp.float32)
        )[1]
        d_resid_part, d_gain_two, d_bias_two = norm_pull_two(d_normed_two)
        d_residual = grad_out + d_resid_part
        grad_attn = d_residual.astype(jnp.bfloat16)
        d_w_output = jnp.einsum(
            "cm,cd->md", attended, grad_attn, preferred_element_type=jnp.float32
        )
        d_bias_output = jnp.sum(grad_attn.astype(jnp.float32), axis=0)
        d_attended = jnp.einsum(
            "cd,md->cm", grad_attn, w_output, preferred_element_type=jnp.float32
        ).astype(jnp.bfloat16)
        d_head = lax.all_to_all(d_attended, "seq", split_axis=1, concat_axis=0, tiled=True)

        def grad_block(carry, operands):
            key_acc, value_acc = carry
            query_block, head_grad_block, allowed_block, log_block = operands
            scores = masked_scores(query_block, key_rows, allowed_block)
            attn_probs = jnp.exp(scores - log_block)
            d_weights = jnp.einsum(
                "qhd,khd->hqk",
                split_heads(head_grad_block),
                split_heads(value_rows),
                preferred_element_type=jnp.float32,
            )
            row_dot = jnp.sum(attn_probs * d_weights, axis=-1, keepdims=True)
            d_scores = (attn_probs * (d_weights - row_dot) * score_scale).astype(jnp.bfloat16)
            d_query_block = (
                jnp.einsum(
                    "hqk,khd->qhd",
                    d_scores,
                    split_heads(key_rows),
                    preferred_element_type=jnp.float32,
                )
                .reshape(query_block.shape)
                .astype(jnp.bfloat16)
            )
            key_acc = key_acc + jnp.einsum(
                "hqk,qhd->khd",
                d_scores,
                split_heads(query_block),
                preferred_element_type=jnp.float32,
            ).reshape(key_rows.shape)
            value_acc = value_acc + jnp.einsum(
                "hqk,qhd->khd",
                attn_probs.astype(jnp.bfloat16),
                split_heads(head_grad_block),
                preferred_element_type=jnp.float32,
            ).reshape(value_rows.shape)
            return ((key_acc, value_acc), d_query_block)

        empty_terms = (
            jnp.zeros(key_rows.shape, jnp.float32),
            jnp.zeros(value_rows.shape, jnp.float32),
        )
        (key_term, value_term), query_blocks = lax.scan(
            grad_block,
            empty_terms,
            (
                block_rows(queries, block_len),
                block_rows(d_head, block_len),
                block_rows(backward_allowed, block_len),
                log_total,
            ),
        )
        d_query = query_blocks.reshape(queries.shape)
        d_key = lax.psum_scatter(key_term, "fsdp", scatter_dimension=0, tiled=True)
        d_value = lax.psum_scatter(value_term, "fsdp", scatter_dimension=0, tiled=True)
        d_heads = jnp.stack(
            [d_query, d_key.astype(jnp.bfloat16), d_value.astype(jnp.bfloat16)], axis=1
        )
        d_mixed = lax.all_to_all(d_heads, "seq", split_axis=0, concat_axis=2, tiled=True)
        d_flat = d_mixed.reshape(tok_rows, 3 * width)
        d_w_mixed = jnp.einsum("cm,cn->mn", normed, d_flat, preferred_element_type=jnp.float32)
        d_bias_query = jnp.sum(d_mixed[:, 0].astype(jnp.float32), axis=0)
        d_bias_value = jnp.sum(d_mixed[:, 2].astype(jnp.float32), axis=0)
        d_normed = jnp.einsum("cn,mn->cm", d_flat, w_mixed, preferred_element_type=jnp.float32)
        norm_pull_one = jax.vjp(
            layer_norm,
            backward_layer_in,
            gain_one.astype(jnp.float32),
            bias_one.astype(jnp.float32),
        )[1]
        d_in_part, d_gain_one, d_bias_one = norm_pull_one(d_normed)
        d_in = d_residual + d_in_part
        d_in, local_grads = (
            d_in,
            (
                d_gain_one,
                d_bias_one,
                d_w_mixed,
                d_bias_query,
                d_bias_value,
                d_w_output,
                d_bias_output,
                d_gain_two,
                d_bias_two,
                d_w_hidden,
                d_bias_hidden,
                d_w_back,
                d_bias_back,
            ),
        )
        input_grads.append(d_in)
        shared = (
            lax.psum_scatter(local_grads[0], ("seq", "fsdp"), scatter_dimension=0, tiled=True),
            lax.psum_scatter(local_grads[1], ("seq", "fsdp"), scatter_dimension=0, tiled=True),
            lax.psum_scatter(local_grads[2], ("seq", "fsdp"), scatter_dimension=0, tiled=True),
            lax.psum_scatter(local_grads[3], ("seq", "fsdp"), scatter_dimension=0, tiled=True),
            lax.psum_scatter(local_grads[4], ("seq", "fsdp"), scatter_dimension=0, tiled=True),
            lax.psum_scatter(local_grads[5], ("seq", "fsdp"), scatter_dimension=0, tiled=True),
            lax.psum_scatter(local_grads[6], ("seq", "fsdp"), scatter_dimension=0, tiled=True),
            lax.psum_scatter(local_grads[7], ("seq", "fsdp"), scatter_dimension=0, tiled=True),
            lax.psum_scatter(local_grads[8], ("seq", "fsdp"), scatter_dimension=0, tiled=True),
            lax.psum_scatter(local_grads[9], ("seq", "fsdp"), scatter_dimension=0, tiled=True),
            lax.psum_scatter(local_grads[10], ("seq", "fsdp"), scatter_dimension=0, tiled=True),
            lax.psum_scatter(local_grads[11], ("seq", "fsdp"), scatter_dimension=0, tiled=True),
            lax.psum_scatter(local_grads[12], ("seq", "fsdp"), scatter_dimension=0, tiled=True),
        )
        totals = shared if totals is None else jax.tree.map(jnp.add, totals, shared)
        if tick_index < micro:
            sent_back = shifted(d_in.astype(jnp.bfloat16), "section", -1)
    section_tops = jnp.stack(layer_outs[1:])
    bottom_grads = jnp.stack(input_grads[1:])
    relay_ends = jnp.where(last_section, section_tops, bottom_grads)[None]
    return (relay_ends,) + tuple((grad_part[None] for grad_part in totals))


BF = jnp.bfloat16
F32 = jnp.float32
GROUP = 4
SECTION, SEQ, FSDP = "section", "seq", "fsdp"


def nt(left, right):
    return lax.dot_general(left, right, (((1,), (1,)), ((), ())), preferred_element_type=F32)


def tn(left, right):
    return lax.dot_general(left, right, (((0,), (0,)), ((), ())), preferred_element_type=F32)


def nn(left, right):
    return jnp.dot(left, right, preferred_element_type=F32)


def spot(start, size):
    return pl.ds(pl.multiple_of(start, size), size)


def call(kernel, ids, args, outs, scratch, anywhere, mib):
    places = [pltpu.HBM if i in anywhere else pltpu.VMEM for i in range(len(args))]
    args = [
        pltpu.with_memory_space_constraint(a, pltpu.HBM) if i in anywhere else a
        for i, a in enumerate(args)
    ]
    return pl.pallas_call(
        kernel,
        name=kernel.__name__.removesuffix("_kernel"),
        out_shape=[jax.ShapeDtypeStruct(shape, dtype) for shape, dtype in outs],
        in_specs=[pl.BlockSpec(memory_space=pltpu.SMEM)]
        + [pl.BlockSpec(memory_space=place) for place in places],
        out_specs=[pl.BlockSpec(memory_space=pltpu.VMEM)] * len(outs),
        scratch_shapes=list(scratch),
        compiler_params=pltpu.CompilerParams(vmem_limit_bytes=mib * 1024 * 1024),
        cost_estimate=pl.CostEstimate(flops=0, bytes_accessed=0, transcendentals=0),
    )(ids, *args)


def after(value, *earlier):
    return lax.optimization_barrier((value, earlier))[0]


def exchange(block, axis, d):
    return lax.ppermute(block, axis, [(i, i ^ d) for i in range(GROUP)])


def trade(blocks, axis):
    return [blocks[0]] + [exchange(blocks[d], axis, d) for d in range(1, GROUP)]


def far_first(blocks):
    return blocks[:1] + blocks[:0:-1]


def gather(block, axis):
    return trade([block] * GROUP, axis)


def swap(block):
    return lax.ppermute(block, SECTION, [(0, 1), (1, 0)])


def normed_rows(values, gain_vec, bias_vec):
    average = jnp.mean(values, axis=-1, keepdims=True)
    centred = values - average
    variance = jnp.mean(centred * centred, axis=-1, keepdims=True)
    return centred * lax.rsqrt(variance + EPSILON) * gain_vec + bias_vec


def norm_pull(values, gain_vec, grad):
    average = jnp.mean(values, axis=-1, keepdims=True)
    centred = values - average
    variance = jnp.mean(centred * centred, axis=-1, keepdims=True)
    inverse = lax.rsqrt(variance + EPSILON)
    unit = centred * inverse
    scaled = grad * gain_vec
    first = jnp.mean(scaled, axis=-1, keepdims=True)
    second = jnp.mean(scaled * unit, axis=-1, keepdims=True)
    pulled = inverse * (scaled - first - unit * second)
    return (
        pulled,
        jnp.sum(grad * unit, axis=0, keepdims=True),
        jnp.sum(grad, axis=0, keepdims=True),
    )


def pick_kernel(ids, w_ref, out_ref, *refs):
    vector_refs, fc_bias_ref, x_ref, g_ref, fc_ref, proj_ref = refs[:8], *refs[8:13]
    mine_ref, send_ref, feed_mine_ref, feed_send_ref, x_out, g_out = refs[13:19]
    held, rows_held, lines, fc_line, sem = refs[19:]
    s, c = ids[0], ids[2]
    width = w_ref.shape[2] // 3
    sources = [w_ref.at[0, spot(s * 64, 64), :]]
    targets = [held]
    for k in range(GROUP):
        sources.append(out_ref.at[0, pl.ds(pl.multiple_of(k * 64 + s * 16, 16), 16), :])
        targets.append(rows_held.at[k])
    for i, ref in enumerate(vector_refs):
        sources.append(ref)
        targets.append(lines.at[i])
    sources += [fc_bias_ref, x_ref.at[c], g_ref.at[c]]
    targets += [fc_line, x_out, g_out]
    first = len(sources)
    for ref, half in ((feed_send_ref, 1 - c), (feed_mine_ref, c)):
        for k in range(GROUP):
            for j in range(GROUP):
                lanes = spot(j * 1024 + k * 256 + half * 128, 128)
                sources.append(fc_ref.at[0, spot(s * 64, 64), lanes])
                targets.append(ref.at[k, 0:64, j * 128 : (j + 1) * 128])
            rows = spot(k * 256 + half * 128 + s * 32, 32)
            sources += [proj_ref.at[0, rows, 0:512], proj_ref.at[0, rows, 512:1024]]
            targets += [ref.at[k, 64:96, :], ref.at[k, 96:128, :]]
    copies = [
        pltpu.make_async_copy(source, target, sem.at[i])
        for i, (source, target) in enumerate(zip(sources, targets))
    ]
    for copy in copies:
        copy.start()
    for copy in copies[:first]:
        copy.wait()

    def head(t, j, k):
        tile = held[:, spot(t * width + j * 256 + (k >> 1) * 128, 128)].astype(F32)
        return tile[:, DH:] if k & 1 else tile[:, :DH]

    foot = [lines[i].astype(F32) for i in range(len(vector_refs))]
    foot += [fc_line[:, k * 256 : (k + 1) * 256].astype(F32) for k in range(GROUP)]
    foot.append(jnp.zeros((4, 256), F32))
    foot = jnp.concatenate(foot, axis=0).astype(BF)
    foot = jnp.concatenate([foot, jnp.zeros((16, 256), BF)], axis=1)
    for ref, half in ((mine_ref, c), (send_ref, 1 - c)):
        for k in range(GROUP):
            for i in range(2):
                j = 2 * half + i
                pair = jnp.concatenate([head(0, j, k), head(1, j, k)], axis=1)
                ref[k, 0:64, i * 128 : (i + 1) * 128] = pair.astype(BF)
            pair = jnp.concatenate([head(2, 2 * half, k), head(2, 2 * half + 1, k)], axis=1)
            ref[k, 0:64, 256:384] = pair.astype(BF)
            for q in range(GROUP):
                ref[k, q * 16 : (q + 1) * 16, 384:512] = rows_held[
                    k, :, spot(half * 512 + q * 128, 128)
                ]
            ref[k, 64:80, :] = foot
    for copy in copies[first:]:
        copy.wait()


def settle_heads_kernel(ids, mine_ref, got_ref, x_ref, *refs):
    first, z = ids[2] == 0, ids[1]
    for d in range(GROUP):
        mine, got = mine_ref[z ^ d], got_ref[z ^ d]
        lower, upper = jnp.where(first, mine, got), jnp.where(first, got, mine)
        refs[d][0:64, :] = lower[0:64]
        refs[d][64:80, 0:256] = lower[64:80, 0:256]
        refs[d][64:80, 256:512] = upper[64:80, 0:256]
        refs[d][80:144, :] = x_ref[:, 0:512]
        refs[d][144:208, :] = x_ref[:, 512:1024]
        refs[GROUP][d] = upper[0:64]


def settle_feed_kernel(ids, mine_ref, got_ref, heads_ref, seg_ref, g_ref, *refs):
    first, z = ids[2] == 0, ids[1]
    numbers = jnp.where(first, seg_ref[0:1, :], seg_ref[1:2, :]).astype(F32)
    marked = jnp.where(numbers > 0.0, numbers, -1.0)
    refs[8][...] = jnp.broadcast_to(marked, (128, numbers.shape[1])).T[:, 0:1]
    refs[9][...] = numbers
    for d in range(GROUP):
        mine, got = mine_ref[z ^ d], got_ref[z ^ d]
        refs[d][0:128, :] = jnp.where(first, mine, got)
        refs[d][128:192, :] = heads_ref[d]
        refs[GROUP + d][0:128, :] = jnp.where(first, got, mine)
        refs[GROUP + d][128:192, :] = g_ref[:, 0:512]
        refs[GROUP + d][192:256, :] = g_ref[:, 512:1024]


def first_heads_kernel(ids, *refs):
    z = ids[1]
    heads_ref, x_refs, vec_refs = refs[GROUP], refs[5:9], refs[9:11]
    for d in range(GROUP):
        block = refs[d][...]
        x_refs[d][:, 0:512] = block[80:144]
        x_refs[d][:, 512:1024] = block[144:208]
        heads_ref[z ^ d] = block[0:64]
        lanes = spot((z ^ d) * 256, 256)
        for layer in range(2):
            rows = block[64:80, layer * 256 : (layer + 1) * 256].astype(F32)
            row = rows[8:9, :]
            for k in range(1, GROUP):
                row = jnp.where(z == k, rows[8 + k : 9 + k, :], row)
            vec_refs[layer][0:8, lanes] = rows[0:8, :]
            vec_refs[layer][8:9, lanes] = row


def part_kernel(ids, *refs):
    for d in range(GROUP):
        refs[GROUP][ids[1] ^ d] = refs[d][0:128, :]
        refs[GROUP + 1][ids[1] ^ d] = refs[d][128:192, :]


def turn_part_kernel(ids, *refs):
    for d in range(GROUP):
        refs[GROUP][ids[1] ^ d] = refs[d][0:128, :]
        refs[GROUP + 1 + d][:, 0:512] = refs[d][128:192, :]
        refs[GROUP + 1 + d][:, 512:1024] = refs[d][192:256, :]


def place_kernel(axis, ids, *refs):
    for d in range(GROUP):
        refs[GROUP][ids[axis] ^ d] = refs[d][...]


def mixed_piece(ref, level):
    return jnp.concatenate([ref[k, level, :, 0:384] for k in range(GROUP)], axis=0)


def head_rows(ref, s):
    rows = []
    for d in range(GROUP):
        for k in range(GROUP):
            tiles = [ref[k, s ^ d, q * 16 : (q + 1) * 16, 384:512] for q in range(GROUP)]
            rows.append(jnp.concatenate(tiles, axis=1))
    return jnp.concatenate(rows, axis=0)


def hidden_piece(ref, level):
    return jnp.concatenate([ref[k, level, 0:64, :] for k in range(GROUP)], axis=0)


def back_share(ref):
    rows = []
    for j in range(GROUP):
        for k in range(GROUP):
            rows.append(jnp.concatenate([ref[k, j, 64:96, :], ref[k, j, 96:128, :]], axis=1))
    return jnp.concatenate(rows, axis=0)


def mixed_kernel(ids, *refs):
    x_refs, own_ref, oth_ref, vec = refs[:4], refs[4], refs[5], refs[6]
    out_refs, nf_ref, packed = refs[7:11], refs[11], refs[12]
    s, z, c = ids[0], ids[1], ids[2]
    gain_vec, bias_vec = vec[0:1, :], vec[1:2, :]
    for d in range(GROUP):
        nf_ref[d * 64 : (d + 1) * 64, :] = normed_rows(
            x_refs[d][...].astype(F32), gain_vec, bias_vec
        ).astype(BF)

    def bias_of(row, j):
        tile = vec[row : row + 1, spot(j * 256 + (z >> 1) * 128, 128)]
        return jnp.where((z & 1) == 1, tile[:, DH:], tile[:, :DH])

    empty = jnp.zeros((1, DH), F32)
    for ref, half in ((own_ref, c), (oth_ref, 1 - c)):
        total = jnp.zeros((GROUP * 64, 384), F32)
        for k in range(GROUP):
            total = total + nn(nf_ref[:, k * 256 : (k + 1) * 256], mixed_piece(ref, k))
        j = 2 * half
        row = jnp.concatenate(
            [
                bias_of(2, j),
                empty,
                bias_of(2, j + 1),
                empty,
                bias_of(3, j),
                bias_of(3, j + 1),
            ],
            axis=1,
        )
        total = total + row
        for i in range(2):
            packed[j + i, 0:256, :] = total[:, i * 128 : (i + 1) * 128].astype(BF)
            values = total[:, 256 + i * DH : 256 + (i + 1) * DH]
            packed[j + i, 256:384, :] = jnp.concatenate(
                [values[:128], values[128:]], axis=1
            ).astype(BF)
    for d in range(GROUP):
        out_refs[d][...] = packed[s ^ d]


def spread(ids, pieces, qk_ref, v_ref):
    s, z = ids[0], ids[1]
    for d in range(GROUP):
        for e in range(GROUP):
            rows = spot(((s ^ d) * GROUP + (z ^ e)) * 64, 64)
            qk_ref[rows, :] = pieces[d][e * 64 : (e + 1) * 64, :]
            lanes = slice(0, DH) if e < 2 else slice(DH, 128)
            start = 256 + (e & 1) * 64
            v_ref[rows, :] = pieces[d][start : start + 64, lanes]


def block_scores(qk_ref, seg_col, seg_row, start, size):
    stop = start + size
    queries = qk_ref[start:stop, 0:DH] * jnp.asarray(DH ** (-0.5), BF)
    scores = nt(queries, qk_ref[0:stop, DH:128])
    same = seg_col[start:stop, :] == seg_row[:, 0:stop]
    q_place = lax.broadcasted_iota(jnp.int32, (size, size), 0)
    k_place = lax.broadcasted_iota(jnp.int32, (size, size), 1)
    near = ((k_place <= q_place) & same[:, start:stop]) | (k_place == q_place)
    near = jnp.where(near, scores[:, start:stop], NEGATIVE)
    if start == 0:
        return near
    return jnp.concatenate([jnp.where(same[:, :start], scores[:, :start], NEGATIVE), near], axis=1)


def attend_kernel(ids, *refs):
    pieces, seg_col, seg_row = refs[:4], refs[4], refs[5]
    out_refs, qk_ref, v_ref, probs_ref, o_ref = refs[6:10], *refs[10:14]
    s, z = ids[0], ids[1]
    spread(ids, pieces, qk_ref, v_ref)
    count = qk_ref.shape[0]
    size = 256
    for start in range(0, count, size):
        scores = block_scores(qk_ref, seg_col, seg_row, start, size)
        top = jnp.max(scores, axis=-1, keepdims=True)
        grown = jnp.exp(scores - top)
        total = jnp.sum(grown, axis=-1, keepdims=True)
        probs = grown * (1.0 / total)
        probs_ref[start : start + size, 0 : start + size] = probs
        o_ref[start : start + size, :] = nn(
            probs.astype(BF), v_ref[0 : start + size, :]
        ).astype(BF)
    for d in range(GROUP):
        for e in range(2):
            left = o_ref[spot(((s ^ d) * GROUP + (z ^ e)) * 64, 64), :]
            right = o_ref[spot(((s ^ d) * GROUP + (z ^ (e + 2))) * 64, 64), :]
            out_refs[d][e * 64 : (e + 1) * 64, :] = jnp.concatenate([left, right], axis=1)


def unpacked(piece):
    return jnp.concatenate([piece[:, :DH], piece[:, DH:]], axis=0)


def output_kernel(ids, *refs):
    pieces, own_ref, oth_ref = refs[:4], refs[4], refs[5]
    out_refs, att_ref = refs[6:10], refs[10]
    s, c = ids[0], ids[2]
    att = jnp.concatenate([unpacked(pieces[d][...]) for d in range(GROUP)], axis=1)
    att_ref[...] = att
    for w_ref, half in ((own_ref, c), (oth_ref, 1 - c)):
        part = nn(att, head_rows(w_ref, s)).astype(BF)
        for d in range(GROUP):
            out_refs[d][:, spot(half * 512, 512)] = part[d * 64 : (d + 1) * 64, :]


def summed(refs):
    blocks = []
    for ref in refs:
        blocks += [ref[...]] if len(ref.shape) == 2 else [ref[k] for k in range(GROUP)]
    total = blocks[0].astype(F32)
    for block in blocks[1:]:
        total = total + block.astype(F32)
    return total


def residual_kernel(ids, *refs):
    x_ref, vec = refs[4], refs[5]
    res_ref, n_ref = refs[6], refs[7]
    res = x_ref[...].astype(F32) + summed(refs[:4]) + vec[4:5, :]
    res_ref[...] = res
    n_ref[...] = normed_rows(res, vec[5:6, :], vec[6:7, :]).astype(BF)


ROOT = math.sqrt(2.0 / math.pi)


def hidden_bias(vec, half):
    return jnp.concatenate(
        [vec[8:9, spot(j * 256 + half * 128, 128)] for j in range(GROUP)], axis=1
    )


def feed_forward(n_refs, shares, vec, c, nf_ref, keep):
    for d in range(GROUP):
        nf_ref[d * 64 : (d + 1) * 64, :] = n_refs[d][...]
    part = jnp.zeros(nf_ref.shape, F32)
    for place, half in ((0, c), (1, 1 - c)):
        cols = slice(place * 512, (place + 1) * 512)
        pre = jnp.zeros((GROUP * 64, 512), F32)
        for d in range(GROUP):
            pre = pre + nn(nf_ref[:, d * 256 : (d + 1) * 256], hidden_piece(shares[place], d))
        pre = pre + hidden_bias(vec, half)
        square = pre * pre
        bend = jnp.tanh(ROOT * pre * (1.0 + 0.044715 * square))
        act = (0.5 * pre * (1.0 + bend)).astype(BF)
        slope = 0.5 * (1.0 + bend) + (0.5 * ROOT) * pre * (1.0 - bend * bend) * (
            1.0 + (3.0 * 0.044715) * square
        )
        keep(cols, act, slope)
        part = part + nn(act, back_share(shares[place]))
    return part.astype(BF)


def feed_backward(g_blocks, shares, slope_ref, out_refs, d_pre_ref, gf_ref):
    for d in range(GROUP):
        gf_ref[d * 64 : (d + 1) * 64, :] = g_blocks[d]
    for place in range(2):
        cols = slice(place * 512, (place + 1) * 512)
        d_act = nt(gf_ref[...], back_share(shares[place]))
        d_pre_ref[:, cols] = (d_act * slope_ref[:, cols]).astype(BF)
    for d in range(GROUP):
        part = nt(d_pre_ref[:, 0:512], hidden_piece(shares[0], d))
        part = (part + nt(d_pre_ref[:, 512:1024], hidden_piece(shares[1], d))).astype(BF)
        for e in range(GROUP):
            out_refs[e][:, d * 256 : (d + 1) * 256] = part[e * 64 : (e + 1) * 64, :]


def feed_kernel(ids, *refs):
    slope_ref, act_ref, nf_ref = refs[11:14]

    def keep(cols, act, slope):
        act_ref[:, cols] = act
        slope_ref[:, cols] = slope

    part = feed_forward(refs[:4], refs[4:6], refs[6], ids[2], nf_ref, keep)
    for d in range(GROUP):
        refs[7 + d][...] = part[d * 64 : (d + 1) * 64, :]


def feed_back_kernel(ids, *refs):
    blocks = [ref[...] for ref in refs[:4]]
    feed_backward(blocks, refs[4:6], refs[6], refs[7:11], refs[11], refs[12])


def feed_turn_kernel(ids, *refs):
    shares, vec, top_refs, outs = refs[8:10], refs[10], refs[11:15], refs[15:19]
    act_ref, nf_ref, d_pre_ref, gf_ref, slope_ref = refs[19:24]

    def keep(cols, act, slope):
        act_ref[:, cols] = act
        slope_ref[:, cols] = slope

    part = feed_forward(refs[:4], shares, vec, ids[2], nf_ref, keep)
    for d in range(GROUP):
        top_refs[d][...] = part[d * 64 : (d + 1) * 64, :]
    blocks = [ref[...] for ref in refs[4:8]]
    feed_backward(blocks, shares, slope_ref, outs, d_pre_ref, gf_ref)


def close_kernel(ids, *refs):
    res_ref, vec, out_ref = refs[4:]
    out = res_ref[...] + summed(refs[:4]) + vec[7:8, :]
    out_ref[...] = out.astype(out_ref.dtype)


def norm_two_back_kernel(ids, *refs):
    res_ref, g_ref, vec = refs[4], refs[5], refs[6]
    d_res_ref, ga_ref, rows_ref = refs[7:10]
    grad = g_ref[...].astype(F32)
    pulled, d_gain, d_bias = norm_pull(res_ref[...], vec[5:6, :], summed(refs[:4]))
    d_res = grad + pulled
    low = d_res.astype(BF)
    d_res_ref[...] = d_res
    ga_ref[...] = low
    rows_ref[0:1, :] = jnp.sum(low.astype(F32), axis=0, keepdims=True)
    rows_ref[1:2, :] = d_gain
    rows_ref[2:3, :] = d_bias
    rows_ref[3:4, :] = jnp.sum(grad.astype(BF).astype(F32), axis=0, keepdims=True)
    rows_ref[4:8, :] = jnp.zeros((4, grad.shape[1]), F32)


def output_back_kernel(ids, *refs):
    g_refs, own_ref, oth_ref = refs[:4], refs[4], refs[5]
    out_refs, gf_ref = refs[6:10], refs[10]
    s, c = ids[0], ids[2]
    for d in range(GROUP):
        gf_ref[d * 64 : (d + 1) * 64, :] = g_refs[d][...]
    d_att = nt(gf_ref[:, spot(c * 512, 512)], head_rows(own_ref, s))
    d_att = d_att + nt(gf_ref[:, spot((1 - c) * 512, 512)], head_rows(oth_ref, s))
    for d in range(GROUP):
        cols = d_att[:, d * DH : (d + 1) * DH]
        out_refs[d][...] = jnp.concatenate([cols[:128], cols[128:]], axis=1).astype(BF)


def feed_grads_kernel(ids, *refs):
    act_ref, gb_ref, nf_ref, d_pre_ref = refs[:4]
    keep_ref, send_ref, sums_ref = refs[4:7]
    for place, out_ref in ((0, keep_ref), (1, send_ref)):
        cols = slice(place * 512, (place + 1) * 512)
        d_fc = tn(nf_ref[...], d_pre_ref[:, cols]).astype(BF)
        for k in range(GROUP):
            out_ref[k, 0:256, :] = d_fc[k * 256 : (k + 1) * 256, :]
        d_proj = tn(act_ref[:, cols], gb_ref[...]).astype(BF)
        for j in range(GROUP):
            rows = d_proj[j * 128 : (j + 1) * 128, :]
            out_ref[j, 256:384, :] = rows[:, 0:512]
            out_ref[j, 384:512, :] = rows[:, 512:1024]
    sums_ref[...] = jnp.sum(d_pre_ref[...].astype(F32), axis=0, keepdims=True)


def attend_back_kernel(ids, *refs):
    d_pieces, qk_ref, v_ref, probs_ref, out_refs = refs[0:4], *refs[4:7], refs[7:11]
    do_ref, dq_ref, dk_ref, dv_ref = refs[11:15]
    s, z = ids[0], ids[1]
    for d in range(GROUP):
        for e in range(GROUP):
            rows = spot(((s ^ d) * GROUP + (z ^ e)) * 64, 64)
            lanes = slice(0, DH) if e < 2 else slice(DH, 128)
            start = (e & 1) * 64
            do_ref[rows, :] = d_pieces[d][start : start + 64, lanes]
    count = qk_ref.shape[0]
    size = 256
    for start in range(0, count, size):
        stop = start + size
        probs = probs_ref[start:stop, 0:stop]
        d_out = do_ref[start:stop, :]
        d_weights = nt(d_out, v_ref[0:stop, :])
        row_dot = jnp.sum(probs * d_weights, axis=-1, keepdims=True)
        d_scores = (probs * (d_weights - row_dot) * DH ** (-0.5)).astype(BF)
        dq_ref[start:stop, :] = nn(d_scores, qk_ref[0:stop, DH:128])
        dk = tn(d_scores, qk_ref[start:stop, 0:DH])
        dv = tn(probs.astype(BF), d_out)
        if start:
            dk_ref[0:start, :] += dk[0:start]
            dv_ref[0:start, :] += dv[0:start]
        dk_ref[start:stop, :] = dk[start:stop]
        dv_ref[start:stop, :] = dv[start:stop]
    for d in range(GROUP):
        for e in range(GROUP):
            rows = spot(((s ^ d) * GROUP + (z ^ e)) * 64, 64)
            out_refs[d][e * 64 : (e + 1) * 64, :] = jnp.concatenate(
                [dq_ref[rows, :], dk_ref[rows, :]], axis=1
            ).astype(BF)
        for e in range(2):
            left = dv_ref[spot(((s ^ d) * GROUP + (z ^ e)) * 64, 64), :]
            right = dv_ref[spot(((s ^ d) * GROUP + (z ^ (e + 2))) * 64, 64), :]
            out_refs[d][256 + e * 64 : 320 + e * 64, :] = jnp.concatenate(
                [left, right], axis=1
            ).astype(BF)


def mixed_back_kernel(ids, *refs):
    pieces, own_ref, oth_ref = refs[:4], refs[4], refs[5]
    out_refs, dm_ref, held = refs[6:10], refs[10], refs[11]
    s, c = ids[0], ids[2]
    for d in range(GROUP):
        held[d] = pieces[d][...]
    for place, half in ((0, c), (1, 1 - c)):
        base = place * 384
        values = []
        for i in range(2):
            d = (2 * half + i) ^ s
            dm_ref[:, base + i * 128 : base + (i + 1) * 128] = held[d, 0:256, :]
            values.append(unpacked(held[d, 256:384, :]))
        dm_ref[:, base + 256 : base + 384] = jnp.concatenate(values, axis=1)
    for k in range(GROUP):
        part = nt(dm_ref[:, 0:384], mixed_piece(own_ref, k))
        part = (part + nt(dm_ref[:, 384:768], mixed_piece(oth_ref, k))).astype(BF)
        for d in range(GROUP):
            out_refs[d][:, k * 256 : (k + 1) * 256] = part[d * 64 : (d + 1) * 64, :]


def attend_grads_kernel(ids, *refs):
    nf_ref, dm_ref, att_ref, ga_ref, two_ref, fc_ref = refs[:6]
    part_refs, x_refs = refs[6:10], refs[10:14]
    keep_ref, send_ref, lines = refs[14:17]
    s, c = ids[0], ids[2]
    d_gain = d_bias = 0.0
    for d in range(GROUP):
        grad = part_refs[d][...].astype(F32)
        values = x_refs[d][...].astype(F32)
        average = jnp.mean(values, axis=-1, keepdims=True)
        centred = values - average
        variance = jnp.mean(centred * centred, axis=-1, keepdims=True)
        unit = centred * lax.rsqrt(variance + EPSILON)
        d_gain = d_gain + jnp.sum(grad * unit, axis=0, keepdims=True)
        d_bias = d_bias + jnp.sum(grad, axis=0, keepdims=True)
    lines[0:1, :] = d_gain
    lines[1:2, :] = d_bias
    lines[2:6, :] = two_ref[0:4, :]
    lines[6:8, :] = jnp.zeros((2, d_gain.shape[1]), F32)
    for place, out_ref, half in ((0, keep_ref, c), (1, send_ref, 1 - c)):
        base = place * 384
        d_w = tn(nf_ref[...], dm_ref[:, base : base + 384]).astype(BF)
        sums = jnp.sum(dm_ref[:, base : base + 384].astype(F32), axis=0, keepdims=True)
        for k in range(GROUP):
            out_ref[k, 0:256, 0:384] = d_w[k * 256 : (k + 1) * 256, :]
            mine = (k >> 1) == half
            i = k & 1
            query = sums[:, i * 128 : i * 128 + DH]
            value = sums[:, 256 + i * DH : 256 + (i + 1) * DH]
            first = place * 512 + k * 128
            line = jnp.concatenate(
                [
                    fc_ref[:, first : first + 128],
                    jnp.where(mine, query, 0.0),
                    jnp.where(mine, value, 0.0),
                    jnp.zeros((1, 128), F32),
                ],
                axis=1,
            )
            foot = jnp.concatenate([line, jnp.zeros((7, 384), F32)], axis=0)
            foot = jnp.concatenate([lines[:, spot(k * 256 + half * 128, 128)], foot], axis=1)
            foot = jnp.concatenate([foot, jnp.zeros((8, 512), F32)], axis=0)
            out_ref[k, 256:272, :] = foot.astype(BF)
        d_out = tn(att_ref[...], ga_ref[:, spot(half * 512, 512)]).astype(BF)
        for d in range(GROUP):
            for q in range(GROUP):
                out_ref[s ^ d, q * 64 : (q + 1) * 64, 384:512] = d_out[
                    d * 64 : (d + 1) * 64, q * 128 : (q + 1) * 128
                ]


def norm_one_back_kernel(ids, *refs):
    x_ref, d_res_ref, vec = refs[4], refs[5], refs[6]
    pulled, _, _ = norm_pull(x_ref[...].astype(F32), vec[0:1, :], summed(refs[:4]))
    refs[7][...] = (d_res_ref[...] + pulled).astype(BF)


def ends_kernel(ids, *refs):
    x_ref, d_res_ref, vec, top_ref = refs[4:8]
    pulled, _, _ = norm_pull(x_ref[...].astype(F32), vec[0:1, :], summed(refs[:4]))
    bottom, top = d_res_ref[...] + pulled, top_ref[...]
    first = ids[2] == 0
    refs[8][...] = jnp.where(first, bottom, top)
    refs[9][...] = jnp.where(first, top, bottom)


def add_kernel(ids, left_ref, right_ref, *out_refs):
    for d in range(GROUP):
        k = ids[0] ^ d
        out_refs[d][...] = (left_ref[k].astype(F32) + right_ref[k].astype(F32)).astype(BF)


def choose_kernel(ids, *refs):
    lower, upper = summed(refs[:4]).astype(BF), summed(refs[4:8]).astype(BF)
    first = ids[2] == 0
    refs[8][...] = jnp.where(first, lower, upper)
    refs[9][...] = jnp.where(first, upper, lower)


def split_feed_kernel(ids, own_ref, oth_ref, *refs):
    for d in range(GROUP):
        rows = spot((ids[1] ^ d) * 64, 64)
        refs[d][:, 0:512] = own_ref[rows, :]
        refs[d][:, 512:1024] = oth_ref[rows, :]


def split_attend_kernel(ids, own_ref, oth_ref, *refs):
    bfc_ref, query_ref, value_ref = refs[GROUP:]
    s, z, c = ids[0], ids[1], ids[2]
    foots = (own_ref[256:272, :], oth_ref[256:272, :])
    for d in range(GROUP):
        rows = spot((z ^ d) * 64, 64)
        refs[d][0:64, 0:384] = own_ref[rows, 0:384]
        refs[d][0:64, 384:768] = oth_ref[rows, 0:384]
        lines = jnp.where(((z ^ d) >> 1) == c, foots[0][:, 0:128], foots[1][:, 0:128])
        refs[d][64:80, :] = jnp.concatenate([lines, jnp.zeros((16, 640), BF)], axis=1)
    own, oth = foots[0][0:1, :].astype(F32), foots[1][0:1, :].astype(F32)
    lower, upper = jnp.where(c == 0, own, oth), jnp.where(c == 0, oth, own)
    bfc_ref[:, 0:128] = lower[:, 128:256]
    bfc_ref[:, 128:256] = upper[:, 128:256]
    line = jnp.where((s >> 1) == 0, lower, upper)
    query_ref[...] = line[:, 256 : 256 + DH]
    value_ref[...] = line[:, 256 + DH : 384]


def final_feed_kernel(ids, *refs):
    mine_ref, got_ref, *rest_refs, fc_out, relay_out, back_out, output_out = refs[GROUP:]
    for place, half in ((0, ids[2]), (1, 1 - ids[2])):
        feed_ref, attend_ref = rest_refs[place], rest_refs[2 + place]
        rows = spot(half * 128, 128)
        back_out[0, rows, 0:512] = feed_ref[256:384, :].astype(F32)
        back_out[0, rows, 512:1024] = feed_ref[384:512, :].astype(F32)
        for q in range(GROUP):
            output_out[0, :, spot(half * 512 + q * 128, 128)] = attend_ref[
                q * 64 : (q + 1) * 64, 384:512
            ].astype(F32)
    first = ids[2] == 0
    mine, got = mine_ref[...], got_ref[...]
    relay_out[0, 0] = jnp.where(first, mine, got)
    relay_out[0, 1] = jnp.where(first, got, mine)
    for place, half in ((0, ids[2]), (1, 1 - ids[2])):
        for d in range(GROUP):
            for j in range(GROUP):
                start = place * 512 + j * 128
                lanes = spot(j * 1024 + (ids[1] ^ d) * 256 + half * 128, 128)
                fc_out[0, :, lanes] = refs[d][:, start : start + 128].astype(F32)


def final_attend_kernel(ids, *refs):
    mixed, mixed_out, line_outs, held = refs[:4], refs[4], refs[5:11], refs[11]
    z, c = ids[1], ids[2]
    width = mixed_out.shape[2] // 3
    lines = 0.0
    for d in range(GROUP):
        held[z ^ d] = mixed[d][0:64, :]
        lines = lines + mixed[d][64:80, 0:128].astype(F32)
    lines = jnp.where((z & 1) == 1, lines[:, DH:], lines[:, :DH])
    for i, ref in enumerate(line_outs):
        ref[...] = lines[i : i + 1, :]
    for place, half in ((0, c), (1, 1 - c)):
        base = place * 384
        for pair in range(2):
            for i in range(2):
                tiles = []
                for source in (2 * pair, 2 * pair + 1):
                    qk = held[source, :, base + i * 128 : base + (i + 1) * 128].astype(F32)
                    v = held[source, :, base + 256 + i * DH : base + 256 + (i + 1) * DH]
                    tiles.append((qk[:, :DH], qk[:, DH:], v.astype(F32)))
                for t in range(3):
                    start = t * width + (2 * half + i) * 256 + pair * 128
                    mixed_out[0, :, spot(start, 128)] = jnp.concatenate(
                        [tiles[0][t], tiles[1][t]], axis=1
                    )


def fast_body(
    inputs,
    cotangent,
    segment_ids,
    ln1_gain,
    ln1_bias,
    w_qkv,
    b_query,
    b_value,
    w_out,
    b_out,
    ln2_gain,
    ln2_bias,
    w_fc,
    b_fc,
    w_proj,
    b_proj,
):
    s, z, c = lax.axis_index(SEQ), lax.axis_index(FSDP), lax.axis_index("section")
    ids = jnp.stack([s, z, c]).astype(jnp.int32)
    tok, width = inputs.shape[1:]
    count = segment_ids.shape[1]
    tall = GROUP * tok
    piece = ((384, 128), BF)
    small = ((128, 128), BF)
    part = ((tok, width), BF)
    wide = ((tall, width), BF)
    line = ((tok, width), F32)
    share = ((272, 512), BF)
    feed_share = ((512, 512), BF)
    done, awaited, lagging = [], [], []

    def run(kernel, args, outs, *scratch, anywhere=(), mib=16, aside=False):
        args = list(args)
        earlier = done[-1:] + ([] if aside else list(awaited))
        if earlier:
            args[0] = after(args[0], *earlier)
        if not aside:
            awaited[:] = lagging
            lagging.clear()
        result = list(call(kernel, ids, args, outs, scratch, anywhere, mib))
        done.append(result[-1])
        return result

    def beside(blocks, got, axis, *which, lag=False):
        for d in which:
            got[d] = exchange(after(blocks[d], done[-1]), axis, d)
            (lagging if lag else awaited).append(got[d])

    def now(blocks):
        return [after(block, done[-1]) for block in blocks]

    def of(kernel, axis):
        def bound(*refs):
            kernel(axis, *refs)

        bound.__name__ = kernel.__name__
        return bound

    def shared(pieces, axis, shape, aside=False):
        (whole,) = run(of(place_kernel, axis), pieces, [(shape, BF)], aside=aside)
        return [whole, swap(whole)]

    mine, send, feed_mine, feed_send, x, grad = run(
        pick_kernel,
        [w_qkv, w_out]
        + [ln1_gain, ln1_bias, b_query, b_value, b_out, ln2_gain, ln2_bias, b_proj, b_fc]
        + [inputs, cotangent, w_fc, w_proj],
        [((GROUP, 80, 512), BF)] * 2 + [((GROUP, 128, 512), BF)] * 2 + [part] * 2,
        pltpu.VMEM((64, 3 * width), BF),
        pltpu.VMEM((GROUP, 16, width), BF),
        pltpu.VMEM((8, 1, 256), BF),
        pltpu.VMEM((1, 1024), BF),
        pltpu.SemaphoreType.DMA((64,)),
        anywhere=range(15),
    )
    *heads, upper_heads = run(
        settle_heads_kernel,
        [mine, swap(send), x],
        [((208, 512), BF)] * 4 + [((GROUP, 64, 512), BF)],
    )
    heads = trade(heads, FSDP)
    feed_got = swap(feed_send)
    *rest, seg_col, seg_row = run(
        settle_feed_kernel,
        [feed_mine, feed_got, upper_heads, segment_ids, grad],
        [((192, 512), BF)] * 4
        + [((256, 512), BF)] * 4
        + [((count, 1), F32), ((1, count), F32)],
        aside=True,
    )
    rests = [rest[:4], rest[4:]]
    rest_got = [list(blocks) for blocks in rests]
    heads, *rest = run(
        first_heads_kernel,
        heads,
        [((GROUP, 64, 512), BF)] + [part] * 4 + [((16, width), F32)] * 2,
    )
    x_all, vec = rest[:4], rest[4:]
    heads = gather(heads, SEQ)
    for blocks, got in zip(rests, rest_got):
        beside(blocks, got, FSDP, 1)
    head_w = [shared(heads, 0, (GROUP, GROUP, 64, 512)), None]

    feed_w = [None, None]
    kept = []
    for layer in range(2):
        *packed, normed = run(
            mixed_kernel,
            x_all + head_w[layer] + [vec[layer]],
            [piece] * 4 + [wide],
            pltpu.VMEM((GROUP, 384, 128), BF),
        )
        qkv = trade(packed, SEQ)
        got = rest_got[layer]
        beside(rests[layer], got, FSDP, 3, 2, lag=True)
        *heads, qk_rows, v_rows, probs = run(
            attend_kernel,
            qkv + [seg_col, seg_row],
            [small] * 4 + [((count, 128), BF), ((count, DH), BF), ((count, count), F32)],
            pltpu.VMEM((count, DH), BF),
        )
        heads = trade(heads, SEQ)
        *parts, att = run(
            output_kernel,
            heads + head_w[layer],
            [part] * 4 + [((tall, 256), BF)],
        )
        parts = trade(parts, FSDP)
        if layer == 0:
            feed, heads_later = run(
                part_kernel,
                got,
                [((GROUP, 128, 512), BF), ((GROUP, 64, 512), BF)],
                aside=True,
            )
        else:
            feed, *grad_all = run(
                turn_part_kernel, got, [((GROUP, 128, 512), BF)] + [part] * 4, aside=True
            )
        feeds = [feed] * GROUP
        beside(feeds, feeds, SEQ, 1, 2)
        res, n_two = run(
            residual_kernel, far_first(parts) + [x, vec[layer]], [line, part]
        )
        n_all = gather(n_two, FSDP)
        beside([feed] * GROUP, feeds, SEQ, 3)
        feeds[0] = after(feeds[0], *n_all)
        feed_w[layer] = shared(feeds, 0, (GROUP, GROUP, 128, 512))
        kept.append((x, normed, (qk_rows, v_rows, probs), att, res, x_all))
        if layer == 0:
            *parts, slope, act, n_full = run(
                feed_kernel,
                n_all + feed_w[0] + [vec[0]],
                [part] * 4 + [((tall, 1024), F32), ((tall, 1024), BF), wide],
            )
            parts = trade(parts, FSDP)
            heads = [heads_later] * GROUP
            beside(heads, heads, SEQ, 1, 2)
            (x,) = run(close_kernel, far_first(parts) + [res, vec[0]], [part])
            x_all = gather(x, FSDP)
            beside([heads_later] * GROUP, heads, SEQ, 3)
            heads[0] = after(heads[0], *x_all)
            head_w[1] = shared(heads, 0, (GROUP, GROUP, 64, 512))
        else:
            turn = run(
                feed_turn_kernel,
                n_all + grad_all + feed_w[1] + [vec[1]],
                [part] * 8 + [((tall, 1024), BF), wide, ((tall, 1024), BF), wide],
                pltpu.VMEM((tall, 1024), F32),
                mib=20,
            )

    def feed_terms(act, gb_full, n_full, d_pre):
        keep, send, sums = run(
            feed_grads_kernel,
            [act, gb_full, n_full, d_pre],
            [((GROUP, 512, 512), BF)] * 2 + [((1, 1024), F32)],
            aside=True,
        )
        return keep, swap(send), sums

    def attend_terms(layer, two_rows, fc_sums, parts, d_mixed, ga_full):
        x, normed, _, att, _, x_all = kept[layer]
        keep, send = run(
            attend_grads_kernel,
            [normed, d_mixed, att, ga_full, two_rows, fc_sums] + parts + x_all,
            [((GROUP,) + share[0], BF)] * 2,
            pltpu.VMEM((8, width), F32),
            aside=True,
        )
        return keep, swap(send)

    def total(keep, got, shape):
        return run(add_kernel, [keep, got], [shape] * 4, aside=True)

    def norm_two_back(layer, parts, grad):
        return run(
            norm_two_back_kernel,
            far_first(parts) + [kept[layer][4], grad, vec[layer]],
            [line, part, ((8, width), F32)],
        )

    def output_back(layer, ga_all):
        return run(
            output_back_kernel,
            ga_all + head_w[layer],
            [small] * 4 + [wide],
        )

    def attend_back(layer, d_heads):
        return run(
            attend_back_kernel,
            d_heads + list(kept[layer][2]),
            [piece] * 4,
            pltpu.VMEM((count, DH), BF),
            *[pltpu.VMEM((count, DH), F32)] * 3,
        )

    def mixed_back(layer, d_pieces):
        return run(
            mixed_back_kernel,
            d_pieces + head_w[layer],
            [part] * 4 + [((tall, 768), BF)],
            pltpu.VMEM((GROUP, 384, 128), BF),
        )

    def norm_one_back(layer, parts, d_res):
        return run(
            norm_one_back_kernel,
            far_first(parts) + [kept[layer][0], d_res, vec[layer]],
            [part],
        )[0]

    top_parts, parts = turn[:4], trade(turn[4:8], FSDP)
    tops = list(top_parts)
    beside(top_parts, tops, FSDP, 1)
    keep, got, fc_sums = feed_terms(turn[8], turn[11], turn[9], turn[10])
    terms = total(keep, got, feed_share)
    d_res, ga, two_rows = norm_two_back(1, parts, grad)
    ga_all = gather(ga, FSDP)
    upper_feed = list(terms)
    beside(terms, upper_feed, SEQ, 1, 2)
    *d_heads, ga_full = output_back(1, ga_all)
    d_heads = trade(d_heads, SEQ)
    beside(top_parts, tops, FSDP, 3, 2, lag=True)
    d_pieces = trade(attend_back(1, d_heads), SEQ)
    *sent, d_mixed = mixed_back(1, d_pieces)
    parts = trade(sent, FSDP)
    beside(terms, upper_feed, SEQ, 3)
    keep, got = attend_terms(1, two_rows, fc_sums, sent, d_mixed, ga_full)
    (top,) = run(close_kernel, tops + [kept[1][4], vec[1]], [line], aside=True)
    upper_terms = total(keep, got, share)
    low = norm_one_back(1, parts, d_res)
    g_all = gather(low, FSDP)
    upper_attend = list(upper_terms)
    beside(upper_terms, upper_attend, SEQ, 1, 2)

    *parts, d_pre, gb_full = run(
        feed_back_kernel,
        g_all + feed_w[0] + [slope],
        [part] * 4 + [((tall, 1024), BF), wide],
    )
    parts = trade(parts, FSDP)
    beside(upper_terms, upper_attend, SEQ, 3)
    keep, got, fc_sums = feed_terms(act, gb_full, n_full, d_pre)
    terms = total(keep, got, feed_share)
    d_res, ga, two_rows = norm_two_back(0, parts, low)
    ga_all = gather(ga, FSDP)
    lower_feed = list(terms)
    beside(terms, lower_feed, SEQ, 1, 2)
    *d_heads, ga_full = output_back(0, ga_all)
    d_heads = trade(d_heads, SEQ)
    beside(terms, lower_feed, SEQ, 3)
    d_pieces = trade(attend_back(0, d_heads), SEQ)
    mine, theirs = run(choose_kernel, lower_feed + upper_feed, [feed_share] * 2, aside=True)
    got = swap(theirs)
    blocks = run(
        split_feed_kernel,
        [mine, got],
        [((64, 1024), BF)] * 4,
        aside=True,
    )
    feed_pair = [mine, got]
    fc_parts = list(blocks)
    beside(blocks, fc_parts, FSDP, 3, 2)
    *sent, d_mixed = mixed_back(0, d_pieces)
    keep, got = attend_terms(0, two_rows, fc_sums, sent, d_mixed, ga_full)
    lower_attend = trade(total(keep, got, share), SEQ)

    parts = trade(now(sent), FSDP)
    lower_attend[0] = after(lower_attend[0], *parts)
    mine, theirs = run(choose_kernel, lower_attend + upper_attend, [share] * 2)
    got = swap(theirs)
    ends_mine, ends_theirs = run(
        ends_kernel, far_first(parts) + [kept[0][0], d_res, vec[0], top], [line] * 2
    )
    ends_got = swap(ends_theirs)
    *blocks, g_bfc, g_query, g_value = run(
        split_attend_kernel,
        [mine, got],
        [((80, 768), BF)] * 4
        + [((1, 256), F32), ((1, 64), F32), ((1, 64), F32)],
    )
    mixed_parts = trade(blocks, FSDP)
    fc_parts[1] = exchange(after(fc_parts[1], g_bfc), FSDP, 1)
    g_fc, relay, g_proj, g_out = run(
        final_feed_kernel,
        fc_parts + [ends_mine, ends_got] + feed_pair + [mine, got],
        [((1, 64, 4096), F32), ((1, 2, tok, width), F32)]
        + [((1, 256, width), F32), ((1, 64, width), F32)],
    )
    g_mixed, *lines = run(
        final_attend_kernel,
        mixed_parts,
        [((1, 64, 3 * width), F32)] + [((1, 64), F32)] * 6,
        pltpu.VMEM((GROUP, 64, 768), BF),
    )

    return (
        relay,
        lines[0],
        lines[1],
        g_mixed,
        g_query,
        g_value,
        g_out,
        lines[2],
        lines[3],
        lines[4],
        g_fc,
        g_bfc,
        g_proj,
        lines[5],
    )


def plan(mesh):
    fits = mesh.shape[SECTION] == 2 and mesh.shape[SEQ] == mesh.shape[FSDP] == GROUP
    return fast_body if fits else body


def solution(mesh):
    placed = (
        P(None, ("seq", "fsdp"), None),
        P(None, ("seq", "fsdp"), None),
        P(),
        P("section", "fsdp"),
        P("section", "fsdp"),
        P("section", "fsdp", None),
        P("section", "fsdp"),
        P("section", "fsdp"),
        P("section", "fsdp", None),
        P("section", "fsdp"),
        P("section", "fsdp"),
        P("section", "fsdp"),
        P("section", "fsdp", None),
        P("section", "fsdp"),
        P("section", "fsdp", None),
        P("section", "fsdp"),
    )
    return jax.shard_map(
        plan(mesh),
        mesh=mesh,
        in_specs=placed,
        out_specs=(
            P("section", None, ("seq", "fsdp"), None),
            P("section", ("seq", "fsdp")),
            P("section", ("seq", "fsdp")),
            P("section", ("seq", "fsdp"), None),
            P("section", ("seq", "fsdp")),
            P("section", ("seq", "fsdp")),
            P("section", ("seq", "fsdp"), None),
            P("section", ("seq", "fsdp")),
            P("section", ("seq", "fsdp")),
            P("section", ("seq", "fsdp")),
            P("section", ("seq", "fsdp"), None),
            P("section", ("seq", "fsdp")),
            P("section", ("seq", "fsdp"), None),
            P("section", ("seq", "fsdp")),
        ),
        check_vma=False,
    )
```
